32 devices in a mesh: tiles: 8 (over z, x), far: 4 (over y, core).
Axes of the slice: x: 2, y: 2, z: 4, core: 2. Of those that a mesh axis runs over, the one named last changes fastest.
Arguments:
- panel_geometry: float32 [32, 6, 128], P('tiles'), may hold values from -1 to 1
- adjoint: bfloat16 [32, 16, 128], P('tiles', 'far'), may hold values from -6 to 6
- strengths: bfloat16 [32, 16, 128], P('tiles', 'far'), may hold values from -6 to 6
- pair_target: int32 [256], P('tiles'), may hold values from 0 to 3
- pair_owner: int32 [256, 1], P('tiles'), may hold values from 0 to 7; in each aligned block of 32 rows (0 to 31, 32 to 63, ...) at most 8 rows name the same one
- pair_source: int32 [256], P('tiles'), may hold values from 0 to 3
- pair_order: int32 [256], P('tiles'), may hold values from 1 to 3
- pair_count: int32 [8], P('tiles'), may hold values from 24 to 32, as said below
- corner_vertex: int32 [32, 4, 128], P('tiles'), may hold values from 0 to 4095, as said below
Outputs:
- vertex_grad: float32 [3, 4096], P(None, 'tiles')
The draws below stay inside these ranges and needn't reach their ends.
Inputs may be any that keep to these rules, and one draw needn't show every extreme that they name: `pair_owner`: in the 32 slots of one list no owner is named more than 8 times; some list names one owner exactly 8 times. `pair_count`: some list is full with 32 live pairs. `corner_vertex`: every corner of a panel on tiles index t is a vertex owned by index t, t - 1, t + 1 or t + 8 / 2 (cyclically; the last is the mirrored half of the airframe); vertex v is owned by index v // 512.
All inputs are finite; a program needn't handle non-finite values.
Results may differ from the reference program's by a relative error of at most 0.00035.
Values may be sent and summed in bfloat16 or wider, within the bound.
No kernel may reach another device: no remote copies, remote signals or barrier semaphores. Data moves between devices by JAX's collectives and lax.ppermute only.
A program may use at most 128 MiB of HBM per device.

```python
import math
import jax
import jax.numpy as jnp
import numpy as np
from jax import lax

PB = 128
B_DEV = 4
PAIRS_DEV = 32
CH = 16
BLOCKS = 32
PAIRS = 256
CAP = 8
VERTS = 4096
N_TILES = 8


def draw_pair_count(key, part):
    base = jax.random.randint(jax.random.fold_in(key, 11), (N_TILES,), 3 * PAIRS_DEV // 4, PAIRS_DEV + 1, dtype=jnp.int32)
    busiest = jax.random.permutation(jax.random.fold_in(key, 12), N_TILES)[:max(1, N_TILES // 16)]
    return base.at[busiest].set(jnp.int32(PAIRS_DEV))


def draw_corner_vertex(key, part):
    vertex_width = B_DEV * PB
    owners = jnp.arange(BLOCKS, dtype=jnp.int32) // B_DEV
    rolled = jax.random.randint(jax.random.fold_in(key, 21), (BLOCKS, 4, PB), 0, 20, dtype=jnp.int32)
    moved = jnp.where(rolled < 3, -1, jnp.where(rolled < 5, N_TILES // 2, jnp.where(rolled > 16, 1, 0))).astype(jnp.int32)
    holder = (owners[:, None, None] + moved + N_TILES) % N_TILES
    within = jax.random.randint(jax.random.fold_in(key, 22), (BLOCKS, 4, PB), 0, vertex_width, dtype=jnp.int32)
    return holder * vertex_width + within


def set_ends(result, key, low, top_value):
    place = [jax.random.randint(jax.random.fold_in(key, axis), (), 0, length) for axis, length in enumerate(result.shape)]
    longest = result.shape.index(max(result.shape))
    neighbour = place[:longest] + [(place[longest] + 1) % result.shape[longest]] + place[longest + 1:]
    return result.at[tuple(place)].set(low).at[tuple(neighbour)].set(top_value)


def steps_of(stream_key, dims, split, least, largest):
    loudness = 1.0
    for axis_at, parts in split:
        draws = jax.random.uniform(jax.random.fold_in(jax.random.fold_in(stream_key, 6), axis_at), (parts,), jnp.float32, least / len(split), largest / len(split))
        loudness = loudness * jnp.repeat(jnp.exp(draws), dims[axis_at] // parts).reshape((-1,) + (1,) * (len(dims) - 1 - axis_at))
    return loudness


def shared_out(own_key, own, number, rows, number_of, top, limit, lean):
    ranking = jax.random.permutation(own_key, number_of)
    crowded, usual = load_shares(number_of, rows * top, limit, lean, True), load_shares(number_of, rows * top, limit, lean, False)
    places = jnp.arange(number_of)

    def named(lengths, offset_by):
        used = int((lengths > 0).sum())
        fixed = max(1, used // 4)
        shifted = fixed + (places - fixed + offset_by * (used - fixed)) % max(1, number_of - fixed)
        return jnp.zeros((number_of,), jnp.int32).at[ranking[jnp.where(places < fixed, places, shifted)]].set(jnp.asarray(lengths, jnp.int32))

    lengths = jnp.where(number % 4 == 0, named(crowded, number // 4), named(usual, number - number // 4 - 1))
    mixed = jax.random.permutation(jax.random.fold_in(own, 3), number_of)
    giver, sink = mixed[0:number_of // 2 * 2:2], mixed[1:number_of // 2 * 2:2]
    room = jnp.minimum(lengths[giver] - 1, limit - lengths[sink]) // 2
    room = jnp.where((giver == ranking[0]) | (sink == ranking[0]) | (lengths[sink] == 0), 0, jnp.maximum(room, 0))
    shifted = jax.random.randint(jax.random.fold_in(own, 4), (number_of // 2,), 0, 1 << 20) % (room + 1)
    lengths = lengths.at[giver].add(-shifted).at[sink].add(shifted)
    labels = jnp.searchsorted(jnp.cumsum(lengths), jnp.arange(rows * top), side="right").astype(jnp.int32)
    grid = labels.reshape(top, rows).T
    grid = grid[jax.random.permutation(jax.random.fold_in(own, 1), rows)]
    offset_by = jax.random.randint(jax.random.fold_in(own, 2), (rows, 1), 0, top)
    return jnp.take_along_axis(grid, (jnp.arange(top)[None, :] + offset_by) % top, axis=1)


def load_shares(count, total, bound, skew, full):
    portions = [(1 << 20) // math.isqrt(standing ** skew) + 1 for standing in range(1, count + 1)]
    largest = bound if full else min(bound, max(-(-total // count), total * portions[0] // sum(portions)))
    least = 1 if total - largest >= count - 1 else 0
    holding, spare = [largest] + [least] * (count - 1), total - largest - least * (count - 1)
    while spare > 0:
        candidates = [i for i in range(1, count) if holding[i] < largest] or [i for i in range(1, count) if holding[i] < bound]
        pool, remaining = sum([portions[i] for i in candidates]), spare
        for i in candidates:
            addition = min(bound - holding[i], max(1, remaining * portions[i] // pool), spare)
            holding[i] = holding[i] + addition
            spare = spare - addition
    return np.array(holding)


def gaussian(key, shape, width, reach, cuts=(), kind=jnp.bfloat16):
    loudness = steps_of(key, shape, cuts, -0.22, 0.18) if cuts else 1.0
    values = jax.random.normal(key, shape, jnp.float32) * width * loudness
    return jnp.minimum(jnp.maximum(values, -reach), reach).astype(kind)


def setup_inputs(seed: int = 0) -> dict:
    streams_of = jax.random.split(jax.random.key(seed), 10)
    panel_geometry = jnp.clip(jax.random.uniform(streams_of[0], (BLOCKS, 6, PB), jnp.float32, -1.0, 1.0) * steps_of(streams_of[0], (BLOCKS, 6, PB), ((0, 8),), -0.4, 0.0), -1.0, 1.0)
    adjoint = gaussian(streams_of[1], (BLOCKS, CH, PB), 1.0, 6.0, ((0, 8), (1, 4)))
    strengths = gaussian(streams_of[2], (BLOCKS, CH, PB), 1.0, 6.0, ((0, 8), (1, 4)))
    pair_target = set_ends(jax.random.randint(streams_of[3], (PAIRS,), 0, B_DEV), jax.random.fold_in(streams_of[3], 1), 0, B_DEV - 1).astype(jnp.int32)
    pair_owner_keys = jax.random.split(jax.random.fold_in(streams_of[4], 1), PAIRS // PAIRS_DEV)
    pair_owner_turns = jax.random.permutation(jax.random.fold_in(streams_of[4], 3), PAIRS // PAIRS_DEV)
    pair_owner = jax.vmap(lambda own, number: shared_out(jax.random.fold_in(streams_of[4], 2), own, number, PAIRS_DEV, N_TILES, 1, CAP, 1))(pair_owner_keys, pair_owner_turns).reshape((PAIRS, 1))
    pair_source = set_ends(jax.random.randint(streams_of[5], (PAIRS,), 0, B_DEV), jax.random.fold_in(streams_of[5], 1), 0, B_DEV - 1).astype(jnp.int32)
    pair_order = set_ends(jax.random.randint(streams_of[6], (PAIRS,), 1, 4), jax.random.fold_in(streams_of[6], 1), 1, 3).astype(jnp.int32)
    pair_count = draw_pair_count(jax.random.fold_in(streams_of[9], 71), 0)
    corner_vertex = draw_corner_vertex(jax.random.fold_in(streams_of[9], 71), 0)
    return dict(panel_geometry=panel_geometry, adjoint=adjoint, strengths=strengths, pair_target=pair_target, pair_owner=pair_owner, pair_source=pair_source, pair_order=pair_order, pair_count=pair_count, corner_vertex=corner_vertex)


def quadrature(orders):
    first = (orders == 1)[:, None]
    second = (orders == 2)[:, None]
    root_half = 0.5773502691896258
    root_fifth = 0.7745966692414834
    nodes = jnp.where(first, jnp.array([0.0, 0.0, 0.0], dtype=jnp.float32), jnp.where(second, jnp.array([-root_half, root_half, 0.0], dtype=jnp.float32), jnp.array([0.0, -root_fifth, root_fifth], dtype=jnp.float32)))
    weights = jnp.where(first, jnp.array([1.0, 0.0, 0.0], dtype=jnp.float32), jnp.where(second, jnp.array([0.5, 0.5, 0.0], dtype=jnp.float32), jnp.array([4.0 / 9.0, 5.0 / 18.0, 5.0 / 18.0], dtype=jnp.float32)))
    return (nodes, weights)

def tile_terms(target_geom, target_adjoint, source_geom, source_strength, orders):
    panel_coupling = jnp.einsum('avk,avu->aku', target_adjoint.astype(jnp.float32), source_strength.astype(jnp.float32), precision=lax.Precision.HIGHEST)
    nodes, weights = quadrature(orders)
    centre = target_geom[:, 0:3]
    target_grad = jnp.zeros(centre.shape, jnp.float32)
    source_grad = jnp.zeros(centre.shape, jnp.float32)
    for gauss_node_index in range(3):
        points = source_geom[:, 0:3] + 0.25 * nodes[:, gauss_node_index, None, None] * source_geom[:, 3:6]
        spread = centre[:, :, :, None] - points[:, :, None, :]
        squared = lax.optimization_barrier(jnp.sum(spread * spread, axis=1)) + 0.0625
        factor = weights[:, gauss_node_index, None, None] * panel_coupling / (squared * jnp.sqrt(squared))
        pulled = spread * factor[:, None]
        target_grad = target_grad - lax.optimization_barrier(jnp.sum(pulled, axis=3))
        source_grad = source_grad + lax.optimization_barrier(jnp.sum(pulled, axis=2))
    return (target_grad * 0.0078125, source_grad * 0.0078125)

def reference(panel_geometry, adjoint, strengths, pair_target, pair_owner, pair_source, pair_order, pair_count, corner_vertex):
    total = pair_target.shape[0]
    pair_ids = jnp.arange(total, dtype=jnp.int32)
    list_ids = pair_ids // PAIRS_DEV
    targets = list_ids * B_DEV + pair_target
    sources = pair_owner[:, 0] * B_DEV + pair_source
    alive = (pair_ids % PAIRS_DEV < pair_count[list_ids]).astype(jnp.float32)
    group_rows = 32

    def accumulate(panel_grad, group_index):
        start_row = group_index * group_rows
        group_targets = lax.dynamic_slice_in_dim(targets, start_row, group_rows, 0)
        tile_source_rows = lax.dynamic_slice_in_dim(sources, start_row, group_rows, 0)
        group_orders = lax.dynamic_slice_in_dim(pair_order, start_row, group_rows, 0)
        group_alive = lax.dynamic_slice_in_dim(alive, start_row, group_rows, 0)[:, None, None]
        target_grad, source_grad = tile_terms(panel_geometry[group_targets], adjoint[group_targets], panel_geometry[tile_source_rows], strengths[tile_source_rows], group_orders)
        panel_grad = panel_grad.at[group_targets].add(target_grad * group_alive)
        panel_grad = panel_grad.at[tile_source_rows].add(source_grad * group_alive)
        return (panel_grad, None)
    start_grad = jnp.zeros((BLOCKS, 3, PB), jnp.float32)
    panel_grad, _ = lax.scan(accumulate, start_grad, jnp.arange(total // group_rows, dtype=jnp.int32))
    corner_values = jnp.broadcast_to(0.25 * panel_grad[:, :, None, :], (BLOCKS, 3, 4, PB))
    corner_values = corner_values.transpose(1, 0, 2, 3).reshape(3, -1)
    flat_ids = corner_vertex.reshape(-1)
    return jnp.zeros((3, VERTS), jnp.float32).at[:, flat_ids].add(corner_values)
```

```python
import jax
import jax.numpy as jnp
from jax import lax
from jax.experimental import pallas as pl
from jax.experimental.pallas import tpu as pltpu
from jax.sharding import PartitionSpec as P

PACK = 16
ROWS = 16
SMEM = pltpu.SMEM
VMEM = pltpu.VMEM


def pack_kernel(geom_ref, strength_ref, corner_ref, out_ref):
    blocks = geom_ref.shape[0]
    for b in range(blocks):
        both = jnp.concatenate(
            [strength_ref[b].astype(jnp.float32), corner_ref[b].astype(jnp.float32)], axis=0
        )
        for t in range(out_ref.shape[0]):
            out_ref[t, b, 0:6] = geom_ref[b]
            out_ref[t, b, 6:8] = jnp.zeros((2, 128), jnp.float32)
            out_ref[t, b, 8:16] = both


def pair_kernel(
    me_ref,
    target_ref,
    owner_ref,
    source_ref,
    order_ref,
    count_ref,
    adjoint_ref,
    got_ref,
    out_ref,
    centre_ref,
    adjoint_cols,
    row_acc,
    grad_ref,
    vertex_ref,
):
    tiles = got_ref.shape[0]
    blocks = got_ref.shape[1]
    width = got_ref.shape[3]
    me = me_ref[0]
    live = count_ref[0]
    grad_ref[...] = jnp.zeros(grad_ref.shape, jnp.float32)
    row_acc[...] = jnp.zeros(row_acc.shape, jnp.float32)
    vertex_ref[...] = jnp.zeros(vertex_ref.shape, jnp.float32)
    for b in range(blocks):
        centre = got_ref[me, b, 0:8].T
        for c in range(3):
            centre_ref[b, c] = jnp.broadcast_to(centre[:, c : c + 1], (width, width))
        padded = jnp.concatenate(
            [adjoint_ref[b].astype(jnp.float32), jnp.zeros((4, width), jnp.float32)], axis=0
        )
        adjoint_cols[b] = padded.T

    def one_pair(k):
        target = target_ref[k]
        owner = owner_ref[k]
        source = source_ref[k]
        order = order_ref[k]
        alive = jnp.where(k < live, 0.25 * 0.0078125, 0.0).astype(jnp.float32)
        first = order == 1
        second = order == 2
        middle = alive * jnp.where(first, 1.0, jnp.where(second, 0.0, 4.0 / 9.0))
        side = alive * jnp.where(first, 0.0, jnp.where(second, 0.5, 5.0 / 18.0))
        reach = 0.25 * jnp.where(
            first, 0.0, jnp.where(second, 0.5773502691896258, 0.7745966692414834)
        )
        coupling = jnp.dot(
            adjoint_cols[target].astype(jnp.bfloat16),
            got_ref[owner, source, 8:16].astype(jnp.bfloat16),
            preferred_element_type=jnp.float32,
        )
        point = [got_ref[owner, source, c : c + 1] for c in range(3)]
        extent = [got_ref[owner, source, 3 + c : 4 + c] * reach for c in range(3)]
        twice = [2.0 * e for e in extent]
        extent_square = (
            extent[0] * extent[0] + extent[1] * extent[1] + extent[2] * extent[2] + 0.0625
        )
        step = 8
        columns = [jnp.zeros((step, width), jnp.float32) for _ in range(3)]
        for start in range(0, width, step):
            rows = slice(start, start + step)
            away = [centre_ref[target, c, rows] - point[c] for c in range(3)]
            square = away[0] * away[0] + away[1] * away[1] + away[2] * away[2]
            along = away[0] * twice[0] + away[1] * twice[1] + away[2] * twice[2]
            outer = square + extent_square
            i_mid = lax.rsqrt(square + 0.0625)
            i_plus = lax.rsqrt(outer - along)
            i_minus = lax.rsqrt(outer + along)
            f_mid = i_mid * i_mid * i_mid
            f_plus = i_plus * i_plus * i_plus
            f_minus = i_minus * i_minus * i_minus
            pair_c = coupling[rows]
            even = pair_c * (middle * f_mid + side * (f_plus + f_minus))
            odd = (pair_c * side) * (f_plus - f_minus)
            for c in range(3):
                pulled = even * away[c] - odd * extent[c]
                row_acc[target, c, rows] += pulled
                columns[c] = columns[c] + pulled
        sums = jnp.concatenate(
            [jnp.sum(columns[c], axis=0, keepdims=True) for c in range(3)], axis=0
        )
        at = owner * blocks + source
        grad_ref[at, 0:3] += sums

    def pairs(step, carry):
        one_pair(2 * step)
        one_pair(2 * step + 1)
        return carry

    lax.fori_loop(0, (live + 1) // 2, pairs, 0)
    for b in range(blocks):
        total = jnp.concatenate(
            [jnp.sum(row_acc[b, c], axis=1, keepdims=True) for c in range(3)]
            + [jnp.zeros((width, 5), jnp.float32)],
            axis=1,
        )
        grad_ref[me * blocks + b] -= total.T

    lanes = 128
    high = blocks * width // lanes
    shift = (blocks * width).bit_length() - 1

    def scatter(tile, carry):
        parts = []
        hots = []
        for b in range(blocks):
            grad = grad_ref[tile * blocks + b]
            upper = grad.astype(jnp.bfloat16).astype(jnp.float32)
            lower = grad - upper
            for j in range(4):
                vertex = got_ref[tile, b, 12 + j : 13 + j].astype(jnp.int32)
                offset = (vertex >> shift) - tile
                offset = jnp.where(offset < 0, offset + tiles, offset)
                slot = jnp.where(
                    offset == 0,
                    0,
                    jnp.where(offset == 1, 1, jnp.where(offset == tiles - 1, 2, 3)),
                )
                key = slot * high + ((vertex >> 7) & (high - 1))
                mask = lax.broadcasted_iota(jnp.int32, (4 * high, width), 0) == key
                pieces = []
                for c in range(3):
                    for part in (upper, lower):
                        pieces.append(jnp.where(mask, part[c : c + 1], 0.0))
                parts.append(jnp.concatenate(pieces, axis=0).astype(jnp.bfloat16))
                hot = lax.broadcasted_iota(jnp.int32, (lanes, width), 0) == (vertex & (lanes - 1))
                hots.append(jnp.where(hot, 1.0, 0.0).astype(jnp.bfloat16))
        result = lax.dot_general(
            jnp.concatenate(parts, axis=1),
            jnp.concatenate(hots, axis=1),
            (((1,), (1,)), ((), ())),
            preferred_element_type=jnp.float32,
        )
        for slot, shift_by in enumerate((0, 1, tiles - 1, tiles // 2)):
            dest = lax.rem(tile + shift_by, tiles)
            picked = []
            for c in range(3):
                base = 2 * c * 4 * high + slot * high
                other = base + 4 * high
                picked.append(result[base : base + high] + result[other : other + high])
            vertex_ref[dest] += jnp.concatenate(picked, axis=0)
        return carry

    lax.fori_loop(0, tiles, scatter, 0)
    for f in range(out_ref.shape[1]):
        out_ref[:, f] = vertex_ref[...]


def sum_kernel(got_ref, out_ref):
    lanes = got_ref.shape[2]
    rows = got_ref.shape[1]
    high = rows // 3
    total = jnp.sum(got_ref[...], axis=0)
    for c in range(3):
        for h in range(high):
            r = c * high + h
            out_ref[c : c + 1, h * lanes : (h + 1) * lanes] = total[r : r + 1]


def per_device(
    panel_geometry,
    adjoint,
    strengths,
    pair_target,
    pair_owner,
    pair_source,
    pair_order,
    pair_count,
    corner_vertex,
):
    tiles = lax.axis_size("tiles")
    far = lax.axis_size("far")
    blocks, _, width = panel_geometry.shape
    high = blocks * width // 128
    me = lax.axis_index("tiles").astype(jnp.int32).reshape(1)
    packed = pl.pallas_call(
        pack_kernel,
        out_shape=jax.ShapeDtypeStruct((tiles, blocks, PACK, width), jnp.float32),
    )(panel_geometry, strengths, corner_vertex)
    got = lax.all_to_all(packed, "tiles", split_axis=0, concat_axis=0, tiled=True)
    smem = pl.BlockSpec(memory_space=SMEM)
    vmem = pl.BlockSpec(memory_space=VMEM)
    partial = pl.pallas_call(
        pair_kernel,
        out_shape=jax.ShapeDtypeStruct((tiles, far, 3 * high, 128), jnp.float32),
        in_specs=[smem] * 6 + [vmem] * 2,
        out_specs=vmem,
        scratch_shapes=[
            VMEM((blocks, 3, width, width), jnp.float32),
            VMEM((blocks, width, 8), jnp.float32),
            VMEM((blocks, 3, width, width), jnp.float32),
            VMEM((tiles * blocks, 8, width), jnp.float32),
            VMEM((tiles, 3 * high, 128), jnp.float32),
        ],
        compiler_params=pltpu.CompilerParams(vmem_limit_bytes=48 * 1024 * 1024),
    )(
        me,
        pair_target,
        pair_owner[:, 0],
        pair_source,
        pair_order,
        pair_count,
        adjoint,
        got,
    )
    partial = partial.reshape(tiles * far, 3 * high, 128)
    shares = lax.all_to_all(partial, ("tiles", "far"), split_axis=0, concat_axis=0, tiled=True)
    return pl.pallas_call(
        sum_kernel,
        out_shape=jax.ShapeDtypeStruct((3, blocks * width), jnp.float32),
        compiler_params=pltpu.CompilerParams(vmem_limit_bytes=48 * 1024 * 1024),
    )(shares)


def solution(mesh):
    placed = (
        P("tiles", None, None),
        P("tiles", "far", None),
        P("tiles", "far", None),
        P("tiles"),
        P("tiles", None),
        P("tiles"),
        P("tiles"),
        P("tiles"),
        P("tiles", None, None),
    )
    return jax.shard_map(
        per_device, mesh=mesh, in_specs=placed, out_specs=P(None, "tiles"), check_vma=False
    )
```

```python
import jax
import jax.numpy as jnp
from jax import lax
from jax.experimental import pallas as pl
from jax.experimental.pallas import tpu as pltpu
from jax.sharding import PartitionSpec as P

PACK = 16
DIRECT = 8
SMEM = pltpu.SMEM
VMEM = pltpu.VMEM


def pack_kernel(geom_ref, strength_ref, corner_ref, out_ref):
    blocks = strength_ref.shape[0]
    width = strength_ref.shape[2]
    for b in range(blocks):
        block = jnp.concatenate(
            [geom_ref[i, b : b + 1] for i in range(6)]
            + [jnp.zeros((2, width), jnp.float32)]
            + [strength_ref[b].astype(jnp.float32), corner_ref[b].astype(jnp.float32)],
            axis=0,
        )
        if len(out_ref.shape) == 3:
            out_ref[b] = block
        else:
            for t in range(out_ref.shape[0]):
                out_ref[t, b] = block


def pair_kernel(
    me_ref,
    target_ref,
    owner_ref,
    source_ref,
    order_ref,
    count_ref,
    adjoint_ref,
    *refs,
):
    *arrived, out_ref, centre_ref, adjoint_cols, row_acc, grad_ref, vertex_ref, held_ref = refs
    me = me_ref[0]
    if len(arrived) == 1:
        got_ref = arrived[0]
    else:
        got_ref = held_ref
        for d, ref in enumerate(arrived):
            held_ref[lax.rem(me + d, len(arrived))] = ref[...]
    tiles = got_ref.shape[0]
    blocks = got_ref.shape[1]
    width = got_ref.shape[3]
    live = count_ref[0]
    grad_ref[...] = jnp.zeros(grad_ref.shape, jnp.float32)
    row_acc[...] = jnp.zeros(row_acc.shape, jnp.float32)
    vertex_ref[...] = jnp.zeros(vertex_ref.shape, jnp.float32)
    for b in range(blocks):
        centre = got_ref[me, b, 0:8].T
        for c in range(3):
            centre_ref[b, c] = jnp.broadcast_to(centre[:, c : c + 1], (width, width))
        padded = jnp.concatenate(
            [adjoint_ref[b].astype(jnp.float32), jnp.zeros((4, width), jnp.float32)], axis=0
        )
        adjoint_cols[b] = padded.T

    def one_pair(k):
        target = target_ref[k]
        owner = owner_ref[k]
        source = source_ref[k]
        order = order_ref[k]
        alive = jnp.where(k < live, 0.25 * 0.0078125, 0.0).astype(jnp.float32)
        first = order == 1
        second = order == 2
        middle = alive * jnp.where(first, 1.0, jnp.where(second, 0.0, 4.0 / 9.0))
        side = alive * jnp.where(first, 0.0, jnp.where(second, 0.5, 5.0 / 18.0))
        reach = 0.25 * jnp.where(
            first, 0.0, jnp.where(second, 0.5773502691896258, 0.7745966692414834)
        )
        coupling = jnp.dot(
            adjoint_cols[target].astype(jnp.bfloat16),
            got_ref[owner, source, 8:16].astype(jnp.bfloat16),
            preferred_element_type=jnp.float32,
        )
        point = [got_ref[owner, source, c : c + 1] for c in range(3)]
        extent = [got_ref[owner, source, 3 + c : 4 + c] * reach for c in range(3)]
        twice = [2.0 * e for e in extent]
        extent_square = (
            extent[0] * extent[0] + extent[1] * extent[1] + extent[2] * extent[2] + 0.0625
        )
        step = 8
        columns = [jnp.zeros((step, width), jnp.float32) for _ in range(3)]
        for start in range(0, width, step):
            rows = slice(start, start + step)
            away = [centre_ref[target, c, rows] - point[c] for c in range(3)]
            square = away[0] * away[0] + away[1] * away[1] + away[2] * away[2]
            along = away[0] * twice[0] + away[1] * twice[1] + away[2] * twice[2]
            outer = square + extent_square
            i_mid = lax.rsqrt(square + 0.0625)
            i_plus = lax.rsqrt(outer - along)
            i_minus = lax.rsqrt(outer + along)
            f_mid = i_mid * i_mid * i_mid
            f_plus = i_plus * i_plus * i_plus
            f_minus = i_minus * i_minus * i_minus
            pair_c = coupling[rows]
            even = pair_c * (middle * f_mid + side * (f_plus + f_minus))
            odd = (pair_c * side) * (f_plus - f_minus)
            for c in range(3):
                pulled = even * away[c] - odd * extent[c]
                row_acc[target, c, rows] += pulled
                columns[c] = columns[c] + pulled
        sums = jnp.concatenate(
            [jnp.sum(columns[c], axis=0, keepdims=True) for c in range(3)], axis=0
        )
        at = owner * blocks + source
        grad_ref[at, 0:3] += sums

    def pairs(step, carry):
        one_pair(2 * step)
        one_pair(2 * step + 1)
        return carry

    lax.fori_loop(0, (live + 1) // 2, pairs, 0)
    for b in range(blocks):
        total = jnp.concatenate(
            [jnp.sum(row_acc[b, c], axis=1, keepdims=True) for c in range(3)]
            + [jnp.zeros((width, 5), jnp.float32)],
            axis=1,
        )
        grad_ref[me * blocks + b] -= total.T

    lanes = 128
    high = blocks * width // lanes
    shift = (blocks * width).bit_length() - 1

    def scatter(tile, carry):
        parts = []
        hots = []
        for b in range(blocks):
            grad = grad_ref[tile * blocks + b]
            upper = grad.astype(jnp.bfloat16).astype(jnp.float32)
            lower = grad - upper
            for j in range(4):
                vertex = got_ref[tile, b, 12 + j : 13 + j].astype(jnp.int32)
                offset = (vertex >> shift) - tile
                offset = jnp.where(offset < 0, offset + tiles, offset)
                slot = jnp.where(
                    offset == 0,
                    0,
                    jnp.where(offset == 1, 1, jnp.where(offset == tiles - 1, 2, 3)),
                )
                key = slot * high + ((vertex >> 7) & (high - 1))
                mask = lax.broadcasted_iota(jnp.int32, (4 * high, width), 0) == key
                pieces = []
                for c in range(3):
                    for part in (upper, lower):
                        pieces.append(jnp.where(mask, part[c : c + 1], 0.0))
                parts.append(jnp.concatenate(pieces, axis=0).astype(jnp.bfloat16))
                hot = lax.broadcasted_iota(jnp.int32, (lanes, width), 0) == (vertex & (lanes - 1))
                hots.append(jnp.where(hot, 1.0, 0.0).astype(jnp.bfloat16))
        result = lax.dot_general(
            jnp.concatenate(parts, axis=1),
            jnp.concatenate(hots, axis=1),
            (((1,), (1,)), ((), ())),
            preferred_element_type=jnp.float32,
        )
        for slot, shift_by in enumerate((0, 1, tiles - 1, tiles // 2)):
            dest = lax.rem(tile + shift_by, tiles)
            picked = []
            for c in range(3):
                base = 2 * c * 4 * high + slot * high
                other = base + 4 * high
                picked.append(result[base : base + high] + result[other : other + high])
            vertex_ref[dest] += jnp.concatenate(picked, axis=0)
        return carry

    lax.fori_loop(0, tiles, scatter, 0)
    for f in range(out_ref.shape[1]):
        out_ref[:, f] = vertex_ref[...]


def sum_kernel(got_ref, out_ref):
    lanes = got_ref.shape[2]
    rows = got_ref.shape[1]
    high = rows // 3
    total = jnp.sum(got_ref[...], axis=0)
    for c in range(3):
        for h in range(high):
            r = c * high + h
            out_ref[c : c + 1, h * lanes : (h + 1) * lanes] = total[r : r + 1]


def per_device(
    panel_geometry,
    adjoint,
    strengths,
    pair_target,
    pair_owner,
    pair_source,
    pair_order,
    pair_count,
    corner_vertex,
):
    tiles = lax.axis_size("tiles")
    far = lax.axis_size("far")
    blocks, _, width = panel_geometry.shape
    high = blocks * width // 128
    me = lax.axis_index("tiles").astype(jnp.int32).reshape(1)
    direct = tiles <= DIRECT
    copies = () if direct else (tiles,)
    packed = pl.pallas_call(
        pack_kernel,
        out_shape=jax.ShapeDtypeStruct(copies + (blocks, PACK, width), jnp.float32),
    )(panel_geometry.transpose(1, 0, 2), strengths, corner_vertex)
    if direct:
        arrived = [packed] + [
            lax.ppermute(packed, "tiles", [((t + d) % tiles, t) for t in range(tiles)])
            for d in range(1, tiles)
        ]
        held = (tiles, blocks, PACK, width)
    else:
        arrived = [lax.all_to_all(packed, "tiles", split_axis=0, concat_axis=0, tiled=True)]
        held = (1, 1, 8, 128)
    smem = pl.BlockSpec(memory_space=SMEM)
    vmem = pl.BlockSpec(memory_space=VMEM)
    partial = pl.pallas_call(
        pair_kernel,
        out_shape=jax.ShapeDtypeStruct((tiles, far, 3 * high, 128), jnp.float32),
        in_specs=[smem] * 6 + [vmem] * (1 + len(arrived)),
        out_specs=vmem,
        scratch_shapes=[
            VMEM((blocks, 3, width, width), jnp.float32),
            VMEM((blocks, width, 8), jnp.float32),
            VMEM((blocks, 3, width, width), jnp.float32),
            VMEM((tiles * blocks, 8, width), jnp.float32),
            VMEM((tiles, 3 * high, 128), jnp.float32),
            VMEM(held, jnp.float32),
        ],
        compiler_params=pltpu.CompilerParams(vmem_limit_bytes=48 * 1024 * 1024),
    )(
        me,
        pair_target,
        pair_owner[:, 0],
        pair_source,
        pair_order,
        pair_count,
        adjoint,
        *arrived,
    )
    partial = partial.reshape(tiles * far, 3 * high, 128)
    shares = lax.all_to_all(partial, ("tiles", "far"), split_axis=0, concat_axis=0, tiled=True)
    return pl.pallas_call(
        sum_kernel,
        out_shape=jax.ShapeDtypeStruct((3, blocks * width), jnp.float32),
        compiler_params=pltpu.CompilerParams(vmem_limit_bytes=48 * 1024 * 1024),
    )(shares)


def solution(mesh):
    placed = (
        P("tiles", None, None),
        P("tiles", "far", None),
        P("tiles", "far", None),
        P("tiles"),
        P("tiles", None),
        P("tiles"),
        P("tiles"),
        P("tiles"),
        P("tiles", None, None),
    )
    return jax.shard_map(
        per_device, mesh=mesh, in_specs=placed, out_specs=P(None, "tiles"), check_vma=False
    )
```

```python
import jax
import jax.numpy as jnp
from jax import lax
from jax.experimental import pallas as pl
from jax.experimental.pallas import tpu as pltpu
from jax.sharding import PartitionSpec as P

PACK = 16
SMEM = pltpu.SMEM
VMEM = pltpu.VMEM


def pack_kernel(geom_ref, strength_ref, corner_ref, out_ref):
    blocks = strength_ref.shape[0]
    width = strength_ref.shape[2]
    for b in range(blocks):
        block = jnp.concatenate(
            [geom_ref[i, b : b + 1] for i in range(6)]
            + [jnp.zeros((2, width), jnp.float32)]
            + [strength_ref[b].astype(jnp.float32), corner_ref[b].astype(jnp.float32)],
            axis=0,
        )
        if len(out_ref.shape) == 3:
            out_ref[b] = block
        else:
            for t in range(out_ref.shape[0]):
                out_ref[t, b] = block


def pair_kernel(
    me_ref,
    target_ref,
    owner_ref,
    source_ref,
    order_ref,
    count_ref,
    adjoint_ref,
    *refs,
):
    got_ref, out_ref, centre_ref, adjoint_cols, row_acc, grad_ref = refs
    vertex_ref = out_ref
    me = me_ref[0]
    tiles = got_ref.shape[0]
    blocks = got_ref.shape[1]
    width = got_ref.shape[3]
    live = count_ref[0]
    grad_ref[...] = jnp.zeros(grad_ref.shape, jnp.float32)
    row_acc[...] = jnp.zeros(row_acc.shape, jnp.float32)
    vertex_ref[...] = jnp.zeros(vertex_ref.shape, jnp.float32)
    for b in range(blocks):
        centre = got_ref[me, b, 0:8].T
        for c in range(3):
            centre_ref[b, c] = jnp.broadcast_to(centre[:, c : c + 1], (width, width))
        padded = jnp.concatenate(
            [adjoint_ref[b].astype(jnp.float32), jnp.zeros((4, width), jnp.float32)], axis=0
        )
        adjoint_cols[b] = padded.T

    def one_pair(k):
        target = target_ref[k]
        owner = owner_ref[k]
        source = source_ref[k]
        order = order_ref[k]
        alive = jnp.where(k < live, 0.25 * 0.0078125, 0.0).astype(jnp.float32)
        first = order == 1
        second = order == 2
        middle = alive * jnp.where(first, 1.0, jnp.where(second, 0.0, 4.0 / 9.0))
        side = alive * jnp.where(first, 0.0, jnp.where(second, 0.5, 5.0 / 18.0))
        reach = 0.25 * jnp.where(
            first, 0.0, jnp.where(second, 0.5773502691896258, 0.7745966692414834)
        )
        coupling = jnp.dot(
            adjoint_cols[target].astype(jnp.bfloat16),
            got_ref[owner, source, 8:16].astype(jnp.bfloat16),
            preferred_element_type=jnp.float32,
        )
        point = [got_ref[owner, source, c : c + 1] for c in range(3)]
        extent = [got_ref[owner, source, 3 + c : 4 + c] * reach for c in range(3)]
        twice = [2.0 * e for e in extent]
        extent_square = (
            extent[0] * extent[0] + extent[1] * extent[1] + extent[2] * extent[2] + 0.0625
        )
        step = 8
        columns = [jnp.zeros((step, width), jnp.float32) for _ in range(3)]
        for start in range(0, width, step):
            rows = slice(start, start + step)
            away = [centre_ref[target, c, rows] - point[c] for c in range(3)]
            square = away[0] * away[0] + away[1] * away[1] + away[2] * away[2]
            along = away[0] * twice[0] + away[1] * twice[1] + away[2] * twice[2]
            outer = square + extent_square
            i_mid = lax.rsqrt(square + 0.0625)
            i_plus = lax.rsqrt(outer - along)
            i_minus = lax.rsqrt(outer + along)
            f_mid = i_mid * i_mid * i_mid
            f_plus = i_plus * i_plus * i_plus
            f_minus = i_minus * i_minus * i_minus
            pair_c = coupling[rows]
            even = pair_c * (middle * f_mid + side * (f_plus + f_minus))
            odd = (pair_c * side) * (f_plus - f_minus)
            for c in range(3):
                pulled = even * away[c] - odd * extent[c]
                row_acc[target, c, rows] += pulled
                columns[c] = columns[c] + pulled
        sums = jnp.concatenate(
            [jnp.sum(columns[c], axis=0, keepdims=True) for c in range(3)], axis=0
        )
        at = owner * blocks + source
        grad_ref[at, 0:3] += sums

    def pairs(step, carry):
        one_pair(2 * step)
        one_pair(2 * step + 1)
        return carry

    lax.fori_loop(0, (live + 1) // 2, pairs, 0)
    for b in range(blocks):
        total = jnp.concatenate(
            [jnp.sum(row_acc[b, c], axis=1, keepdims=True) for c in range(3)]
            + [jnp.zeros((width, 5), jnp.float32)],
            axis=1,
        )
        grad_ref[me * blocks + b] -= total.T

    lanes = 128
    high = blocks * width // lanes
    shift = (blocks * width).bit_length() - 1

    def scatter(tile, carry):
        parts = []
        hots = []
        for b in range(blocks):
            grad = grad_ref[tile * blocks + b]
            upper = grad.astype(jnp.bfloat16).astype(jnp.float32)
            lower = grad - upper
            for j in range(4):
                vertex = got_ref[tile, b, 12 + j : 13 + j].astype(jnp.int32)
                offset = (vertex >> shift) - tile
                offset = jnp.where(offset < 0, offset + tiles, offset)
                slot = jnp.where(
                    offset == 0,
                    0,
                    jnp.where(offset == 1, 1, jnp.where(offset == tiles - 1, 2, 3)),
                )
                key = slot * high + ((vertex >> 7) & (high - 1))
                mask = lax.broadcasted_iota(jnp.int32, (4 * high, width), 0) == key
                pieces = []
                for c in range(3):
                    for part in (upper, lower):
                        pieces.append(jnp.where(mask, part[c : c + 1], 0.0))
                parts.append(jnp.concatenate(pieces, axis=0).astype(jnp.bfloat16))
                hot = lax.broadcasted_iota(jnp.int32, (lanes, width), 0) == (vertex & (lanes - 1))
                hots.append(jnp.where(hot, 1.0, 0.0).astype(jnp.bfloat16))
        result = lax.dot_general(
            jnp.concatenate(parts, axis=1),
            jnp.concatenate(hots, axis=1),
            (((1,), (1,)), ((), ())),
            preferred_element_type=jnp.float32,
        )
        for slot, shift_by in enumerate((0, 1, tiles - 1, tiles // 2)):
            dest = lax.rem(tile + shift_by, tiles)
            picked = []
            for c in range(3):
                base = 2 * c * 4 * high + slot * high
                other = base + 4 * high
                picked.append(result[base : base + high] + result[other : other + high])
            vertex_ref[dest] += jnp.concatenate(picked, axis=0)
        return carry

    lax.fori_loop(0, tiles, scatter, 0)


def own_kernel(me_ref, got_ref, out_ref):
    lanes = got_ref.shape[2]
    rows = got_ref.shape[1]
    high = rows // 3
    total = got_ref[me_ref[0]]
    for c in range(3):
        for h in range(high):
            r = c * high + h
            out_ref[c : c + 1, h * lanes : (h + 1) * lanes] = total[r : r + 1]


def per_device(
    panel_geometry,
    adjoint,
    strengths,
    pair_target,
    pair_owner,
    pair_source,
    pair_order,
    pair_count,
    corner_vertex,
):
    tiles = lax.axis_size("tiles")
    blocks, _, width = panel_geometry.shape
    high = blocks * width // 128
    me = lax.axis_index("tiles").astype(jnp.int32).reshape(1)
    packed = pl.pallas_call(
        pack_kernel,
        out_shape=jax.ShapeDtypeStruct((blocks, PACK, width), jnp.float32),
    )(panel_geometry.transpose(1, 0, 2), strengths, corner_vertex)
    arrived = [lax.all_gather(packed, "tiles")]
    smem = pl.BlockSpec(memory_space=SMEM)
    vmem = pl.BlockSpec(memory_space=VMEM)
    partial = pl.pallas_call(
        pair_kernel,
        out_shape=jax.ShapeDtypeStruct((tiles, 3 * high, 128), jnp.float32),
        in_specs=[smem] * 6 + [vmem] * (1 + len(arrived)),
        out_specs=vmem,
        scratch_shapes=[
            VMEM((blocks, 3, width, width), jnp.float32),
            VMEM((blocks, width, 8), jnp.float32),
            VMEM((blocks, 3, width, width), jnp.float32),
            VMEM((tiles * blocks, 8, width), jnp.float32),
        ],
        compiler_params=pltpu.CompilerParams(vmem_limit_bytes=48 * 1024 * 1024),
    )(
        me,
        pair_target,
        pair_owner[:, 0],
        pair_source,
        pair_order,
        pair_count,
        adjoint,
        *arrived,
    )
    total = lax.psum(partial, ("tiles", "far"))
    return pl.pallas_call(
        own_kernel,
        out_shape=jax.ShapeDtypeStruct((3, blocks * width), jnp.float32),
        in_specs=[smem, vmem],
        out_specs=vmem,
        compiler_params=pltpu.CompilerParams(vmem_limit_bytes=48 * 1024 * 1024),
    )(me, total)


def solution(mesh):
    placed = (
        P("tiles", None, None),
        P("tiles", "far", None),
        P("tiles", "far", None),
        P("tiles"),
        P("tiles", None),
        P("tiles"),
        P("tiles"),
        P("tiles"),
        P("tiles", None, None),
    )
    return jax.shard_map(
        per_device, mesh=mesh, in_specs=placed, out_specs=P(None, "tiles"), check_vma=False
    )
```

```python
import jax
import jax.numpy as jnp
from jax import lax
from jax.experimental import pallas as pl
from jax.experimental.pallas import tpu as pltpu
from jax.sharding import PartitionSpec as P

SMEM = pltpu.SMEM
VMEM = pltpu.VMEM
LANES = 128
LIMIT = 48 * 1024 * 1024


def pack_kernel(me_ref, geom_ref, strength_ref, corner_ref, out_ref):
    tiles, blocks, _, _ = out_ref.shape
    width = strength_ref.shape[2]
    shift = (blocks * width).bit_length() - 1
    me = me_ref[0]
    for b in range(blocks):
        vertex = corner_ref[b]
        offset = (vertex >> shift) - me
        offset = jnp.where(offset < 0, offset + tiles, offset)
        slot = jnp.where(
            offset == 0,
            0,
            jnp.where(offset == 1, 1, jnp.where(offset == tiles - 1, 2, 3)),
        )
        place = ((slot << shift) + (vertex & ((1 << shift) - 1))).astype(jnp.float32)
        span = float(4 << shift)
        first = place[0:1] * span + place[1:2]
        second = place[2:3] * span + place[3:4]
        block = jnp.concatenate(
            [
                strength_ref[b].astype(jnp.float32),
                jnp.concatenate([geom_ref[c, b : b + 1] for c in range(3)] + [first], axis=0),
                jnp.concatenate([geom_ref[3 + c, b : b + 1] for c in range(3)] + [second], axis=0),
            ],
            axis=1,
        )
        for t in range(tiles):
            out_ref[t, b] = block


def pair_kernel(
    me_ref,
    target_ref,
    owner_ref,
    source_ref,
    order_ref,
    count_ref,
    adjoint_ref,
    got_ref,
    out_ref,
    centre_ref,
    adjoint_cols,
    coupling_ref,
    row_acc,
    grad_ref,
    vertex_ref,
):
    tiles, blocks, _, _ = got_ref.shape
    width = adjoint_ref.shape[2]
    pairs = target_ref.shape[0]
    at_point, at_extent = width, 2 * width
    me = me_ref[0]
    live = count_ref[0]
    grad_ref[...] = jnp.zeros(grad_ref.shape, jnp.float32)
    row_acc[...] = jnp.zeros(row_acc.shape, jnp.float32)
    vertex_ref[...] = jnp.zeros(vertex_ref.shape, jnp.float32)
    blank = jnp.zeros((4, width), jnp.float32)
    for b in range(blocks):
        own = got_ref[me, b, :, at_point : at_point + width]
        both = jnp.concatenate([own, adjoint_ref[b].astype(jnp.float32)], axis=0).T
        for c in range(3):
            centre_ref[b, c] = jnp.broadcast_to(both[:, c : c + 1], (width, width))
        swapped = jnp.concatenate([adjoint_ref[b].astype(jnp.float32), blank], axis=0).T
        adjoint_cols[b] = swapped.astype(jnp.bfloat16)

    def couple(k, slot):
        k = jnp.minimum(k, pairs - 1)
        values = got_ref[owner_ref[k], source_ref[k], :, 0:width]
        coupling_ref[slot] = jnp.dot(
            adjoint_cols[target_ref[k]],
            jnp.concatenate([values, blank], axis=0).astype(jnp.bfloat16),
            preferred_element_type=jnp.float32,
        )

    def one_pair(k, slot):
        target = target_ref[k]
        owner = owner_ref[k]
        source = source_ref[k]
        order = order_ref[k]
        alive = jnp.where(k < live, 0.25 * 0.0078125, 0.0).astype(jnp.float32)
        third = order == 3
        side = alive * jnp.where(third, 5.0 / 18.0, 0.5)
        ratio = jnp.where(third, 1.6, 0.0)
        reach = 0.25 * jnp.where(
            third, 0.7745966692414834, jnp.where(order == 2, 0.5773502691896258, 0.0)
        )
        point = [got_ref[owner, source, c : c + 1, at_point : at_point + width] for c in range(3)]
        extent = [
            got_ref[owner, source, c : c + 1, at_extent : at_extent + width] * reach
            for c in range(3)
        ]
        twice = [2.0 * e for e in extent]
        extent_square = (
            extent[0] * extent[0] + extent[1] * extent[1] + extent[2] * extent[2] + 0.0625
        )
        step = 8
        columns = [jnp.zeros((step, width), jnp.float32) for _ in range(3)]
        for start in range(0, width, step):
            rows = slice(start, start + step)
            away = [centre_ref[target, c, rows] - point[c] for c in range(3)]
            square = away[0] * away[0] + away[1] * away[1] + away[2] * away[2]
            along = away[0] * twice[0] + away[1] * twice[1] + away[2] * twice[2]
            outer = square + extent_square
            i_mid = lax.rsqrt(square + 0.0625)
            i_plus = lax.rsqrt(outer - along)
            i_minus = lax.rsqrt(outer + along)
            f_mid = i_mid * i_mid * i_mid
            f_plus = i_plus * i_plus * i_plus
            f_minus = i_minus * i_minus * i_minus
            scaled = coupling_ref[slot, rows] * side
            even = scaled * (ratio * f_mid + (f_plus + f_minus))
            odd = scaled * (f_plus - f_minus)
            for c in range(3):
                pulled = even * away[c] - odd * extent[c]
                row_acc[target, c, rows] += pulled
                columns[c] = columns[c] + pulled
        sums = jnp.concatenate(
            [jnp.sum(columns[c], axis=0, keepdims=True) for c in range(3)], axis=0
        )
        at = owner * blocks + source
        grad_ref[at, 0:3] += sums

    def two_pairs(step, carry):
        for slot in range(2):
            one_pair(2 * step + slot, slot)
        for slot in range(2):
            couple(2 * step + 2 + slot, slot)
        return carry

    for slot in range(2):
        couple(slot, slot)
    lax.fori_loop(0, (live + 1) // 2, two_pairs, 0)
    for b in range(blocks):
        total = jnp.concatenate(
            [jnp.sum(row_acc[b, c], axis=1, keepdims=True) for c in range(3)]
            + [jnp.zeros((width, 5), jnp.float32)],
            axis=1,
        )
        grad_ref[me * blocks + b] -= total.T

    high = blocks * width // LANES
    keys = 4 * high
    shift = (blocks * width).bit_length() + 1
    key_ids = lax.broadcasted_iota(jnp.int32, (keys, width), 0).astype(jnp.bfloat16)
    lane_ids = lax.broadcasted_iota(jnp.int32, (LANES, width), 0).astype(jnp.bfloat16)
    one = jnp.ones((LANES, width), jnp.bfloat16)
    zero = jnp.zeros((LANES, width), jnp.bfloat16)

    def scatter(tile, carry):
        parts = []
        hots = []
        for b in range(blocks):
            grad = grad_ref[tile * blocks + b]
            upper = grad.astype(jnp.bfloat16)
            lower = (grad - upper.astype(jnp.float32)).astype(jnp.bfloat16)
            spread = [
                jnp.broadcast_to(part[c : c + 1], (keys, width))
                for c in range(3)
                for part in (upper, lower)
            ]
            for half in (at_point, at_extent):
                code = got_ref[tile, b, 3:4, half : half + width].astype(jnp.int32)
                for place in (code >> shift, code & ((1 << shift) - 1)):
                    key = (place >> 7).astype(jnp.float32).astype(jnp.bfloat16)
                    low = (place & (LANES - 1)).astype(jnp.float32).astype(jnp.bfloat16)
                    mask = key_ids == key
                    parts.append(
                        jnp.concatenate(
                            [jnp.where(mask, s, zero[0:keys]) for s in spread], axis=0
                        )
                    )
                    hots.append(jnp.where(lane_ids == low, one, zero))
        result = lax.dot_general(
            jnp.concatenate(parts, axis=1),
            jnp.concatenate(hots, axis=1),
            (((1,), (1,)), ((), ())),
            preferred_element_type=jnp.float32,
        )
        for slot, shift_by in enumerate((0, 1, tiles - 1, tiles // 2)):
            dest = lax.rem(tile + shift_by, tiles)
            picked = []
            for c in range(3):
                base = 2 * c * keys + slot * high
                other = base + keys
                picked.append(result[base : base + high] + result[other : other + high])
            vertex_ref[dest] += jnp.concatenate(picked, axis=1)
        return carry

    lax.fori_loop(0, tiles, scatter, 0)
    for f in range(out_ref.shape[1]):
        out_ref[:, f] = vertex_ref[...]


def sum_kernel(got_ref, out_ref):
    _, high, _ = got_ref.shape
    total = jnp.sum(got_ref[...], axis=0)
    for c in range(3):
        for h in range(high):
            out_ref[c : c + 1, h * LANES : (h + 1) * LANES] = total[
                h : h + 1, c * LANES : (c + 1) * LANES
            ]


def per_device(
    panel_geometry,
    adjoint,
    strengths,
    pair_target,
    pair_owner,
    pair_source,
    pair_order,
    pair_count,
    corner_vertex,
):
    tiles = lax.axis_size("tiles")
    far = lax.axis_size("far")
    blocks, _, width = panel_geometry.shape
    high = blocks * width // LANES
    me = lax.axis_index("tiles").astype(jnp.int32).reshape(1)
    smem = pl.BlockSpec(memory_space=SMEM)
    vmem = pl.BlockSpec(memory_space=VMEM)
    params = pltpu.CompilerParams(vmem_limit_bytes=LIMIT)
    packed = pl.pallas_call(
        pack_kernel,
        out_shape=jax.ShapeDtypeStruct((tiles, blocks, 4, 3 * width), jnp.float32),
        in_specs=[smem] + [vmem] * 3,
        out_specs=vmem,
        compiler_params=params,
    )(me, panel_geometry.transpose(1, 0, 2), strengths, corner_vertex)
    got = lax.all_to_all(packed, "tiles", split_axis=0, concat_axis=0, tiled=True)
    partial = pl.pallas_call(
        pair_kernel,
        out_shape=jax.ShapeDtypeStruct((tiles, far, high, 3 * LANES), jnp.float32),
        in_specs=[smem] * 6 + [vmem] * 2,
        out_specs=vmem,
        scratch_shapes=[
            VMEM((blocks, 3, width, width), jnp.float32),
            VMEM((blocks, width, 8), jnp.bfloat16),
            VMEM((2, width, width), jnp.float32),
            VMEM((blocks, 3, width, width), jnp.float32),
            VMEM((tiles * blocks, 8, width), jnp.float32),
            VMEM((tiles, high, 3 * LANES), jnp.float32),
        ],
        compiler_params=params,
    )(
        me,
        pair_target,
        pair_owner[:, 0],
        pair_source,
        pair_order,
        pair_count,
        adjoint,
        got,
    )
    partial = partial.reshape(tiles * far, high, 3 * LANES)
    shares = lax.all_to_all(partial, ("tiles", "far"), split_axis=0, concat_axis=0, tiled=True)
    return pl.pallas_call(
        sum_kernel,
        out_shape=jax.ShapeDtypeStruct((3, blocks * width), jnp.float32),
        compiler_params=params,
    )(shares)


def solution(mesh):
    placed = (
        P("tiles", None, None),
        P("tiles", "far", None),
        P("tiles", "far", None),
        P("tiles"),
        P("tiles", None),
        P("tiles"),
        P("tiles"),
        P("tiles"),
        P("tiles", None, None),
    )
    return jax.shard_map(
        per_device, mesh=mesh, in_specs=placed, out_specs=P(None, "tiles"), check_vma=False
    )
```

```python
import jax
import jax.numpy as jnp
from jax import lax
from jax.experimental import pallas as pl
from jax.experimental.pallas import tpu as pltpu
from jax.sharding import PartitionSpec as P

SMEM = pltpu.SMEM
VMEM = pltpu.VMEM
LANES = 128
LIMIT = 48 * 1024 * 1024


def pack_kernel(me_ref, geom_ref, strength_ref, corner_ref, out_ref):
    tiles, blocks, _, _ = out_ref.shape
    width = strength_ref.shape[2]
    shift = (blocks * width).bit_length() - 1
    me = me_ref[0]
    for b in range(blocks):
        vertex = corner_ref[b]
        offset = (vertex >> shift) - me
        offset = jnp.where(offset < 0, offset + tiles, offset)
        slot = jnp.where(
            offset == 0,
            0,
            jnp.where(offset == 1, 1, jnp.where(offset == tiles - 1, 2, 3)),
        )
        place = ((slot << shift) + (vertex & ((1 << shift) - 1))).astype(jnp.float32)
        span = float(4 << shift)
        first = place[0:1] * span + place[1:2]
        second = place[2:3] * span + place[3:4]
        block = jnp.concatenate(
            [
                strength_ref[b].astype(jnp.float32),
                jnp.concatenate([geom_ref[c, b : b + 1] for c in range(3)] + [first], axis=0),
                jnp.concatenate([geom_ref[3 + c, b : b + 1] for c in range(3)] + [second], axis=0),
            ],
            axis=1,
        )
        for t in range(tiles):
            out_ref[t, b] = block


def split3(value):
    first = value.astype(jnp.bfloat16).astype(jnp.float32)
    rest = value - first
    second = rest.astype(jnp.bfloat16).astype(jnp.float32)
    return first, second, rest - second


def prep_kernel(geom_ref, adjoint_ref, centre_ref, left_ref):
    blocks, _, width = adjoint_ref.shape
    for b in range(blocks):
        point = jnp.concatenate([geom_ref[c, b : b + 1] for c in range(3)], axis=0)
        x1, x2, x3 = split3(point)
        n1, n2, n3 = split3(jnp.sum(point * point, axis=0, keepdims=True))
        ones = jnp.ones((3, width), jnp.float32)
        rows = [x1, x1, x1, x2, x2, x3, ones, n1, n2, n3, n1, n2, n1]
        rows += [adjoint_ref[b].astype(jnp.float32), jnp.zeros((1, width), jnp.float32)]
        left_ref[b] = jnp.concatenate(rows, axis=0).T.astype(jnp.bfloat16)
        for c in range(3):
            centre_ref[b, c] = jnp.broadcast_to(point[c : c + 1], (width, width)).T


def pair_kernel(
    me_ref,
    target_ref,
    owner_ref,
    source_ref,
    order_ref,
    count_ref,
    centre_ref,
    left_ref,
    got_ref,
    out_ref,
    right_ref,
    product_ref,
    row_acc,
    grad_ref,
    vertex_ref,
):
    tiles, blocks, _, _ = got_ref.shape
    width = centre_ref.shape[3]
    pairs = target_ref.shape[0]
    at_point, at_extent = width, 2 * width
    me = me_ref[0]
    live = count_ref[0]
    grad_ref[...] = jnp.zeros(grad_ref.shape, jnp.float32)
    row_acc[...] = jnp.zeros(row_acc.shape, jnp.float32)
    vertex_ref[...] = jnp.zeros(vertex_ref.shape, jnp.float32)
    right_ref[...] = jnp.zeros(right_ref.shape, jnp.float32)

    def reach_of(order):
        return 0.25 * jnp.where(
            order == 3, 0.7745966692414834, jnp.where(order == 2, 0.5773502691896258, 0.0)
        )

    def multiply(k, slot):
        alive = jnp.where(k < live, 1.0, 0.0).astype(jnp.float32)
        k = jnp.minimum(k, pairs - 1)
        owner = owner_ref[k]
        source = source_ref[k]
        order = order_ref[k]
        third = order == 3
        reach = reach_of(order)
        scale_mid = jnp.where(third, (4.0 / 9.0 / 512.0) ** (-2.0 / 3.0), 0.0)
        scale_side = jnp.where(
            third, (5.0 / 18.0 / 512.0) ** (-2.0 / 3.0), (0.5 / 512.0) ** (-2.0 / 3.0)
        )
        floor_mid = jnp.where(third, 0.0625 * (4.0 / 9.0 / 512.0) ** (-2.0 / 3.0), 3.0e38)
        point = got_ref[owner, source, 0:3, at_point : at_point + width]
        extent = got_ref[owner, source, 0:3, at_extent : at_extent + width] * reach
        nodes = ((point, scale_mid), (point + extent, scale_side), (point - extent, scale_side))
        for i, (node, scale) in enumerate(nodes):
            lanes = slice(i * width, (i + 1) * width)
            floor = floor_mid if i == 0 else 0.0625 * scale
            y1, y2, y3 = split3(node * (-2.0 * scale))
            n1, n2, n3 = split3(jnp.sum(node * node, axis=0, keepdims=True) * scale + floor)
            k1, k2, k3 = split3(jnp.full((1, width), 1.0, jnp.float32) * scale)
            rows = [y1, y2, y3, y1, y2, y1, n1, n2, n3, k1, k1, k1, k2, k2, k3]
            at = 0
            for row in rows:
                right_ref[slot, at : at + row.shape[0], lanes] = row
                at += row.shape[0]
        right_ref[slot, 27:31, 3 * width : 4 * width] = (
            got_ref[owner, source, :, 0:width] * alive
        )
        product_ref[slot] = jnp.dot(
            left_ref[target_ref[k]],
            right_ref[slot].astype(jnp.bfloat16),
            preferred_element_type=jnp.float32,
        )

    def one_pair(k, slot):
        k = jnp.minimum(k, pairs - 1)
        target = target_ref[k]
        owner = owner_ref[k]
        source = source_ref[k]
        reach = reach_of(order_ref[k])
        point = [got_ref[owner, source, c : c + 1, at_point : at_point + width] for c in range(3)]
        extent = [
            got_ref[owner, source, c : c + 1, at_extent : at_extent + width] * reach
            for c in range(3)
        ]
        step = 8
        columns = [jnp.zeros((step, width), jnp.float32) for _ in range(3)]
        for start in range(0, width, step):
            rows = slice(start, start + step)
            inverse = [
                lax.rsqrt(product_ref[slot, rows, i * width : (i + 1) * width]) for i in range(3)
            ]
            f_mid, f_plus, f_minus = [i * i * i for i in inverse]
            coupling = product_ref[slot, rows, 3 * width : 4 * width]
            even = coupling * (f_mid + (f_plus + f_minus))
            odd = coupling * (f_plus - f_minus)
            for c in range(3):
                pulled = even * (centre_ref[target, c, rows] - point[c]) - odd * extent[c]
                row_acc[target, c, rows] += pulled
                columns[c] = columns[c] + pulled
        sums = jnp.concatenate(
            [jnp.sum(columns[c], axis=0, keepdims=True) for c in range(3)], axis=0
        )
        at = owner * blocks + source
        grad_ref[at, 0:3] += sums

    def two_pairs(step, carry):
        for slot in range(2):
            one_pair(2 * step + slot, slot)
        for slot in range(2):
            multiply(2 * step + 2 + slot, slot)
        return carry

    for slot in range(2):
        multiply(slot, slot)
    lax.fori_loop(0, (live + 1) // 2, two_pairs, 0)
    for b in range(blocks):
        total = jnp.concatenate(
            [jnp.sum(row_acc[b, c], axis=1, keepdims=True) for c in range(3)]
            + [jnp.zeros((width, 5), jnp.float32)],
            axis=1,
        )
        grad_ref[me * blocks + b] -= total.T

    high = blocks * width // LANES
    keys = 4 * high
    shift = (blocks * width).bit_length() + 1
    pack = 16
    key_ids = lax.broadcasted_iota(jnp.int32, (keys, width), 0).astype(jnp.bfloat16)
    lane_ids = lax.broadcasted_iota(jnp.int32, (LANES, width), 0).astype(jnp.bfloat16)
    zero = jnp.zeros((keys, width), jnp.bfloat16)
    low_one = jnp.ones((pack, width), jnp.bfloat16)
    low_zero = jnp.zeros((pack, width), jnp.bfloat16)

    def rows_of(row, count):
        return jnp.broadcast_to(row, (count, width)).astype(jnp.bfloat16)

    def scatter(tile, carry):
        parts = []
        hots = []
        for b in range(blocks):
            grad = grad_ref[tile * blocks + b]
            upper = grad.astype(jnp.bfloat16).astype(jnp.float32)
            lower = grad - upper
            spread = [
                rows_of(part[c : c + 1], keys) for c in range(3) for part in (upper, lower)
            ]
            for half in (at_point, at_extent):
                code = got_ref[tile, b, 3:4, half : half + width].astype(jnp.int32)
                for place in (code >> shift, code & ((1 << shift) - 1)):
                    key = rows_of((place >> 7).astype(jnp.float32), keys)
                    low = rows_of((place & (LANES - 1)).astype(jnp.float32), pack)
                    mask = key_ids == key
                    parts.append(
                        jnp.concatenate([jnp.where(mask, s, zero) for s in spread], axis=0)
                    )
                    hots.append(
                        jnp.concatenate(
                            [
                                jnp.where(lane_ids[g : g + pack] == low, low_one, low_zero)
                                for g in range(0, LANES, pack)
                            ],
                            axis=0,
                        )
                    )
        result = lax.dot_general(
            jnp.concatenate(parts, axis=1),
            jnp.concatenate(hots, axis=1),
            (((1,), (1,)), ((), ())),
            preferred_element_type=jnp.float32,
        )
        joined = [
            result[2 * c * keys : (2 * c + 1) * keys]
            + result[(2 * c + 1) * keys : (2 * c + 2) * keys]
            for c in range(3)
        ]
        for slot, shift_by in enumerate((0, 1, tiles - 1, tiles // 2)):
            dest = lax.rem(tile + shift_by, tiles)
            for c in range(3):
                vertex_ref[dest, :, c * LANES : (c + 1) * LANES] += joined[c][
                    slot * high : (slot + 1) * high
                ]
        return carry

    lax.fori_loop(0, tiles, scatter, 0, unroll=2)
    for f in range(out_ref.shape[1]):
        out_ref[:, f] = vertex_ref[...]


def sum_kernel(got_ref, out_ref):
    _, high, _ = got_ref.shape
    total = jnp.sum(got_ref[...], axis=0)
    for c in range(3):
        for h in range(high):
            out_ref[c : c + 1, h * LANES : (h + 1) * LANES] = total[
                h : h + 1, c * LANES : (c + 1) * LANES
            ]


def per_device(
    panel_geometry,
    adjoint,
    strengths,
    pair_target,
    pair_owner,
    pair_source,
    pair_order,
    pair_count,
    corner_vertex,
):
    tiles = lax.axis_size("tiles")
    far = lax.axis_size("far")
    blocks, _, width = panel_geometry.shape
    high = blocks * width // LANES
    me = lax.axis_index("tiles").astype(jnp.int32).reshape(1)
    smem = pl.BlockSpec(memory_space=SMEM)
    vmem = pl.BlockSpec(memory_space=VMEM)
    params = pltpu.CompilerParams(vmem_limit_bytes=LIMIT)
    geometry = panel_geometry.transpose(1, 0, 2)
    packed = pl.pallas_call(
        pack_kernel,
        out_shape=jax.ShapeDtypeStruct((tiles, blocks, 4, 3 * width), jnp.float32),
        in_specs=[smem] + [vmem] * 3,
        out_specs=vmem,
    )(me, geometry, strengths, corner_vertex)
    got = lax.all_to_all(packed, "tiles", split_axis=0, concat_axis=0, tiled=True)
    centre, left = pl.pallas_call(
        prep_kernel,
        out_shape=(
            jax.ShapeDtypeStruct((blocks, 3, width, width), jnp.float32),
            jax.ShapeDtypeStruct((blocks, width, 32), jnp.bfloat16),
        ),
        compiler_params=params,
        cost_estimate=pl.CostEstimate(flops=4000000, bytes_accessed=900000, transcendentals=0),
    )(geometry, adjoint)
    partial = pl.pallas_call(
        pair_kernel,
        out_shape=jax.ShapeDtypeStruct((tiles, far, high, 3 * LANES), jnp.float32),
        in_specs=[smem] * 6 + [vmem] * 3,
        out_specs=vmem,
        scratch_shapes=[
            VMEM((2, 32, 4 * width), jnp.float32),
            VMEM((2, width, 4 * width), jnp.float32),
            VMEM((blocks, 3, width, width), jnp.float32),
            VMEM((tiles * blocks, 8, width), jnp.float32),
            VMEM((tiles, high, 3 * LANES), jnp.float32),
        ],
        compiler_params=params,
    )(
        me,
        pair_target,
        pair_owner[:, 0],
        pair_source,
        pair_order,
        pair_count,
        centre,
        left,
        got,
    )
    partial = partial.reshape(tiles * far, high, 3 * LANES)
    shares = lax.all_to_all(partial, ("tiles", "far"), split_axis=0, concat_axis=0, tiled=True)
    return pl.pallas_call(
        sum_kernel,
        out_shape=jax.ShapeDtypeStruct((3, blocks * width), jnp.float32),
        compiler_params=params,
    )(shares)


def solution(mesh):
    placed = (
        P("tiles", None, None),
        P("tiles", "far", None),
        P("tiles", "far", None),
        P("tiles"),
        P("tiles", None),
        P("tiles"),
        P("tiles"),
        P("tiles"),
        P("tiles", None, None),
    )
    return jax.shard_map(
        per_device, mesh=mesh, in_specs=placed, out_specs=P(None, "tiles"), check_vma=False
    )
```

```python
import jax
import jax.numpy as jnp
from jax import lax
from jax.experimental import pallas as pl
from jax.experimental.pallas import tpu as pltpu
from jax.sharding import PartitionSpec as P

SMEM = pltpu.SMEM
VMEM = pltpu.VMEM
LANES = 128
FIELDS = 4
SPARE = 2
LIMIT = 48 * 1024 * 1024


def pack_kernel(me_ref, geom_ref, strength_ref, corner_ref, out_ref):
    tiles, blocks, _, _ = out_ref.shape
    width = strength_ref.shape[2]
    shift = (blocks * width).bit_length() - 1
    me = me_ref[0]
    for b in range(blocks):
        vertex = corner_ref[b]
        offset = (vertex >> shift) - me
        offset = jnp.where(offset < 0, offset + tiles, offset)
        slot = jnp.where(
            offset == 0,
            0,
            jnp.where(offset == 1, 1, jnp.where(offset == tiles - 1, 2, 3)),
        )
        place = ((slot << shift) + (vertex & ((1 << shift) - 1))).astype(jnp.float32)
        span = float(4 << shift)
        first = place[0:1] * span + place[1:2]
        second = place[2:3] * span + place[3:4]
        block = jnp.concatenate(
            [
                strength_ref[b].astype(jnp.float32),
                jnp.concatenate([geom_ref[c, b : b + 1] for c in range(3)] + [first], axis=0),
                jnp.concatenate([geom_ref[3 + c, b : b + 1] for c in range(3)] + [second], axis=0),
            ],
            axis=1,
        )
        for t in range(tiles):
            out_ref[t, b] = block


def split3(value):
    first = value.astype(jnp.bfloat16).astype(jnp.float32)
    rest = value - first
    second = rest.astype(jnp.bfloat16).astype(jnp.float32)
    return first, second, rest - second


def prep_kernel(
    me_ref,
    target_ref,
    owner_ref,
    source_ref,
    order_ref,
    count_ref,
    geom_ref,
    adjoint_ref,
    info_ref,
    centre_ref,
    left_ref,
):
    blocks, _, width = adjoint_ref.shape
    pairs = target_ref.shape[0]
    live = count_ref[0]
    info_ref[0] = me_ref[0]
    info_ref[1] = live

    def note(k, carry):
        at = FIELDS * (k + 1)
        from_k = jnp.minimum(k, pairs - 1)
        info_ref[at] = target_ref[from_k]
        info_ref[at + 1] = owner_ref[from_k]
        info_ref[at + 2] = source_ref[from_k]
        info_ref[at + 3] = jnp.where(k < live, order_ref[from_k], 0)
        return carry

    lax.fori_loop(0, pairs + SPARE, note, 0)
    for b in range(blocks):
        point = jnp.concatenate([geom_ref[c, b : b + 1] for c in range(3)], axis=0)
        rows = [point, jnp.ones((1, width), jnp.float32)]
        rows += [jnp.sum(point * point, axis=0, keepdims=True)]
        rows += [jnp.zeros((3, width), jnp.float32)]
        x1, x2, x3 = split3(jnp.concatenate(rows, axis=0))
        values = [adjoint_ref[b].astype(jnp.float32), jnp.zeros((4, width), jnp.float32)]
        rows = [x1, x1, x1, x2, x2, x3] + values
        left_ref[b] = jnp.concatenate(rows, axis=0).T.astype(jnp.bfloat16)
        for c in range(3):
            centre_ref[b, c] = jnp.broadcast_to(point[c : c + 1], (width, width)).T


def pair_kernel(
    info_ref,
    centre_ref,
    left_ref,
    got_ref,
    out_ref,
    product_ref,
    row_acc,
    grad_ref,
    vertex_ref,
):
    tiles, blocks, _, _ = got_ref.shape
    width = centre_ref.shape[3]
    at_point, at_extent = width, 2 * width
    me = info_ref[0]
    live = info_ref[1]
    grad_ref[...] = jnp.zeros(grad_ref.shape, jnp.float32)
    row_acc[...] = jnp.zeros(row_acc.shape, jnp.float32)
    vertex_ref[...] = jnp.zeros(vertex_ref.shape, jnp.float32)
    blank = jnp.zeros((4, width), jnp.float32)
    row_ids = lax.broadcasted_iota(jnp.int32, (8, width), 0)

    def reach_of(order):
        return 0.25 * jnp.where(
            order == 3, 0.7745966692414834, jnp.where(order == 2, 0.5773502691896258, 0.0)
        )

    def multiply(k, slot):
        at = FIELDS * (k + 1)
        target = info_ref[at]
        owner = info_ref[at + 1]
        source = info_ref[at + 2]
        order = info_ref[at + 3]
        third = order == 3
        alive = jnp.where(order > 0, 1.0, 0.0).astype(jnp.float32)
        reach = reach_of(order)
        scale_mid = jnp.where(third, (4.0 / 9.0 / 512.0) ** (-2.0 / 3.0), 0.0)
        scale_side = jnp.where(
            third, (5.0 / 18.0 / 512.0) ** (-2.0 / 3.0), (0.5 / 512.0) ** (-2.0 / 3.0)
        )
        floor_mid = jnp.where(third, 0.0625 * (4.0 / 9.0 / 512.0) ** (-2.0 / 3.0), 3.0e38)
        floor_side = 0.0625 * scale_side
        point = got_ref[owner, source, :, at_point : at_point + width]
        extent = got_ref[owner, source, :, at_extent : at_extent + width] * reach
        inside = row_ids < 3
        point = jnp.where(inside, jnp.concatenate([point, blank], axis=0), 0.0)
        extent = jnp.where(inside, jnp.concatenate([extent, blank], axis=0), 0.0)
        values = jnp.concatenate([got_ref[owner, source, :, 0:width] * alive, blank], axis=0)
        empty = jnp.zeros((8, width), jnp.float32)
        nodes = (
            (point, scale_mid, floor_mid),
            (point + extent, scale_side, floor_side),
            (point - extent, scale_side, floor_side),
        )
        columns = []
        for node, scale, floor in nodes:
            norm = jnp.sum(node * node, axis=0, keepdims=True) * scale + floor
            rows = jnp.where(
                row_ids == 3,
                norm,
                jnp.where(row_ids == 4, scale, node * (-2.0 * scale)),
            )
            p1, p2, p3 = split3(rows)
            columns.append(jnp.concatenate([p1, p2, p3, p1, p2, p1, empty], axis=0))
        columns.append(jnp.concatenate([empty] * 6 + [values], axis=0))
        product_ref[slot] = jnp.dot(
            left_ref[target],
            jnp.concatenate(columns, axis=1).astype(jnp.bfloat16),
            preferred_element_type=jnp.float32,
        )

    def one_pair(k, slot):
        at = FIELDS * (k + 1)
        target = info_ref[at]
        owner = info_ref[at + 1]
        source = info_ref[at + 2]
        reach = reach_of(info_ref[at + 3])
        point = [got_ref[owner, source, c : c + 1, at_point : at_point + width] for c in range(3)]
        extent = [
            got_ref[owner, source, c : c + 1, at_extent : at_extent + width] * reach
            for c in range(3)
        ]
        step = 8
        columns = [jnp.zeros((step, width), jnp.float32) for _ in range(3)]
        for start in range(0, width, step):
            rows = slice(start, start + step)
            inverse = [
                lax.rsqrt(product_ref[slot, rows, i * width : (i + 1) * width]) for i in range(3)
            ]
            f_mid, f_plus, f_minus = [i * i * i for i in inverse]
            coupling = product_ref[slot, rows, 3 * width : 4 * width]
            even = coupling * (f_mid + (f_plus + f_minus))
            odd = coupling * (f_plus - f_minus)
            for c in range(3):
                pulled = even * (centre_ref[target, c, rows] - point[c]) - odd * extent[c]
                row_acc[target, c, rows] += pulled
                columns[c] = columns[c] + pulled
        sums = jnp.concatenate(
            [jnp.sum(columns[c], axis=0, keepdims=True) for c in range(3)], axis=0
        )
        grad_ref[owner * blocks + source, 0:3] += sums

    def two_pairs(step, carry):
        for slot in range(2):
            multiply(2 * step + slot + 1, 1 - slot)
            one_pair(2 * step + slot, slot)
        return carry

    multiply(0, 0)
    lax.fori_loop(0, (live + 1) // 2, two_pairs, 0)
    for b in range(blocks):
        total = jnp.concatenate(
            [jnp.sum(row_acc[b, c], axis=1, keepdims=True) for c in range(3)]
            + [jnp.zeros((width, 5), jnp.float32)],
            axis=1,
        )
        grad_ref[me * blocks + b] -= total.T

    high = blocks * width // LANES
    keys = 4 * high
    shift = (blocks * width).bit_length() + 1
    pack = 16
    key_ids = lax.broadcasted_iota(jnp.int32, (keys, width), 0).astype(jnp.bfloat16)
    lane_ids = lax.broadcasted_iota(jnp.int32, (LANES, width), 0).astype(jnp.bfloat16)
    zero = jnp.zeros((keys, width), jnp.bfloat16)
    low_one = jnp.ones((pack, width), jnp.bfloat16)
    low_zero = jnp.zeros((pack, width), jnp.bfloat16)

    def rows_of(row, count):
        return jnp.broadcast_to(row, (count, width)).astype(jnp.bfloat16)

    def scatter(tile, carry):
        parts = []
        hots = []
        for b in range(blocks):
            grad = grad_ref[tile * blocks + b]
            upper = grad.astype(jnp.bfloat16).astype(jnp.float32)
            lower = grad - upper
            spread = [
                rows_of(part[c : c + 1], keys) for c in range(3) for part in (upper, lower)
            ]
            for half in (at_point, at_extent):
                code = got_ref[tile, b, 3:4, half : half + width].astype(jnp.int32)
                for place in (code >> shift, code & ((1 << shift) - 1)):
                    key = rows_of((place >> 7).astype(jnp.float32), keys)
                    low = rows_of((place & (LANES - 1)).astype(jnp.float32), pack)
                    mask = key_ids == key
                    parts.append(
                        jnp.concatenate([jnp.where(mask, s, zero) for s in spread], axis=0)
                    )
                    hots.append(
                        jnp.concatenate(
                            [
                                jnp.where(lane_ids[g : g + pack] == low, low_one, low_zero)
                                for g in range(0, LANES, pack)
                            ],
                            axis=0,
                        )
                    )
        result = lax.dot_general(
            jnp.concatenate(parts, axis=1),
            jnp.concatenate(hots, axis=1),
            (((1,), (1,)), ((), ())),
            preferred_element_type=jnp.float32,
        )
        joined = [
            result[2 * c * keys : (2 * c + 1) * keys]
            + result[(2 * c + 1) * keys : (2 * c + 2) * keys]
            for c in range(3)
        ]
        for slot, shift_by in enumerate((0, 1, tiles - 1, tiles // 2)):
            dest = lax.rem(tile + shift_by, tiles)
            for c in range(3):
                vertex_ref[dest, :, c * LANES : (c + 1) * LANES] += joined[c][
                    slot * high : (slot + 1) * high
                ]
        return carry

    lax.fori_loop(0, tiles, scatter, 0, unroll=2)
    for f in range(out_ref.shape[1]):
        out_ref[:, f] = vertex_ref[...]


def sum_kernel(got_ref, out_ref):
    _, high, _ = got_ref.shape
    total = jnp.sum(got_ref[...], axis=0)
    for c in range(3):
        for h in range(high):
            out_ref[c : c + 1, h * LANES : (h + 1) * LANES] = total[
                h : h + 1, c * LANES : (c + 1) * LANES
            ]


def per_device(
    panel_geometry,
    adjoint,
    strengths,
    pair_target,
    pair_owner,
    pair_source,
    pair_order,
    pair_count,
    corner_vertex,
):
    tiles = lax.axis_size("tiles")
    far = lax.axis_size("far")
    blocks, _, width = panel_geometry.shape
    high = blocks * width // LANES
    me = lax.axis_index("tiles").astype(jnp.int32).reshape(1)
    smem = pl.BlockSpec(memory_space=SMEM)
    vmem = pl.BlockSpec(memory_space=VMEM)
    params = pltpu.CompilerParams(vmem_limit_bytes=LIMIT)
    geometry = panel_geometry.transpose(1, 0, 2)
    packed = pl.pallas_call(
        pack_kernel,
        out_shape=jax.ShapeDtypeStruct((tiles, blocks, 4, 3 * width), jnp.float32),
        in_specs=[smem] + [vmem] * 3,
        out_specs=vmem,
    )(me, geometry, strengths, corner_vertex)
    got = lax.all_to_all(packed, "tiles", split_axis=0, concat_axis=0, tiled=True)
    pairs = pair_target.shape[0]
    info, centre, left = pl.pallas_call(
        prep_kernel,
        out_shape=(
            jax.ShapeDtypeStruct((FIELDS * (pairs + SPARE + 1),), jnp.int32),
            jax.ShapeDtypeStruct((blocks, 3, width, width), jnp.float32),
            jax.ShapeDtypeStruct((blocks, width, 56), jnp.bfloat16),
        ),
        in_specs=[smem] * 6 + [vmem] * 2,
        out_specs=(smem, vmem, vmem),
        compiler_params=params,
        cost_estimate=pl.CostEstimate(flops=4000000, bytes_accessed=900000, transcendentals=0),
    )(
        me,
        pair_target,
        pair_owner[:, 0],
        pair_source,
        pair_order,
        pair_count,
        geometry,
        adjoint,
    )
    partial = pl.pallas_call(
        pair_kernel,
        out_shape=jax.ShapeDtypeStruct((tiles, far, high, 3 * LANES), jnp.float32),
        in_specs=[smem] + [vmem] * 3,
        out_specs=vmem,
        scratch_shapes=[
            VMEM((2, width, 4 * width), jnp.float32),
            VMEM((blocks, 3, width, width), jnp.float32),
            VMEM((tiles * blocks, 8, width), jnp.float32),
            VMEM((tiles, high, 3 * LANES), jnp.float32),
        ],
        compiler_params=params,
    )(info, centre, left, got)
    partial = partial.reshape(tiles * far, high, 3 * LANES)
    shares = lax.all_to_all(partial, ("tiles", "far"), split_axis=0, concat_axis=0, tiled=True)
    return pl.pallas_call(
        sum_kernel,
        out_shape=jax.ShapeDtypeStruct((3, blocks * width), jnp.float32),
        compiler_params=params,
    )(shares)


def solution(mesh):
    placed = (
        P("tiles", None, None),
        P("tiles", "far", None),
        P("tiles", "far", None),
        P("tiles"),
        P("tiles", None),
        P("tiles"),
        P("tiles"),
        P("tiles"),
        P("tiles", None, None),
    )
    return jax.shard_map(
        per_device, mesh=mesh, in_specs=placed, out_specs=P(None, "tiles"), check_vma=False
    )
```

```python
import jax
import jax.numpy as jnp
from jax import lax
from jax.experimental import pallas as pl
from jax.experimental.pallas import tpu as pltpu
from jax.sharding import PartitionSpec as P

SMEM = pltpu.SMEM
VMEM = pltpu.VMEM
LANES = 128
FIELDS = 4
SPARE = 2
GROUP = 32
LIMIT = 48 * 1024 * 1024


def pack_kernel(me_ref, geom_ref, strength_ref, corner_ref, out_ref):
    tiles, blocks, _, _ = out_ref.shape
    width = strength_ref.shape[2]
    shift = (blocks * width).bit_length() - 1
    me = me_ref[0]
    for b in range(blocks):
        vertex = corner_ref[b]
        offset = (vertex >> shift) - me
        offset = jnp.where(offset < 0, offset + tiles, offset)
        slot = jnp.where(
            offset == 0,
            0,
            jnp.where(offset == 1, 1, jnp.where(offset == tiles - 1, 2, 3)),
        )
        place = ((slot << shift) + (vertex & ((1 << shift) - 1))).astype(jnp.float32)
        span = float(4 << shift)
        first = place[0:1] * span + place[1:2]
        second = place[2:3] * span + place[3:4]
        block = jnp.concatenate(
            [
                strength_ref[b].astype(jnp.float32),
                jnp.concatenate([geom_ref[c, b : b + 1] for c in range(3)] + [first], axis=0),
                jnp.concatenate([geom_ref[3 + c, b : b + 1] for c in range(3)] + [second], axis=0),
            ],
            axis=1,
        )
        for t in range(tiles):
            out_ref[t, b] = block


def split3(value):
    first = value.astype(jnp.bfloat16).astype(jnp.float32)
    rest = value - first
    second = rest.astype(jnp.bfloat16).astype(jnp.float32)
    return first, second, rest - second


def prep_kernel(
    me_ref,
    target_ref,
    owner_ref,
    source_ref,
    order_ref,
    count_ref,
    geom_ref,
    adjoint_ref,
    info_ref,
    centre_ref,
    left_ref,
):
    blocks, _, width = adjoint_ref.shape
    pairs = target_ref.shape[0]
    live = count_ref[0]
    info_ref[0] = me_ref[0]
    info_ref[1] = live

    def note(k, carry):
        at = FIELDS * (k + 1)
        from_k = jnp.minimum(k, pairs - 1)
        info_ref[at] = target_ref[from_k]
        info_ref[at + 1] = owner_ref[from_k]
        info_ref[at + 2] = source_ref[from_k]
        info_ref[at + 3] = jnp.where(k < live, order_ref[from_k], 0)
        return carry

    lax.fori_loop(0, pairs + SPARE, note, 0)
    for b in range(blocks):
        point = jnp.concatenate([geom_ref[c, b : b + 1] for c in range(3)], axis=0)
        rows = [point, jnp.ones((1, width), jnp.float32)]
        rows += [jnp.sum(point * point, axis=0, keepdims=True)]
        rows += [jnp.zeros((3, width), jnp.float32)]
        x1, x2, x3 = split3(jnp.concatenate(rows, axis=0))
        values = [adjoint_ref[b].astype(jnp.float32), jnp.zeros((4, width), jnp.float32)]
        rows = [x1, x1, x1, x2, x2, x3] + values
        left_ref[b] = jnp.concatenate(rows, axis=0).T.astype(jnp.bfloat16)
        for c in range(3):
            centre_ref[b, c] = jnp.broadcast_to(point[c : c + 1], (width, width)).T


def pair_kernel(
    info_ref,
    centre_ref,
    left_ref,
    got_ref,
    out_ref,
    product_ref,
    row_acc,
    grad_ref,
    vertex_ref,
):
    tiles, blocks, _, _ = got_ref.shape
    width = centre_ref.shape[3]
    at_point, at_extent = width, 2 * width
    me = info_ref[0]
    live = info_ref[1]
    grad_ref[...] = jnp.zeros(grad_ref.shape, jnp.float32)
    row_acc[...] = jnp.zeros(row_acc.shape, jnp.float32)
    vertex_ref[...] = jnp.zeros(vertex_ref.shape, jnp.float32)
    blank = jnp.zeros((4, width), jnp.float32)
    row_ids = lax.broadcasted_iota(jnp.int32, (8, width), 0)

    def reach_of(order):
        return 0.25 * jnp.where(
            order == 3, 0.7745966692414834, jnp.where(order == 2, 0.5773502691896258, 0.0)
        )

    def multiply(k, slot):
        at = FIELDS * (k + 1)
        target = info_ref[at]
        owner = info_ref[at + 1]
        source = info_ref[at + 2]
        order = info_ref[at + 3]
        third = order == 3
        alive = jnp.where(order > 0, 1.0, 0.0).astype(jnp.float32)
        reach = reach_of(order)
        scale_mid = jnp.where(third, (4.0 / 9.0 / 512.0) ** (-2.0 / 3.0), 0.0)
        scale_side = jnp.where(
            third, (5.0 / 18.0 / 512.0) ** (-2.0 / 3.0), (0.5 / 512.0) ** (-2.0 / 3.0)
        )
        floor_mid = jnp.where(third, 0.0625 * (4.0 / 9.0 / 512.0) ** (-2.0 / 3.0), 3.0e38)
        floor_side = 0.0625 * scale_side
        point = got_ref[owner, source, :, at_point : at_point + width]
        extent = got_ref[owner, source, :, at_extent : at_extent + width] * reach
        inside = row_ids < 3
        point = jnp.where(inside, jnp.concatenate([point, blank], axis=0), 0.0)
        extent = jnp.where(inside, jnp.concatenate([extent, blank], axis=0), 0.0)
        values = jnp.concatenate([got_ref[owner, source, :, 0:width] * alive, blank], axis=0)
        empty = jnp.zeros((8, width), jnp.float32)
        nodes = (
            (point, scale_mid, floor_mid),
            (point + extent, scale_side, floor_side),
            (point - extent, scale_side, floor_side),
        )
        columns = []
        for node, scale, floor in nodes:
            norm = jnp.sum(node * node, axis=0, keepdims=True) * scale + floor
            rows = jnp.where(
                row_ids == 3,
                norm,
                jnp.where(row_ids == 4, scale, node * (-2.0 * scale)),
            )
            p1, p2, p3 = split3(rows)
            columns.append(jnp.concatenate([p1, p2, p3, p1, p2, p1, empty], axis=0))
        columns.append(jnp.concatenate([empty] * 6 + [values], axis=0))
        product_ref[slot] = jnp.dot(
            left_ref[target],
            jnp.concatenate(columns, axis=1).astype(jnp.bfloat16),
            preferred_element_type=jnp.float32,
        )

    def one_pair(k, slot):
        at = FIELDS * (k + 1)
        target = info_ref[at]
        owner = info_ref[at + 1]
        source = info_ref[at + 2]
        reach = reach_of(info_ref[at + 3])
        point = [got_ref[owner, source, c : c + 1, at_point : at_point + width] for c in range(3)]
        extent = [
            got_ref[owner, source, c : c + 1, at_extent : at_extent + width] * reach
            for c in range(3)
        ]
        columns = [jnp.zeros((8, width), jnp.float32) for _ in range(3)]
        for start in range(0, width, GROUP):
            rows = slice(start, start + GROUP)
            sums = [row_acc[target, c, rows] for c in range(3)]
            inverse = [
                lax.rsqrt(product_ref[slot, rows, i * width : (i + 1) * width]) for i in range(3)
            ]
            f_mid, f_plus, f_minus = [i * i * i for i in inverse]
            coupling = product_ref[slot, rows, 3 * width : 4 * width]
            even = coupling * (f_mid + (f_plus + f_minus))
            odd = coupling * (f_plus - f_minus)
            for c in range(3):
                pulled = even * (centre_ref[target, c, rows] - point[c]) - odd * extent[c]
                sums[c] = sums[c] + pulled
                for r in range(0, GROUP, 8):
                    columns[c] = columns[c] + pulled[r : r + 8]
            for c in range(3):
                row_acc[target, c, rows] = sums[c]
        sums = jnp.concatenate(
            [jnp.sum(columns[c], axis=0, keepdims=True) for c in range(3)], axis=0
        )
        grad_ref[owner * blocks + source, 0:3] += sums

    def two_pairs(step, carry):
        for slot in range(2):
            multiply(2 * step + slot + 1, 1 - slot)
            one_pair(2 * step + slot, slot)
        return carry

    multiply(0, 0)
    lax.fori_loop(0, (live + 1) // 2, two_pairs, 0)
    for b in range(blocks):
        total = jnp.concatenate(
            [jnp.sum(row_acc[b, c], axis=1, keepdims=True) for c in range(3)]
            + [jnp.zeros((width, 5), jnp.float32)],
            axis=1,
        )
        grad_ref[me * blocks + b] -= total.T

    high = blocks * width // LANES
    keys = 4 * high
    shift = (blocks * width).bit_length() + 1
    pack = 16
    key_ids = lax.broadcasted_iota(jnp.int32, (keys, width), 0).astype(jnp.bfloat16)
    lane_ids = lax.broadcasted_iota(jnp.int32, (LANES, width), 0).astype(jnp.bfloat16)
    zero = jnp.zeros((keys, width), jnp.bfloat16)
    low_one = jnp.ones((pack, width), jnp.bfloat16)
    low_zero = jnp.zeros((pack, width), jnp.bfloat16)

    def rows_of(row, count):
        return jnp.broadcast_to(row, (count, width)).astype(jnp.bfloat16)

    def scatter(tile, carry):
        parts = []
        hots = []
        for b in range(blocks):
            grad = grad_ref[tile * blocks + b]
            upper = grad.astype(jnp.bfloat16).astype(jnp.float32)
            lower = grad - upper
            spread = [
                rows_of(part[c : c + 1], keys) for c in range(3) for part in (upper, lower)
            ]
            for half in (at_point, at_extent):
                code = got_ref[tile, b, 3:4, half : half + width].astype(jnp.int32)
                for place in (code >> shift, code & ((1 << shift) - 1)):
                    key = rows_of((place >> 7).astype(jnp.float32), keys)
                    low = rows_of((place & (LANES - 1)).astype(jnp.float32), pack)
                    mask = key_ids == key
                    parts.append(
                        jnp.concatenate([jnp.where(mask, s, zero) for s in spread], axis=0)
                    )
                    hots.append(
                        jnp.concatenate(
                            [
                                jnp.where(lane_ids[g : g + pack] == low, low_one, low_zero)
                                for g in range(0, LANES, pack)
                            ],
                            axis=0,
                        )
                    )
        result = lax.dot_general(
            jnp.concatenate(parts, axis=1),
            jnp.concatenate(hots, axis=1),
            (((1,), (1,)), ((), ())),
            preferred_element_type=jnp.float32,
        )
        joined = [
            result[2 * c * keys : (2 * c + 1) * keys]
            + result[(2 * c + 1) * keys : (2 * c + 2) * keys]
            for c in range(3)
        ]
        places = [lax.rem(tile + by, tiles) for by in (0, 1, tiles - 1, tiles // 2)]
        before = [vertex_ref[dest] for dest in places]
        for slot, dest in enumerate(places):
            added = jnp.concatenate(
                [joined[c][slot * high : (slot + 1) * high] for c in range(3)], axis=1
            )
            vertex_ref[dest] = before[slot] + added
        return carry

    lax.fori_loop(0, tiles, scatter, 0, unroll=2)
    for f in range(out_ref.shape[1]):
        out_ref[:, f] = vertex_ref[...]


def sum_kernel(got_ref, out_ref):
    _, high, _ = got_ref.shape
    total = jnp.sum(got_ref[...], axis=0)
    for c in range(3):
        for h in range(high):
            out_ref[c : c + 1, h * LANES : (h + 1) * LANES] = total[
                h : h + 1, c * LANES : (c + 1) * LANES
            ]


def per_device(
    panel_geometry,
    adjoint,
    strengths,
    pair_target,
    pair_owner,
    pair_source,
    pair_order,
    pair_count,
    corner_vertex,
):
    tiles = lax.axis_size("tiles")
    far = lax.axis_size("far")
    blocks, _, width = panel_geometry.shape
    high = blocks * width // LANES
    me = lax.axis_index("tiles").astype(jnp.int32).reshape(1)
    smem = pl.BlockSpec(memory_space=SMEM)
    vmem = pl.BlockSpec(memory_space=VMEM)
    params = pltpu.CompilerParams(vmem_limit_bytes=LIMIT)
    geometry = panel_geometry.transpose(1, 0, 2)
    packed = pl.pallas_call(
        pack_kernel,
        out_shape=jax.ShapeDtypeStruct((tiles, blocks, 4, 3 * width), jnp.float32),
        in_specs=[smem] + [vmem] * 3,
        out_specs=vmem,
    )(me, geometry, strengths, corner_vertex)
    got = lax.all_to_all(packed, "tiles", split_axis=0, concat_axis=0, tiled=True)
    pairs = pair_target.shape[0]
    info, centre, left = pl.pallas_call(
        prep_kernel,
        out_shape=(
            jax.ShapeDtypeStruct((FIELDS * (pairs + SPARE + 1),), jnp.int32),
            jax.ShapeDtypeStruct((blocks, 3, width, width), jnp.float32),
            jax.ShapeDtypeStruct((blocks, width, 56), jnp.bfloat16),
        ),
        in_specs=[smem] * 6 + [vmem] * 2,
        out_specs=(smem, vmem, vmem),
        compiler_params=params,
        cost_estimate=pl.CostEstimate(flops=4000000, bytes_accessed=900000, transcendentals=0),
    )(
        me,
        pair_target,
        pair_owner[:, 0],
        pair_source,
        pair_order,
        pair_count,
        geometry,
        adjoint,
    )
    partial = pl.pallas_call(
        pair_kernel,
        out_shape=jax.ShapeDtypeStruct((tiles, far, high, 3 * LANES), jnp.float32),
        in_specs=[smem] + [vmem] * 3,
        out_specs=vmem,
        scratch_shapes=[
            VMEM((2, width, 4 * width), jnp.float32),
            VMEM((blocks, 3, width, width), jnp.float32),
            VMEM((tiles * blocks, 8, width), jnp.float32),
            VMEM((tiles, high, 3 * LANES), jnp.float32),
        ],
        compiler_params=params,
    )(info, centre, left, got)
    partial = partial.reshape(tiles * far, high, 3 * LANES)
    shares = lax.all_to_all(partial, ("tiles", "far"), split_axis=0, concat_axis=0, tiled=True)
    return pl.pallas_call(
        sum_kernel,
        out_shape=jax.ShapeDtypeStruct((3, blocks * width), jnp.float32),
        compiler_params=params,
    )(shares)


def solution(mesh):
    placed = (
        P("tiles", None, None),
        P("tiles", "far", None),
        P("tiles", "far", None),
        P("tiles"),
        P("tiles", None),
        P("tiles"),
        P("tiles"),
        P("tiles"),
        P("tiles", None, None),
    )
    return jax.shard_map(
        per_device, mesh=mesh, in_specs=placed, out_specs=P(None, "tiles"), check_vma=False
    )
```

```python
import jax
import jax.numpy as jnp
from jax import lax
from jax.experimental import pallas as pl
from jax.experimental.pallas import tpu as pltpu
from jax.sharding import PartitionSpec as P

SMEM = pltpu.SMEM
VMEM = pltpu.VMEM
LANES = 128
HEAD = 4
SPARE = 2
GROUP = 32
LIMIT = 48 * 1024 * 1024


def pack_kernel(me_ref, geom_ref, strength_ref, corner_ref, out_ref):
    tiles, blocks, _, _ = out_ref.shape
    width = strength_ref.shape[2]
    shift = (blocks * width).bit_length() - 1
    me = me_ref[0]
    for b in range(blocks):
        vertex = corner_ref[b]
        offset = (vertex >> shift) - me
        offset = jnp.where(offset < 0, offset + tiles, offset)
        slot = jnp.where(
            offset == 0,
            0,
            jnp.where(offset == 1, 1, jnp.where(offset == tiles - 1, 2, 3)),
        )
        place = ((slot << shift) + (vertex & ((1 << shift) - 1))).astype(jnp.float32)
        span = float(4 << shift)
        first = place[0:1] * span + place[1:2]
        second = place[2:3] * span + place[3:4]
        block = jnp.concatenate(
            [
                strength_ref[b].astype(jnp.float32),
                jnp.concatenate([geom_ref[c, b : b + 1] for c in range(3)] + [first], axis=0),
                jnp.concatenate([geom_ref[3 + c, b : b + 1] for c in range(3)] + [second], axis=0),
            ],
            axis=1,
        )
        for t in range(tiles):
            out_ref[t, b] = block


def split3(value):
    first = value.astype(jnp.bfloat16).astype(jnp.float32)
    rest = value - first
    second = rest.astype(jnp.bfloat16).astype(jnp.float32)
    return first, second, rest - second


def prep_kernel(
    me_ref,
    target_ref,
    owner_ref,
    source_ref,
    order_ref,
    count_ref,
    geom_ref,
    adjoint_ref,
    info_ref,
    centre_ref,
    left_ref,
):
    blocks, _, width = adjoint_ref.shape
    live = count_ref[0]
    total = target_ref.shape[0]
    for k in range(HEAD + total, HEAD + total + SPARE):
        info_ref[k] = 0

    def note(order, first):
        def one(k, at):
            mine = order_ref[k] == order
            word = (owner_ref[k] << 18) | (order << 16) | (source_ref[k] << 8) | target_ref[k]
            info_ref[at] = word
            return at + jnp.where(mine, 1, 0)

        return lax.fori_loop(0, live, one, first)

    third = note(3, HEAD)
    second = note(2, third)
    first = note(1, second)
    for k in range(SPARE):
        info_ref[first + k] = 0
    info_ref[0] = me_ref[0]
    info_ref[1] = (third - HEAD + 1) // 2
    info_ref[2] = (second - HEAD + 1) // 2
    info_ref[3] = (live + 1) // 2
    for b in range(blocks):
        point = jnp.concatenate([geom_ref[c, b : b + 1] for c in range(3)], axis=0)
        rows = [point, jnp.ones((1, width), jnp.float32)]
        rows += [jnp.sum(point * point, axis=0, keepdims=True)]
        rows += [jnp.zeros((3, width), jnp.float32)]
        x1, x2, x3 = split3(jnp.concatenate(rows, axis=0))
        values = [adjoint_ref[b].astype(jnp.float32), jnp.zeros((4, width), jnp.float32)]
        rows = [x1, x1, x1, x2, x2, x3] + values
        left_ref[b] = jnp.concatenate(rows, axis=0).T.astype(jnp.bfloat16)
        for c in range(3):
            centre_ref[b, c] = jnp.broadcast_to(point[c : c + 1], (width, width)).T


def pair_kernel(
    info_ref,
    centre_ref,
    left_ref,
    got_ref,
    out_ref,
    product_ref,
    row_acc,
    grad_ref,
    joined_ref,
):
    tiles, blocks, _, _ = got_ref.shape
    width = centre_ref.shape[3]
    at_point, at_extent = width, 2 * width
    me = info_ref[0]
    grad_ref[...] = jnp.zeros(grad_ref.shape, jnp.float32)
    row_acc[...] = jnp.zeros(row_acc.shape, jnp.float32)
    blank = jnp.zeros((4, width), jnp.float32)
    row_ids = lax.broadcasted_iota(jnp.int32, (8, width), 0)

    def reach_of(order):
        return 0.25 * jnp.where(
            order == 3, 0.7745966692414834, jnp.where(order == 2, 0.5773502691896258, 0.0)
        )

    def read(k):
        word = info_ref[HEAD + k]
        return word & 255, word >> 18, (word >> 8) & 255, (word >> 16) & 3

    def multiply(k, slot):
        target, owner, source, order = read(k)
        third = order == 3
        alive = jnp.where(order > 0, 1.0, 0.0).astype(jnp.float32)
        reach = reach_of(order)
        scale_mid = jnp.where(third, (4.0 / 9.0 / 512.0) ** (-2.0 / 3.0), 0.0)
        scale_side = jnp.where(
            third, (5.0 / 18.0 / 512.0) ** (-2.0 / 3.0), (0.5 / 512.0) ** (-2.0 / 3.0)
        )
        floor_mid = jnp.where(third, 0.0625 * (4.0 / 9.0 / 512.0) ** (-2.0 / 3.0), 3.0e38)
        floor_side = 0.0625 * scale_side
        point = got_ref[owner, source, :, at_point : at_point + width]
        extent = got_ref[owner, source, :, at_extent : at_extent + width] * reach
        inside = row_ids < 3
        point = jnp.where(inside, jnp.concatenate([point, blank], axis=0), 0.0)
        extent = jnp.where(inside, jnp.concatenate([extent, blank], axis=0), 0.0)
        values = jnp.concatenate([got_ref[owner, source, :, 0:width] * alive, blank], axis=0)
        empty = jnp.zeros((8, width), jnp.float32)
        nodes = (
            (point, scale_mid, floor_mid),
            (point + extent, scale_side, floor_side),
            (point - extent, scale_side, floor_side),
        )
        columns = []
        for node, scale, floor in nodes:
            norm = jnp.sum(node * node, axis=0, keepdims=True) * scale + floor
            rows = jnp.where(
                row_ids == 3,
                norm,
                jnp.where(row_ids == 4, scale, node * (-2.0 * scale)),
            )
            p1, p2, p3 = split3(rows)
            columns.append(jnp.concatenate([p1, p2, p3, p1, p2, p1, empty], axis=0))
        columns.append(jnp.concatenate([empty] * 6 + [values], axis=0))
        product_ref[slot] = jnp.dot(
            left_ref[target],
            jnp.concatenate(columns, axis=1).astype(jnp.bfloat16),
            preferred_element_type=jnp.float32,
        )

    def one_pair(k, slot, nodes):
        target, owner, source, order = read(k)
        reach = reach_of(order)
        point = [got_ref[owner, source, c : c + 1, at_point : at_point + width] for c in range(3)]
        extent = [
            got_ref[owner, source, c : c + 1, at_extent : at_extent + width] * reach
            for c in range(3)
        ]
        columns = [jnp.zeros((8, width), jnp.float32) for _ in range(3)]
        for start in range(0, width, GROUP):
            rows = slice(start, start + GROUP)
            sums = [row_acc[target, c, rows] for c in range(3)]

            def cubed(node):
                i = lax.rsqrt(product_ref[slot, rows, node * width : (node + 1) * width])
                return i * i * i

            coupling = product_ref[slot, rows, 3 * width : 4 * width]
            f_plus = cubed(1)
            if nodes == 1:
                even = (coupling + coupling) * f_plus
            else:
                f_minus = cubed(2)
                both = f_plus + f_minus
                even = coupling * (both + cubed(0) if nodes == 3 else both)
                odd = coupling * (f_plus - f_minus)
            for c in range(3):
                pulled = even * (centre_ref[target, c, rows] - point[c])
                if nodes > 1:
                    pulled = pulled - odd * extent[c]
                sums[c] = sums[c] + pulled
                for r in range(0, GROUP, 8):
                    columns[c] = columns[c] + pulled[r : r + 8]
            for c in range(3):
                row_acc[target, c, rows] = sums[c]
        sums = jnp.concatenate(
            [jnp.sum(columns[c], axis=0, keepdims=True) for c in range(3)], axis=0
        )
        grad_ref[owner * blocks + source, 0:3] += sums

    def two_pairs(nodes):
        def body(step, carry):
            for slot in range(2):
                multiply(2 * step + slot + 1, 1 - slot)
                one_pair(2 * step + slot, slot, nodes)
            return carry

        return body

    multiply(0, 0)
    lax.fori_loop(0, info_ref[1], two_pairs(3), 0)
    lax.fori_loop(info_ref[1], info_ref[2], two_pairs(2), 0)
    lax.fori_loop(info_ref[2], info_ref[3], two_pairs(1), 0)
    for b in range(blocks):
        total = jnp.concatenate(
            [jnp.sum(row_acc[b, c], axis=1, keepdims=True) for c in range(3)]
            + [jnp.zeros((width, 5), jnp.float32)],
            axis=1,
        )
        grad_ref[me * blocks + b] -= total.T

    high = blocks * width // LANES
    keys = 4 * high
    shift = (blocks * width).bit_length() + 1
    pack = 16
    key_ids = lax.broadcasted_iota(jnp.int32, (keys, width), 0).astype(jnp.bfloat16)
    lane_ids = lax.broadcasted_iota(jnp.int32, (LANES, width), 0).astype(jnp.bfloat16)
    zero = jnp.zeros((keys, width), jnp.bfloat16)
    low_one = jnp.ones((pack, width), jnp.bfloat16)
    low_zero = jnp.zeros((pack, width), jnp.bfloat16)

    def rows_of(row, count):
        return jnp.broadcast_to(row, (count, width)).astype(jnp.bfloat16)

    def scatter(tile, carry):
        parts = []
        hots = []
        for b in range(blocks):
            grad = grad_ref[tile * blocks + b]
            upper = grad.astype(jnp.bfloat16).astype(jnp.float32)
            lower = grad - upper
            spread = [
                rows_of(part[c : c + 1], keys) for c in range(3) for part in (upper, lower)
            ]
            for half in (at_point, at_extent):
                code = got_ref[tile, b, 3:4, half : half + width].astype(jnp.int32)
                for place in (code >> shift, code & ((1 << shift) - 1)):
                    key = rows_of((place >> 7).astype(jnp.float32), keys)
                    low = rows_of((place & (LANES - 1)).astype(jnp.float32), pack)
                    mask = key_ids == key
                    parts.append(
                        jnp.concatenate([jnp.where(mask, s, zero) for s in spread], axis=0)
                    )
                    hots.append(
                        jnp.concatenate(
                            [
                                jnp.where(lane_ids[g : g + pack] == low, low_one, low_zero)
                                for g in range(0, LANES, pack)
                            ],
                            axis=0,
                        )
                    )
        result = lax.dot_general(
            jnp.concatenate(parts, axis=1),
            jnp.concatenate(hots, axis=1),
            (((1,), (1,)), ((), ())),
            preferred_element_type=jnp.float32,
        )
        for c in range(3):
            joined_ref[tile, c] = (
                result[2 * c * keys : (2 * c + 1) * keys]
                + result[(2 * c + 1) * keys : (2 * c + 2) * keys]
            )
        return carry

    def collect(dest, carry):
        for c in range(3):
            total = jnp.zeros((high, LANES), jnp.float32)
            for slot, by in enumerate((0, tiles - 1, 1, tiles - tiles // 2)):
                tile = lax.rem(dest + by, tiles)
                total = total + joined_ref[tile, c, slot * high : (slot + 1) * high]
            for f in range(out_ref.shape[1]):
                out_ref[dest, f, :, c * LANES : (c + 1) * LANES] = total
        return carry

    lax.fori_loop(0, tiles, scatter, 0, unroll=min(tiles, 8))
    lax.fori_loop(0, tiles, collect, 0, unroll=min(tiles, 8))


def sum_kernel(got_ref, out_ref):
    _, high, _ = got_ref.shape
    total = jnp.sum(got_ref[...], axis=0)
    for c in range(3):
        for h in range(high):
            out_ref[c : c + 1, h * LANES : (h + 1) * LANES] = total[
                h : h + 1, c * LANES : (c + 1) * LANES
            ]


def per_device(
    panel_geometry,
    adjoint,
    strengths,
    pair_target,
    pair_owner,
    pair_source,
    pair_order,
    pair_count,
    corner_vertex,
):
    tiles = lax.axis_size("tiles")
    far = lax.axis_size("far")
    blocks, _, width = panel_geometry.shape
    high = blocks * width // LANES
    me = lax.axis_index("tiles").astype(jnp.int32).reshape(1)
    smem = pl.BlockSpec(memory_space=SMEM)
    vmem = pl.BlockSpec(memory_space=VMEM)
    params = pltpu.CompilerParams(vmem_limit_bytes=LIMIT)
    geometry = panel_geometry.transpose(1, 0, 2)
    packed = pl.pallas_call(
        pack_kernel,
        out_shape=jax.ShapeDtypeStruct((tiles, blocks, 4, 3 * width), jnp.float32),
        in_specs=[smem] + [vmem] * 3,
        out_specs=vmem,
    )(me, geometry, strengths, corner_vertex)
    got = lax.all_to_all(packed, "tiles", split_axis=0, concat_axis=0, tiled=True)
    pairs = pair_target.shape[0]
    info, centre, left = pl.pallas_call(
        prep_kernel,
        out_shape=(
            jax.ShapeDtypeStruct((HEAD + pairs + SPARE,), jnp.int32),
            jax.ShapeDtypeStruct((blocks, 3, width, width), jnp.float32),
            jax.ShapeDtypeStruct((blocks, width, 56), jnp.bfloat16),
        ),
        in_specs=[smem] * 6 + [vmem] * 2,
        out_specs=(smem, vmem, vmem),
        compiler_params=params,
        cost_estimate=pl.CostEstimate(flops=4000000, bytes_accessed=900000, transcendentals=0),
    )(
        me,
        pair_target,
        pair_owner[:, 0],
        pair_source,
        pair_order,
        pair_count,
        geometry,
        adjoint,
    )
    partial = pl.pallas_call(
        pair_kernel,
        out_shape=jax.ShapeDtypeStruct((tiles, far, high, 3 * LANES), jnp.float32),
        in_specs=[smem] + [vmem] * 3,
        out_specs=vmem,
        scratch_shapes=[
            VMEM((2, width, 4 * width), jnp.float32),
            VMEM((blocks, 3, width, width), jnp.float32),
            VMEM((tiles * blocks, 8, width), jnp.float32),
            VMEM((tiles, 3, 4 * high, LANES), jnp.float32),
        ],
        compiler_params=params,
    )(info, centre, left, got)
    partial = partial.reshape(tiles * far, high, 3 * LANES)
    shares = lax.all_to_all(partial, ("tiles", "far"), split_axis=0, concat_axis=0, tiled=True)
    return pl.pallas_call(
        sum_kernel,
        out_shape=jax.ShapeDtypeStruct((3, blocks * width), jnp.float32),
        compiler_params=params,
    )(shares)


def solution(mesh):
    placed = (
        P("tiles", None, None),
        P("tiles", "far", None),
        P("tiles", "far", None),
        P("tiles"),
        P("tiles", None),
        P("tiles"),
        P("tiles"),
        P("tiles"),
        P("tiles", None, None),
    )
    return jax.shard_map(
        per_device, mesh=mesh, in_specs=placed, out_specs=P(None, "tiles"), check_vma=False
    )
```

```python
import jax
import jax.numpy as jnp
from jax import lax
from jax.experimental import pallas as pl
from jax.experimental.pallas import tpu as pltpu
from jax.sharding import PartitionSpec as P

SMEM = pltpu.SMEM
VMEM = pltpu.VMEM
LANES = 128
HEAD = 4
SPARE = 2
GROUP = 32
LIMIT = 48 * 1024 * 1024


def pack_kernel(me_ref, geom_ref, strength_ref, corner_ref, out_ref):
    tiles, blocks, _, _ = out_ref.shape
    width = strength_ref.shape[2]
    shift = (blocks * width).bit_length() - 1
    me = me_ref[0]
    for b in range(blocks):
        vertex = corner_ref[b]
        offset = (vertex >> shift) - me
        offset = jnp.where(offset < 0, offset + tiles, offset)
        slot = jnp.where(
            offset == 0,
            0,
            jnp.where(offset == 1, 1, jnp.where(offset == tiles - 1, 2, 3)),
        )
        place = ((slot << shift) + (vertex & ((1 << shift) - 1))).astype(jnp.float32)
        span = float(4 << shift)
        first = place[0:1] * span + place[1:2]
        second = place[2:3] * span + place[3:4]
        block = jnp.concatenate(
            [
                strength_ref[b].astype(jnp.float32),
                jnp.concatenate([geom_ref[c, b : b + 1] for c in range(3)] + [first], axis=0),
                jnp.concatenate([geom_ref[3 + c, b : b + 1] for c in range(3)] + [second], axis=0),
            ],
            axis=1,
        )
        for t in range(tiles):
            out_ref[t, b] = block


def split3(value):
    first = value.astype(jnp.bfloat16).astype(jnp.float32)
    rest = value - first
    second = rest.astype(jnp.bfloat16).astype(jnp.float32)
    return first, second, rest - second


def prep_kernel(
    me_ref,
    target_ref,
    owner_ref,
    source_ref,
    order_ref,
    count_ref,
    geom_ref,
    adjoint_ref,
    info_ref,
    centre_ref,
    left_ref,
):
    blocks, _, width = adjoint_ref.shape
    live = count_ref[0]
    total = target_ref.shape[0]
    for k in range(HEAD + total, HEAD + total + SPARE):
        info_ref[k] = 0

    def note(order, first):
        def one(k, at):
            mine = order_ref[k] == order
            word = (owner_ref[k] << 18) | (order << 16) | (source_ref[k] << 8) | target_ref[k]
            info_ref[at] = word
            return at + jnp.where(mine, 1, 0)

        return lax.fori_loop(0, live, one, first)

    third = note(3, HEAD)
    second = note(2, third)
    first = note(1, second)
    for k in range(SPARE):
        info_ref[first + k] = 0
    info_ref[0] = me_ref[0]
    info_ref[1] = (third - HEAD + 1) // 2
    info_ref[2] = (second - HEAD + 1) // 2
    info_ref[3] = (live + 1) // 2
    for b in range(blocks):
        point = jnp.concatenate([geom_ref[c, b : b + 1] for c in range(3)], axis=0)
        rows = [point, jnp.ones((1, width), jnp.float32)]
        rows += [jnp.sum(point * point, axis=0, keepdims=True)]
        rows += [jnp.zeros((3, width), jnp.float32)]
        x1, x2, x3 = split3(jnp.concatenate(rows, axis=0))
        values = [adjoint_ref[b].astype(jnp.float32), jnp.zeros((4, width), jnp.float32)]
        rows = [x1, x1, x1, x2, x2, x3] + values
        left_ref[b] = jnp.concatenate(rows, axis=0).T.astype(jnp.bfloat16)
        for c in range(3):
            centre_ref[b, c] = jnp.broadcast_to(point[c : c + 1], (width, width)).T


def pair_kernel(
    info_ref,
    centre_ref,
    left_ref,
    got_ref,
    out_ref,
    product_ref,
    row_acc,
    grad_ref,
    joined_ref,
):
    tiles, blocks, _, _ = got_ref.shape
    width = centre_ref.shape[3]
    at_point, at_extent = width, 2 * width
    me = info_ref[0]
    grad_ref[...] = jnp.zeros(grad_ref.shape, jnp.float32)
    row_acc[...] = jnp.zeros(row_acc.shape, jnp.float32)
    blank = jnp.zeros((4, width), jnp.float32)
    row_ids = lax.broadcasted_iota(jnp.int32, (8, width), 0)

    def reach_of(order):
        return 0.25 * jnp.where(
            order == 3, 0.7745966692414834, jnp.where(order == 2, 0.5773502691896258, 0.0)
        )

    def read(k):
        word = info_ref[HEAD + k]
        return word & 255, word >> 18, (word >> 8) & 255, (word >> 16) & 3

    def multiply(k, slot):
        target, owner, source, order = read(k)
        third = order == 3
        alive = jnp.where(order > 0, 1.0, 0.0).astype(jnp.float32)
        reach = reach_of(order)
        scale_mid = jnp.where(third, (4.0 / 9.0 / 512.0) ** (-2.0 / 3.0), 0.0)
        scale_side = jnp.where(
            third, (5.0 / 18.0 / 512.0) ** (-2.0 / 3.0), (0.5 / 512.0) ** (-2.0 / 3.0)
        )
        floor_mid = jnp.where(third, 0.0625 * (4.0 / 9.0 / 512.0) ** (-2.0 / 3.0), 3.0e38)
        floor_side = 0.0625 * scale_side
        point = got_ref[owner, source, :, at_point : at_point + width]
        extent = got_ref[owner, source, :, at_extent : at_extent + width] * reach
        inside = row_ids < 3
        point = jnp.where(inside, jnp.concatenate([point, blank], axis=0), 0.0)
        extent = jnp.where(inside, jnp.concatenate([extent, blank], axis=0), 0.0)
        values = jnp.concatenate([got_ref[owner, source, :, 0:width] * alive, blank], axis=0)
        empty = jnp.zeros((8, width), jnp.float32)
        nodes = (
            (point, scale_mid, floor_mid),
            (point + extent, scale_side, floor_side),
            (point - extent, scale_side, floor_side),
        )
        columns = []
        for node, scale, floor in nodes:
            norm = jnp.sum(node * node, axis=0, keepdims=True) * scale + floor
            rows = jnp.where(
                row_ids == 3,
                norm,
                jnp.where(row_ids == 4, scale, node * (-2.0 * scale)),
            )
            p1, p2, p3 = split3(rows)
            columns.append(jnp.concatenate([p1, p2, p3, p1, p2, p1, empty], axis=0))
        columns.append(jnp.concatenate([empty] * 6 + [values], axis=0))
        product_ref[slot] = jnp.dot(
            left_ref[target],
            jnp.concatenate(columns, axis=1).astype(jnp.bfloat16),
            preferred_element_type=jnp.float32,
        )

    def one_pair(k, slot, nodes):
        target, owner, source, order = read(k)
        reach = reach_of(order)
        point = [got_ref[owner, source, c : c + 1, at_point : at_point + width] for c in range(3)]
        extent = [
            got_ref[owner, source, c : c + 1, at_extent : at_extent + width] * reach
            for c in range(3)
        ]
        columns = [jnp.zeros((8, width), jnp.float32) for _ in range(3)]
        for start in range(0, width, GROUP):
            rows = slice(start, start + GROUP)
            sums = [row_acc[target, c, rows] for c in range(3)]

            def cubed(node):
                i = lax.rsqrt(product_ref[slot, rows, node * width : (node + 1) * width])
                return i * i * i

            coupling = product_ref[slot, rows, 3 * width : 4 * width]
            f_plus = cubed(1)
            if nodes == 1:
                even = (coupling + coupling) * f_plus
            else:
                f_minus = cubed(2)
                both = f_plus + f_minus
                even = coupling * (both + cubed(0) if nodes == 3 else both)
                odd = coupling * (f_plus - f_minus)
            for c in range(3):
                pulled = even * (centre_ref[target, c, rows] - point[c])
                if nodes > 1:
                    pulled = pulled - odd * extent[c]
                sums[c] = sums[c] + pulled
                for r in range(0, GROUP, 8):
                    columns[c] = columns[c] + pulled[r : r + 8]
            for c in range(3):
                row_acc[target, c, rows] = sums[c]
        sums = jnp.concatenate(
            [jnp.sum(columns[c], axis=0, keepdims=True) for c in range(3)], axis=0
        )
        grad_ref[owner * blocks + source, 0:3] += sums

    def two_pairs(nodes):
        def body(step, carry):
            for slot in range(2):
                multiply(2 * step + slot + 1, 1 - slot)
                one_pair(2 * step + slot, slot, nodes)
            return carry

        return body

    multiply(0, 0)
    lax.fori_loop(0, info_ref[1], two_pairs(3), 0)
    lax.fori_loop(info_ref[1], info_ref[2], two_pairs(2), 0)
    lax.fori_loop(info_ref[2], info_ref[3], two_pairs(1), 0)
    for b in range(blocks):
        total = jnp.concatenate(
            [jnp.sum(row_acc[b, c], axis=1, keepdims=True) for c in range(3)]
            + [jnp.zeros((width, 5), jnp.float32)],
            axis=1,
        )
        grad_ref[me * blocks + b] -= total.T

    high = blocks * width // LANES
    keys = 4 * high
    shift = (blocks * width).bit_length() + 1
    pack = 16
    key_ids = lax.broadcasted_iota(jnp.int32, (keys, width), 0).astype(jnp.bfloat16)
    lane_ids = lax.broadcasted_iota(jnp.int32, (LANES, width), 0).astype(jnp.bfloat16)
    zero = jnp.zeros((keys, width), jnp.bfloat16)
    low_one = jnp.ones((pack, width), jnp.bfloat16)
    low_zero = jnp.zeros((pack, width), jnp.bfloat16)

    def rows_of(row, count):
        return jnp.broadcast_to(row, (count, width)).astype(jnp.bfloat16)

    def scatter(tile, carry):
        parts = []
        hots = []
        for b in range(blocks):
            grad = grad_ref[tile * blocks + b]
            upper = grad.astype(jnp.bfloat16).astype(jnp.float32)
            lower = grad - upper
            spread = [
                rows_of(part[c : c + 1], keys) for c in range(3) for part in (upper, lower)
            ]
            for half in (at_point, at_extent):
                code = got_ref[tile, b, 3:4, half : half + width].astype(jnp.int32)
                for place in (code >> shift, code & ((1 << shift) - 1)):
                    key = rows_of((place >> 7).astype(jnp.float32), keys)
                    low = rows_of((place & (LANES - 1)).astype(jnp.float32), pack)
                    mask = key_ids == key
                    parts.append(
                        jnp.concatenate([jnp.where(mask, s, zero) for s in spread], axis=0)
                    )
                    hots.append(
                        jnp.concatenate(
                            [
                                jnp.where(lane_ids[g : g + pack] == low, low_one, low_zero)
                                for g in range(0, LANES, pack)
                            ],
                            axis=0,
                        )
                    )
        result = lax.dot_general(
            jnp.concatenate(parts, axis=1),
            jnp.concatenate(hots, axis=1),
            (((1,), (1,)), ((), ())),
            preferred_element_type=jnp.float32,
        )
        for c in range(3):
            joined_ref[tile, c] = (
                result[2 * c * keys : (2 * c + 1) * keys]
                + result[(2 * c + 1) * keys : (2 * c + 2) * keys]
            )
        return carry

    def collect(dest, carry):
        for c in range(3):
            total = jnp.zeros((high, LANES), jnp.float32)
            for slot, by in enumerate((0, tiles - 1, 1, tiles - tiles // 2)):
                tile = lax.rem(dest + by, tiles)
                total = total + joined_ref[tile, c, slot * high : (slot + 1) * high]
            out_ref[dest, :, c * LANES : (c + 1) * LANES] = total
        return carry

    lax.fori_loop(0, tiles, scatter, 0, unroll=min(tiles, 8))
    lax.fori_loop(0, tiles, collect, 0, unroll=min(tiles, 8))


def sum_kernel(got_ref, out_ref):
    out_ref[...] = jnp.sum(got_ref[...], axis=0)


def last_kernel(*refs):
    *got_refs, out_ref = refs
    total = got_refs[0][...]
    for ref in got_refs[1:]:
        total = total + ref[...]
    high = total.shape[0]
    for c in range(3):
        for h in range(high):
            out_ref[c : c + 1, h * LANES : (h + 1) * LANES] = total[
                h : h + 1, c * LANES : (c + 1) * LANES
            ]


def per_device(
    panel_geometry,
    adjoint,
    strengths,
    pair_target,
    pair_owner,
    pair_source,
    pair_order,
    pair_count,
    corner_vertex,
):
    tiles = lax.axis_size("tiles")
    far = lax.axis_size("far")
    blocks, _, width = panel_geometry.shape
    high = blocks * width // LANES
    me = lax.axis_index("tiles").astype(jnp.int32).reshape(1)
    smem = pl.BlockSpec(memory_space=SMEM)
    vmem = pl.BlockSpec(memory_space=VMEM)
    params = pltpu.CompilerParams(vmem_limit_bytes=LIMIT)
    geometry = panel_geometry.transpose(1, 0, 2)
    packed = pl.pallas_call(
        pack_kernel,
        out_shape=jax.ShapeDtypeStruct((tiles, blocks, 4, 3 * width), jnp.float32),
        in_specs=[smem] + [vmem] * 3,
        out_specs=vmem,
    )(me, geometry, strengths, corner_vertex)
    got = lax.all_to_all(packed, "tiles", split_axis=0, concat_axis=0, tiled=True)
    pairs = pair_target.shape[0]
    info, centre, left = pl.pallas_call(
        prep_kernel,
        out_shape=(
            jax.ShapeDtypeStruct((HEAD + pairs + SPARE,), jnp.int32),
            jax.ShapeDtypeStruct((blocks, 3, width, width), jnp.float32),
            jax.ShapeDtypeStruct((blocks, width, 56), jnp.bfloat16),
        ),
        in_specs=[smem] * 6 + [vmem] * 2,
        out_specs=(smem, vmem, vmem),
        compiler_params=params,
        cost_estimate=pl.CostEstimate(flops=4000000, bytes_accessed=900000, transcendentals=0),
    )(
        me,
        pair_target,
        pair_owner[:, 0],
        pair_source,
        pair_order,
        pair_count,
        geometry,
        adjoint,
    )
    partial = pl.pallas_call(
        pair_kernel,
        out_shape=jax.ShapeDtypeStruct((tiles, high, 3 * LANES), jnp.float32),
        in_specs=[smem] + [vmem] * 3,
        out_specs=vmem,
        scratch_shapes=[
            VMEM((2, width, 4 * width), jnp.float32),
            VMEM((blocks, 3, width, width), jnp.float32),
            VMEM((tiles * blocks, 8, width), jnp.float32),
            VMEM((tiles, 3, 4 * high, LANES), jnp.float32),
        ],
        compiler_params=params,
    )(info, centre, left, got)
    shares = lax.all_to_all(partial, "tiles", split_axis=0, concat_axis=0, tiled=True)
    mine = pl.pallas_call(
        sum_kernel,
        out_shape=jax.ShapeDtypeStruct((high, 3 * LANES), jnp.float32),
        compiler_params=params,
    )(shares)
    others = [
        lax.ppermute(mine, "far", [((f + d) % far, f) for f in range(far)]) for d in range(1, far)
    ]
    return pl.pallas_call(
        last_kernel,
        out_shape=jax.ShapeDtypeStruct((3, blocks * width), jnp.float32),
        compiler_params=params,
    )(mine, *others)


def solution(mesh):
    placed = (
        P("tiles", None, None),
        P("tiles", "far", None),
        P("tiles", "far", None),
        P("tiles"),
        P("tiles", None),
        P("tiles"),
        P("tiles"),
        P("tiles"),
        P("tiles", None, None),
    )
    return jax.shard_map(
        per_device, mesh=mesh, in_specs=placed, out_specs=P(None, "tiles"), check_vma=False
    )
```

```python
import jax
import jax.numpy as jnp
from jax import lax
from jax.experimental import pallas as pl
from jax.experimental.pallas import tpu as pltpu
from jax.sharding import PartitionSpec as P

SMEM = pltpu.SMEM
VMEM = pltpu.VMEM
LANES = 128
HEAD = 4
SPARE = 2
GROUP = 32
LIMIT = 48 * 1024 * 1024


def pack_kernel(me_ref, geom_ref, strength_ref, corner_ref, out_ref):
    tiles, blocks, _, _ = out_ref.shape
    width = strength_ref.shape[2]
    shift = (blocks * width).bit_length() - 1
    me = me_ref[0]
    for b in range(blocks):
        vertex = corner_ref[b]
        offset = (vertex >> shift) - me
        offset = jnp.where(offset < 0, offset + tiles, offset)
        slot = jnp.where(
            offset == 0,
            0,
            jnp.where(offset == 1, 1, jnp.where(offset == tiles - 1, 2, 3)),
        )
        place = ((slot << shift) + (vertex & ((1 << shift) - 1))).astype(jnp.float32)
        span = float(4 << shift)
        first = place[0:1] * span + place[1:2]
        second = place[2:3] * span + place[3:4]
        block = jnp.concatenate(
            [
                strength_ref[b].astype(jnp.float32),
                jnp.concatenate([geom_ref[c, b : b + 1] for c in range(3)] + [first], axis=0),
                jnp.concatenate([geom_ref[3 + c, b : b + 1] for c in range(3)] + [second], axis=0),
            ],
            axis=1,
        )
        for t in range(tiles):
            out_ref[t, b] = block


def split3(value):
    first = value.astype(jnp.bfloat16).astype(jnp.float32)
    rest = value - first
    second = rest.astype(jnp.bfloat16).astype(jnp.float32)
    return first, second, rest - second


def prep_kernel(
    me_ref,
    target_ref,
    owner_ref,
    source_ref,
    order_ref,
    count_ref,
    geom_ref,
    adjoint_ref,
    info_ref,
    centre_ref,
    left_ref,
):
    blocks, _, width = adjoint_ref.shape
    live = count_ref[0]
    total = target_ref.shape[0]
    for k in range(HEAD + total, HEAD + total + SPARE):
        info_ref[k] = 0

    def note(order, first):
        def one(k, at):
            mine = order_ref[k] == order
            word = (owner_ref[k] << 18) | (order << 16) | (source_ref[k] << 8) | target_ref[k]
            info_ref[at] = word
            return at + jnp.where(mine, 1, 0)

        return lax.fori_loop(0, live, one, first)

    third = note(3, HEAD)
    second = note(2, third)
    first = note(1, second)
    for k in range(SPARE):
        info_ref[first + k] = 0
    info_ref[0] = me_ref[0]
    info_ref[1] = (third - HEAD + 1) // 2
    info_ref[2] = (second - HEAD + 1) // 2
    info_ref[3] = (live + 1) // 2
    for b in range(blocks):
        point = jnp.concatenate([geom_ref[c, b : b + 1] for c in range(3)], axis=0)
        rows = [point, jnp.ones((1, width), jnp.float32)]
        rows += [jnp.sum(point * point, axis=0, keepdims=True)]
        rows += [jnp.zeros((3, width), jnp.float32)]
        x1, x2, x3 = split3(jnp.concatenate(rows, axis=0))
        values = [adjoint_ref[b].astype(jnp.float32), jnp.zeros((4, width), jnp.float32)]
        rows = [x1, x1, x1, x2, x2, x3] + values
        left_ref[b] = jnp.concatenate(rows, axis=0).T.astype(jnp.bfloat16)
        for c in range(3):
            centre_ref[b, c] = jnp.broadcast_to(point[c : c + 1], (width, width)).T


def pair_kernel(
    info_ref,
    centre_ref,
    left_ref,
    got_ref,
    out_ref,
    product_ref,
    row_acc,
    grad_ref,
    joined_ref,
):
    tiles, blocks, _, _ = got_ref.shape
    width = centre_ref.shape[3]
    at_point, at_extent = width, 2 * width
    me = info_ref[0]
    grad_ref[...] = jnp.zeros(grad_ref.shape, jnp.float32)
    row_acc[...] = jnp.zeros(row_acc.shape, jnp.float32)
    blank = jnp.zeros((4, width), jnp.float32)
    row_ids = lax.broadcasted_iota(jnp.int32, (8, width), 0)

    def reach_of(order):
        return 0.25 * jnp.where(
            order == 3, 0.7745966692414834, jnp.where(order == 2, 0.5773502691896258, 0.0)
        )

    def read(k):
        word = info_ref[HEAD + k]
        return word & 255, word >> 18, (word >> 8) & 255, (word >> 16) & 3

    def multiply(k, slot):
        target, owner, source, order = read(k)
        third = order == 3
        alive = jnp.where(order > 0, 1.0, 0.0).astype(jnp.float32)
        reach = reach_of(order)
        scale_mid = jnp.where(third, (4.0 / 9.0 / 512.0) ** (-2.0 / 3.0), 0.0)
        scale_side = jnp.where(
            third, (5.0 / 18.0 / 512.0) ** (-2.0 / 3.0), (0.5 / 512.0) ** (-2.0 / 3.0)
        )
        floor_mid = jnp.where(third, 0.0625 * (4.0 / 9.0 / 512.0) ** (-2.0 / 3.0), 3.0e38)
        floor_side = 0.0625 * scale_side
        point = got_ref[owner, source, :, at_point : at_point + width]
        extent = got_ref[owner, source, :, at_extent : at_extent + width] * reach
        inside = row_ids < 3
        point = jnp.where(inside, jnp.concatenate([point, blank], axis=0), 0.0)
        extent = jnp.where(inside, jnp.concatenate([extent, blank], axis=0), 0.0)
        values = jnp.concatenate([got_ref[owner, source, :, 0:width] * alive, blank], axis=0)
        empty = jnp.zeros((8, width), jnp.float32)
        nodes = (
            (point, scale_mid, floor_mid),
            (point + extent, scale_side, floor_side),
            (point - extent, scale_side, floor_side),
        )
        columns = []
        for node, scale, floor in nodes:
            norm = jnp.sum(node * node, axis=0, keepdims=True) * scale + floor
            rows = jnp.where(
                row_ids == 3,
                norm,
                jnp.where(row_ids == 4, scale, node * (-2.0 * scale)),
            )
            p1, p2, p3 = split3(rows)
            columns.append(jnp.concatenate([p1, p2, p3, p1, p2, p1, empty], axis=0))
        columns.append(jnp.concatenate([empty] * 6 + [values], axis=0))
        product_ref[slot] = jnp.dot(
            left_ref[target],
            jnp.concatenate(columns, axis=1).astype(jnp.bfloat16),
            preferred_element_type=jnp.float32,
        )

    def one_pair(k, slot, nodes):
        target, owner, source, order = read(k)
        reach = reach_of(order)
        point = [got_ref[owner, source, c : c + 1, at_point : at_point + width] for c in range(3)]
        extent = [
            got_ref[owner, source, c : c + 1, at_extent : at_extent + width] * reach
            for c in range(3)
        ]
        columns = [jnp.zeros((8, width), jnp.float32) for _ in range(3)]
        for start in range(0, width, GROUP):
            rows = slice(start, start + GROUP)
            sums = [row_acc[target, c, rows] for c in range(3)]

            def cubed(node):
                squared = product_ref[slot, rows, node * width : (node + 1) * width]
                return jnp.exp2(jnp.log(squared) * (-1.5 * 1.4426950408889634))

            coupling = product_ref[slot, rows, 3 * width : 4 * width]
            f_plus = cubed(1)
            if nodes == 1:
                even = (coupling + coupling) * f_plus
            else:
                f_minus = cubed(2)
                both = f_plus + f_minus
                even = coupling * (both + cubed(0) if nodes == 3 else both)
                odd = coupling * (f_plus - f_minus)
            for c in range(3):
                pulled = even * (centre_ref[target, c, rows] - point[c])
                if nodes > 1:
                    pulled = pulled - odd * extent[c]
                sums[c] = sums[c] + pulled
                for r in range(0, GROUP, 8):
                    columns[c] = columns[c] + pulled[r : r + 8]
            for c in range(3):
                row_acc[target, c, rows] = sums[c]
        sums = jnp.concatenate(
            [jnp.sum(columns[c], axis=0, keepdims=True) for c in range(3)], axis=0
        )
        grad_ref[owner * blocks + source, 0:3] += sums

    def two_pairs(nodes):
        def body(step, carry):
            for slot in range(2):
                multiply(2 * step + slot + 1, 1 - slot)
                one_pair(2 * step + slot, slot, nodes)
            return carry

        return body

    multiply(0, 0)
    lax.fori_loop(0, info_ref[1], two_pairs(3), 0)
    lax.fori_loop(info_ref[1], info_ref[2], two_pairs(2), 0)
    lax.fori_loop(info_ref[2], info_ref[3], two_pairs(1), 0)
    for b in range(blocks):
        total = jnp.concatenate(
            [jnp.sum(row_acc[b, c], axis=1, keepdims=True) for c in range(3)]
            + [jnp.zeros((width, 5), jnp.float32)],
            axis=1,
        )
        grad_ref[me * blocks + b] -= total.T

    high = blocks * width // LANES
    keys = 4 * high
    shift = (blocks * width).bit_length() + 1
    pack = 16
    key_ids = lax.broadcasted_iota(jnp.int32, (keys, width), 0).astype(jnp.bfloat16)
    lane_ids = lax.broadcasted_iota(jnp.int32, (LANES, width), 0).astype(jnp.bfloat16)
    zero = jnp.zeros((keys, width), jnp.bfloat16)
    low_one = jnp.ones((pack, width), jnp.bfloat16)
    low_zero = jnp.zeros((pack, width), jnp.bfloat16)

    def rows_of(row, count):
        return jnp.broadcast_to(row, (count, width)).astype(jnp.bfloat16)

    def scatter(tile, carry):
        parts = []
        hots = []
        for b in range(blocks):
            grad = grad_ref[tile * blocks + b]
            upper = grad.astype(jnp.bfloat16).astype(jnp.float32)
            lower = grad - upper
            spread = [
                rows_of(part[c : c + 1], keys) for c in range(3) for part in (upper, lower)
            ]
            for half in (at_point, at_extent):
                code = got_ref[tile, b, 3:4, half : half + width].astype(jnp.int32)
                for place in (code >> shift, code & ((1 << shift) - 1)):
                    key = rows_of((place >> 7).astype(jnp.float32), keys)
                    low = rows_of((place & (LANES - 1)).astype(jnp.float32), pack)
                    mask = key_ids == key
                    parts.append(
                        jnp.concatenate([jnp.where(mask, s, zero) for s in spread], axis=0)
                    )
                    hots.append(
                        jnp.concatenate(
                            [
                                jnp.where(lane_ids[g : g + pack] == low, low_one, low_zero)
                                for g in range(0, LANES, pack)
                            ],
                            axis=0,
                        )
                    )
        result = lax.dot_general(
            jnp.concatenate(parts, axis=1),
            jnp.concatenate(hots, axis=1),
            (((1,), (1,)), ((), ())),
            preferred_element_type=jnp.float32,
        )
        for c in range(3):
            joined_ref[tile, c] = (
                result[2 * c * keys : (2 * c + 1) * keys]
                + result[(2 * c + 1) * keys : (2 * c + 2) * keys]
            )
        return carry

    def collect(dest, carry):
        for c in range(3):
            total = jnp.zeros((high, LANES), jnp.float32)
            for slot, by in enumerate((0, tiles - 1, 1, tiles - tiles // 2)):
                tile = lax.rem(dest + by, tiles)
                total = total + joined_ref[tile, c, slot * high : (slot + 1) * high]
            for f in range(out_ref.shape[1]):
                out_ref[dest, f, :, c * LANES : (c + 1) * LANES] = total
        return carry

    lax.fori_loop(0, tiles, scatter, 0, unroll=min(tiles, 8))
    lax.fori_loop(0, tiles, collect, 0, unroll=min(tiles, 8))


def sum_kernel(got_ref, out_ref):
    _, high, _ = got_ref.shape
    total = jnp.sum(got_ref[...], axis=0)
    for c in range(3):
        for h in range(high):
            out_ref[c : c + 1, h * LANES : (h + 1) * LANES] = total[
                h : h + 1, c * LANES : (c + 1) * LANES
            ]


def per_device(
    panel_geometry,
    adjoint,
    strengths,
    pair_target,
    pair_owner,
    pair_source,
    pair_order,
    pair_count,
    corner_vertex,
):
    tiles = lax.axis_size("tiles")
    far = lax.axis_size("far")
    blocks, _, width = panel_geometry.shape
    high = blocks * width // LANES
    me = lax.axis_index("tiles").astype(jnp.int32).reshape(1)
    smem = pl.BlockSpec(memory_space=SMEM)
    vmem = pl.BlockSpec(memory_space=VMEM)
    params = pltpu.CompilerParams(vmem_limit_bytes=LIMIT)
    geometry = panel_geometry.transpose(1, 0, 2)
    packed = pl.pallas_call(
        pack_kernel,
        out_shape=jax.ShapeDtypeStruct((tiles, blocks, 4, 3 * width), jnp.float32),
        in_specs=[smem] + [vmem] * 3,
        out_specs=vmem,
    )(me, geometry, strengths, corner_vertex)
    got = lax.all_to_all(packed, "tiles", split_axis=0, concat_axis=0, tiled=True)
    pairs = pair_target.shape[0]
    info, centre, left = pl.pallas_call(
        prep_kernel,
        out_shape=(
            jax.ShapeDtypeStruct((HEAD + pairs + SPARE,), jnp.int32),
            jax.ShapeDtypeStruct((blocks, 3, width, width), jnp.float32),
            jax.ShapeDtypeStruct((blocks, width, 56), jnp.bfloat16),
        ),
        in_specs=[smem] * 6 + [vmem] * 2,
        out_specs=(smem, vmem, vmem),
        compiler_params=params,
        cost_estimate=pl.CostEstimate(flops=4000000, bytes_accessed=900000, transcendentals=0),
    )(
        me,
        pair_target,
        pair_owner[:, 0],
        pair_source,
        pair_order,
        pair_count,
        geometry,
        adjoint,
    )
    partial = pl.pallas_call(
        pair_kernel,
        out_shape=jax.ShapeDtypeStruct((tiles, far, high, 3 * LANES), jnp.float32),
        in_specs=[smem] + [vmem] * 3,
        out_specs=vmem,
        scratch_shapes=[
            VMEM((2, width, 4 * width), jnp.float32),
            VMEM((blocks, 3, width, width), jnp.float32),
            VMEM((tiles * blocks, 8, width), jnp.float32),
            VMEM((tiles, 3, 4 * high, LANES), jnp.float32),
        ],
        compiler_params=params,
    )(info, centre, left, got)
    partial = partial.reshape(tiles * far, high, 3 * LANES)
    shares = lax.all_to_all(partial, ("tiles", "far"), split_axis=0, concat_axis=0, tiled=True)
    return pl.pallas_call(
        sum_kernel,
        out_shape=jax.ShapeDtypeStruct((3, blocks * width), jnp.float32),
        compiler_params=params,
    )(shares)


def solution(mesh):
    placed = (
        P("tiles", None, None),
        P("tiles", "far", None),
        P("tiles", "far", None),
        P("tiles"),
        P("tiles", None),
        P("tiles"),
        P("tiles"),
        P("tiles"),
        P("tiles", None, None),
    )
    return jax.shard_map(
        per_device, mesh=mesh, in_specs=placed, out_specs=P(None, "tiles"), check_vma=False
    )
```

```python
import jax
import jax.numpy as jnp
from jax import lax
from jax.experimental import pallas as pl
from jax.experimental.pallas import tpu as pltpu
from jax.sharding import PartitionSpec as P

SMEM = pltpu.SMEM
VMEM = pltpu.VMEM
LANES = 128
HEAD = 4
SPARE = 2
GROUP = 32
LIMIT = 48 * 1024 * 1024


def pack_kernel(me_ref, geom_ref, strength_ref, corner_ref, out_ref):
    tiles, blocks, _, _ = out_ref.shape
    width = strength_ref.shape[2]
    shift = (blocks * width).bit_length() - 1
    me = me_ref[0]
    for b in range(blocks):
        vertex = corner_ref[b]
        offset = (vertex >> shift) - me
        offset = jnp.where(offset < 0, offset + tiles, offset)
        slot = jnp.where(
            offset == 0,
            0,
            jnp.where(offset == 1, 1, jnp.where(offset == tiles - 1, 2, 3)),
        )
        place = ((slot << shift) + (vertex & ((1 << shift) - 1))).astype(jnp.float32)
        span = float(4 << shift)
        first = place[0:1] * span + place[1:2]
        second = place[2:3] * span + place[3:4]
        block = jnp.concatenate(
            [
                strength_ref[b].astype(jnp.float32),
                jnp.concatenate([geom_ref[c, b : b + 1] for c in range(3)] + [first], axis=0),
                jnp.concatenate([geom_ref[3 + c, b : b + 1] for c in range(3)] + [second], axis=0),
            ],
            axis=1,
        )
        for t in range(tiles):
            out_ref[t, b] = block


def split3(value):
    first = value.astype(jnp.bfloat16).astype(jnp.float32)
    rest = value - first
    second = rest.astype(jnp.bfloat16).astype(jnp.float32)
    return first, second, rest - second


def prep_kernel(
    me_ref,
    target_ref,
    owner_ref,
    source_ref,
    order_ref,
    count_ref,
    geom_ref,
    adjoint_ref,
    info_ref,
    centre_ref,
    left_ref,
):
    blocks, _, width = adjoint_ref.shape
    live = count_ref[0]
    total = target_ref.shape[0]
    for k in range(HEAD + total, HEAD + total + SPARE):
        info_ref[k] = 0

    def note(order, first):
        def one(k, at):
            mine = order_ref[k] == order
            word = (owner_ref[k] << 18) | (order << 16) | (source_ref[k] << 8) | target_ref[k]
            info_ref[at] = word
            return at + jnp.where(mine, 1, 0)

        return lax.fori_loop(0, live, one, first)

    third = note(3, HEAD)
    second = note(2, third)
    first = note(1, second)
    for k in range(SPARE):
        info_ref[first + k] = 0
    info_ref[0] = me_ref[0]
    info_ref[1] = (third - HEAD + 1) // 2
    info_ref[2] = (second - HEAD + 1) // 2
    info_ref[3] = (live + 1) // 2
    for b in range(blocks):
        point = jnp.concatenate([geom_ref[c, b : b + 1] for c in range(3)], axis=0)
        rows = [point, jnp.ones((1, width), jnp.float32)]
        rows += [jnp.sum(point * point, axis=0, keepdims=True)]
        rows += [jnp.zeros((3, width), jnp.float32)]
        x1, x2, x3 = split3(jnp.concatenate(rows, axis=0))
        values = [adjoint_ref[b].astype(jnp.float32), jnp.zeros((4, width), jnp.float32)]
        rows = [x1, x1, x1, x2, x2, x3] + values
        left_ref[b] = jnp.concatenate(rows, axis=0).T.astype(jnp.bfloat16)
        for c in range(3):
            centre_ref[b, c] = jnp.broadcast_to(point[c : c + 1], (width, width)).T


def pair_kernel(
    info_ref,
    centre_ref,
    left_ref,
    got_ref,
    out_ref,
    product_ref,
    row_acc,
    grad_ref,
    joined_ref,
):
    tiles, blocks, _, _ = got_ref.shape
    width = centre_ref.shape[3]
    at_point, at_extent = width, 2 * width
    me = info_ref[0]
    grad_ref[...] = jnp.zeros(grad_ref.shape, jnp.float32)
    row_acc[...] = jnp.zeros(row_acc.shape, jnp.float32)
    blank = jnp.zeros((4, width), jnp.float32)
    row_ids = lax.broadcasted_iota(jnp.int32, (8, width), 0)

    def reach_of(order):
        return 0.25 * jnp.where(
            order == 3, 0.7745966692414834, jnp.where(order == 2, 0.5773502691896258, 0.0)
        )

    def read(k):
        word = info_ref[HEAD + k]
        return word & 255, word >> 18, (word >> 8) & 255, (word >> 16) & 3

    def multiply(k, slot):
        target, owner, source, order = read(k)
        third = order == 3
        alive = jnp.where(order > 0, 1.0, 0.0).astype(jnp.float32)
        reach = reach_of(order)
        scale_mid = jnp.where(third, (4.0 / 9.0 / 512.0) ** (-2.0 / 3.0), 0.0)
        scale_side = jnp.where(
            third, (5.0 / 18.0 / 512.0) ** (-2.0 / 3.0), (0.5 / 512.0) ** (-2.0 / 3.0)
        )
        floor_mid = jnp.where(third, 0.0625 * (4.0 / 9.0 / 512.0) ** (-2.0 / 3.0), 3.0e38)
        floor_side = 0.0625 * scale_side
        point = got_ref[owner, source, :, at_point : at_point + width]
        extent = got_ref[owner, source, :, at_extent : at_extent + width] * reach
        inside = row_ids < 3
        point = jnp.where(inside, jnp.concatenate([point, blank], axis=0), 0.0)
        extent = jnp.where(inside, jnp.concatenate([extent, blank], axis=0), 0.0)
        values = jnp.concatenate([got_ref[owner, source, :, 0:width] * alive, blank], axis=0)
        empty = jnp.zeros((8, width), jnp.float32)
        nodes = (
            (point, scale_mid, floor_mid),
            (point + extent, scale_side, floor_side),
            (point - extent, scale_side, floor_side),
        )
        columns = []
        for node, scale, floor in nodes:
            norm = jnp.sum(node * node, axis=0, keepdims=True) * scale + floor
            rows = jnp.where(
                row_ids == 3,
                norm,
                jnp.where(row_ids == 4, scale, node * (-2.0 * scale)),
            )
            p1, p2, p3 = split3(rows)
            columns.append(jnp.concatenate([p1, p2, p3, p1, p2, p1, empty], axis=0))
        columns.append(jnp.concatenate([empty] * 6 + [values], axis=0))
        product_ref[slot] = jnp.dot(
            left_ref[target],
            jnp.concatenate(columns, axis=1).astype(jnp.bfloat16),
            preferred_element_type=jnp.float32,
        )

    def one_pair(k, slot, nodes):
        target, owner, source, order = read(k)
        reach = reach_of(order)
        point = [got_ref[owner, source, c : c + 1, at_point : at_point + width] for c in range(3)]
        extent = [
            got_ref[owner, source, c : c + 1, at_extent : at_extent + width] * reach
            for c in range(3)
        ]
        columns = [jnp.zeros((8, width), jnp.float32) for _ in range(3)]
        for start in range(0, width, GROUP):
            rows = slice(start, start + GROUP)
            sums = [row_acc[target, c, rows] for c in range(3)]

            def cubed(node):
                i = lax.rsqrt(product_ref[slot, rows, node * width : (node + 1) * width])
                return i * i * i

            coupling = product_ref[slot, rows, 3 * width : 4 * width]
            f_plus = cubed(1)
            if nodes == 1:
                even = (coupling + coupling) * f_plus
            else:
                f_minus = cubed(2)
                both = f_plus + f_minus
                even = coupling * (both + cubed(0) if nodes == 3 else both)
                odd = coupling * (f_plus - f_minus)
            for c in range(3):
                pulled = even * (centre_ref[target, c, rows] - point[c])
                if nodes > 1:
                    pulled = pulled - odd * extent[c]
                sums[c] = sums[c] + pulled
                for r in range(0, GROUP, 8):
                    columns[c] = columns[c] + pulled[r : r + 8]
            for c in range(3):
                row_acc[target, c, rows] = sums[c]
        sums = jnp.concatenate(
            [jnp.sum(columns[c], axis=0, keepdims=True) for c in range(3)], axis=0
        )
        grad_ref[owner * blocks + source, 0:3] += sums

    def two_pairs(nodes):
        def body(step, carry):
            for slot in range(2):
                multiply(2 * step + slot + 1, 1 - slot)
                one_pair(2 * step + slot, slot, nodes)
            return carry

        return body

    multiply(0, 0)
    lax.fori_loop(0, info_ref[1], two_pairs(3), 0)
    lax.fori_loop(info_ref[1], info_ref[2], two_pairs(2), 0)
    lax.fori_loop(info_ref[2], info_ref[3], two_pairs(1), 0)
    for b in range(blocks):
        total = jnp.concatenate(
            [jnp.sum(row_acc[b, c], axis=1, keepdims=True) for c in range(3)]
            + [jnp.zeros((width, 5), jnp.float32)],
            axis=1,
        )
        grad_ref[me * blocks + b] -= total.T

    high = blocks * width // LANES
    keys = 4 * high
    shift = (blocks * width).bit_length() + 1
    key_ids = lax.broadcasted_iota(jnp.int32, (keys, width), 0).astype(jnp.bfloat16)
    lane_ids = lax.broadcasted_iota(jnp.int32, (LANES, width), 0).astype(jnp.bfloat16)
    zero = jnp.zeros((keys, width), jnp.bfloat16)
    one = jnp.ones((keys, width), jnp.bfloat16)

    def wide(row):
        return jnp.broadcast_to(row, (keys, width))

    def narrow(value):
        return value.astype(jnp.float32).astype(jnp.bfloat16)

    def scatter(tile, carry):
        result = None
        for b in range(blocks):
            spread = []
            for c in range(3):
                grad = wide(grad_ref[tile * blocks + b, c : c + 1])
                upper = grad.astype(jnp.bfloat16)
                spread += [upper, (grad - upper.astype(jnp.float32)).astype(jnp.bfloat16)]
            parts = []
            hots = []
            for half in (at_point, at_extent):
                code = wide(got_ref[tile, b, 3:4, half : half + width]).astype(jnp.int32)
                for place in (code >> shift, code & ((1 << shift) - 1)):
                    mask = key_ids == narrow(place >> 7)
                    low = narrow(place & (LANES - 1))
                    parts.append(
                        jnp.concatenate([jnp.where(mask, s, zero) for s in spread], axis=0)
                    )
                    hots.append(
                        jnp.concatenate(
                            [
                                jnp.where(lane_ids[g : g + keys] == low, one, zero)
                                for g in range(0, LANES, keys)
                            ],
                            axis=0,
                        )
                    )
            product = lax.dot_general(
                jnp.concatenate(parts, axis=1),
                jnp.concatenate(hots, axis=1),
                (((1,), (1,)), ((), ())),
                preferred_element_type=jnp.float32,
            )
            result = product if result is None else result + product
        for c in range(3):
            joined_ref[tile, c] = (
                result[2 * c * keys : (2 * c + 1) * keys]
                + result[(2 * c + 1) * keys : (2 * c + 2) * keys]
            )
        return carry

    def collect(dest, carry):
        for c in range(3):
            total = jnp.zeros((high, LANES), jnp.float32)
            for slot, by in enumerate((0, tiles - 1, 1, tiles - tiles // 2)):
                tile = lax.rem(dest + by, tiles)
                total = total + joined_ref[tile, c, slot * high : (slot + 1) * high]
            for f in range(out_ref.shape[1]):
                out_ref[dest, f, :, c * LANES : (c + 1) * LANES] = total
        return carry

    lax.fori_loop(0, tiles, scatter, 0, unroll=min(tiles, 8))
    lax.fori_loop(0, tiles, collect, 0, unroll=min(tiles, 8))


def sum_kernel(got_ref, out_ref):
    _, high, _ = got_ref.shape
    total = jnp.sum(got_ref[...], axis=0)
    for c in range(3):
        for h in range(high):
            out_ref[c : c + 1, h * LANES : (h + 1) * LANES] = total[
                h : h + 1, c * LANES : (c + 1) * LANES
            ]


def per_device(
    panel_geometry,
    adjoint,
    strengths,
    pair_target,
    pair_owner,
    pair_source,
    pair_order,
    pair_count,
    corner_vertex,
):
    tiles = lax.axis_size("tiles")
    far = lax.axis_size("far")
    blocks, _, width = panel_geometry.shape
    high = blocks * width // LANES
    me = lax.axis_index("tiles").astype(jnp.int32).reshape(1)
    smem = pl.BlockSpec(memory_space=SMEM)
    vmem = pl.BlockSpec(memory_space=VMEM)
    params = pltpu.CompilerParams(vmem_limit_bytes=LIMIT)
    geometry = panel_geometry.transpose(1, 0, 2)
    packed = pl.pallas_call(
        pack_kernel,
        out_shape=jax.ShapeDtypeStruct((tiles, blocks, 4, 3 * width), jnp.float32),
        in_specs=[smem] + [vmem] * 3,
        out_specs=vmem,
    )(me, geometry, strengths, corner_vertex)
    got = lax.all_to_all(packed, "tiles", split_axis=0, concat_axis=0, tiled=True)
    pairs = pair_target.shape[0]
    info, centre, left = pl.pallas_call(
        prep_kernel,
        out_shape=(
            jax.ShapeDtypeStruct((HEAD + pairs + SPARE,), jnp.int32),
            jax.ShapeDtypeStruct((blocks, 3, width, width), jnp.float32),
            jax.ShapeDtypeStruct((blocks, width, 56), jnp.bfloat16),
        ),
        in_specs=[smem] * 6 + [vmem] * 2,
        out_specs=(smem, vmem, vmem),
        compiler_params=params,
        cost_estimate=pl.CostEstimate(flops=4000000, bytes_accessed=900000, transcendentals=0),
    )(
        me,
        pair_target,
        pair_owner[:, 0],
        pair_source,
        pair_order,
        pair_count,
        geometry,
        adjoint,
    )
    partial = pl.pallas_call(
        pair_kernel,
        out_shape=jax.ShapeDtypeStruct((tiles, far, high, 3 * LANES), jnp.float32),
        in_specs=[smem] + [vmem] * 3,
        out_specs=vmem,
        scratch_shapes=[
            VMEM((2, width, 4 * width), jnp.float32),
            VMEM((blocks, 3, width, width), jnp.float32),
            VMEM((tiles * blocks, 8, width), jnp.float32),
            VMEM((tiles, 3, 4 * high, LANES), jnp.float32),
        ],
        compiler_params=params,
    )(info, centre, left, got)
    partial = partial.reshape(tiles * far, high, 3 * LANES)
    shares = lax.all_to_all(partial, ("tiles", "far"), split_axis=0, concat_axis=0, tiled=True)
    return pl.pallas_call(
        sum_kernel,
        out_shape=jax.ShapeDtypeStruct((3, blocks * width), jnp.float32),
        compiler_params=params,
    )(shares)


def solution(mesh):
    placed = (
        P("tiles", None, None),
        P("tiles", "far", None),
        P("tiles", "far", None),
        P("tiles"),
        P("tiles", None),
        P("tiles"),
        P("tiles"),
        P("tiles"),
        P("tiles", None, None),
    )
    return jax.shard_map(
        per_device, mesh=mesh, in_specs=placed, out_specs=P(None, "tiles"), check_vma=False
    )
```

```python
import functools

import jax
import jax.numpy as jnp
from jax import lax
from jax.experimental import pallas as pl
from jax.experimental.pallas import tpu as pltpu
from jax.sharding import PartitionSpec as P

SMEM = pltpu.SMEM
VMEM = pltpu.VMEM
LANES = 128
HEAD = 4
SPARE = 2
GROUP = 32
LIMIT = 48 * 1024 * 1024


def pack_kernel(tiles, me_ref, geom_ref, strength_ref, corner_ref, *out_refs):
    blocks, _, width = strength_ref.shape
    shift = (blocks * width).bit_length() - 1
    me = me_ref[0]
    for b in range(blocks):
        vertex = corner_ref[b]
        offset = (vertex >> shift) - me
        offset = jnp.where(offset < 0, offset + tiles, offset)
        slot = jnp.where(
            offset == 0,
            0,
            jnp.where(offset == 1, 1, jnp.where(offset == tiles - 1, 2, 3)),
        )
        place = ((slot << shift) + (vertex & ((1 << shift) - 1))).astype(jnp.float32)
        span = float(4 << shift)
        first = place[0:1] * span + place[1:2]
        second = place[2:3] * span + place[3:4]
        block = jnp.concatenate(
            [
                strength_ref[b].astype(jnp.float32),
                jnp.concatenate([geom_ref[c, b : b + 1] for c in range(3)] + [first], axis=0),
                jnp.concatenate([geom_ref[3 + c, b : b + 1] for c in range(3)] + [second], axis=0),
            ],
            axis=1,
        )
        for ref in out_refs:
            if len(ref.shape) == 3:
                ref[b] = block
            else:
                for t in range(tiles):
                    ref[t, b] = block


def join_kernel(*refs):
    *part_refs, send_ref, keep_ref = refs
    for i, ref in enumerate(part_refs):
        send_ref[i] = ref[...]
        keep_ref[i] = ref[...]


def split3(value):
    first = value.astype(jnp.bfloat16).astype(jnp.float32)
    rest = value - first
    second = rest.astype(jnp.bfloat16).astype(jnp.float32)
    return first, second, rest - second


def prep_kernel(
    me_ref,
    target_ref,
    owner_ref,
    source_ref,
    order_ref,
    count_ref,
    geom_ref,
    adjoint_ref,
    info_ref,
    centre_ref,
    left_ref,
):
    blocks, _, width = adjoint_ref.shape
    live = count_ref[0]
    total = target_ref.shape[0]
    for k in range(HEAD + total, HEAD + total + SPARE):
        info_ref[k] = 0

    def note(order, first):
        def one(k, at):
            mine = order_ref[k] == order
            word = (owner_ref[k] << 18) | (order << 16) | (source_ref[k] << 8) | target_ref[k]
            info_ref[at] = word
            return at + jnp.where(mine, 1, 0)

        return lax.fori_loop(0, live, one, first)

    third = note(3, HEAD)
    second = note(2, third)
    first = note(1, second)
    for k in range(SPARE):
        info_ref[first + k] = 0
    info_ref[0] = me_ref[0]
    info_ref[1] = (third - HEAD + 1) // 2
    info_ref[2] = (second - HEAD + 1) // 2
    info_ref[3] = (live + 1) // 2
    for b in range(blocks):
        point = jnp.concatenate([geom_ref[c, b : b + 1] for c in range(3)], axis=0)
        rows = [point, jnp.ones((1, width), jnp.float32)]
        rows += [jnp.sum(point * point, axis=0, keepdims=True)]
        rows += [jnp.zeros((3, width), jnp.float32)]
        x1, x2, x3 = split3(jnp.concatenate(rows, axis=0))
        values = [adjoint_ref[b].astype(jnp.float32), jnp.zeros((4, width), jnp.float32)]
        rows = [x1, x1, x1, x2, x2, x3] + values
        left_ref[b] = jnp.concatenate(rows, axis=0).T.astype(jnp.bfloat16)
        for c in range(3):
            centre_ref[b, c] = jnp.broadcast_to(point[c : c + 1], (width, width)).T


def pair_kernel(
    info_ref,
    centre_ref,
    left_ref,
    *refs,
):
    *arrived, out_ref, product_ref, row_acc, grad_ref, joined_ref, held_ref = refs
    tiles, blocks = joined_ref.shape[0], centre_ref.shape[0]
    width = centre_ref.shape[3]
    at_point, at_extent = width, 2 * width
    me = info_ref[0]
    if len(arrived) == 1:
        got_ref = arrived[0]
    else:
        got_ref = held_ref
        own = me & 1
        for side, ref in ((own, arrived[0]), (1 - own, arrived[1])):
            for d in range(ref.shape[0]):
                held_ref[lax.rem(me - own + 2 * d, tiles) + side] = ref[d]
    grad_ref[...] = jnp.zeros(grad_ref.shape, jnp.float32)
    row_acc[...] = jnp.zeros(row_acc.shape, jnp.float32)
    blank = jnp.zeros((4, width), jnp.float32)
    row_ids = lax.broadcasted_iota(jnp.int32, (8, width), 0)

    def reach_of(order):
        return 0.25 * jnp.where(
            order == 3, 0.7745966692414834, jnp.where(order == 2, 0.5773502691896258, 0.0)
        )

    def read(k):
        word = info_ref[HEAD + k]
        return word & 255, word >> 18, (word >> 8) & 255, (word >> 16) & 3

    def multiply(k, slot):
        target, owner, source, order = read(k)
        third = order == 3
        alive = jnp.where(order > 0, 1.0, 0.0).astype(jnp.float32)
        reach = reach_of(order)
        scale_mid = jnp.where(third, (4.0 / 9.0 / 512.0) ** (-2.0 / 3.0), 0.0)
        scale_side = jnp.where(
            third, (5.0 / 18.0 / 512.0) ** (-2.0 / 3.0), (0.5 / 512.0) ** (-2.0 / 3.0)
        )
        floor_mid = jnp.where(third, 0.0625 * (4.0 / 9.0 / 512.0) ** (-2.0 / 3.0), 3.0e38)
        floor_side = 0.0625 * scale_side
        point = got_ref[owner, source, :, at_point : at_point + width]
        extent = got_ref[owner, source, :, at_extent : at_extent + width] * reach
        inside = row_ids < 3
        point = jnp.where(inside, jnp.concatenate([point, blank], axis=0), 0.0)
        extent = jnp.where(inside, jnp.concatenate([extent, blank], axis=0), 0.0)
        values = jnp.concatenate([got_ref[owner, source, :, 0:width] * alive, blank], axis=0)
        empty = jnp.zeros((8, width), jnp.float32)
        nodes = (
            (point, scale_mid, floor_mid),
            (point + extent, scale_side, floor_side),
            (point - extent, scale_side, floor_side),
        )
        columns = []
        for node, scale, floor in nodes:
            norm = jnp.sum(node * node, axis=0, keepdims=True) * scale + floor
            rows = jnp.where(
                row_ids == 3,
                norm,
                jnp.where(row_ids == 4, scale, node * (-2.0 * scale)),
            )
            p1, p2, p3 = split3(rows)
            columns.append(jnp.concatenate([p1, p2, p3, p1, p2, p1, empty], axis=0))
        columns.append(jnp.concatenate([empty] * 6 + [values], axis=0))
        product_ref[slot] = jnp.dot(
            left_ref[target],
            jnp.concatenate(columns, axis=1).astype(jnp.bfloat16),
            preferred_element_type=jnp.float32,
        )

    def one_pair(k, slot, nodes):
        target, owner, source, order = read(k)
        reach = reach_of(order)
        point = [got_ref[owner, source, c : c + 1, at_point : at_point + width] for c in range(3)]
        extent = [
            got_ref[owner, source, c : c + 1, at_extent : at_extent + width] * reach
            for c in range(3)
        ]
        columns = [jnp.zeros((8, width), jnp.float32) for _ in range(3)]
        for start in range(0, width, GROUP):
            rows = slice(start, start + GROUP)
            sums = [row_acc[target, c, rows] for c in range(3)]

            def cubed(node):
                i = lax.rsqrt(product_ref[slot, rows, node * width : (node + 1) * width])
                return i * i * i

            coupling = product_ref[slot, rows, 3 * width : 4 * width]
            f_plus = cubed(1)
            if nodes == 1:
                even = (coupling + coupling) * f_plus
            else:
                f_minus = cubed(2)
                both = f_plus + f_minus
                even = coupling * (both + cubed(0) if nodes == 3 else both)
                odd = coupling * (f_plus - f_minus)
            for c in range(3):
                pulled = even * (centre_ref[target, c, rows] - point[c])
                if nodes > 1:
                    pulled = pulled - odd * extent[c]
                sums[c] = sums[c] + pulled
                for r in range(0, GROUP, 8):
                    columns[c] = columns[c] + pulled[r : r + 8]
            for c in range(3):
                row_acc[target, c, rows] = sums[c]
        sums = jnp.concatenate(
            [jnp.sum(columns[c], axis=0, keepdims=True) for c in range(3)], axis=0
        )
        grad_ref[owner * blocks + source, 0:3] += sums

    def two_pairs(nodes):
        def body(step, carry):
            for slot in range(2):
                multiply(2 * step + slot + 1, 1 - slot)
                one_pair(2 * step + slot, slot, nodes)
            return carry

        return body

    multiply(0, 0)
    lax.fori_loop(0, info_ref[1], two_pairs(3), 0)
    lax.fori_loop(info_ref[1], info_ref[2], two_pairs(2), 0)
    lax.fori_loop(info_ref[2], info_ref[3], two_pairs(1), 0)
    for b in range(blocks):
        total = jnp.concatenate(
            [jnp.sum(row_acc[b, c], axis=1, keepdims=True) for c in range(3)]
            + [jnp.zeros((width, 5), jnp.float32)],
            axis=1,
        )
        grad_ref[me * blocks + b] -= total.T

    high = blocks * width // LANES
    keys = 4 * high
    shift = (blocks * width).bit_length() + 1
    key_ids = lax.broadcasted_iota(jnp.int32, (keys, width), 0).astype(jnp.bfloat16)
    lane_ids = lax.broadcasted_iota(jnp.int32, (LANES, width), 0).astype(jnp.bfloat16)
    zero = jnp.zeros((keys, width), jnp.bfloat16)
    one = jnp.ones((keys, width), jnp.bfloat16)

    def wide(row):
        return jnp.broadcast_to(row, (keys, width))

    def narrow(value):
        return value.astype(jnp.float32).astype(jnp.bfloat16)

    def scatter(tile, carry):
        result = None
        for b in range(blocks):
            spread = []
            for c in range(3):
                grad = wide(grad_ref[tile * blocks + b, c : c + 1])
                upper = grad.astype(jnp.bfloat16)
                spread += [upper, (grad - upper.astype(jnp.float32)).astype(jnp.bfloat16)]
            parts = []
            hots = []
            for half in (at_point, at_extent):
                code = wide(got_ref[tile, b, 3:4, half : half + width]).astype(jnp.int32)
                for place in (code >> shift, code & ((1 << shift) - 1)):
                    mask = key_ids == narrow(place >> 7)
                    low = narrow(place & (LANES - 1))
                    parts.append(
                        jnp.concatenate([jnp.where(mask, s, zero) for s in spread], axis=0)
                    )
                    hots.append(
                        jnp.concatenate(
                            [
                                jnp.where(lane_ids[g : g + keys] == low, one, zero)
                                for g in range(0, LANES, keys)
                            ],
                            axis=0,
                        )
                    )
            product = lax.dot_general(
                jnp.concatenate(parts, axis=1),
                jnp.concatenate(hots, axis=1),
                (((1,), (1,)), ((), ())),
                preferred_element_type=jnp.float32,
            )
            result = product if result is None else result + product
        for c in range(3):
            joined_ref[tile, c] = (
                result[2 * c * keys : (2 * c + 1) * keys]
                + result[(2 * c + 1) * keys : (2 * c + 2) * keys]
            )
        return carry

    def collect(dest, carry):
        for c in range(3):
            total = jnp.zeros((high, LANES), jnp.float32)
            for slot, by in enumerate((0, tiles - 1, 1, tiles - tiles // 2)):
                tile = lax.rem(dest + by, tiles)
                total = total + joined_ref[tile, c, slot * high : (slot + 1) * high]
            for f in range(out_ref.shape[1]):
                out_ref[dest, f, :, c * LANES : (c + 1) * LANES] = total
        return carry

    lax.fori_loop(0, tiles, scatter, 0, unroll=min(tiles, 8))
    lax.fori_loop(0, tiles, collect, 0, unroll=min(tiles, 8))


def sum_kernel(got_ref, out_ref):
    _, high, _ = got_ref.shape
    total = jnp.sum(got_ref[...], axis=0)
    for c in range(3):
        for h in range(high):
            out_ref[c : c + 1, h * LANES : (h + 1) * LANES] = total[
                h : h + 1, c * LANES : (c + 1) * LANES
            ]


def per_device(
    panel_geometry,
    adjoint,
    strengths,
    pair_target,
    pair_owner,
    pair_source,
    pair_order,
    pair_count,
    corner_vertex,
):
    tiles = lax.axis_size("tiles")
    far = lax.axis_size("far")
    blocks, _, width = panel_geometry.shape
    high = blocks * width // LANES
    me = lax.axis_index("tiles").astype(jnp.int32).reshape(1)
    smem = pl.BlockSpec(memory_space=SMEM)
    vmem = pl.BlockSpec(memory_space=VMEM)
    params = pltpu.CompilerParams(vmem_limit_bytes=LIMIT)
    geometry = panel_geometry.transpose(1, 0, 2)
    sources = (me, geometry, strengths, corner_vertex)
    block = (blocks, 4, 3 * width)
    staged = tiles <= 8 and tiles % 2 == 0
    if staged:
        depth = tiles // 2
        send, keep = pl.pallas_call(
            functools.partial(pack_kernel, tiles),
            out_shape=(jax.ShapeDtypeStruct(block, jnp.float32),) * 2,
            in_specs=[smem] + [vmem] * 3,
            out_specs=(vmem, vmem),
        )(*sources)
        others = [
            lax.ppermute(send, "tiles", [((i + 2 * d) % tiles, i) for i in range(tiles)])
            for d in range(1, depth)
        ]
        send, keep = pl.pallas_call(
            join_kernel,
            out_shape=(jax.ShapeDtypeStruct((depth,) + block, jnp.float32),) * 2,
        )(keep, *others)
        arrived = [keep, lax.ppermute(send, "tiles", [(i ^ 1, i) for i in range(tiles)])]
        held = (tiles,) + block
    else:
        packed = pl.pallas_call(
            functools.partial(pack_kernel, tiles),
            out_shape=jax.ShapeDtypeStruct((tiles,) + block, jnp.float32),
            in_specs=[smem] + [vmem] * 3,
            out_specs=vmem,
        )(*sources)
        arrived = [lax.all_to_all(packed, "tiles", split_axis=0, concat_axis=0, tiled=True)]
        held = (1, 1, 8, LANES)
    pairs = pair_target.shape[0]
    info, centre, left = pl.pallas_call(
        prep_kernel,
        out_shape=(
            jax.ShapeDtypeStruct((HEAD + pairs + SPARE,), jnp.int32),
            jax.ShapeDtypeStruct((blocks, 3, width, width), jnp.float32),
            jax.ShapeDtypeStruct((blocks, width, 56), jnp.bfloat16),
        ),
        in_specs=[smem] * 6 + [vmem] * 2,
        out_specs=(smem, vmem, vmem),
        compiler_params=params,
        cost_estimate=pl.CostEstimate(flops=4000000, bytes_accessed=900000, transcendentals=0),
    )(
        me,
        pair_target,
        pair_owner[:, 0],
        pair_source,
        pair_order,
        pair_count,
        geometry,
        adjoint,
    )
    partial = pl.pallas_call(
        pair_kernel,
        out_shape=jax.ShapeDtypeStruct((tiles, far, high, 3 * LANES), jnp.float32),
        in_specs=[smem] + [vmem] * (2 + len(arrived)),
        out_specs=vmem,
        scratch_shapes=[
            VMEM((2, width, 4 * width), jnp.float32),
            VMEM((blocks, 3, width, width), jnp.float32),
            VMEM((tiles * blocks, 8, width), jnp.float32),
            VMEM((tiles, 3, 4 * high, LANES), jnp.float32),
            VMEM(held, jnp.float32),
        ],
        compiler_params=params,
    )(info, centre, left, *arrived)
    partial = partial.reshape(tiles * far, high, 3 * LANES)
    shares = lax.all_to_all(partial, ("tiles", "far"), split_axis=0, concat_axis=0, tiled=True)
    return pl.pallas_call(
        sum_kernel,
        out_shape=jax.ShapeDtypeStruct((3, blocks * width), jnp.float32),
        compiler_params=params,
    )(shares)


def solution(mesh):
    placed = (
        P("tiles", None, None),
        P("tiles", "far", None),
        P("tiles", "far", None),
        P("tiles"),
        P("tiles", None),
        P("tiles"),
        P("tiles"),
        P("tiles"),
        P("tiles", None, None),
    )
    return jax.shard_map(
        per_device, mesh=mesh, in_specs=placed, out_specs=P(None, "tiles"), check_vma=False
    )
```

```python
import functools

import jax
import jax.numpy as jnp
from jax import lax
from jax.experimental import pallas as pl
from jax.experimental.pallas import tpu as pltpu
from jax.sharding import PartitionSpec as P

SMEM = pltpu.SMEM
VMEM = pltpu.VMEM
LANES = 128
HEAD = 4
SPARE = 2
GROUP = 32
LIMIT = 48 * 1024 * 1024


def pack_kernel(tiles, me_ref, geom_ref, strength_ref, corner_ref, *out_refs):
    blocks, _, width = strength_ref.shape
    shift = (blocks * width).bit_length() - 1
    me = me_ref[0]
    for b in range(blocks):
        vertex = corner_ref[b]
        offset = (vertex >> shift) - me
        offset = jnp.where(offset < 0, offset + tiles, offset)
        slot = jnp.where(
            offset == 0,
            0,
            jnp.where(offset == 1, 1, jnp.where(offset == tiles - 1, 2, 3)),
        )
        place = ((slot << shift) + (vertex & ((1 << shift) - 1))).astype(jnp.float32)
        span = float(4 << shift)
        first = place[0:1] * span + place[1:2]
        second = place[2:3] * span + place[3:4]
        block = jnp.concatenate(
            [
                strength_ref[b].astype(jnp.float32),
                jnp.concatenate([geom_ref[c, b : b + 1] for c in range(3)] + [first], axis=0),
                jnp.concatenate([geom_ref[3 + c, b : b + 1] for c in range(3)] + [second], axis=0),
            ],
            axis=1,
        )
        for ref in out_refs:
            if len(ref.shape) == 3:
                ref[b] = block
            else:
                for t in range(tiles):
                    ref[t, b] = block


def split3(value):
    first = value.astype(jnp.bfloat16).astype(jnp.float32)
    rest = value - first
    second = rest.astype(jnp.bfloat16).astype(jnp.float32)
    return first, second, rest - second


def prep_kernel(
    me_ref,
    target_ref,
    owner_ref,
    source_ref,
    order_ref,
    count_ref,
    geom_ref,
    adjoint_ref,
    info_ref,
    centre_ref,
    left_ref,
):
    blocks, _, width = adjoint_ref.shape
    live = count_ref[0]
    total = target_ref.shape[0]
    for k in range(HEAD + total, HEAD + total + SPARE):
        info_ref[k] = 0

    def note(order, first):
        def one(k, at):
            mine = order_ref[k] == order
            word = (owner_ref[k] << 18) | (order << 16) | (source_ref[k] << 8) | target_ref[k]
            info_ref[at] = word
            return at + jnp.where(mine, 1, 0)

        return lax.fori_loop(0, live, one, first)

    third = note(3, HEAD)
    second = note(2, third)
    first = note(1, second)
    for k in range(SPARE):
        info_ref[first + k] = 0
    info_ref[0] = me_ref[0]
    info_ref[1] = (third - HEAD + 1) // 2
    info_ref[2] = (second - HEAD + 1) // 2
    info_ref[3] = (live + 1) // 2
    for b in range(blocks):
        point = jnp.concatenate([geom_ref[c, b : b + 1] for c in range(3)], axis=0)
        rows = [point, jnp.ones((1, width), jnp.float32)]
        rows += [jnp.sum(point * point, axis=0, keepdims=True)]
        rows += [jnp.zeros((3, width), jnp.float32)]
        x1, x2, x3 = split3(jnp.concatenate(rows, axis=0))
        values = [adjoint_ref[b].astype(jnp.float32), jnp.zeros((4, width), jnp.float32)]
        rows = [x1, x1, x1, x2, x2, x3] + values
        left_ref[b] = jnp.concatenate(rows, axis=0).T.astype(jnp.bfloat16)
        for c in range(3):
            centre_ref[b, c] = jnp.broadcast_to(point[c : c + 1], (width, width)).T


def pair_kernel(
    info_ref,
    centre_ref,
    left_ref,
    *refs,
):
    *arrived, out_ref, product_ref, row_acc, grad_ref, joined_ref, held_ref = refs
    tiles, blocks = joined_ref.shape[0], centre_ref.shape[0]
    width = centre_ref.shape[3]
    at_point, at_extent = width, 2 * width
    me = info_ref[0]
    if len(arrived) == 1:
        got_ref = arrived[0]
    else:
        got_ref = held_ref
        own = me & 1
        for i, ref in enumerate(arrived):
            side = own if i < tiles // 2 else 1 - own
            held_ref[lax.rem(me - own + 2 * i, tiles) + side] = ref[...]
    grad_ref[...] = jnp.zeros(grad_ref.shape, jnp.float32)
    row_acc[...] = jnp.zeros(row_acc.shape, jnp.float32)
    blank = jnp.zeros((4, width), jnp.float32)
    row_ids = lax.broadcasted_iota(jnp.int32, (8, width), 0)

    def reach_of(order):
        return 0.25 * jnp.where(
            order == 3, 0.7745966692414834, jnp.where(order == 2, 0.5773502691896258, 0.0)
        )

    def read(k):
        word = info_ref[HEAD + k]
        return word & 255, word >> 18, (word >> 8) & 255, (word >> 16) & 3

    def multiply(k, slot):
        target, owner, source, order = read(k)
        third = order == 3
        alive = jnp.where(order > 0, 1.0, 0.0).astype(jnp.float32)
        reach = reach_of(order)
        scale_mid = jnp.where(third, (4.0 / 9.0 / 512.0) ** (-2.0 / 3.0), 0.0)
        scale_side = jnp.where(
            third, (5.0 / 18.0 / 512.0) ** (-2.0 / 3.0), (0.5 / 512.0) ** (-2.0 / 3.0)
        )
        floor_mid = jnp.where(third, 0.0625 * (4.0 / 9.0 / 512.0) ** (-2.0 / 3.0), 3.0e38)
        floor_side = 0.0625 * scale_side
        point = got_ref[owner, source, :, at_point : at_point + width]
        extent = got_ref[owner, source, :, at_extent : at_extent + width] * reach
        inside = row_ids < 3
        point = jnp.where(inside, jnp.concatenate([point, blank], axis=0), 0.0)
        extent = jnp.where(inside, jnp.concatenate([extent, blank], axis=0), 0.0)
        values = jnp.concatenate([got_ref[owner, source, :, 0:width] * alive, blank], axis=0)
        empty = jnp.zeros((8, width), jnp.float32)
        nodes = (
            (point, scale_mid, floor_mid),
            (point + extent, scale_side, floor_side),
            (point - extent, scale_side, floor_side),
        )
        columns = []
        for node, scale, floor in nodes:
            norm = jnp.sum(node * node, axis=0, keepdims=True) * scale + floor
            rows = jnp.where(
                row_ids == 3,
                norm,
                jnp.where(row_ids == 4, scale, node * (-2.0 * scale)),
            )
            p1, p2, p3 = split3(rows)
            columns.append(jnp.concatenate([p1, p2, p3, p1, p2, p1, empty], axis=0))
        columns.append(jnp.concatenate([empty] * 6 + [values], axis=0))
        product_ref[slot] = jnp.dot(
            left_ref[target],
            jnp.concatenate(columns, axis=1).astype(jnp.bfloat16),
            preferred_element_type=jnp.float32,
        )

    def one_pair(k, slot, nodes):
        target, owner, source, order = read(k)
        reach = reach_of(order)
        point = [got_ref[owner, source, c : c + 1, at_point : at_point + width] for c in range(3)]
        extent = [
            got_ref[owner, source, c : c + 1, at_extent : at_extent + width] * reach
            for c in range(3)
        ]
        columns = [jnp.zeros((8, width), jnp.float32) for _ in range(3)]
        for start in range(0, width, GROUP):
            rows = slice(start, start + GROUP)
            sums = [row_acc[target, c, rows] for c in range(3)]

            def cubed(node):
                i = lax.rsqrt(product_ref[slot, rows, node * width : (node + 1) * width])
                return i * i * i

            coupling = product_ref[slot, rows, 3 * width : 4 * width]
            f_plus = cubed(1)
            if nodes == 1:
                even = (coupling + coupling) * f_plus
            else:
                f_minus = cubed(2)
                both = f_plus + f_minus
                even = coupling * (both + cubed(0) if nodes == 3 else both)
                odd = coupling * (f_plus - f_minus)
            for c in range(3):
                pulled = even * (centre_ref[target, c, rows] - point[c])
                if nodes > 1:
                    pulled = pulled - odd * extent[c]
                sums[c] = sums[c] + pulled
                for r in range(0, GROUP, 8):
                    columns[c] = columns[c] + pulled[r : r + 8]
            for c in range(3):
                row_acc[target, c, rows] = sums[c]
        sums = jnp.concatenate(
            [jnp.sum(columns[c], axis=0, keepdims=True) for c in range(3)], axis=0
        )
        grad_ref[owner * blocks + source, 0:3] += sums

    def two_pairs(nodes):
        def body(step, carry):
            for slot in range(2):
                multiply(2 * step + slot + 1, 1 - slot)
                one_pair(2 * step + slot, slot, nodes)
            return carry

        return body

    multiply(0, 0)
    lax.fori_loop(0, info_ref[1], two_pairs(3), 0)
    lax.fori_loop(info_ref[1], info_ref[2], two_pairs(2), 0)
    lax.fori_loop(info_ref[2], info_ref[3], two_pairs(1), 0)
    for b in range(blocks):
        total = jnp.concatenate(
            [jnp.sum(row_acc[b, c], axis=1, keepdims=True) for c in range(3)]
            + [jnp.zeros((width, 5), jnp.float32)],
            axis=1,
        )
        grad_ref[me * blocks + b] -= total.T

    high = blocks * width // LANES
    keys = 4 * high
    shift = (blocks * width).bit_length() + 1
    key_ids = lax.broadcasted_iota(jnp.int32, (keys, width), 0).astype(jnp.bfloat16)
    lane_ids = lax.broadcasted_iota(jnp.int32, (LANES, width), 0).astype(jnp.bfloat16)
    zero = jnp.zeros((keys, width), jnp.bfloat16)
    one = jnp.ones((keys, width), jnp.bfloat16)

    def wide(row):
        return jnp.broadcast_to(row, (keys, width))

    def narrow(value):
        return value.astype(jnp.float32).astype(jnp.bfloat16)

    def scatter(tile, carry):
        result = None
        for b in range(blocks):
            spread = []
            for c in range(3):
                grad = wide(grad_ref[tile * blocks + b, c : c + 1])
                upper = grad.astype(jnp.bfloat16)
                spread += [upper, (grad - upper.astype(jnp.float32)).astype(jnp.bfloat16)]
            parts = []
            hots = []
            for half in (at_point, at_extent):
                code = wide(got_ref[tile, b, 3:4, half : half + width]).astype(jnp.int32)
                for place in (code >> shift, code & ((1 << shift) - 1)):
                    mask = key_ids == narrow(place >> 7)
                    low = narrow(place & (LANES - 1))
                    parts.append(
                        jnp.concatenate([jnp.where(mask, s, zero) for s in spread], axis=0)
                    )
                    hots.append(
                        jnp.concatenate(
                            [
                                jnp.where(lane_ids[g : g + keys] == low, one, zero)
                                for g in range(0, LANES, keys)
                            ],
                            axis=0,
                        )
                    )
            product = lax.dot_general(
                jnp.concatenate(parts, axis=1),
                jnp.concatenate(hots, axis=1),
                (((1,), (1,)), ((), ())),
                preferred_element_type=jnp.float32,
            )
            result = product if result is None else result + product
        for c in range(3):
            joined_ref[tile, c] = (
                result[2 * c * keys : (2 * c + 1) * keys]
                + result[(2 * c + 1) * keys : (2 * c + 2) * keys]
            )
        return carry

    def collect(dest, carry):
        for c in range(3):
            total = jnp.zeros((high, LANES), jnp.float32)
            for slot, by in enumerate((0, tiles - 1, 1, tiles - tiles // 2)):
                tile = lax.rem(dest + by, tiles)
                total = total + joined_ref[tile, c, slot * high : (slot + 1) * high]
            for f in range(out_ref.shape[1]):
                out_ref[dest, f, :, c * LANES : (c + 1) * LANES] = total
        return carry

    lax.fori_loop(0, tiles, scatter, 0, unroll=min(tiles, 8))
    lax.fori_loop(0, tiles, collect, 0, unroll=min(tiles, 8))


def sum_kernel(got_ref, out_ref):
    _, high, _ = got_ref.shape
    total = jnp.sum(got_ref[...], axis=0)
    for c in range(3):
        for h in range(high):
            out_ref[c : c + 1, h * LANES : (h + 1) * LANES] = total[
                h : h + 1, c * LANES : (c + 1) * LANES
            ]


def per_device(
    panel_geometry,
    adjoint,
    strengths,
    pair_target,
    pair_owner,
    pair_source,
    pair_order,
    pair_count,
    corner_vertex,
):
    tiles = lax.axis_size("tiles")
    far = lax.axis_size("far")
    blocks, _, width = panel_geometry.shape
    high = blocks * width // LANES
    me = lax.axis_index("tiles").astype(jnp.int32).reshape(1)
    smem = pl.BlockSpec(memory_space=SMEM)
    vmem = pl.BlockSpec(memory_space=VMEM)
    params = pltpu.CompilerParams(vmem_limit_bytes=LIMIT)
    geometry = panel_geometry.transpose(1, 0, 2)
    pairs = pair_target.shape[0]
    info, centre, left = pl.pallas_call(
        prep_kernel,
        out_shape=(
            jax.ShapeDtypeStruct((HEAD + pairs + SPARE,), jnp.int32),
            jax.ShapeDtypeStruct((blocks, 3, width, width), jnp.float32),
            jax.ShapeDtypeStruct((blocks, width, 56), jnp.bfloat16),
        ),
        in_specs=[smem] * 6 + [vmem] * 2,
        out_specs=(smem, vmem, vmem),
        compiler_params=params,
        cost_estimate=pl.CostEstimate(flops=4000000, bytes_accessed=900000, transcendentals=0),
    )(
        me,
        pair_target,
        pair_owner[:, 0],
        pair_source,
        pair_order,
        pair_count,
        geometry,
        adjoint,
    )
    sources = (me, geometry, strengths, corner_vertex)
    block = (blocks, 4, 3 * width)
    if tiles <= 8 and tiles % 2 == 0:
        send, keep = pl.pallas_call(
            functools.partial(pack_kernel, tiles),
            out_shape=(jax.ShapeDtypeStruct(block, jnp.float32),) * 2,
            in_specs=[smem] + [vmem] * 3,
            out_specs=(vmem, vmem),
        )(*sources)
        along = [
            lax.ppermute(send, "tiles", [((i + 2 * d) % tiles, i) for i in range(tiles)])
            for d in range(1, tiles // 2)
        ]
        swap = [(i ^ 1, i) for i in range(tiles)]
        across = [lax.ppermute(send, "tiles", swap)]
        for part in along:
            part, info = lax.optimization_barrier((part, info))
            across.append(lax.ppermute(part, "tiles", swap))
        arrived = [keep] + along + across
        held = (tiles,) + block
    else:
        packed = pl.pallas_call(
            functools.partial(pack_kernel, tiles),
            out_shape=jax.ShapeDtypeStruct((tiles,) + block, jnp.float32),
            in_specs=[smem] + [vmem] * 3,
            out_specs=vmem,
        )(*sources)
        arrived = [lax.all_to_all(packed, "tiles", split_axis=0, concat_axis=0, tiled=True)]
        held = (1, 1, 8, LANES)
    partial = pl.pallas_call(
        pair_kernel,
        out_shape=jax.ShapeDtypeStruct((tiles, far, high, 3 * LANES), jnp.float32),
        in_specs=[smem] + [vmem] * (2 + len(arrived)),
        out_specs=vmem,
        scratch_shapes=[
            VMEM((2, width, 4 * width), jnp.float32),
            VMEM((blocks, 3, width, width), jnp.float32),
            VMEM((tiles * blocks, 8, width), jnp.float32),
            VMEM((tiles, 3, 4 * high, LANES), jnp.float32),
            VMEM(held, jnp.float32),
        ],
        compiler_params=params,
    )(info, centre, left, *arrived)
    partial = partial.reshape(tiles * far, high, 3 * LANES)
    shares = lax.all_to_all(partial, ("tiles", "far"), split_axis=0, concat_axis=0, tiled=True)
    return pl.pallas_call(
        sum_kernel,
        out_shape=jax.ShapeDtypeStruct((3, blocks * width), jnp.float32),
        compiler_params=params,
    )(shares)


def solution(mesh):
    placed = (
        P("tiles", None, None),
        P("tiles", "far", None),
        P("tiles", "far", None),
        P("tiles"),
        P("tiles", None),
        P("tiles"),
        P("tiles"),
        P("tiles"),
        P("tiles", None, None),
    )
    return jax.shard_map(
        per_device, mesh=mesh, in_specs=placed, out_specs=P(None, "tiles"), check_vma=False
    )
```

```python
import jax
import jax.numpy as jnp
from jax import lax
from jax.experimental import pallas as pl
from jax.experimental.pallas import tpu as pltpu
from jax.sharding import PartitionSpec as P

SMEM = pltpu.SMEM
VMEM = pltpu.VMEM
LANES = 128
HEAD = 4
SPARE = 2
GROUP = 32
LIMIT = 48 * 1024 * 1024


def pack_kernel(me_ref, geom_ref, strength_ref, corner_ref, out_ref):
    tiles, blocks, _, _ = out_ref.shape
    width = strength_ref.shape[2]
    shift = (blocks * width).bit_length() - 1
    me = me_ref[0]
    for b in range(blocks):
        vertex = corner_ref[b]
        offset = (vertex >> shift) - me
        offset = jnp.where(offset < 0, offset + tiles, offset)
        slot = jnp.where(
            offset == 0,
            0,
            jnp.where(offset == 1, 1, jnp.where(offset == tiles - 1, 2, 3)),
        )
        place = ((slot << shift) + (vertex & ((1 << shift) - 1))).astype(jnp.float32)
        span = float(4 << shift)
        first = place[0:1] * span + place[1:2]
        second = place[2:3] * span + place[3:4]
        block = jnp.concatenate(
            [
                strength_ref[b].astype(jnp.float32),
                jnp.concatenate([geom_ref[c, b : b + 1] for c in range(3)] + [first], axis=0),
                jnp.concatenate([geom_ref[3 + c, b : b + 1] for c in range(3)] + [second], axis=0),
            ],
            axis=1,
        )
        for t in range(tiles):
            out_ref[t, b] = block


def split3(value):
    first = value.astype(jnp.bfloat16).astype(jnp.float32)
    rest = value - first
    second = rest.astype(jnp.bfloat16).astype(jnp.float32)
    return first, second, rest - second


def prep_kernel(
    me_ref,
    target_ref,
    owner_ref,
    source_ref,
    order_ref,
    count_ref,
    geom_ref,
    adjoint_ref,
    info_ref,
    centre_ref,
    left_ref,
):
    blocks, _, width = adjoint_ref.shape
    live = count_ref[0]
    total = target_ref.shape[0]
    for k in range(HEAD + total, HEAD + total + SPARE):
        info_ref[k] = 0

    def note(order, first):
        def one(k, at):
            mine = order_ref[k] == order
            word = (owner_ref[k] << 18) | (order << 16) | (source_ref[k] << 8) | target_ref[k]
            info_ref[at] = word
            return at + jnp.where(mine, 1, 0)

        return lax.fori_loop(0, live, one, first)

    third = note(3, HEAD)
    second = note(2, third)
    first = note(1, second)
    for k in range(SPARE):
        info_ref[first + k] = 0
    info_ref[0] = me_ref[0]
    info_ref[1] = (third - HEAD + 1) // 2
    info_ref[2] = (second - HEAD + 1) // 2
    info_ref[3] = (live + 1) // 2
    for b in range(blocks):
        point = jnp.concatenate([geom_ref[c, b : b + 1] for c in range(3)], axis=0)
        rows = [point, jnp.ones((1, width), jnp.float32)]
        rows += [jnp.sum(point * point, axis=0, keepdims=True)]
        rows += [jnp.zeros((3, width), jnp.float32)]
        x1, x2, x3 = split3(jnp.concatenate(rows, axis=0))
        values = [adjoint_ref[b].astype(jnp.float32), jnp.zeros((4, width), jnp.float32)]
        rows = [x1, x1, x1, x2, x2, x3] + values
        left_ref[b] = jnp.concatenate(rows, axis=0).T.astype(jnp.bfloat16)
        for c in range(3):
            centre_ref[b, c] = jnp.broadcast_to(point[c : c + 1], (width, width)).T


def pair_kernel(
    info_ref,
    centre_ref,
    left_ref,
    got_ref,
    out_ref,
    product_ref,
    row_acc,
    grad_ref,
    joined_ref,
):
    tiles, blocks, _, _ = got_ref.shape
    width = centre_ref.shape[3]
    at_point, at_extent = width, 2 * width
    me = info_ref[0]
    grad_ref[...] = jnp.zeros(grad_ref.shape, jnp.float32)
    row_acc[...] = jnp.zeros(row_acc.shape, jnp.float32)
    blank = jnp.zeros((4, width), jnp.float32)
    row_ids = lax.broadcasted_iota(jnp.int32, (8, width), 0)

    def reach_of(order):
        return 0.25 * jnp.where(
            order == 3, 0.7745966692414834, jnp.where(order == 2, 0.5773502691896258, 0.0)
        )

    def read(k):
        word = info_ref[HEAD + k]
        return word & 255, word >> 18, (word >> 8) & 255, (word >> 16) & 3

    def multiply(k, slot):
        target, owner, source, order = read(k)
        third = order == 3
        alive = jnp.where(order > 0, 1.0, 0.0).astype(jnp.float32)
        reach = reach_of(order)
        scale_mid = jnp.where(third, (4.0 / 9.0 / 512.0) ** (-2.0 / 3.0), 0.0)
        scale_side = jnp.where(
            third, (5.0 / 18.0 / 512.0) ** (-2.0 / 3.0), (0.5 / 512.0) ** (-2.0 / 3.0)
        )
        floor_mid = jnp.where(third, 0.0625 * (4.0 / 9.0 / 512.0) ** (-2.0 / 3.0), 3.0e38)
        floor_side = 0.0625 * scale_side
        point = got_ref[owner, source, :, at_point : at_point + width]
        extent = got_ref[owner, source, :, at_extent : at_extent + width] * reach
        inside = row_ids < 3
        point = jnp.where(inside, jnp.concatenate([point, blank], axis=0), 0.0)
        extent = jnp.where(inside, jnp.concatenate([extent, blank], axis=0), 0.0)
        values = jnp.concatenate([got_ref[owner, source, :, 0:width] * alive, blank], axis=0)
        empty = jnp.zeros((8, width), jnp.float32)
        nodes = (
            (point, scale_mid, floor_mid),
            (point + extent, scale_side, floor_side),
            (point - extent, scale_side, floor_side),
        )
        columns = []
        for node, scale, floor in nodes:
            norm = jnp.sum(node * node, axis=0, keepdims=True) * scale + floor
            rows = jnp.where(
                row_ids == 3,
                norm,
                jnp.where(row_ids == 4, scale, node * (-2.0 * scale)),
            )
            p1, p2, p3 = split3(rows)
            columns.append(jnp.concatenate([p1, p2, p3, p1, p2, p1, empty], axis=0))
        columns.append(jnp.concatenate([empty] * 6 + [values], axis=0))
        product_ref[slot] = jnp.dot(
            left_ref[target],
            jnp.concatenate(columns, axis=1).astype(jnp.bfloat16),
            preferred_element_type=jnp.float32,
        )

    def one_pair(k, slot, nodes):
        target, owner, source, order = read(k)
        reach = reach_of(order)
        point = [got_ref[owner, source, c : c + 1, at_point : at_point + width] for c in range(3)]
        extent = [
            got_ref[owner, source, c : c + 1, at_extent : at_extent + width] * reach
            for c in range(3)
        ]
        columns = [jnp.zeros((8, width), jnp.float32) for _ in range(3)]
        for start in range(0, width, GROUP):
            rows = slice(start, start + GROUP)
            sums = [row_acc[target, c, rows] for c in range(3)]

            def cubed(node):
                i = lax.rsqrt(product_ref[slot, rows, node * width : (node + 1) * width])
                return i * i * i

            coupling = product_ref[slot, rows, 3 * width : 4 * width]
            f_plus = cubed(1)
            if nodes == 1:
                even = (coupling + coupling) * f_plus
            else:
                f_minus = cubed(2)
                both = f_plus + f_minus
                even = coupling * (both + cubed(0) if nodes == 3 else both)
                odd = coupling * (f_plus - f_minus)
            for c in range(3):
                pulled = even * (centre_ref[target, c, rows] - point[c])
                if nodes > 1:
                    pulled = pulled - odd * extent[c]
                sums[c] = sums[c] + pulled
                for r in range(0, GROUP, 8):
                    columns[c] = columns[c] + pulled[r : r + 8]
            for c in range(3):
                row_acc[target, c, rows] = sums[c]
        sums = jnp.concatenate(
            [jnp.sum(columns[c], axis=0, keepdims=True) for c in range(3)], axis=0
        )
        grad_ref[owner * blocks + source, 0:3] += sums

    def two_pairs(nodes):
        def body(step, carry):
            for slot in range(2):
                multiply(2 * step + slot + 1, 1 - slot)
                one_pair(2 * step + slot, slot, nodes)
            return carry

        return body

    multiply(0, 0)
    lax.fori_loop(0, info_ref[1], two_pairs(3), 0)
    lax.fori_loop(info_ref[1], info_ref[2], two_pairs(2), 0)
    lax.fori_loop(info_ref[2], info_ref[3], two_pairs(1), 0)
    for b in range(blocks):
        total = jnp.concatenate(
            [jnp.sum(row_acc[b, c], axis=1, keepdims=True) for c in range(3)]
            + [jnp.zeros((width, 5), jnp.float32)],
            axis=1,
        )
        grad_ref[me * blocks + b] -= total.T

    high = blocks * width // LANES
    keys = 4 * high
    shift = (blocks * width).bit_length() + 1
    key_ids = lax.broadcasted_iota(jnp.int32, (keys, width), 0).astype(jnp.bfloat16)
    lane_ids = lax.broadcasted_iota(jnp.int32, (LANES, width), 0).astype(jnp.bfloat16)
    zero = jnp.zeros((keys, width), jnp.bfloat16)
    one = jnp.ones((keys, width), jnp.bfloat16)

    def wide(row):
        return jnp.broadcast_to(row, (keys, width))

    def narrow(value):
        return value.astype(jnp.float32).astype(jnp.bfloat16)

    def scatter(tile, carry):
        result = None
        for b in range(blocks):
            spread = []
            for c in range(3):
                grad = wide(grad_ref[tile * blocks + b, c : c + 1])
                upper = grad.astype(jnp.bfloat16)
                spread += [upper, (grad - upper.astype(jnp.float32)).astype(jnp.bfloat16)]
            parts = []
            hots = []
            for half in (at_point, at_extent):
                code = wide(got_ref[tile, b, 3:4, half : half + width]).astype(jnp.int32)
                for place in (code >> shift, code & ((1 << shift) - 1)):
                    mask = key_ids == narrow(place >> 7)
                    low = narrow(place & (LANES - 1))
                    parts.append(
                        jnp.concatenate([jnp.where(mask, s, zero) for s in spread], axis=0)
                    )
                    hots.append(
                        jnp.concatenate(
                            [
                                jnp.where(lane_ids[g : g + keys] == low, one, zero)
                                for g in range(0, LANES, keys)
                            ],
                            axis=0,
                        )
                    )
            product = lax.dot_general(
                jnp.concatenate(parts, axis=1),
                jnp.concatenate(hots, axis=1),
                (((1,), (1,)), ((), ())),
                preferred_element_type=jnp.float32,
            )
            result = product if result is None else result + product
        for c in range(3):
            joined_ref[tile, c] = (
                result[2 * c * keys : (2 * c + 1) * keys]
                + result[(2 * c + 1) * keys : (2 * c + 2) * keys]
            )
        return carry

    def collect(dest, carry):
        for c in range(3):
            total = jnp.zeros((high, LANES), jnp.float32)
            for slot, by in enumerate((0, tiles - 1, 1, tiles - tiles // 2)):
                tile = lax.rem(dest + by, tiles)
                total = total + joined_ref[tile, c, slot * high : (slot + 1) * high]
            part = out_ref.shape[2]
            for f in range(out_ref.shape[1]):
                first = f * part % high
                out_ref[dest, f, :, c * LANES : (c + 1) * LANES] = total[first : first + part]
        return carry

    lax.fori_loop(0, tiles, scatter, 0, unroll=min(tiles, 8))
    lax.fori_loop(0, tiles, collect, 0, unroll=min(tiles, 8))


def sum_kernel(got_ref, out_ref):
    out_ref[...] = jnp.sum(got_ref[...], axis=0)


def last_kernel(parity_ref, mine_ref, other_ref, out_ref):
    part = mine_ref.shape[0]
    even = parity_ref[0] == 0
    mine, other = mine_ref[...], other_ref[...]
    halves = (jnp.where(even, mine, other), jnp.where(even, other, mine))
    for i, half in enumerate(halves):
        for r in range(part):
            h = i * part + r
            for c in range(3):
                out_ref[c : c + 1, h * LANES : (h + 1) * LANES] = half[
                    r : r + 1, c * LANES : (c + 1) * LANES
                ]


def per_device(
    panel_geometry,
    adjoint,
    strengths,
    pair_target,
    pair_owner,
    pair_source,
    pair_order,
    pair_count,
    corner_vertex,
):
    tiles = lax.axis_size("tiles")
    far = lax.axis_size("far")
    blocks, _, width = panel_geometry.shape
    high = blocks * width // LANES
    me = lax.axis_index("tiles").astype(jnp.int32).reshape(1)
    smem = pl.BlockSpec(memory_space=SMEM)
    vmem = pl.BlockSpec(memory_space=VMEM)
    params = pltpu.CompilerParams(vmem_limit_bytes=LIMIT)
    geometry = panel_geometry.transpose(1, 0, 2)
    packed = pl.pallas_call(
        pack_kernel,
        out_shape=jax.ShapeDtypeStruct((tiles, blocks, 4, 3 * width), jnp.float32),
        in_specs=[smem] + [vmem] * 3,
        out_specs=vmem,
    )(me, geometry, strengths, corner_vertex)
    got = lax.all_to_all(packed, "tiles", split_axis=0, concat_axis=0, tiled=True)
    pairs = pair_target.shape[0]
    info, centre, left = pl.pallas_call(
        prep_kernel,
        out_shape=(
            jax.ShapeDtypeStruct((HEAD + pairs + SPARE,), jnp.int32),
            jax.ShapeDtypeStruct((blocks, 3, width, width), jnp.float32),
            jax.ShapeDtypeStruct((blocks, width, 56), jnp.bfloat16),
        ),
        in_specs=[smem] * 6 + [vmem] * 2,
        out_specs=(smem, vmem, vmem),
        compiler_params=params,
        cost_estimate=pl.CostEstimate(flops=4000000, bytes_accessed=900000, transcendentals=0),
    )(
        me,
        pair_target,
        pair_owner[:, 0],
        pair_source,
        pair_order,
        pair_count,
        geometry,
        adjoint,
    )
    partial = pl.pallas_call(
        pair_kernel,
        out_shape=jax.ShapeDtypeStruct((tiles, far, high // 2, 3 * LANES), jnp.float32),
        in_specs=[smem] + [vmem] * 3,
        out_specs=vmem,
        scratch_shapes=[
            VMEM((2, width, 4 * width), jnp.float32),
            VMEM((blocks, 3, width, width), jnp.float32),
            VMEM((tiles * blocks, 8, width), jnp.float32),
            VMEM((tiles, 3, 4 * high, LANES), jnp.float32),
        ],
        compiler_params=params,
    )(info, centre, left, got)
    partial = partial.reshape(tiles * far, high // 2, 3 * LANES)
    shares = lax.all_to_all(partial, ("tiles", "far"), split_axis=0, concat_axis=0, tiled=True)
    mine = pl.pallas_call(
        sum_kernel,
        out_shape=jax.ShapeDtypeStruct((high // 2, 3 * LANES), jnp.float32),
        compiler_params=params,
    )(shares)
    other = lax.ppermute(mine, "far", [(f ^ 1, f) for f in range(far)])
    parity = (lax.axis_index("far") & 1).astype(jnp.int32).reshape(1)
    return pl.pallas_call(
        last_kernel,
        out_shape=jax.ShapeDtypeStruct((3, blocks * width), jnp.float32),
        in_specs=[smem, vmem, vmem],
        out_specs=vmem,
        compiler_params=params,
    )(parity, mine, other)


def solution(mesh):
    placed = (
        P("tiles", None, None),
        P("tiles", "far", None),
        P("tiles", "far", None),
        P("tiles"),
        P("tiles", None),
        P("tiles"),
        P("tiles"),
        P("tiles"),
        P("tiles", None, None),
    )
    return jax.shard_map(
        per_device, mesh=mesh, in_specs=placed, out_specs=P(None, "tiles"), check_vma=False
    )
```

```python
import jax
import jax.numpy as jnp
from jax import lax
from jax.experimental import pallas as pl
from jax.experimental.pallas import tpu as pltpu
from jax.sharding import PartitionSpec as P

SMEM = pltpu.SMEM
VMEM = pltpu.VMEM
LANES = 128
HEAD = 5
SPARE = 2
GROUP = 32
LIMIT = 48 * 1024 * 1024


def pack_kernel(me_ref, parity_ref, geom_ref, strength_ref, corner_ref, out_ref):
    tiles, blocks, _, _ = out_ref.shape
    width = strength_ref.shape[2]
    shift = (blocks * width).bit_length() - 1
    me = me_ref[0]
    even = parity_ref[0] == 0
    shapes = []
    for b in range(blocks):
        vertex = corner_ref[b]
        offset = (vertex >> shift) - me
        offset = jnp.where(offset < 0, offset + tiles, offset)
        slot = jnp.where(
            offset == 0,
            0,
            jnp.where(offset == 1, 1, jnp.where(offset == tiles - 1, 2, 3)),
        )
        place = ((slot << shift) + (vertex & ((1 << shift) - 1))).astype(jnp.float32)
        span = float(4 << shift)
        for half in range(2):
            code = place[2 * half : 2 * half + 1] * span + place[2 * half + 1 : 2 * half + 2]
            rows = [geom_ref[3 * half + c, b : b + 1] for c in range(3)] + [code]
            shapes.append(jnp.concatenate(rows, axis=0))
    for b in range(blocks):
        shape = jnp.where(even, shapes[b], shapes[blocks + b])
        block = jnp.concatenate([strength_ref[b].astype(jnp.float32), shape], axis=1)
        for t in range(tiles):
            out_ref[t, b] = block


def split3(value):
    first = value.astype(jnp.bfloat16).astype(jnp.float32)
    rest = value - first
    second = rest.astype(jnp.bfloat16).astype(jnp.float32)
    return first, second, rest - second


def sort_kernel(
    me_ref,
    parity_ref,
    target_ref,
    owner_ref,
    source_ref,
    order_ref,
    count_ref,
    info_ref,
):
    live = count_ref[0]
    total = target_ref.shape[0]
    for k in range(HEAD + total, HEAD + total + SPARE):
        info_ref[k] = 0

    def note(order, state):
        def one(k, state):
            at, turn = state
            mine = order_ref[k] == order
            word = (owner_ref[k] << 18) | (order << 16) | (source_ref[k] << 8) | target_ref[k]
            info_ref[at] = word
            return at + jnp.where(mine, turn, 0), jnp.where(mine, 1 - turn, turn)

        return lax.fori_loop(0, live, one, state)

    third = note(3, (HEAD, 1 - parity_ref[0]))
    second = note(2, third)
    first, _ = note(1, second)
    for k in range(SPARE):
        info_ref[first + k] = 0
    info_ref[0] = me_ref[0]
    info_ref[1] = (third[0] - HEAD + 1) // 2
    info_ref[2] = (second[0] - HEAD + 1) // 2
    info_ref[3] = (first - HEAD + 1) // 2
    info_ref[4] = parity_ref[0]


def prep_kernel(geom_ref, adjoint_ref, partner_ref, centre_ref, left_ref):
    blocks, _, width = adjoint_ref.shape
    for b in range(blocks):
        point = jnp.concatenate([geom_ref[c, b : b + 1] for c in range(3)], axis=0)
        rows = [point, jnp.ones((1, width), jnp.float32)]
        rows += [jnp.sum(point * point, axis=0, keepdims=True)]
        rows += [jnp.zeros((3, width), jnp.float32)]
        x1, x2, x3 = split3(jnp.concatenate(rows, axis=0))
        values = [adjoint_ref[b].astype(jnp.float32), partner_ref[b].astype(jnp.float32)]
        rows = [x1, x1, x1, x2, x2, x3] + values
        left_ref[b] = jnp.concatenate(rows, axis=0).T.astype(jnp.bfloat16)
        for c in range(3):
            centre_ref[b, c] = jnp.broadcast_to(point[c : c + 1], (width, width)).T


def pair_kernel(
    info_ref,
    centre_ref,
    left_ref,
    mine_ref,
    other_ref,
    out_ref,
    product_ref,
    row_acc,
    grad_ref,
    joined_ref,
    shape_ref,
):
    tiles, blocks, _, _ = mine_ref.shape
    width = centre_ref.shape[3]
    me = info_ref[0]
    even = info_ref[4] == 0

    def settle(tile, carry):
        for b in range(blocks):
            mine = mine_ref[tile, b, :, width : 2 * width]
            other = other_ref[tile, b, :, width : 2 * width]
            shape_ref[tile, b] = jnp.where(even, mine, other)
            shape_ref[tile, blocks + b] = jnp.where(even, other, mine)
        return carry

    lax.fori_loop(0, tiles, settle, 0, unroll=min(tiles, 8))
    grad_ref[...] = jnp.zeros(grad_ref.shape, jnp.float32)
    row_acc[...] = jnp.zeros(row_acc.shape, jnp.float32)
    blank = jnp.zeros((4, width), jnp.float32)
    row_ids = lax.broadcasted_iota(jnp.int32, (8, width), 0)

    def reach_of(order):
        return 0.25 * jnp.where(
            order == 3, 0.7745966692414834, jnp.where(order == 2, 0.5773502691896258, 0.0)
        )

    def read(k):
        word = info_ref[HEAD + k]
        return word & 255, word >> 18, (word >> 8) & 255, (word >> 16) & 3

    def multiply(k, slot):
        target, owner, source, order = read(k)
        third = order == 3
        alive = jnp.where(order > 0, 1.0, 0.0).astype(jnp.float32)
        reach = reach_of(order)
        scale_mid = jnp.where(third, (4.0 / 9.0 / 512.0) ** (-2.0 / 3.0), 0.0)
        scale_side = jnp.where(
            third, (5.0 / 18.0 / 512.0) ** (-2.0 / 3.0), (0.5 / 512.0) ** (-2.0 / 3.0)
        )
        floor_mid = jnp.where(third, 0.0625 * (4.0 / 9.0 / 512.0) ** (-2.0 / 3.0), 3.0e38)
        floor_side = 0.0625 * scale_side
        point = shape_ref[owner, 2 * source]
        extent = shape_ref[owner, 2 * source + 1] * reach
        inside = row_ids < 3
        point = jnp.where(inside, jnp.concatenate([point, blank], axis=0), 0.0)
        extent = jnp.where(inside, jnp.concatenate([extent, blank], axis=0), 0.0)
        values = [ref[owner, source, :, 0:width] * alive for ref in (mine_ref, other_ref)]
        empty = jnp.zeros((8, width), jnp.float32)
        nodes = (
            (point, scale_mid, floor_mid),
            (point + extent, scale_side, floor_side),
            (point - extent, scale_side, floor_side),
        )
        columns = []
        for node, scale, floor in nodes:
            norm = jnp.sum(node * node, axis=0, keepdims=True) * scale + floor
            rows = jnp.where(
                row_ids == 3,
                norm,
                jnp.where(row_ids == 4, scale, node * (-2.0 * scale)),
            )
            p1, p2, p3 = split3(rows)
            columns.append(jnp.concatenate([p1, p2, p3, p1, p2, p1, empty], axis=0))
        columns.append(jnp.concatenate([empty] * 6 + values, axis=0))
        product_ref[slot] = jnp.dot(
            left_ref[target],
            jnp.concatenate(columns, axis=1).astype(jnp.bfloat16),
            preferred_element_type=jnp.float32,
        )

    def one_pair(k, slot, nodes):
        target, owner, source, order = read(k)
        reach = reach_of(order)
        point = [shape_ref[owner, 2 * source, c : c + 1] for c in range(3)]
        extent = [shape_ref[owner, 2 * source + 1, c : c + 1] * reach for c in range(3)]
        columns = [jnp.zeros((8, width), jnp.float32) for _ in range(3)]
        for start in range(0, width, GROUP):
            rows = slice(start, start + GROUP)
            sums = [row_acc[target, c, rows] for c in range(3)]

            def cubed(node):
                i = lax.rsqrt(product_ref[slot, rows, node * width : (node + 1) * width])
                return i * i * i

            coupling = product_ref[slot, rows, 3 * width : 4 * width]
            f_plus = cubed(1)
            if nodes == 1:
                even = (coupling + coupling) * f_plus
            else:
                f_minus = cubed(2)
                both = f_plus + f_minus
                even = coupling * (both + cubed(0) if nodes == 3 else both)
                odd = coupling * (f_plus - f_minus)
            for c in range(3):
                pulled = even * (centre_ref[target, c, rows] - point[c])
                if nodes > 1:
                    pulled = pulled - odd * extent[c]
                sums[c] = sums[c] + pulled
                for r in range(0, GROUP, 8):
                    columns[c] = columns[c] + pulled[r : r + 8]
            for c in range(3):
                row_acc[target, c, rows] = sums[c]
        sums = jnp.concatenate(
            [jnp.sum(columns[c], axis=0, keepdims=True) for c in range(3)], axis=0
        )
        grad_ref[owner * blocks + source, 0:3] += sums

    def two_pairs(nodes):
        def body(step, carry):
            for slot in range(2):
                multiply(2 * step + slot + 1, 1 - slot)
                one_pair(2 * step + slot, slot, nodes)
            return carry

        return body

    multiply(0, 0)
    lax.fori_loop(0, info_ref[1], two_pairs(3), 0)
    lax.fori_loop(info_ref[1], info_ref[2], two_pairs(2), 0)
    lax.fori_loop(info_ref[2], info_ref[3], two_pairs(1), 0)
    for b in range(blocks):
        total = jnp.concatenate(
            [jnp.sum(row_acc[b, c], axis=1, keepdims=True) for c in range(3)]
            + [jnp.zeros((width, 5), jnp.float32)],
            axis=1,
        )
        grad_ref[me * blocks + b] -= total.T

    high = blocks * width // LANES
    keys = 4 * high
    shift = (blocks * width).bit_length() + 1
    key_ids = lax.broadcasted_iota(jnp.int32, (keys, width), 0).astype(jnp.bfloat16)
    lane_ids = lax.broadcasted_iota(jnp.int32, (LANES, width), 0).astype(jnp.bfloat16)
    zero = jnp.zeros((keys, width), jnp.bfloat16)
    one = jnp.ones((keys, width), jnp.bfloat16)

    def wide(row):
        return jnp.broadcast_to(row, (keys, width))

    def narrow(value):
        return value.astype(jnp.float32).astype(jnp.bfloat16)

    def scatter(tile, carry):
        result = None
        for b in range(blocks):
            spread = []
            for c in range(3):
                grad = wide(grad_ref[tile * blocks + b, c : c + 1])
                upper = grad.astype(jnp.bfloat16)
                spread += [upper, (grad - upper.astype(jnp.float32)).astype(jnp.bfloat16)]
            parts = []
            hots = []
            for half in range(2):
                code = wide(shape_ref[tile, 2 * b + half, 3:4]).astype(jnp.int32)
                for place in (code >> shift, code & ((1 << shift) - 1)):
                    mask = key_ids == narrow(place >> 7)
                    low = narrow(place & (LANES - 1))
                    parts.append(
                        jnp.concatenate([jnp.where(mask, s, zero) for s in spread], axis=0)
                    )
                    hots.append(
                        jnp.concatenate(
                            [
                                jnp.where(lane_ids[g : g + keys] == low, one, zero)
                                for g in range(0, LANES, keys)
                            ],
                            axis=0,
                        )
                    )
            product = lax.dot_general(
                jnp.concatenate(parts, axis=1),
                jnp.concatenate(hots, axis=1),
                (((1,), (1,)), ((), ())),
                preferred_element_type=jnp.float32,
            )
            result = product if result is None else result + product
        for c in range(3):
            joined_ref[tile, c] = (
                result[2 * c * keys : (2 * c + 1) * keys]
                + result[(2 * c + 1) * keys : (2 * c + 2) * keys]
            )
        return carry

    def collect(dest, carry):
        for c in range(3):
            total = jnp.zeros((high, LANES), jnp.float32)
            for slot, by in enumerate((0, tiles - 1, 1, tiles - tiles // 2)):
                tile = lax.rem(dest + by, tiles)
                total = total + joined_ref[tile, c, slot * high : (slot + 1) * high]
            part = out_ref.shape[2]
            for f in range(out_ref.shape[1]):
                first = f * part % high
                out_ref[dest, f, :, c * LANES : (c + 1) * LANES] = total[first : first + part]
        return carry

    lax.fori_loop(0, tiles, scatter, 0, unroll=min(tiles, 8))
    lax.fori_loop(0, tiles, collect, 0, unroll=min(tiles, 8))


def sum_kernel(got_ref, out_ref):
    out_ref[...] = jnp.sum(got_ref[...], axis=0)


def last_kernel(parity_ref, mine_ref, other_ref, out_ref):
    part = mine_ref.shape[0]
    even = parity_ref[0] == 0
    mine, other = mine_ref[...], other_ref[...]
    halves = (jnp.where(even, mine, other), jnp.where(even, other, mine))
    for i, half in enumerate(halves):
        for r in range(part):
            h = i * part + r
            for c in range(3):
                out_ref[c : c + 1, h * LANES : (h + 1) * LANES] = half[
                    r : r + 1, c * LANES : (c + 1) * LANES
                ]


def per_device(
    panel_geometry,
    adjoint,
    strengths,
    pair_target,
    pair_owner,
    pair_source,
    pair_order,
    pair_count,
    corner_vertex,
):
    tiles = lax.axis_size("tiles")
    far = lax.axis_size("far")
    blocks, _, width = panel_geometry.shape
    high = blocks * width // LANES
    parity = lax.axis_index("far").astype(jnp.int32) & 1
    me = lax.axis_index("tiles").astype(jnp.int32).reshape(1)
    parity = parity.reshape(1)
    swap = [(f ^ 1, f) for f in range(far)]
    smem = pl.BlockSpec(memory_space=SMEM)
    vmem = pl.BlockSpec(memory_space=VMEM)
    params = pltpu.CompilerParams(vmem_limit_bytes=LIMIT)
    geometry = panel_geometry.transpose(1, 0, 2)
    packed = pl.pallas_call(
        pack_kernel,
        out_shape=jax.ShapeDtypeStruct((tiles, blocks, 4, 2 * width), jnp.float32),
        in_specs=[smem] * 2 + [vmem] * 3,
        out_specs=vmem,
    )(me, parity, geometry, strengths, corner_vertex)
    got = lax.all_to_all(packed, "tiles", split_axis=0, concat_axis=0, tiled=True)
    partner = lax.ppermute(adjoint, "far", swap)
    pairs = pair_target.shape[0]
    info = pl.pallas_call(
        sort_kernel,
        out_shape=jax.ShapeDtypeStruct((HEAD + pairs + SPARE,), jnp.int32),
        in_specs=[smem] * 7,
        out_specs=smem,
        cost_estimate=pl.CostEstimate(flops=4000000, bytes_accessed=900000, transcendentals=0),
    )(
        me,
        parity,
        pair_target,
        pair_owner[:, 0],
        pair_source,
        pair_order,
        pair_count,
    )
    centre, left = pl.pallas_call(
        prep_kernel,
        out_shape=(
            jax.ShapeDtypeStruct((blocks, 3, width, width), jnp.float32),
            jax.ShapeDtypeStruct((blocks, width, 56), jnp.bfloat16),
        ),
        compiler_params=params,
        cost_estimate=pl.CostEstimate(flops=4000000, bytes_accessed=900000, transcendentals=0),
    )(geometry, adjoint, partner)
    got, info, left = lax.optimization_barrier((got, info, left))
    other = lax.ppermute(got, "far", swap)
    partial = pl.pallas_call(
        pair_kernel,
        out_shape=jax.ShapeDtypeStruct((tiles, far, high // 2, 3 * LANES), jnp.float32),
        in_specs=[smem] + [vmem] * 4,
        out_specs=vmem,
        scratch_shapes=[
            VMEM((2, width, 4 * width), jnp.float32),
            VMEM((blocks, 3, width, width), jnp.float32),
            VMEM((tiles * blocks, 8, width), jnp.float32),
            VMEM((tiles, 3, 4 * high, LANES), jnp.float32),
            VMEM((tiles, 2 * blocks, 4, width), jnp.float32),
        ],
        compiler_params=params,
    )(info, centre, left, got, other)
    partial = partial.reshape(tiles * far, high // 2, 3 * LANES)
    shares = lax.all_to_all(partial, ("tiles", "far"), split_axis=0, concat_axis=0, tiled=True)
    mine = pl.pallas_call(
        sum_kernel,
        out_shape=jax.ShapeDtypeStruct((high // 2, 3 * LANES), jnp.float32),
        compiler_params=params,
    )(shares)
    other = lax.ppermute(mine, "far", swap)
    return pl.pallas_call(
        last_kernel,
        out_shape=jax.ShapeDtypeStruct((3, blocks * width), jnp.float32),
        in_specs=[smem, vmem, vmem],
        out_specs=vmem,
        compiler_params=params,
    )(parity, mine, other)


def solution(mesh):
    placed = (
        P("tiles", None, None),
        P("tiles", "far", None),
        P("tiles", "far", None),
        P("tiles"),
        P("tiles", None),
        P("tiles"),
        P("tiles"),
        P("tiles"),
        P("tiles", None, None),
    )
    return jax.shard_map(
        per_device, mesh=mesh, in_specs=placed, out_specs=P(None, "tiles"), check_vma=False
    )
```

```python
import jax
import jax.numpy as jnp
from jax import lax
from jax.experimental import pallas as pl
from jax.experimental.pallas import tpu as pltpu
from jax.sharding import PartitionSpec as P

SMEM = pltpu.SMEM
VMEM = pltpu.VMEM
LANES = 128
HEAD = 5
SPARE = 2
GROUP = 32
LIMIT = 48 * 1024 * 1024


def pack_kernel(me_ref, parity_ref, geom_ref, strength_ref, corner_ref, out_ref):
    tiles, blocks, _, _ = out_ref.shape
    width = strength_ref.shape[2]
    shift = (blocks * width).bit_length() - 1
    me = me_ref[0]
    even = parity_ref[0] == 0
    shapes = []
    for b in range(blocks):
        vertex = corner_ref[b]
        offset = (vertex >> shift) - me
        offset = jnp.where(offset < 0, offset + tiles, offset)
        slot = jnp.where(
            offset == 0,
            0,
            jnp.where(offset == 1, 1, jnp.where(offset == tiles - 1, 2, 3)),
        )
        place = ((slot << shift) + (vertex & ((1 << shift) - 1))).astype(jnp.float32)
        span = float(4 << shift)
        for half in range(2):
            code = place[2 * half : 2 * half + 1] * span + place[2 * half + 1 : 2 * half + 2]
            rows = [geom_ref[3 * half + c, b : b + 1] for c in range(3)] + [code]
            shapes.append(jnp.concatenate(rows, axis=0))
    for b in range(blocks):
        shape = jnp.where(even, shapes[b], shapes[blocks + b])
        block = jnp.concatenate([strength_ref[b].astype(jnp.float32), shape], axis=1)
        for t in range(tiles):
            out_ref[t, b] = block


def split3(value):
    first = value.astype(jnp.bfloat16).astype(jnp.float32)
    rest = value - first
    second = rest.astype(jnp.bfloat16).astype(jnp.float32)
    return first, second, rest - second


def sort_kernel(
    me_ref,
    parity_ref,
    target_ref,
    owner_ref,
    source_ref,
    order_ref,
    count_ref,
    blocks,
    info_ref,
):
    pairs = order_ref.shape[1]
    lanes = info_ref.shape[1]
    bits = (blocks - 1).bit_length()
    parity = parity_ref[0]
    order = order_ref[...]
    place = lax.broadcasted_iota(jnp.int32, (1, pairs), 1)
    live = place < count_ref[0]
    word = (owner_ref[...] << bits | source_ref[...]) << bits | target_ref[...]
    word = (word << 2 | order).astype(jnp.float32)
    key = jnp.where(live, (3 - order) * pairs + place, 3 * pairs + place).astype(jnp.float32)
    across = lax.broadcasted_iota(jnp.int32, (pairs, pairs), 1)
    down = lax.broadcasted_iota(jnp.int32, (pairs, pairs), 0)

    def upright(row):
        spread = jnp.broadcast_to(row, (pairs, pairs))
        return jnp.sum(jnp.where(across == down, spread, 0.0), axis=1, keepdims=True)

    key_down = upright(key)
    rank = jnp.sum(jnp.where(key < key_down, 1.0, 0.0), axis=1, keepdims=True).astype(jnp.int32)
    kept = (rank & 1 == parity) & (rank < count_ref[0])
    at = jnp.where(kept, HEAD + (rank >> 1), -1)
    wide_lane = lax.broadcasted_iota(jnp.int32, (pairs, lanes), 1)
    words = jnp.sum(jnp.where(wide_lane == at, upright(word), 0.0), axis=0, keepdims=True)
    info = words.astype(jnp.int32)
    lane = lax.broadcasted_iota(jnp.int32, (1, lanes), 1)
    info = jnp.where(lane == 0, me_ref[0], jnp.where(lane == 4, parity, info))
    for i in range(3):
        upto = jnp.where(live & (order >= 3 - i), 1.0, 0.0)
        total = jnp.sum(upto, axis=1, keepdims=True).astype(jnp.int32)
        info = jnp.where(lane == i + 1, (((total + 1 - parity) >> 1) + 1) >> 1, info)
    info_ref[...] = info


def prep_kernel(geom_ref, adjoint_ref, partner_ref, centre_ref, left_ref):
    blocks, _, width = adjoint_ref.shape
    for b in range(blocks):
        point = jnp.concatenate([geom_ref[c, b : b + 1] for c in range(3)], axis=0)
        rows = [point, jnp.ones((1, width), jnp.float32)]
        rows += [jnp.sum(point * point, axis=0, keepdims=True)]
        rows += [jnp.zeros((3, width), jnp.float32)]
        x1, x2, x3 = split3(jnp.concatenate(rows, axis=0))
        values = [adjoint_ref[b].astype(jnp.float32), partner_ref[b].astype(jnp.float32)]
        rows = [x1, x1, x1, x2, x2, x3] + values
        left_ref[b] = jnp.concatenate(rows, axis=0).T.astype(jnp.bfloat16)
        for c in range(3):
            centre_ref[b, c] = jnp.broadcast_to(point[c : c + 1], (width, width)).T


def pair_kernel(
    info_ref,
    centre_ref,
    left_ref,
    mine_ref,
    other_ref,
    out_ref,
    product_ref,
    row_acc,
    grad_ref,
    joined_ref,
    shape_ref,
):
    tiles, blocks, _, _ = mine_ref.shape
    width = centre_ref.shape[3]
    bits = (blocks - 1).bit_length()
    me = info_ref[0, 0]
    even = info_ref[0, 4] == 0

    def settle(tile, carry):
        for b in range(blocks):
            mine = mine_ref[tile, b, :, width : 2 * width]
            other = other_ref[tile, b, :, width : 2 * width]
            shape_ref[tile, b] = jnp.where(even, mine, other)
            shape_ref[tile, blocks + b] = jnp.where(even, other, mine)
        return carry

    lax.fori_loop(0, tiles, settle, 0, unroll=min(tiles, 8))
    grad_ref[...] = jnp.zeros(grad_ref.shape, jnp.float32)
    row_acc[...] = jnp.zeros(row_acc.shape, jnp.float32)
    blank = jnp.zeros((4, width), jnp.float32)
    row_ids = lax.broadcasted_iota(jnp.int32, (8, width), 0)

    def reach_of(order):
        return 0.25 * jnp.where(
            order == 3, 0.7745966692414834, jnp.where(order == 2, 0.5773502691896258, 0.0)
        )

    def read(k):
        word = info_ref[0, HEAD + k]
        inner = word >> 2
        outer = inner >> bits
        return inner & (blocks - 1), outer >> bits, outer & (blocks - 1), word & 3

    def multiply(k, slot):
        target, owner, source, order = read(k)
        third = order == 3
        alive = jnp.where(order > 0, 1.0, 0.0).astype(jnp.float32)
        reach = reach_of(order)
        scale_mid = jnp.where(third, (4.0 / 9.0 / 512.0) ** (-2.0 / 3.0), 0.0)
        scale_side = jnp.where(
            third, (5.0 / 18.0 / 512.0) ** (-2.0 / 3.0), (0.5 / 512.0) ** (-2.0 / 3.0)
        )
        floor_mid = jnp.where(third, 0.0625 * (4.0 / 9.0 / 512.0) ** (-2.0 / 3.0), 3.0e38)
        floor_side = 0.0625 * scale_side
        point = shape_ref[owner, 2 * source]
        extent = shape_ref[owner, 2 * source + 1] * reach
        inside = row_ids < 3
        point = jnp.where(inside, jnp.concatenate([point, blank], axis=0), 0.0)
        extent = jnp.where(inside, jnp.concatenate([extent, blank], axis=0), 0.0)
        values = [ref[owner, source, :, 0:width] * alive for ref in (mine_ref, other_ref)]
        empty = jnp.zeros((8, width), jnp.float32)
        nodes = (
            (point, scale_mid, floor_mid),
            (point + extent, scale_side, floor_side),
            (point - extent, scale_side, floor_side),
        )
        columns = []
        for node, scale, floor in nodes:
            norm = jnp.sum(node * node, axis=0, keepdims=True) * scale + floor
            rows = jnp.where(
                row_ids == 3,
                norm,
                jnp.where(row_ids == 4, scale, node * (-2.0 * scale)),
            )
            p1, p2, p3 = split3(rows)
            columns.append(jnp.concatenate([p1, p2, p3, p1, p2, p1, empty], axis=0))
        columns.append(jnp.concatenate([empty] * 6 + values, axis=0))
        product_ref[slot] = jnp.dot(
            left_ref[target],
            jnp.concatenate(columns, axis=1).astype(jnp.bfloat16),
            preferred_element_type=jnp.float32,
        )

    def one_pair(k, slot, nodes):
        target, owner, source, order = read(k)
        reach = reach_of(order)
        point = [shape_ref[owner, 2 * source, c : c + 1] for c in range(3)]
        extent = [shape_ref[owner, 2 * source + 1, c : c + 1] * reach for c in range(3)]
        columns = [jnp.zeros((8, width), jnp.float32) for _ in range(3)]
        for start in range(0, width, GROUP):
            rows = slice(start, start + GROUP)
            sums = [row_acc[target, c, rows] for c in range(3)]

            def cubed(node):
                i = lax.rsqrt(product_ref[slot, rows, node * width : (node + 1) * width])
                return i * i * i

            coupling = product_ref[slot, rows, 3 * width : 4 * width]
            f_plus = cubed(1)
            if nodes == 1:
                even = (coupling + coupling) * f_plus
            else:
                f_minus = cubed(2)
                both = f_plus + f_minus
                even = coupling * (both + cubed(0) if nodes == 3 else both)
                odd = coupling * (f_plus - f_minus)
            for c in range(3):
                pulled = even * (centre_ref[target, c, rows] - point[c])
                if nodes > 1:
                    pulled = pulled - odd * extent[c]
                sums[c] = sums[c] + pulled
                for r in range(0, GROUP, 8):
                    columns[c] = columns[c] + pulled[r : r + 8]
            for c in range(3):
                row_acc[target, c, rows] = sums[c]
        sums = jnp.concatenate(
            [jnp.sum(columns[c], axis=0, keepdims=True) for c in range(3)], axis=0
        )
        grad_ref[owner * blocks + source, 0:3] += sums

    def two_pairs(nodes):
        def body(step, carry):
            for slot in range(2):
                multiply(2 * step + slot + 1, 1 - slot)
                one_pair(2 * step + slot, slot, nodes)
            return carry

        return body

    multiply(0, 0)
    lax.fori_loop(0, info_ref[0, 1], two_pairs(3), 0)
    lax.fori_loop(info_ref[0, 1], info_ref[0, 2], two_pairs(2), 0)
    lax.fori_loop(info_ref[0, 2], info_ref[0, 3], two_pairs(1), 0)
    for b in range(blocks):
        total = jnp.concatenate(
            [jnp.sum(row_acc[b, c], axis=1, keepdims=True) for c in range(3)]
            + [jnp.zeros((width, 5), jnp.float32)],
            axis=1,
        )
        grad_ref[me * blocks + b] -= total.T

    high = blocks * width // LANES
    keys = 4 * high
    shift = (blocks * width).bit_length() + 1
    key_ids = lax.broadcasted_iota(jnp.int32, (keys, width), 0).astype(jnp.bfloat16)
    lane_ids = lax.broadcasted_iota(jnp.int32, (LANES, width), 0).astype(jnp.bfloat16)
    zero = jnp.zeros((keys, width), jnp.bfloat16)
    one = jnp.ones((keys, width), jnp.bfloat16)

    def wide(row):
        return jnp.broadcast_to(row, (keys, width))

    def narrow(value):
        return value.astype(jnp.float32).astype(jnp.bfloat16)

    def scatter(tile, carry):
        result = None
        for b in range(blocks):
            spread = []
            for c in range(3):
                grad = wide(grad_ref[tile * blocks + b, c : c + 1])
                upper = grad.astype(jnp.bfloat16)
                spread += [upper, (grad - upper.astype(jnp.float32)).astype(jnp.bfloat16)]
            parts = []
            hots = []
            for half in range(2):
                code = wide(shape_ref[tile, 2 * b + half, 3:4]).astype(jnp.int32)
                for place in (code >> shift, code & ((1 << shift) - 1)):
                    mask = key_ids == narrow(place >> 7)
                    low = narrow(place & (LANES - 1))
                    parts.append(
                        jnp.concatenate([jnp.where(mask, s, zero) for s in spread], axis=0)
                    )
                    hots.append(
                        jnp.concatenate(
                            [
                                jnp.where(lane_ids[g : g + keys] == low, one, zero)
                                for g in range(0, LANES, keys)
                            ],
                            axis=0,
                        )
                    )
            product = lax.dot_general(
                jnp.concatenate(parts, axis=1),
                jnp.concatenate(hots, axis=1),
                (((1,), (1,)), ((), ())),
                preferred_element_type=jnp.float32,
            )
            result = product if result is None else result + product
        for c in range(3):
            joined_ref[tile, c] = (
                result[2 * c * keys : (2 * c + 1) * keys]
                + result[(2 * c + 1) * keys : (2 * c + 2) * keys]
            )
        return carry

    def collect(dest, carry):
        for c in range(3):
            total = jnp.zeros((high, LANES), jnp.float32)
            for slot, by in enumerate((0, tiles - 1, 1, tiles - tiles // 2)):
                tile = lax.rem(dest + by, tiles)
                total = total + joined_ref[tile, c, slot * high : (slot + 1) * high]
            part = out_ref.shape[2]
            for f in range(out_ref.shape[1]):
                first = f * part % high
                out_ref[dest, f, :, c * LANES : (c + 1) * LANES] = total[first : first + part]
        return carry

    lax.fori_loop(0, tiles, scatter, 0, unroll=min(tiles, 8))
    lax.fori_loop(0, tiles, collect, 0, unroll=min(tiles, 8))


def sum_kernel(got_ref, out_ref):
    out_ref[...] = jnp.sum(got_ref[...], axis=0)


def last_kernel(parity_ref, mine_ref, other_ref, out_ref):
    part = mine_ref.shape[0]
    even = parity_ref[0] == 0
    mine, other = mine_ref[...], other_ref[...]
    halves = (jnp.where(even, mine, other), jnp.where(even, other, mine))
    for i, half in enumerate(halves):
        for r in range(part):
            h = i * part + r
            for c in range(3):
                out_ref[c : c + 1, h * LANES : (h + 1) * LANES] = half[
                    r : r + 1, c * LANES : (c + 1) * LANES
                ]


def per_device(
    panel_geometry,
    adjoint,
    strengths,
    pair_target,
    pair_owner,
    pair_source,
    pair_order,
    pair_count,
    corner_vertex,
):
    tiles = lax.axis_size("tiles")
    far = lax.axis_size("far")
    blocks, _, width = panel_geometry.shape
    high = blocks * width // LANES
    parity = lax.axis_index("far").astype(jnp.int32) & 1
    me = lax.axis_index("tiles").astype(jnp.int32).reshape(1)
    parity = parity.reshape(1)
    swap = [(f ^ 1, f) for f in range(far)]
    smem = pl.BlockSpec(memory_space=SMEM)
    vmem = pl.BlockSpec(memory_space=VMEM)
    params = pltpu.CompilerParams(vmem_limit_bytes=LIMIT)
    geometry = panel_geometry.transpose(1, 0, 2)
    packed = pl.pallas_call(
        pack_kernel,
        out_shape=jax.ShapeDtypeStruct((tiles, blocks, 4, 2 * width), jnp.float32),
        in_specs=[smem] * 2 + [vmem] * 3,
        out_specs=vmem,
    )(me, parity, geometry, strengths, corner_vertex)
    got = lax.all_to_all(packed, "tiles", split_axis=0, concat_axis=0, tiled=True)
    partner = lax.ppermute(adjoint, "far", swap)
    pairs = pair_target.shape[0]
    info = pl.pallas_call(
        lambda *refs: sort_kernel(*refs[:-1], blocks, refs[-1]),
        out_shape=jax.ShapeDtypeStruct((1, -(-(HEAD + pairs // 2 + SPARE + 1) // LANES) * LANES), jnp.int32),
        in_specs=[smem] * 2 + [vmem] * 4 + [smem],
        out_specs=vmem,
        cost_estimate=pl.CostEstimate(flops=4000000, bytes_accessed=900000, transcendentals=0),
    )(
        me,
        parity,
        pair_target.reshape(1, pairs),
        pair_owner.reshape(1, pairs),
        pair_source.reshape(1, pairs),
        pair_order.reshape(1, pairs),
        pair_count,
    )
    centre, left = pl.pallas_call(
        prep_kernel,
        out_shape=(
            jax.ShapeDtypeStruct((blocks, 3, width, width), jnp.float32),
            jax.ShapeDtypeStruct((blocks, width, 56), jnp.bfloat16),
        ),
        compiler_params=params,
        cost_estimate=pl.CostEstimate(flops=4000000, bytes_accessed=900000, transcendentals=0),
    )(geometry, adjoint, partner)
    got, info, left = lax.optimization_barrier((got, info, left))
    other = lax.ppermute(got, "far", swap)
    partial = pl.pallas_call(
        pair_kernel,
        out_shape=jax.ShapeDtypeStruct((tiles, far, high // 2, 3 * LANES), jnp.float32),
        in_specs=[smem] + [vmem] * 4,
        out_specs=vmem,
        scratch_shapes=[
            VMEM((2, width, 4 * width), jnp.float32),
            VMEM((blocks, 3, width, width), jnp.float32),
            VMEM((tiles * blocks, 8, width), jnp.float32),
            VMEM((tiles, 3, 4 * high, LANES), jnp.float32),
            VMEM((tiles, 2 * blocks, 4, width), jnp.float32),
        ],
        compiler_params=params,
    )(info, centre, left, got, other)
    partial = partial.reshape(tiles * far, high // 2, 3 * LANES)
    shares = lax.all_to_all(partial, ("tiles", "far"), split_axis=0, concat_axis=0, tiled=True)
    mine = pl.pallas_call(
        sum_kernel,
        out_shape=jax.ShapeDtypeStruct((high // 2, 3 * LANES), jnp.float32),
        compiler_params=params,
    )(shares)
    other = lax.ppermute(mine, "far", swap)
    return pl.pallas_call(
        last_kernel,
        out_shape=jax.ShapeDtypeStruct((3, blocks * width), jnp.float32),
        in_specs=[smem, vmem, vmem],
        out_specs=vmem,
        compiler_params=params,
    )(parity, mine, other)


def solution(mesh):
    placed = (
        P("tiles", None, None),
        P("tiles", "far", None),
        P("tiles", "far", None),
        P("tiles"),
        P("tiles", None),
        P("tiles"),
        P("tiles"),
        P("tiles"),
        P("tiles", None, None),
    )
    return jax.shard_map(
        per_device, mesh=mesh, in_specs=placed, out_specs=P(None, "tiles"), check_vma=False
    )
```

```python
import jax
import jax.numpy as jnp
from jax import lax
from jax.experimental import pallas as pl
from jax.experimental.pallas import tpu as pltpu
from jax.sharding import PartitionSpec as P

SMEM = pltpu.SMEM
VMEM = pltpu.VMEM
LANES = 128
HEAD = 5
SPARE = 2
GROUP = 32
LIMIT = 48 * 1024 * 1024


def pack_kernel(me_ref, parity_ref, geom_ref, strength_ref, corner_ref, out_ref):
    tiles, blocks, _, _ = out_ref.shape
    width = strength_ref.shape[2]
    shift = (blocks * width).bit_length() - 1
    me = me_ref[0]
    even = parity_ref[0] == 0
    shapes = []
    for b in range(blocks):
        vertex = corner_ref[b]
        offset = (vertex >> shift) - me
        offset = jnp.where(offset < 0, offset + tiles, offset)
        slot = jnp.where(
            offset == 0,
            0,
            jnp.where(offset == 1, 1, jnp.where(offset == tiles - 1, 2, 3)),
        )
        place = ((slot << shift) + (vertex & ((1 << shift) - 1))).astype(jnp.float32)
        span = float(4 << shift)
        for half in range(2):
            code = place[2 * half : 2 * half + 1] * span + place[2 * half + 1 : 2 * half + 2]
            rows = [geom_ref[3 * half + c, b : b + 1] for c in range(3)] + [code]
            shapes.append(jnp.concatenate(rows, axis=0))
    for b in range(blocks):
        shape = jnp.where(even, shapes[b], shapes[blocks + b])
        block = jnp.concatenate([strength_ref[b].astype(jnp.float32), shape], axis=1)
        for t in range(tiles):
            out_ref[t, b] = block


def split3(value):
    first = value.astype(jnp.bfloat16).astype(jnp.float32)
    rest = value - first
    second = rest.astype(jnp.bfloat16).astype(jnp.float32)
    return first, second, rest - second


def sort_kernel(
    me_ref,
    parity_ref,
    target_ref,
    owner_ref,
    source_ref,
    order_ref,
    count_ref,
    blocks,
    info_ref,
):
    pairs = order_ref.shape[1]
    lanes = info_ref.shape[1]
    bits = (blocks - 1).bit_length()
    parity = parity_ref[0]
    order = order_ref[...]
    place = lax.broadcasted_iota(jnp.int32, (1, pairs), 1)
    live = place < count_ref[0]
    word = (owner_ref[...] << bits | source_ref[...]) << bits | target_ref[...]
    word = (word << 2 | order).astype(jnp.float32)
    key = jnp.where(live, (3 - order) * pairs + place, 3 * pairs + place).astype(jnp.float32)
    across = lax.broadcasted_iota(jnp.int32, (pairs, pairs), 1)
    down = lax.broadcasted_iota(jnp.int32, (pairs, pairs), 0)

    def upright(row):
        spread = jnp.broadcast_to(row, (pairs, pairs))
        return jnp.sum(jnp.where(across == down, spread, 0.0), axis=1, keepdims=True)

    key_down = upright(key)
    rank = jnp.sum(jnp.where(key < key_down, 1.0, 0.0), axis=1, keepdims=True).astype(jnp.int32)
    kept = (rank & 1 == parity) & (rank < count_ref[0])
    at = jnp.where(kept, HEAD + (rank >> 1), -1)
    wide_lane = lax.broadcasted_iota(jnp.int32, (pairs, lanes), 1)
    words = jnp.sum(jnp.where(wide_lane == at, upright(word), 0.0), axis=0, keepdims=True)
    info = words.astype(jnp.int32)
    lane = lax.broadcasted_iota(jnp.int32, (1, lanes), 1)
    info = jnp.where(lane == 0, me_ref[0], jnp.where(lane == 4, parity, info))
    for i in range(3):
        upto = jnp.where(live & (order >= 3 - i), 1.0, 0.0)
        total = jnp.sum(upto, axis=1, keepdims=True).astype(jnp.int32)
        info = jnp.where(lane == i + 1, (((total + 1 - parity) >> 1) + 1) >> 1, info)
    info_ref[...] = info


def prep_kernel(geom_ref, adjoint_ref, partner_ref, centre_ref, left_ref):
    blocks, _, width = adjoint_ref.shape
    for b in range(blocks):
        point = jnp.concatenate([geom_ref[c, b : b + 1] for c in range(3)], axis=0)
        rows = [point, jnp.ones((1, width), jnp.float32)]
        rows += [jnp.sum(point * point, axis=0, keepdims=True)]
        rows += [jnp.zeros((3, width), jnp.float32)]
        x1, x2, x3 = split3(jnp.concatenate(rows, axis=0))
        values = [adjoint_ref[b].astype(jnp.float32), partner_ref[b].astype(jnp.float32)]
        rows = [x1, x1, x1, x2, x2, x3] + values
        left_ref[b] = jnp.concatenate(rows, axis=0).T.astype(jnp.bfloat16)
        for c in range(3):
            centre_ref[b, c] = jnp.broadcast_to(point[c : c + 1], (width, width)).T


def pair_kernel(
    info_ref,
    centre_ref,
    left_ref,
    mine_ref,
    other_ref,
    out_ref,
    product_ref,
    row_acc,
    sums_ref,
    joined_ref,
    shape_ref,
):
    tiles, blocks, _, _ = mine_ref.shape
    width = centre_ref.shape[3]
    bits = (blocks - 1).bit_length()
    me = info_ref[0, 0]
    even = info_ref[0, 4] == 0

    def settle(tile, carry):
        for b in range(blocks):
            mine = mine_ref[tile, b, :, width : 2 * width]
            other = other_ref[tile, b, :, width : 2 * width]
            shape_ref[tile, b] = jnp.where(even, mine, other)
            shape_ref[tile, blocks + b] = jnp.where(even, other, mine)
        return carry

    lax.fori_loop(0, tiles, settle, 0, unroll=min(tiles, 8))
    sums_ref[...] = jnp.zeros(sums_ref.shape, jnp.float32)
    joined_ref[...] = jnp.zeros(joined_ref.shape, jnp.float32)
    row_acc[...] = jnp.zeros(row_acc.shape, jnp.float32)
    blank = jnp.zeros((4, width), jnp.float32)
    row_ids = lax.broadcasted_iota(jnp.int32, (8, width), 0)

    def reach_of(order):
        return 0.25 * jnp.where(
            order == 3, 0.7745966692414834, jnp.where(order == 2, 0.5773502691896258, 0.0)
        )

    def read(k):
        word = info_ref[0, HEAD + k]
        inner = word >> 2
        outer = inner >> bits
        return inner & (blocks - 1), outer >> bits, outer & (blocks - 1), word & 3

    def multiply(k, slot):
        target, owner, source, order = read(k)
        third = order == 3
        alive = jnp.where(order > 0, 1.0, 0.0).astype(jnp.float32)
        reach = reach_of(order)
        scale_mid = jnp.where(third, (4.0 / 9.0 / 512.0) ** (-2.0 / 3.0), 0.0)
        scale_side = jnp.where(
            third, (5.0 / 18.0 / 512.0) ** (-2.0 / 3.0), (0.5 / 512.0) ** (-2.0 / 3.0)
        )
        floor_mid = jnp.where(third, 0.0625 * (4.0 / 9.0 / 512.0) ** (-2.0 / 3.0), 3.0e38)
        floor_side = 0.0625 * scale_side
        point = shape_ref[owner, 2 * source]
        extent = shape_ref[owner, 2 * source + 1] * reach
        inside = row_ids < 3
        point = jnp.where(inside, jnp.concatenate([point, blank], axis=0), 0.0)
        extent = jnp.where(inside, jnp.concatenate([extent, blank], axis=0), 0.0)
        values = [ref[owner, source, :, 0:width] * alive for ref in (mine_ref, other_ref)]
        empty = jnp.zeros((8, width), jnp.float32)
        nodes = (
            (point, scale_mid, floor_mid),
            (point + extent, scale_side, floor_side),
            (point - extent, scale_side, floor_side),
        )
        columns = []
        for node, scale, floor in nodes:
            norm = jnp.sum(node * node, axis=0, keepdims=True) * scale + floor
            rows = jnp.where(
                row_ids == 3,
                norm,
                jnp.where(row_ids == 4, scale, node * (-2.0 * scale)),
            )
            p1, p2, p3 = split3(rows)
            columns.append(jnp.concatenate([p1, p2, p3, p1, p2, p1, empty], axis=0))
        columns.append(jnp.concatenate([empty] * 6 + values, axis=0))
        product_ref[slot] = jnp.dot(
            left_ref[target],
            jnp.concatenate(columns, axis=1).astype(jnp.bfloat16),
            preferred_element_type=jnp.float32,
        )

    def one_pair(k, slot, nodes):
        target, owner, source, order = read(k)
        reach = reach_of(order)
        point = [shape_ref[owner, 2 * source, c : c + 1] for c in range(3)]
        extent = [shape_ref[owner, 2 * source + 1, c : c + 1] * reach for c in range(3)]
        columns = [jnp.zeros((8, width), jnp.float32) for _ in range(3)]
        for start in range(0, width, GROUP):
            rows = slice(start, start + GROUP)
            sums = [row_acc[target, c, rows] for c in range(3)]

            def cubed(node):
                i = lax.rsqrt(product_ref[slot, rows, node * width : (node + 1) * width])
                return i * i * i

            coupling = product_ref[slot, rows, 3 * width : 4 * width]
            f_plus = cubed(1)
            if nodes == 1:
                even = (coupling + coupling) * f_plus
            else:
                f_minus = cubed(2)
                both = f_plus + f_minus
                even = coupling * (both + cubed(0) if nodes == 3 else both)
                odd = coupling * (f_plus - f_minus)
            for c in range(3):
                pulled = even * (centre_ref[target, c, rows] - point[c])
                if nodes > 1:
                    pulled = pulled - odd * extent[c]
                sums[c] = sums[c] + pulled
                for r in range(0, GROUP, 8):
                    columns[c] = columns[c] + pulled[r : r + 8]
            for c in range(3):
                row_acc[target, c, rows] = sums[c]
        for c in range(3):
            sums_ref[slot, c : c + 1] = jnp.sum(columns[c], axis=0, keepdims=True)

    high = blocks * width // LANES
    keys = 4 * high
    shift = (blocks * width).bit_length() + 1
    key_ids = lax.broadcasted_iota(jnp.int32, (keys, width), 0).astype(jnp.bfloat16)
    lane_ids = lax.broadcasted_iota(jnp.int32, (LANES, width), 0).astype(jnp.bfloat16)
    zero = jnp.zeros((keys, width), jnp.bfloat16)
    one = jnp.ones((keys, width), jnp.bfloat16)

    def wide(row):
        return jnp.broadcast_to(row, (keys, width))

    def narrow(value):
        return value.astype(jnp.float32).astype(jnp.bfloat16)

    def scatter(tile, b, slot):
        spread = []
        for c in range(3):
            grad = wide(sums_ref[slot, c : c + 1])
            upper = grad.astype(jnp.bfloat16)
            spread += [upper, (grad - upper.astype(jnp.float32)).astype(jnp.bfloat16)]
        parts = []
        hots = []
        for half in range(2):
            code = wide(shape_ref[tile, 2 * b + half, 3:4]).astype(jnp.int32)
            for place in (code >> shift, code & ((1 << shift) - 1)):
                mask = key_ids == narrow(place >> 7)
                low = narrow(place & (LANES - 1))
                parts.append(jnp.concatenate([jnp.where(mask, s, zero) for s in spread], axis=0))
                hots.append(
                    jnp.concatenate(
                        [
                            jnp.where(lane_ids[g : g + keys] == low, one, zero)
                            for g in range(0, LANES, keys)
                        ],
                        axis=0,
                    )
                )
        result = lax.dot_general(
            jnp.concatenate(parts, axis=1),
            jnp.concatenate(hots, axis=1),
            (((1,), (1,)), ((), ())),
            preferred_element_type=jnp.float32,
        )
        before = [joined_ref[tile, c] for c in range(3)]
        for c in range(3):
            joined_ref[tile, c] = (
                before[c]
                + result[2 * c * keys : (2 * c + 1) * keys]
                + result[(2 * c + 1) * keys : (2 * c + 2) * keys]
            )

    def scatter_pair(k, slot):
        _, owner, source, _ = read(k)
        scatter(owner, source, slot)

    def two_pairs(nodes):
        def body(step, carry):
            for slot in range(2):
                k = 2 * step + slot
                multiply(k + 1, 1 - slot)
                scatter_pair(k - 1, 1 - slot)
                one_pair(k, slot, nodes)
            return carry

        return body

    multiply(0, 0)
    lax.fori_loop(0, info_ref[0, 1], two_pairs(3), 0)
    lax.fori_loop(info_ref[0, 1], info_ref[0, 2], two_pairs(2), 0)
    lax.fori_loop(info_ref[0, 2], info_ref[0, 3], two_pairs(1), 0)
    scatter_pair(2 * info_ref[0, 3] - 1, 1)
    for b in range(blocks):
        total = jnp.concatenate(
            [jnp.sum(row_acc[b, c], axis=1, keepdims=True) for c in range(3)]
            + [jnp.zeros((width, 5), jnp.float32)],
            axis=1,
        )
        sums_ref[2 + b] = -total.T
    for b in range(blocks):
        scatter(me, b, 2 + b)

    def collect(dest, carry):
        for c in range(3):
            total = jnp.zeros((high, LANES), jnp.float32)
            for slot, by in enumerate((0, tiles - 1, 1, tiles - tiles // 2)):
                tile = lax.rem(dest + by, tiles)
                total = total + joined_ref[tile, c, slot * high : (slot + 1) * high]
            part = out_ref.shape[2]
            for f in range(out_ref.shape[1]):
                first = f * part % high
                out_ref[dest, f, :, c * LANES : (c + 1) * LANES] = total[first : first + part]
        return carry

    lax.fori_loop(0, tiles, collect, 0, unroll=min(tiles, 8))


def sum_kernel(got_ref, out_ref):
    out_ref[...] = jnp.sum(got_ref[...], axis=0)


def last_kernel(parity_ref, mine_ref, other_ref, out_ref):
    part = mine_ref.shape[0]
    even = parity_ref[0] == 0
    mine, other = mine_ref[...], other_ref[...]
    halves = (jnp.where(even, mine, other), jnp.where(even, other, mine))
    for i, half in enumerate(halves):
        for r in range(part):
            h = i * part + r
            for c in range(3):
                out_ref[c : c + 1, h * LANES : (h + 1) * LANES] = half[
                    r : r + 1, c * LANES : (c + 1) * LANES
                ]


def per_device(
    panel_geometry,
    adjoint,
    strengths,
    pair_target,
    pair_owner,
    pair_source,
    pair_order,
    pair_count,
    corner_vertex,
):
    tiles = lax.axis_size("tiles")
    far = lax.axis_size("far")
    blocks, _, width = panel_geometry.shape
    high = blocks * width // LANES
    parity = lax.axis_index("far").astype(jnp.int32) & 1
    me = lax.axis_index("tiles").astype(jnp.int32).reshape(1)
    parity = parity.reshape(1)
    swap = [(f ^ 1, f) for f in range(far)]
    smem = pl.BlockSpec(memory_space=SMEM)
    vmem = pl.BlockSpec(memory_space=VMEM)
    params = pltpu.CompilerParams(vmem_limit_bytes=LIMIT)
    geometry = panel_geometry.transpose(1, 0, 2)
    packed = pl.pallas_call(
        pack_kernel,
        out_shape=jax.ShapeDtypeStruct((tiles, blocks, 4, 2 * width), jnp.float32),
        in_specs=[smem] * 2 + [vmem] * 3,
        out_specs=vmem,
    )(me, parity, geometry, strengths, corner_vertex)
    got = lax.all_to_all(packed, "tiles", split_axis=0, concat_axis=0, tiled=True)
    partner = lax.ppermute(adjoint, "far", swap)
    pairs = pair_target.shape[0]
    info = pl.pallas_call(
        lambda *refs: sort_kernel(*refs[:-1], blocks, refs[-1]),
        out_shape=jax.ShapeDtypeStruct((1, -(-(HEAD + pairs // 2 + SPARE + 1) // LANES) * LANES), jnp.int32),
        in_specs=[smem] * 2 + [vmem] * 4 + [smem],
        out_specs=vmem,
        cost_estimate=pl.CostEstimate(flops=4000000, bytes_accessed=900000, transcendentals=0),
    )(
        me,
        parity,
        pair_target.reshape(1, pairs),
        pair_owner.reshape(1, pairs),
        pair_source.reshape(1, pairs),
        pair_order.reshape(1, pairs),
        pair_count,
    )
    centre, left = pl.pallas_call(
        prep_kernel,
        out_shape=(
            jax.ShapeDtypeStruct((blocks, 3, width, width), jnp.float32),
            jax.ShapeDtypeStruct((blocks, width, 56), jnp.bfloat16),
        ),
        compiler_params=params,
        cost_estimate=pl.CostEstimate(flops=4000000, bytes_accessed=900000, transcendentals=0),
    )(geometry, adjoint, partner)
    got, info, left = lax.optimization_barrier((got, info, left))
    other = lax.ppermute(got, "far", swap)
    partial = pl.pallas_call(
        pair_kernel,
        out_shape=jax.ShapeDtypeStruct((tiles, far, high // 2, 3 * LANES), jnp.float32),
        in_specs=[smem] + [vmem] * 4,
        out_specs=vmem,
        scratch_shapes=[
            VMEM((2, width, 4 * width), jnp.float32),
            VMEM((blocks, 3, width, width), jnp.float32),
            VMEM((2 + blocks, 8, width), jnp.float32),
            VMEM((tiles, 3, 4 * high, LANES), jnp.float32),
            VMEM((tiles, 2 * blocks, 4, width), jnp.float32),
        ],
        compiler_params=params,
    )(info, centre, left, got, other)
    partial = partial.reshape(tiles * far, high // 2, 3 * LANES)
    shares = lax.all_to_all(partial, ("tiles", "far"), split_axis=0, concat_axis=0, tiled=True)
    mine = pl.pallas_call(
        sum_kernel,
        out_shape=jax.ShapeDtypeStruct((high // 2, 3 * LANES), jnp.float32),
        compiler_params=params,
    )(shares)
    other = lax.ppermute(mine, "far", swap)
    return pl.pallas_call(
        last_kernel,
        out_shape=jax.ShapeDtypeStruct((3, blocks * width), jnp.float32),
        in_specs=[smem, vmem, vmem],
        out_specs=vmem,
        compiler_params=params,
    )(parity, mine, other)


def solution(mesh):
    placed = (
        P("tiles", None, None),
        P("tiles", "far", None),
        P("tiles", "far", None),
        P("tiles"),
        P("tiles", None),
        P("tiles"),
        P("tiles"),
        P("tiles"),
        P("tiles", None, None),
    )
    return jax.shard_map(
        per_device, mesh=mesh, in_specs=placed, out_specs=P(None, "tiles"), check_vma=False
    )
```

```python
import jax
import jax.numpy as jnp
from jax import lax
from jax.experimental import pallas as pl
from jax.experimental.pallas import tpu as pltpu
from jax.sharding import PartitionSpec as P

SMEM = pltpu.SMEM
VMEM = pltpu.VMEM
LANES = 128
HEAD = 5
SPARE = 2
GROUP = 32
LIMIT = 48 * 1024 * 1024


def pack_kernel(me_ref, parity_ref, geom_ref, strength_ref, corner_ref, out_ref):
    tiles, blocks, _, _ = out_ref.shape
    width = strength_ref.shape[2]
    shift = (blocks * width).bit_length() - 1
    me = me_ref[0]
    even = parity_ref[0] == 0
    shapes = []
    for b in range(blocks):
        vertex = corner_ref[b]
        offset = (vertex >> shift) - me
        offset = jnp.where(offset < 0, offset + tiles, offset)
        slot = jnp.where(
            offset == 0,
            0,
            jnp.where(offset == 1, 1, jnp.where(offset == tiles - 1, 2, 3)),
        )
        place = ((slot << shift) + (vertex & ((1 << shift) - 1))).astype(jnp.float32)
        span = float(4 << shift)
        for half in range(2):
            code = place[2 * half : 2 * half + 1] * span + place[2 * half + 1 : 2 * half + 2]
            rows = [geom_ref[3 * half + c, b : b + 1] for c in range(3)] + [code]
            shapes.append(jnp.concatenate(rows, axis=0))
    for b in range(blocks):
        shape = jnp.where(even, shapes[b], shapes[blocks + b])
        block = jnp.concatenate([strength_ref[b].astype(jnp.float32), shape], axis=1)
        for t in range(tiles):
            out_ref[t, b] = block


def split3(value):
    first = value.astype(jnp.bfloat16).astype(jnp.float32)
    rest = value - first
    second = rest.astype(jnp.bfloat16).astype(jnp.float32)
    return first, second, rest - second


def sort_kernel(
    me_ref,
    parity_ref,
    target_ref,
    owner_ref,
    source_ref,
    order_ref,
    count_ref,
    blocks,
    info_ref,
):
    pairs = order_ref.shape[1]
    lanes = info_ref.shape[1]
    bits = (blocks - 1).bit_length()
    parity = parity_ref[0]
    order = order_ref[...]
    place = lax.broadcasted_iota(jnp.int32, (1, pairs), 1)
    live = place < count_ref[0]
    word = (owner_ref[...] << bits | source_ref[...]) << bits | target_ref[...]
    word = (word << 2 | order).astype(jnp.float32)
    key = jnp.where(live, (3 - order) * pairs + place, 3 * pairs + place).astype(jnp.float32)
    across = lax.broadcasted_iota(jnp.int32, (pairs, pairs), 1)
    down = lax.broadcasted_iota(jnp.int32, (pairs, pairs), 0)

    def upright(row):
        spread = jnp.broadcast_to(row, (pairs, pairs))
        return jnp.sum(jnp.where(across == down, spread, 0.0), axis=1, keepdims=True)

    key_down = upright(key)
    rank = jnp.sum(jnp.where(key < key_down, 1.0, 0.0), axis=1, keepdims=True).astype(jnp.int32)
    kept = (rank & 1 == parity) & (rank < count_ref[0])
    at = jnp.where(kept, HEAD + (rank >> 1), -1)
    wide_lane = lax.broadcasted_iota(jnp.int32, (pairs, lanes), 1)
    words = jnp.sum(jnp.where(wide_lane == at, upright(word), 0.0), axis=0, keepdims=True)
    info = words.astype(jnp.int32)
    lane = lax.broadcasted_iota(jnp.int32, (1, lanes), 1)
    info = jnp.where(lane == 0, me_ref[0], jnp.where(lane == 4, parity, info))
    for i in range(3):
        upto = jnp.where(live & (order >= 3 - i), 1.0, 0.0)
        total = jnp.sum(upto, axis=1, keepdims=True).astype(jnp.int32)
        info = jnp.where(lane == i + 1, (((total + 1 - parity) >> 1) + 1) >> 1, info)
    info_ref[...] = info


def prep_kernel(geom_ref, adjoint_ref, partner_ref, centre_ref, left_ref):
    blocks, _, width = adjoint_ref.shape
    for b in range(blocks):
        point = jnp.concatenate([geom_ref[c, b : b + 1] for c in range(3)], axis=0)
        rows = [point, jnp.ones((1, width), jnp.float32)]
        rows += [jnp.sum(point * point, axis=0, keepdims=True)]
        rows += [jnp.zeros((3, width), jnp.float32)]
        x1, x2, x3 = split3(jnp.concatenate(rows, axis=0))
        values = [adjoint_ref[b].astype(jnp.float32), partner_ref[b].astype(jnp.float32)]
        rows = [x1, x1, x1, x2, x2, x3] + values
        left_ref[b] = jnp.concatenate(rows, axis=0).T.astype(jnp.bfloat16)
        for c in range(3):
            centre_ref[b, c] = jnp.broadcast_to(point[c : c + 1], (width, width)).T


def pair_kernel(
    info_ref,
    centre_ref,
    left_ref,
    mine_ref,
    other_ref,
    out_ref,
    product_ref,
    row_acc,
    sums_ref,
    joined_ref,
    shape_ref,
):
    tiles, blocks, _, _ = mine_ref.shape
    width = centre_ref.shape[3]
    bits = (blocks - 1).bit_length()
    me = info_ref[0, 0]
    even = info_ref[0, 4] == 0

    def settle(tile, carry):
        for b in range(blocks):
            mine = mine_ref[tile, b, :, width : 2 * width]
            other = other_ref[tile, b, :, width : 2 * width]
            shape_ref[tile, b] = jnp.where(even, mine, other)
            shape_ref[tile, blocks + b] = jnp.where(even, other, mine)
        return carry

    lax.fori_loop(0, tiles, settle, 0, unroll=min(tiles, 8))
    sums_ref[...] = jnp.zeros(sums_ref.shape, jnp.float32)
    joined_ref[...] = jnp.zeros(joined_ref.shape, jnp.float32)
    row_acc[...] = jnp.zeros(row_acc.shape, jnp.float32)
    blank = jnp.zeros((4, width), jnp.float32)
    row_ids = lax.broadcasted_iota(jnp.int32, (8, width), 0)

    def reach_of(order):
        return 0.25 * jnp.where(
            order == 3, 0.7745966692414834, jnp.where(order == 2, 0.5773502691896258, 0.0)
        )

    def read(k):
        word = info_ref[0, HEAD + k]
        inner = word >> 2
        outer = inner >> bits
        return inner & (blocks - 1), outer >> bits, outer & (blocks - 1), word & 3

    def multiply(k, slot, nodes):
        target, owner, source, order = read(k)
        third = order == 3
        alive = jnp.where(order > 0, 1.0, 0.0).astype(jnp.float32)
        reach = reach_of(order)
        scale_mid = jnp.where(third, (4.0 / 9.0 / 512.0) ** (-2.0 / 3.0), 0.0)
        scale_side = jnp.where(
            third, (5.0 / 18.0 / 512.0) ** (-2.0 / 3.0), (0.5 / 512.0) ** (-2.0 / 3.0)
        )
        floor_mid = jnp.where(third, 0.0625 * (4.0 / 9.0 / 512.0) ** (-2.0 / 3.0), 3.0e38)
        floor_side = 0.0625 * scale_side
        point = shape_ref[owner, 2 * source]
        extent = shape_ref[owner, 2 * source + 1] * reach
        inside = row_ids < 3
        point = jnp.where(inside, jnp.concatenate([point, blank], axis=0), 0.0)
        extent = jnp.where(inside, jnp.concatenate([extent, blank], axis=0), 0.0)
        values = [ref[owner, source, :, 0:width] * alive for ref in (mine_ref, other_ref)]
        empty = jnp.zeros((8, width), jnp.float32)
        quadrature = (
            (point + extent, scale_side, floor_side),
            (point - extent, scale_side, floor_side),
            (point, scale_mid, floor_mid),
        )
        columns = []
        for node, scale, floor in quadrature[:nodes]:
            norm = jnp.sum(node * node, axis=0, keepdims=True) * scale + floor
            rows = jnp.where(
                row_ids == 3,
                norm,
                jnp.where(row_ids == 4, scale, node * (-2.0 * scale)),
            )
            p1, p2, p3 = split3(rows)
            columns.append(jnp.concatenate([p1, p2, p3, p1, p2, p1, empty], axis=0))
        columns.insert(1, jnp.concatenate([empty] * 6 + values, axis=0))
        product_ref[slot, :, 0 : (nodes + 1) * width] = jnp.dot(
            left_ref[target],
            jnp.concatenate(columns, axis=1).astype(jnp.bfloat16),
            preferred_element_type=jnp.float32,
        )

    def one_pair(k, slot, nodes):
        target, owner, source, order = read(k)
        reach = reach_of(order)
        point = [shape_ref[owner, 2 * source, c : c + 1] for c in range(3)]
        extent = [shape_ref[owner, 2 * source + 1, c : c + 1] * reach for c in range(3)]
        columns = [jnp.zeros((8, width), jnp.float32) for _ in range(3)]
        for start in range(0, width, GROUP):
            rows = slice(start, start + GROUP)
            sums = [row_acc[target, c, rows] for c in range(3)]

            def cubed(part):
                i = lax.rsqrt(product_ref[slot, rows, part * width : (part + 1) * width])
                return i * i * i

            coupling = product_ref[slot, rows, width : 2 * width]
            f_plus = cubed(0)
            if nodes == 1:
                even = (coupling + coupling) * f_plus
            else:
                f_minus = cubed(2)
                both = f_plus + f_minus
                even = coupling * (both + cubed(3) if nodes == 3 else both)
                odd = coupling * (f_plus - f_minus)
            for c in range(3):
                pulled = even * (centre_ref[target, c, rows] - point[c])
                if nodes > 1:
                    pulled = pulled - odd * extent[c]
                sums[c] = sums[c] + pulled
                for r in range(0, GROUP, 8):
                    columns[c] = columns[c] + pulled[r : r + 8]
            for c in range(3):
                row_acc[target, c, rows] = sums[c]
        for c in range(3):
            sums_ref[slot, c : c + 1] = jnp.sum(columns[c], axis=0, keepdims=True)

    high = blocks * width // LANES
    keys = 4 * high
    shift = (blocks * width).bit_length() + 1
    key_ids = lax.broadcasted_iota(jnp.int32, (keys, width), 0).astype(jnp.bfloat16)
    lane_ids = lax.broadcasted_iota(jnp.int32, (LANES, width), 0).astype(jnp.bfloat16)
    zero = jnp.zeros((keys, width), jnp.bfloat16)
    one = jnp.ones((keys, width), jnp.bfloat16)

    def wide(row):
        return jnp.broadcast_to(row, (keys, width))

    def narrow(value):
        return value.astype(jnp.float32).astype(jnp.bfloat16)

    def scatter(tile, b, slot):
        spread = []
        for c in range(3):
            grad = wide(sums_ref[slot, c : c + 1])
            upper = grad.astype(jnp.bfloat16)
            spread += [upper, (grad - upper.astype(jnp.float32)).astype(jnp.bfloat16)]
        parts = []
        hots = []
        for half in range(2):
            code = wide(shape_ref[tile, 2 * b + half, 3:4]).astype(jnp.int32)
            for place in (code >> shift, code & ((1 << shift) - 1)):
                mask = key_ids == narrow(place >> 7)
                low = narrow(place & (LANES - 1))
                parts.append(jnp.concatenate([jnp.where(mask, s, zero) for s in spread], axis=0))
                hots.append(
                    jnp.concatenate(
                        [
                            jnp.where(lane_ids[g : g + keys] == low, one, zero)
                            for g in range(0, LANES, keys)
                        ],
                        axis=0,
                    )
                )
        result = lax.dot_general(
            jnp.concatenate(parts, axis=1),
            jnp.concatenate(hots, axis=1),
            (((1,), (1,)), ((), ())),
            preferred_element_type=jnp.float32,
        )
        before = [joined_ref[tile, c] for c in range(3)]
        for c in range(3):
            joined_ref[tile, c] = (
                before[c]
                + result[2 * c * keys : (2 * c + 1) * keys]
                + result[(2 * c + 1) * keys : (2 * c + 2) * keys]
            )

    def scatter_pair(k, slot):
        _, owner, source, _ = read(jnp.maximum(k, 0))
        scatter(owner, source, slot)

    def two_pairs(nodes):
        def body(step, carry):
            for now in range(2):

                @pl.when(lax.rem(step, 2) == now)
                def _():
                    for i in range(2):
                        multiply(2 * step + 2 + i, 2 * (1 - now) + i, nodes)
                    for i in range(2):
                        scatter_pair(2 * step - 2 + i, 2 * (1 - now) + i)
                        one_pair(2 * step + i, 2 * now + i, nodes)

            return carry

        return body

    for i in range(2):
        multiply(i, i, 3)
    steps = info_ref[0, 3]
    lax.fori_loop(0, info_ref[0, 1], two_pairs(3), 0)
    lax.fori_loop(info_ref[0, 1], info_ref[0, 2], two_pairs(2), 0)
    lax.fori_loop(info_ref[0, 2], steps, two_pairs(1), 0)
    for i in range(2):
        scatter_pair(2 * steps - 2 + i, 2 * lax.rem(steps + 1, 2) + i)
    for b in range(blocks):
        total = jnp.concatenate(
            [jnp.sum(row_acc[b, c], axis=1, keepdims=True) for c in range(3)]
            + [jnp.zeros((width, 5), jnp.float32)],
            axis=1,
        )
        sums_ref[4 + b] = -total.T
    for b in range(blocks):
        scatter(me, b, 4 + b)

    def collect(dest, carry):
        for c in range(3):
            total = jnp.zeros((high, LANES), jnp.float32)
            for slot, by in enumerate((0, tiles - 1, 1, tiles - tiles // 2)):
                tile = lax.rem(dest + by, tiles)
                total = total + joined_ref[tile, c, slot * high : (slot + 1) * high]
            part = out_ref.shape[2]
            for f in range(out_ref.shape[1]):
                first = f * part % high
                out_ref[dest, f, :, c * LANES : (c + 1) * LANES] = total[first : first + part]
        return carry

    lax.fori_loop(0, tiles, collect, 0, unroll=min(tiles, 8))


def sum_kernel(got_ref, out_ref):
    out_ref[...] = jnp.sum(got_ref[...], axis=0)


def last_kernel(parity_ref, mine_ref, other_ref, out_ref):
    part = mine_ref.shape[0]
    even = parity_ref[0] == 0
    mine, other = mine_ref[...], other_ref[...]
    halves = (jnp.where(even, mine, other), jnp.where(even, other, mine))
    for i, half in enumerate(halves):
        for r in range(part):
            h = i * part + r
            for c in range(3):
                out_ref[c : c + 1, h * LANES : (h + 1) * LANES] = half[
                    r : r + 1, c * LANES : (c + 1) * LANES
                ]


def per_device(
    panel_geometry,
    adjoint,
    strengths,
    pair_target,
    pair_owner,
    pair_source,
    pair_order,
    pair_count,
    corner_vertex,
):
    tiles = lax.axis_size("tiles")
    far = lax.axis_size("far")
    blocks, _, width = panel_geometry.shape
    high = blocks * width // LANES
    parity = lax.axis_index("far").astype(jnp.int32) & 1
    me = lax.axis_index("tiles").astype(jnp.int32).reshape(1)
    parity = parity.reshape(1)
    swap = [(f ^ 1, f) for f in range(far)]
    smem = pl.BlockSpec(memory_space=SMEM)
    vmem = pl.BlockSpec(memory_space=VMEM)
    params = pltpu.CompilerParams(vmem_limit_bytes=LIMIT)
    geometry = panel_geometry.transpose(1, 0, 2)
    packed = pl.pallas_call(
        pack_kernel,
        out_shape=jax.ShapeDtypeStruct((tiles, blocks, 4, 2 * width), jnp.float32),
        in_specs=[smem] * 2 + [vmem] * 3,
        out_specs=vmem,
    )(me, parity, geometry, strengths, corner_vertex)
    got = lax.all_to_all(packed, "tiles", split_axis=0, concat_axis=0, tiled=True)
    partner = lax.ppermute(adjoint, "far", swap)
    pairs = pair_target.shape[0]
    info = pl.pallas_call(
        lambda *refs: sort_kernel(*refs[:-1], blocks, refs[-1]),
        out_shape=jax.ShapeDtypeStruct((1, -(-(HEAD + pairs // 2 + SPARE + 1) // LANES) * LANES), jnp.int32),
        in_specs=[smem] * 2 + [vmem] * 4 + [smem],
        out_specs=vmem,
        cost_estimate=pl.CostEstimate(flops=4000000, bytes_accessed=900000, transcendentals=0),
    )(
        me,
        parity,
        pair_target.reshape(1, pairs),
        pair_owner.reshape(1, pairs),
        pair_source.reshape(1, pairs),
        pair_order.reshape(1, pairs),
        pair_count,
    )
    centre, left = pl.pallas_call(
        prep_kernel,
        out_shape=(
            jax.ShapeDtypeStruct((blocks, 3, width, width), jnp.float32),
            jax.ShapeDtypeStruct((blocks, width, 56), jnp.bfloat16),
        ),
        compiler_params=params,
        cost_estimate=pl.CostEstimate(flops=4000000, bytes_accessed=900000, transcendentals=0),
    )(geometry, adjoint, partner)
    got, info, left = lax.optimization_barrier((got, info, left))
    other = lax.ppermute(got, "far", swap)
    partial = pl.pallas_call(
        pair_kernel,
        out_shape=jax.ShapeDtypeStruct((tiles, far, high // 2, 3 * LANES), jnp.float32),
        in_specs=[smem] + [vmem] * 4,
        out_specs=vmem,
        scratch_shapes=[
            VMEM((4, width, 4 * width), jnp.float32),
            VMEM((blocks, 3, width, width), jnp.float32),
            VMEM((4 + blocks, 8, width), jnp.float32),
            VMEM((tiles, 3, 4 * high, LANES), jnp.float32),
            VMEM((tiles, 2 * blocks, 4, width), jnp.float32),
        ],
        compiler_params=params,
    )(info, centre, left, got, other)
    partial = partial.reshape(tiles * far, high // 2, 3 * LANES)
    shares = lax.all_to_all(partial, ("tiles", "far"), split_axis=0, concat_axis=0, tiled=True)
    mine = pl.pallas_call(
        sum_kernel,
        out_shape=jax.ShapeDtypeStruct((high // 2, 3 * LANES), jnp.float32),
        compiler_params=params,
    )(shares)
    other = lax.ppermute(mine, "far", swap)
    return pl.pallas_call(
        last_kernel,
        out_shape=jax.ShapeDtypeStruct((3, blocks * width), jnp.float32),
        in_specs=[smem, vmem, vmem],
        out_specs=vmem,
        compiler_params=params,
    )(parity, mine, other)


def solution(mesh):
    placed = (
        P("tiles", None, None),
        P("tiles", "far", None),
        P("tiles", "far", None),
        P("tiles"),
        P("tiles", None),
        P("tiles"),
        P("tiles"),
        P("tiles"),
        P("tiles", None, None),
    )
    return jax.shard_map(
        per_device, mesh=mesh, in_specs=placed, out_specs=P(None, "tiles"), check_vma=False
    )
```

```python
import jax
import jax.numpy as jnp
from jax import lax
from jax.experimental import pallas as pl
from jax.experimental.pallas import tpu as pltpu
from jax.sharding import PartitionSpec as P

SMEM = pltpu.SMEM
VMEM = pltpu.VMEM
LANES = 128
HEAD = 5
SPARE = 2
LIMIT = 48 * 1024 * 1024


def pack_kernel(me_ref, parity_ref, geom_ref, strength_ref, corner_ref, out_ref):
    tiles, blocks, _, _ = out_ref.shape
    width = strength_ref.shape[2]
    shift = (blocks * width).bit_length() - 1
    me = me_ref[0]
    even = parity_ref[0] == 0
    shapes = []
    for b in range(blocks):
        vertex = corner_ref[b]
        offset = (vertex >> shift) - me
        offset = jnp.where(offset < 0, offset + tiles, offset)
        slot = jnp.where(
            offset == 0,
            0,
            jnp.where(offset == 1, 1, jnp.where(offset == tiles - 1, 2, 3)),
        )
        place = ((slot << shift) + (vertex & ((1 << shift) - 1))).astype(jnp.float32)
        span = float(4 << shift)
        for half in range(2):
            code = place[2 * half : 2 * half + 1] * span + place[2 * half + 1 : 2 * half + 2]
            rows = [geom_ref[3 * half + c, b : b + 1] for c in range(3)] + [code]
            shapes.append(jnp.concatenate(rows, axis=0))
    for b in range(blocks):
        shape = jnp.where(even, shapes[b], shapes[blocks + b])
        block = jnp.concatenate([strength_ref[b].astype(jnp.float32), shape], axis=1)
        for t in range(tiles):
            out_ref[t, b] = block


def split3(value):
    first = value.astype(jnp.bfloat16).astype(jnp.float32)
    rest = value - first
    second = rest.astype(jnp.bfloat16).astype(jnp.float32)
    return first, second, rest - second


def sort_kernel(
    me_ref,
    parity_ref,
    target_ref,
    owner_ref,
    source_ref,
    order_ref,
    count_ref,
    blocks,
    info_ref,
):
    pairs = order_ref.shape[1]
    lanes = info_ref.shape[1]
    bits = (blocks - 1).bit_length()
    parity = parity_ref[0]
    order = order_ref[...]
    place = lax.broadcasted_iota(jnp.int32, (1, pairs), 1)
    live = place < count_ref[0]
    word = (owner_ref[...] << bits | source_ref[...]) << bits | target_ref[...]
    word = (word << 2 | order).astype(jnp.float32)
    key = jnp.where(live, (3 - order) * pairs + place, 3 * pairs + place).astype(jnp.float32)
    across = lax.broadcasted_iota(jnp.int32, (pairs, pairs), 1)
    down = lax.broadcasted_iota(jnp.int32, (pairs, pairs), 0)

    def upright(row):
        spread = jnp.broadcast_to(row, (pairs, pairs))
        return jnp.sum(jnp.where(across == down, spread, 0.0), axis=1, keepdims=True)

    key_down = upright(key)
    rank = jnp.sum(jnp.where(key < key_down, 1.0, 0.0), axis=1, keepdims=True).astype(jnp.int32)
    kept = (rank & 1 == parity) & (rank < count_ref[0])
    at = jnp.where(kept, HEAD + (rank >> 1), -1)
    wide_lane = lax.broadcasted_iota(jnp.int32, (pairs, lanes), 1)
    words = jnp.sum(jnp.where(wide_lane == at, upright(word), 0.0), axis=0, keepdims=True)
    info = words.astype(jnp.int32)
    lane = lax.broadcasted_iota(jnp.int32, (1, lanes), 1)
    info = jnp.where(lane == 0, me_ref[0], jnp.where(lane == 4, parity, info))
    for i in range(3):
        upto = jnp.where(live & (order >= 3 - i), 1.0, 0.0)
        total = jnp.sum(upto, axis=1, keepdims=True).astype(jnp.int32)
        info = jnp.where(lane == i + 1, (((total + 1 - parity) >> 1) + 1) >> 1, info)
    info_ref[...] = info


def prep_kernel(geom_ref, adjoint_ref, partner_ref, centre_ref, left_ref):
    blocks, _, width = adjoint_ref.shape
    for b in range(blocks):
        point = jnp.concatenate([geom_ref[c, b : b + 1] for c in range(3)], axis=0)
        rows = [point, jnp.ones((1, width), jnp.float32)]
        rows += [jnp.sum(point * point, axis=0, keepdims=True)]
        rows += [jnp.zeros((3, width), jnp.float32)]
        x1, x2, x3 = split3(jnp.concatenate(rows, axis=0))
        values = [adjoint_ref[b].astype(jnp.float32), partner_ref[b].astype(jnp.float32)]
        rows = [x1, x1, x1, x2, x2, x3] + values
        left_ref[b] = jnp.concatenate(rows, axis=0).T.astype(jnp.bfloat16)
        for c in range(3):
            centre_ref[b, c] = jnp.broadcast_to(point[c : c + 1], (width, width)).T


def pair_kernel(
    info_ref,
    centre_ref,
    left_ref,
    mine_ref,
    other_ref,
    out_ref,
    product_ref,
    row_acc,
    sums_ref,
    joined_ref,
    shape_ref,
):
    tiles, blocks, _, _ = mine_ref.shape
    width = centre_ref.shape[3]
    bits = (blocks - 1).bit_length()
    me = info_ref[0, 0]
    even = info_ref[0, 4] == 0

    def settle(tile, carry):
        for b in range(blocks):
            mine = mine_ref[tile, b, :, width : 2 * width]
            other = other_ref[tile, b, :, width : 2 * width]
            shape_ref[tile, b] = jnp.where(even, mine, other)
            shape_ref[tile, blocks + b] = jnp.where(even, other, mine)
        return carry

    lax.fori_loop(0, tiles, settle, 0, unroll=min(tiles, 8))
    sums_ref[...] = jnp.zeros(sums_ref.shape, jnp.float32)
    joined_ref[...] = jnp.zeros(joined_ref.shape, jnp.float32)
    row_acc[...] = jnp.zeros(row_acc.shape, jnp.float32)
    blank = jnp.zeros((4, width), jnp.float32)
    row_ids = lax.broadcasted_iota(jnp.int32, (8, width), 0)

    def reach_of(order):
        return 0.25 * jnp.where(
            order == 3, 0.7745966692414834, jnp.where(order == 2, 0.5773502691896258, 0.0)
        )

    def read(k):
        word = info_ref[0, HEAD + k]
        inner = word >> 2
        outer = inner >> bits
        return inner & (blocks - 1), outer >> bits, outer & (blocks - 1), word & 3

    def multiply(k, slot, nodes):
        target, owner, source, order = read(k)
        third = order == 3
        alive = jnp.where(order > 0, 1.0, 0.0).astype(jnp.float32)
        reach = reach_of(order)
        scale_mid = jnp.where(third, (4.0 / 9.0 / 512.0) ** (-2.0 / 3.0), 0.0)
        scale_side = jnp.where(
            third, (5.0 / 18.0 / 512.0) ** (-2.0 / 3.0), (0.5 / 512.0) ** (-2.0 / 3.0)
        )
        floor_mid = jnp.where(third, 0.0625 * (4.0 / 9.0 / 512.0) ** (-2.0 / 3.0), 3.0e38)
        floor_side = 0.0625 * scale_side
        point = shape_ref[owner, 2 * source]
        extent = shape_ref[owner, 2 * source + 1] * reach
        inside = row_ids < 3
        point = jnp.where(inside, jnp.concatenate([point, blank], axis=0), 0.0)
        extent = jnp.where(inside, jnp.concatenate([extent, blank], axis=0), 0.0)
        values = [ref[owner, source, :, 0:width] * alive for ref in (mine_ref, other_ref)]
        empty = jnp.zeros((8, width), jnp.float32)
        quadrature = (
            (point + extent, scale_side, floor_side),
            (point - extent, scale_side, floor_side),
            (point, scale_mid, floor_mid),
        )
        columns = []
        for node, scale, floor in quadrature[:nodes]:
            norm = jnp.sum(node * node, axis=0, keepdims=True) * scale + floor
            rows = jnp.where(
                row_ids == 3,
                norm,
                jnp.where(row_ids == 4, scale, node * (-2.0 * scale)),
            )
            p1, p2, p3 = split3(rows)
            columns.append(jnp.concatenate([p1, p2, p3, p1, p2, p1, empty], axis=0))
        columns.insert(1, jnp.concatenate([empty] * 6 + values, axis=0))
        product_ref[slot, :, 0 : (nodes + 1) * width] = jnp.dot(
            left_ref[target],
            jnp.concatenate(columns, axis=1).astype(jnp.bfloat16),
            preferred_element_type=jnp.float32,
        )

    def one_pair(k, slot, nodes):
        target, owner, source, order = read(k)
        reach = reach_of(order)
        eight = (8, width)
        point = [jnp.broadcast_to(shape_ref[owner, 2 * source, c : c + 1], eight) for c in range(3)]
        extent = [
            jnp.broadcast_to(shape_ref[owner, 2 * source + 1, c : c + 1], eight) * reach
            for c in range(3)
        ]
        columns = [jnp.zeros(eight, jnp.float32) for _ in range(3)]
        for start in range(0, width, 8):
            rows = slice(start, start + 8)
            sums = [row_acc[target, c, rows] for c in range(3)]

            def cubed(part):
                i = lax.rsqrt(product_ref[slot, rows, part * width : (part + 1) * width])
                return i * i * i

            coupling = product_ref[slot, rows, width : 2 * width]
            f_plus = cubed(0)
            if nodes == 1:
                even = (coupling + coupling) * f_plus
            else:
                f_minus = cubed(2)
                both = f_plus + f_minus
                even = coupling * (both + cubed(3) if nodes == 3 else both)
                odd = coupling * (f_plus - f_minus)
            for c in range(3):
                pulled = even * (centre_ref[target, c, rows] - point[c])
                if nodes > 1:
                    pulled = pulled - odd * extent[c]
                columns[c] = columns[c] + pulled
                row_acc[target, c, rows] = sums[c] + pulled
        for c in range(3):
            sums_ref[slot, c : c + 1] = jnp.sum(columns[c], axis=0, keepdims=True)

    high = blocks * width // LANES
    keys = 4 * high
    shift = (blocks * width).bit_length() + 1
    key_ids = lax.broadcasted_iota(jnp.int32, (keys, width), 0).astype(jnp.bfloat16)
    lane_ids = lax.broadcasted_iota(jnp.int32, (LANES, width), 0).astype(jnp.bfloat16)
    zero = jnp.zeros((keys, width), jnp.bfloat16)
    one = jnp.ones((keys, width), jnp.bfloat16)

    def wide(row):
        return jnp.broadcast_to(row, (keys, width))

    def narrow(value):
        return value.astype(jnp.float32).astype(jnp.bfloat16)

    def scatter(tile, b, slot):
        spread = []
        for c in range(3):
            grad = wide(sums_ref[slot, c : c + 1])
            upper = grad.astype(jnp.bfloat16)
            spread += [upper, (grad - upper.astype(jnp.float32)).astype(jnp.bfloat16)]
        result = None
        for half in range(2):
            parts = []
            hots = []
            code = wide(shape_ref[tile, 2 * b + half, 3:4]).astype(jnp.int32)
            for place in (code >> shift, code & ((1 << shift) - 1)):
                mask = key_ids == narrow(place >> 7)
                low = narrow(place & (LANES - 1))
                parts.append(jnp.concatenate([jnp.where(mask, s, zero) for s in spread], axis=0))
                hots.append(
                    jnp.concatenate(
                        [
                            jnp.where(lane_ids[g : g + keys] == low, one, zero)
                            for g in range(0, LANES, keys)
                        ],
                        axis=0,
                    )
                )
            product = lax.dot_general(
                jnp.concatenate(parts, axis=1),
                jnp.concatenate(hots, axis=1),
                (((1,), (1,)), ((), ())),
                preferred_element_type=jnp.float32,
            )
            result = product if result is None else result + product
        before = [joined_ref[tile, c] for c in range(3)]
        for c in range(3):
            joined_ref[tile, c] = (
                before[c]
                + result[2 * c * keys : (2 * c + 1) * keys]
                + result[(2 * c + 1) * keys : (2 * c + 2) * keys]
            )

    def scatter_pair(k, slot):
        _, owner, source, _ = read(k)
        scatter(owner, source, slot)

    def two_pairs(nodes):
        def body(step, carry):
            for slot in range(2):
                k = 2 * step + slot
                multiply(k + 1, 1 - slot, nodes)
                scatter_pair(k - 1, 1 - slot)
                one_pair(k, slot, nodes)
            return carry

        return body

    multiply(0, 0, 3)
    lax.fori_loop(0, info_ref[0, 1], two_pairs(3), 0)
    lax.fori_loop(info_ref[0, 1], info_ref[0, 2], two_pairs(2), 0)
    lax.fori_loop(info_ref[0, 2], info_ref[0, 3], two_pairs(1), 0)
    scatter_pair(2 * info_ref[0, 3] - 1, 1)
    for b in range(blocks):
        total = jnp.concatenate(
            [jnp.sum(row_acc[b, c], axis=1, keepdims=True) for c in range(3)]
            + [jnp.zeros((width, 5), jnp.float32)],
            axis=1,
        )
        sums_ref[2 + b] = -total.T
    for b in range(blocks):
        scatter(me, b, 2 + b)

    def collect(dest, carry):
        for c in range(3):
            total = jnp.zeros((high, LANES), jnp.float32)
            for slot, by in enumerate((0, tiles - 1, 1, tiles - tiles // 2)):
                tile = lax.rem(dest + by, tiles)
                total = total + joined_ref[tile, c, slot * high : (slot + 1) * high]
            part = out_ref.shape[2]
            for f in range(out_ref.shape[1]):
                first = f * part % high
                out_ref[dest, f, :, c * LANES : (c + 1) * LANES] = total[first : first + part]
        return carry

    lax.fori_loop(0, tiles, collect, 0, unroll=min(tiles, 8))


def sum_kernel(got_ref, out_ref):
    out_ref[...] = jnp.sum(got_ref[...], axis=0)


def last_kernel(parity_ref, mine_ref, other_ref, out_ref):
    part = mine_ref.shape[0]
    even = parity_ref[0] == 0
    mine, other = mine_ref[...], other_ref[...]
    halves = (jnp.where(even, mine, other), jnp.where(even, other, mine))
    for i, half in enumerate(halves):
        for r in range(part):
            h = i * part + r
            for c in range(3):
                out_ref[c : c + 1, h * LANES : (h + 1) * LANES] = half[
                    r : r + 1, c * LANES : (c + 1) * LANES
                ]


def per_device(
    panel_geometry,
    adjoint,
    strengths,
    pair_target,
    pair_owner,
    pair_source,
    pair_order,
    pair_count,
    corner_vertex,
):
    tiles = lax.axis_size("tiles")
    far = lax.axis_size("far")
    blocks, _, width = panel_geometry.shape
    high = blocks * width // LANES
    parity = lax.axis_index("far").astype(jnp.int32) & 1
    me = lax.axis_index("tiles").astype(jnp.int32).reshape(1)
    parity = parity.reshape(1)
    swap = [(f ^ 1, f) for f in range(far)]
    smem = pl.BlockSpec(memory_space=SMEM)
    vmem = pl.BlockSpec(memory_space=VMEM)
    params = pltpu.CompilerParams(vmem_limit_bytes=LIMIT)
    geometry = panel_geometry.transpose(1, 0, 2)
    packed = pl.pallas_call(
        pack_kernel,
        out_shape=jax.ShapeDtypeStruct((tiles, blocks, 4, 2 * width), jnp.float32),
        in_specs=[smem] * 2 + [vmem] * 3,
        out_specs=vmem,
    )(me, parity, geometry, strengths, corner_vertex)
    got = lax.all_to_all(packed, "tiles", split_axis=0, concat_axis=0, tiled=True)
    partner = lax.ppermute(adjoint, "far", swap)
    pairs = pair_target.shape[0]
    info = pl.pallas_call(
        lambda *refs: sort_kernel(*refs[:-1], blocks, refs[-1]),
        out_shape=jax.ShapeDtypeStruct((1, -(-(HEAD + pairs // 2 + SPARE + 1) // LANES) * LANES), jnp.int32),
        in_specs=[smem] * 2 + [vmem] * 4 + [smem],
        out_specs=vmem,
        cost_estimate=pl.CostEstimate(flops=4000000, bytes_accessed=900000, transcendentals=0),
    )(
        me,
        parity,
        pair_target.reshape(1, pairs),
        pair_owner.reshape(1, pairs),
        pair_source.reshape(1, pairs),
        pair_order.reshape(1, pairs),
        pair_count,
    )
    centre, left = pl.pallas_call(
        prep_kernel,
        out_shape=(
            jax.ShapeDtypeStruct((blocks, 3, width, width), jnp.float32),
            jax.ShapeDtypeStruct((blocks, width, 56), jnp.bfloat16),
        ),
        compiler_params=params,
        cost_estimate=pl.CostEstimate(flops=4000000, bytes_accessed=900000, transcendentals=0),
    )(geometry, adjoint, partner)
    got, info, left = lax.optimization_barrier((got, info, left))
    other = lax.ppermute(got, "far", swap)
    partial = pl.pallas_call(
        pair_kernel,
        out_shape=jax.ShapeDtypeStruct((tiles, far, high // 2, 3 * LANES), jnp.float32),
        in_specs=[smem] + [vmem] * 4,
        out_specs=vmem,
        scratch_shapes=[
            VMEM((2, width, 4 * width), jnp.float32),
            VMEM((blocks, 3, width, width), jnp.float32),
            VMEM((2 + blocks, 8, width), jnp.float32),
            VMEM((tiles, 3, 4 * high, LANES), jnp.float32),
            VMEM((tiles, 2 * blocks, 4, width), jnp.float32),
        ],
        compiler_params=params,
    )(info, centre, left, got, other)
    partial = partial.reshape(tiles * far, high // 2, 3 * LANES)
    shares = lax.all_to_all(partial, ("tiles", "far"), split_axis=0, concat_axis=0, tiled=True)
    mine = pl.pallas_call(
        sum_kernel,
        out_shape=jax.ShapeDtypeStruct((high // 2, 3 * LANES), jnp.float32),
        compiler_params=params,
    )(shares)
    other = lax.ppermute(mine, "far", swap)
    return pl.pallas_call(
        last_kernel,
        out_shape=jax.ShapeDtypeStruct((3, blocks * width), jnp.float32),
        in_specs=[smem, vmem, vmem],
        out_specs=vmem,
        compiler_params=params,
    )(parity, mine, other)


def solution(mesh):
    placed = (
        P("tiles", None, None),
        P("tiles", "far", None),
        P("tiles", "far", None),
        P("tiles"),
        P("tiles", None),
        P("tiles"),
        P("tiles"),
        P("tiles"),
        P("tiles", None, None),
    )
    return jax.shard_map(
        per_device, mesh=mesh, in_specs=placed, out_specs=P(None, "tiles"), check_vma=False
    )
```

```python
import jax
import jax.numpy as jnp
from jax import lax
from jax.experimental import pallas as pl
from jax.experimental.pallas import tpu as pltpu
from jax.sharding import PartitionSpec as P

SMEM = pltpu.SMEM
VMEM = pltpu.VMEM
LANES = 128
HEAD = 5
RING = 4
AHEAD = 2
LIMIT = 48 * 1024 * 1024


def pack_kernel(me_ref, parity_ref, geom_ref, strength_ref, corner_ref, out_ref):
    tiles, blocks, _, _ = out_ref.shape
    width = strength_ref.shape[2]
    shift = (blocks * width).bit_length() - 1
    me = me_ref[0]
    even = parity_ref[0] == 0
    shapes = []
    for b in range(blocks):
        vertex = corner_ref[b]
        offset = (vertex >> shift) - me
        offset = jnp.where(offset < 0, offset + tiles, offset)
        slot = jnp.where(
            offset == 0,
            0,
            jnp.where(offset == 1, 1, jnp.where(offset == tiles - 1, 2, 3)),
        )
        place = ((slot << shift) + (vertex & ((1 << shift) - 1))).astype(jnp.float32)
        span = float(4 << shift)
        for half in range(2):
            code = place[2 * half : 2 * half + 1] * span + place[2 * half + 1 : 2 * half + 2]
            rows = [geom_ref[3 * half + c, b : b + 1] for c in range(3)] + [code]
            shapes.append(jnp.concatenate(rows, axis=0))
    for b in range(blocks):
        shape = jnp.where(even, shapes[b], shapes[blocks + b])
        block = jnp.concatenate([strength_ref[b].astype(jnp.float32), shape], axis=1)
        for t in range(tiles):
            out_ref[t, b] = block


def split3(value):
    first = value.astype(jnp.bfloat16).astype(jnp.float32)
    rest = value - first
    second = rest.astype(jnp.bfloat16).astype(jnp.float32)
    return first, second, rest - second


def sort_kernel(
    me_ref,
    parity_ref,
    target_ref,
    owner_ref,
    source_ref,
    order_ref,
    count_ref,
    blocks,
    info_ref,
):
    pairs = order_ref.shape[1]
    lanes = info_ref.shape[1]
    bits = (blocks - 1).bit_length()
    parity = parity_ref[0]
    order = order_ref[...]
    place = lax.broadcasted_iota(jnp.int32, (1, pairs), 1)
    live = place < count_ref[0]
    word = (owner_ref[...] << bits | source_ref[...]) << bits | target_ref[...]
    word = (word << 2 | order).astype(jnp.float32)
    key = jnp.where(live, (3 - order) * pairs + place, 3 * pairs + place).astype(jnp.float32)
    across = lax.broadcasted_iota(jnp.int32, (pairs, pairs), 1)
    down = lax.broadcasted_iota(jnp.int32, (pairs, pairs), 0)

    def upright(row):
        spread = jnp.broadcast_to(row, (pairs, pairs))
        return jnp.sum(jnp.where(across == down, spread, 0.0), axis=1, keepdims=True)

    key_down = upright(key)
    rank = jnp.sum(jnp.where(key < key_down, 1.0, 0.0), axis=1, keepdims=True).astype(jnp.int32)
    kept = (rank & 1 == parity) & (rank < count_ref[0])
    at = jnp.where(kept, HEAD + (rank >> 1), -1)
    wide_lane = lax.broadcasted_iota(jnp.int32, (pairs, lanes), 1)
    words = jnp.sum(jnp.where(wide_lane == at, upright(word), 0.0), axis=0, keepdims=True)
    info = words.astype(jnp.int32)
    lane = lax.broadcasted_iota(jnp.int32, (1, lanes), 1)
    info = jnp.where(lane == 0, me_ref[0], jnp.where(lane == 4, parity, info))
    for i in range(3):
        upto = jnp.where(live & (order >= 3 - i), 1.0, 0.0)
        total = jnp.sum(upto, axis=1, keepdims=True).astype(jnp.int32)
        steps = (((total + 1 - parity) >> 1) + RING - 1) // RING
        info = jnp.where(lane == i + 1, steps, info)
    info_ref[...] = info


def prep_kernel(geom_ref, adjoint_ref, partner_ref, centre_ref, left_ref):
    blocks, _, width = adjoint_ref.shape
    for b in range(blocks):
        point = jnp.concatenate([geom_ref[c, b : b + 1] for c in range(3)], axis=0)
        rows = [point, jnp.ones((1, width), jnp.float32)]
        rows += [jnp.sum(point * point, axis=0, keepdims=True)]
        rows += [jnp.zeros((3, width), jnp.float32)]
        x1, x2, x3 = split3(jnp.concatenate(rows, axis=0))
        values = [adjoint_ref[b].astype(jnp.float32), partner_ref[b].astype(jnp.float32)]
        rows = [x1, x1, x1, x2, x2, x3] + values
        left_ref[b] = jnp.concatenate(rows, axis=0).T.astype(jnp.bfloat16)
        for c in range(3):
            centre_ref[b, c] = jnp.broadcast_to(point[c : c + 1], (width, width)).T


def pair_kernel(
    info_ref,
    centre_ref,
    left_ref,
    mine_ref,
    other_ref,
    out_ref,
    product_ref,
    row_acc,
    sums_ref,
    joined_ref,
    shape_ref,
):
    tiles, blocks, _, _ = mine_ref.shape
    width = centre_ref.shape[3]
    bits = (blocks - 1).bit_length()
    me = info_ref[0, 0]
    even = info_ref[0, 4] == 0

    def settle(tile, carry):
        for b in range(blocks):
            mine = mine_ref[tile, b, :, width : 2 * width]
            other = other_ref[tile, b, :, width : 2 * width]
            shape_ref[tile, b] = jnp.where(even, mine, other)
            shape_ref[tile, blocks + b] = jnp.where(even, other, mine)
        return carry

    lax.fori_loop(0, tiles, settle, 0, unroll=min(tiles, 8))
    sums_ref[...] = jnp.zeros(sums_ref.shape, jnp.float32)
    joined_ref[...] = jnp.zeros(joined_ref.shape, jnp.float32)
    row_acc[...] = jnp.zeros(row_acc.shape, jnp.float32)
    blank = jnp.zeros((4, width), jnp.float32)
    row_ids = lax.broadcasted_iota(jnp.int32, (8, width), 0)

    def reach_of(order):
        return 0.25 * jnp.where(
            order == 3, 0.7745966692414834, jnp.where(order == 2, 0.5773502691896258, 0.0)
        )

    def read(k):
        word = info_ref[0, HEAD + k]
        inner = word >> 2
        outer = inner >> bits
        return inner & (blocks - 1), outer >> bits, outer & (blocks - 1), word & 3

    def multiply(k, slot, nodes):
        target, owner, source, order = read(k)
        third = order == 3
        alive = jnp.where(order > 0, 1.0, 0.0).astype(jnp.float32)
        reach = reach_of(order)
        scale_mid = jnp.where(third, (4.0 / 9.0 / 512.0) ** (-2.0 / 3.0), 0.0)
        scale_side = jnp.where(
            third, (5.0 / 18.0 / 512.0) ** (-2.0 / 3.0), (0.5 / 512.0) ** (-2.0 / 3.0)
        )
        floor_mid = jnp.where(third, 0.0625 * (4.0 / 9.0 / 512.0) ** (-2.0 / 3.0), 3.0e38)
        floor_side = 0.0625 * scale_side
        point = shape_ref[owner, 2 * source]
        extent = shape_ref[owner, 2 * source + 1] * reach
        inside = row_ids < 3
        point = jnp.where(inside, jnp.concatenate([point, blank], axis=0), 0.0)
        extent = jnp.where(inside, jnp.concatenate([extent, blank], axis=0), 0.0)
        values = [ref[owner, source, :, 0:width] * alive for ref in (mine_ref, other_ref)]
        empty = jnp.zeros((8, width), jnp.float32)
        quadrature = (
            (point + extent, scale_side, floor_side),
            (point - extent, scale_side, floor_side),
            (point, scale_mid, floor_mid),
        )
        columns = []
        for node, scale, floor in quadrature[:nodes]:
            norm = jnp.sum(node * node, axis=0, keepdims=True) * scale + floor
            rows = jnp.where(
                row_ids == 3,
                norm,
                jnp.where(row_ids == 4, scale, node * (-2.0 * scale)),
            )
            p1, p2, p3 = split3(rows)
            columns.append(jnp.concatenate([p1, p2, p3, p1, p2, p1, empty], axis=0))
        columns.insert(1, jnp.concatenate([empty] * 6 + values, axis=0))
        product_ref[slot, :, 0 : (nodes + 1) * width] = jnp.dot(
            left_ref[target],
            jnp.concatenate(columns, axis=1).astype(jnp.bfloat16),
            preferred_element_type=jnp.float32,
        )

    def one_pair(k, slot, nodes):
        target, owner, source, order = read(k)
        reach = reach_of(order)
        eight = (8, width)
        point = [jnp.broadcast_to(shape_ref[owner, 2 * source, c : c + 1], eight) for c in range(3)]
        extent = [
            jnp.broadcast_to(shape_ref[owner, 2 * source + 1, c : c + 1], eight) * reach
            for c in range(3)
        ]
        columns = [jnp.zeros(eight, jnp.float32) for _ in range(3)]
        for start in range(0, width, 8):
            rows = slice(start, start + 8)
            sums = [row_acc[target, c, rows] for c in range(3)]

            def cubed(part):
                i = lax.rsqrt(product_ref[slot, rows, part * width : (part + 1) * width])
                return i * i * i

            coupling = product_ref[slot, rows, width : 2 * width]
            f_plus = cubed(0)
            if nodes == 1:
                even = (coupling + coupling) * f_plus
            else:
                f_minus = cubed(2)
                both = f_plus + f_minus
                even = coupling * (both + cubed(3) if nodes == 3 else both)
                odd = coupling * (f_plus - f_minus)
            for c in range(3):
                pulled = even * (centre_ref[target, c, rows] - point[c])
                if nodes > 1:
                    pulled = pulled - odd * extent[c]
                columns[c] = columns[c] + pulled
                row_acc[target, c, rows] = sums[c] + pulled
        for c in range(3):
            sums_ref[slot, c : c + 1] = jnp.sum(columns[c], axis=0, keepdims=True)

    high = blocks * width // LANES
    keys = 4 * high
    shift = (blocks * width).bit_length() + 1
    key_ids = lax.broadcasted_iota(jnp.int32, (keys, width), 0).astype(jnp.bfloat16)
    lane_ids = lax.broadcasted_iota(jnp.int32, (LANES, width), 0).astype(jnp.bfloat16)
    zero = jnp.zeros((keys, width), jnp.bfloat16)
    one = jnp.ones((keys, width), jnp.bfloat16)

    def wide(row):
        return jnp.broadcast_to(row, (keys, width))

    def narrow(value):
        return value.astype(jnp.float32).astype(jnp.bfloat16)

    def scatter(tile, b, slot):
        spread = []
        for c in range(3):
            grad = wide(sums_ref[slot, c : c + 1])
            upper = grad.astype(jnp.bfloat16)
            spread += [upper, (grad - upper.astype(jnp.float32)).astype(jnp.bfloat16)]
        result = None
        for half in range(2):
            parts = []
            hots = []
            code = wide(shape_ref[tile, 2 * b + half, 3:4]).astype(jnp.int32)
            for place in (code >> shift, code & ((1 << shift) - 1)):
                mask = key_ids == narrow(place >> 7)
                low = narrow(place & (LANES - 1))
                parts.append(jnp.concatenate([jnp.where(mask, s, zero) for s in spread], axis=0))
                hots.append(
                    jnp.concatenate(
                        [
                            jnp.where(lane_ids[g : g + keys] == low, one, zero)
                            for g in range(0, LANES, keys)
                        ],
                        axis=0,
                    )
                )
            product = lax.dot_general(
                jnp.concatenate(parts, axis=1),
                jnp.concatenate(hots, axis=1),
                (((1,), (1,)), ((), ())),
                preferred_element_type=jnp.float32,
            )
            result = product if result is None else result + product
        before = [joined_ref[tile, c] for c in range(3)]
        for c in range(3):
            joined_ref[tile, c] = (
                before[c]
                + result[2 * c * keys : (2 * c + 1) * keys]
                + result[(2 * c + 1) * keys : (2 * c + 2) * keys]
            )

    def scatter_pair(k, slot):
        _, owner, source, _ = read(k)
        scatter(owner, source, slot)

    def some_pairs(nodes):
        def body(step, carry):
            for slot in range(RING):
                k = RING * step + slot
                multiply(k + AHEAD, (slot + AHEAD) % RING, nodes)
                scatter_pair(k - 1, (slot - 1) % RING)
                one_pair(k, slot, nodes)
            return carry

        return body

    for k in range(AHEAD):
        multiply(k, k, 3)
    lax.fori_loop(0, info_ref[0, 1], some_pairs(3), 0)
    lax.fori_loop(info_ref[0, 1], info_ref[0, 2], some_pairs(2), 0)
    lax.fori_loop(info_ref[0, 2], info_ref[0, 3], some_pairs(1), 0)
    scatter_pair(RING * info_ref[0, 3] - 1, RING - 1)
    for b in range(blocks):
        total = jnp.concatenate(
            [jnp.sum(row_acc[b, c], axis=1, keepdims=True) for c in range(3)]
            + [jnp.zeros((width, 5), jnp.float32)],
            axis=1,
        )
        sums_ref[RING + b] = -total.T
    for b in range(blocks):
        scatter(me, b, RING + b)

    def collect(dest, carry):
        for c in range(3):
            total = jnp.zeros((high, LANES), jnp.float32)
            for slot, by in enumerate((0, tiles - 1, 1, tiles - tiles // 2)):
                tile = lax.rem(dest + by, tiles)
                total = total + joined_ref[tile, c, slot * high : (slot + 1) * high]
            part = out_ref.shape[2]
            for f in range(out_ref.shape[1]):
                first = f * part % high
                out_ref[dest, f, :, c * LANES : (c + 1) * LANES] = total[first : first + part]
        return carry

    lax.fori_loop(0, tiles, collect, 0, unroll=min(tiles, 8))


def sum_kernel(got_ref, out_ref):
    out_ref[...] = jnp.sum(got_ref[...], axis=0)


def last_kernel(parity_ref, mine_ref, other_ref, out_ref):
    part = mine_ref.shape[0]
    even = parity_ref[0] == 0
    mine, other = mine_ref[...], other_ref[...]
    halves = (jnp.where(even, mine, other), jnp.where(even, other, mine))
    for i, half in enumerate(halves):
        for r in range(part):
            h = i * part + r
            for c in range(3):
                out_ref[c : c + 1, h * LANES : (h + 1) * LANES] = half[
                    r : r + 1, c * LANES : (c + 1) * LANES
                ]


def per_device(
    panel_geometry,
    adjoint,
    strengths,
    pair_target,
    pair_owner,
    pair_source,
    pair_order,
    pair_count,
    corner_vertex,
):
    tiles = lax.axis_size("tiles")
    far = lax.axis_size("far")
    blocks, _, width = panel_geometry.shape
    high = blocks * width // LANES
    parity = lax.axis_index("far").astype(jnp.int32) & 1
    me = lax.axis_index("tiles").astype(jnp.int32).reshape(1)
    parity = parity.reshape(1)
    swap = [(f ^ 1, f) for f in range(far)]
    smem = pl.BlockSpec(memory_space=SMEM)
    vmem = pl.BlockSpec(memory_space=VMEM)
    params = pltpu.CompilerParams(vmem_limit_bytes=LIMIT)
    geometry = panel_geometry.transpose(1, 0, 2)
    packed = pl.pallas_call(
        pack_kernel,
        out_shape=jax.ShapeDtypeStruct((tiles, blocks, 4, 2 * width), jnp.float32),
        in_specs=[smem] * 2 + [vmem] * 3,
        out_specs=vmem,
    )(me, parity, geometry, strengths, corner_vertex)
    got = lax.all_to_all(packed, "tiles", split_axis=0, concat_axis=0, tiled=True)
    partner = lax.ppermute(adjoint, "far", swap)
    pairs = pair_target.shape[0]
    info = pl.pallas_call(
        lambda *refs: sort_kernel(*refs[:-1], blocks, refs[-1]),
        out_shape=jax.ShapeDtypeStruct((1, -(-(HEAD + pairs // 2 + 1 + RING + AHEAD) // LANES) * LANES), jnp.int32),
        in_specs=[smem] * 2 + [vmem] * 4 + [smem],
        out_specs=vmem,
        cost_estimate=pl.CostEstimate(flops=4000000, bytes_accessed=900000, transcendentals=0),
    )(
        me,
        parity,
        pair_target.reshape(1, pairs),
        pair_owner.reshape(1, pairs),
        pair_source.reshape(1, pairs),
        pair_order.reshape(1, pairs),
        pair_count,
    )
    centre, left = pl.pallas_call(
        prep_kernel,
        out_shape=(
            jax.ShapeDtypeStruct((blocks, 3, width, width), jnp.float32),
            jax.ShapeDtypeStruct((blocks, width, 56), jnp.bfloat16),
        ),
        compiler_params=params,
        cost_estimate=pl.CostEstimate(flops=4000000, bytes_accessed=900000, transcendentals=0),
    )(geometry, adjoint, partner)
    got, info, left = lax.optimization_barrier((got, info, left))
    other = lax.ppermute(got, "far", swap)
    partial = pl.pallas_call(
        pair_kernel,
        out_shape=jax.ShapeDtypeStruct((tiles, far, high // 2, 3 * LANES), jnp.float32),
        in_specs=[smem] + [vmem] * 4,
        out_specs=vmem,
        scratch_shapes=[
            VMEM((RING, width, 4 * width), jnp.float32),
            VMEM((blocks, 3, width, width), jnp.float32),
            VMEM((RING + blocks, 8, width), jnp.float32),
            VMEM((tiles, 3, 4 * high, LANES), jnp.float32),
            VMEM((tiles, 2 * blocks, 4, width), jnp.float32),
        ],
        compiler_params=params,
    )(info, centre, left, got, other)
    partial = partial.reshape(tiles * far, high // 2, 3 * LANES)
    shares = lax.all_to_all(partial, ("tiles", "far"), split_axis=0, concat_axis=0, tiled=True)
    mine = pl.pallas_call(
        sum_kernel,
        out_shape=jax.ShapeDtypeStruct((high // 2, 3 * LANES), jnp.float32),
        compiler_params=params,
    )(shares)
    other = lax.ppermute(mine, "far", swap)
    return pl.pallas_call(
        last_kernel,
        out_shape=jax.ShapeDtypeStruct((3, blocks * width), jnp.float32),
        in_specs=[smem, vmem, vmem],
        out_specs=vmem,
        compiler_params=params,
    )(parity, mine, other)


def solution(mesh):
    placed = (
        P("tiles", None, None),
        P("tiles", "far", None),
        P("tiles", "far", None),
        P("tiles"),
        P("tiles", None),
        P("tiles"),
        P("tiles"),
        P("tiles"),
        P("tiles", None, None),
    )
    return jax.shard_map(
        per_device, mesh=mesh, in_specs=placed, out_specs=P(None, "tiles"), check_vma=False
    )
```

```python
import jax
import jax.numpy as jnp
from jax import lax
from jax.experimental import pallas as pl
from jax.experimental.pallas import tpu as pltpu
from jax.sharding import PartitionSpec as P

SMEM = pltpu.SMEM
VMEM = pltpu.VMEM
LANES = 128
HEAD = 5
SCALE_MID = (4.0 / 9.0 / 512.0) ** (-2.0 / 3.0)
SCALE_SIDE = (5.0 / 18.0 / 512.0) ** (-2.0 / 3.0)
SCALE_TWO = (0.5 / 512.0) ** (-2.0 / 3.0)
SPARE = 2
LIMIT = 48 * 1024 * 1024


def pack_kernel(me_ref, parity_ref, geom_ref, strength_ref, corner_ref, out_ref):
    tiles, blocks, _, _ = out_ref.shape
    width = strength_ref.shape[2]
    shift = (blocks * width).bit_length() - 1
    me = me_ref[0]
    even = parity_ref[0] == 0
    shapes = []
    for b in range(blocks):
        vertex = corner_ref[b]
        offset = (vertex >> shift) - me
        offset = jnp.where(offset < 0, offset + tiles, offset)
        slot = jnp.where(
            offset == 0,
            0,
            jnp.where(offset == 1, 1, jnp.where(offset == tiles - 1, 2, 3)),
        )
        place = ((slot << shift) + (vertex & ((1 << shift) - 1))).astype(jnp.float32)
        span = float(4 << shift)
        for half in range(2):
            code = place[2 * half : 2 * half + 1] * span + place[2 * half + 1 : 2 * half + 2]
            rows = [geom_ref[3 * half + c, b : b + 1] for c in range(3)] + [code]
            shapes.append(jnp.concatenate(rows, axis=0))
    for b in range(blocks):
        shape = jnp.where(even, shapes[b], shapes[blocks + b])
        block = jnp.concatenate([strength_ref[b].astype(jnp.float32), shape], axis=1)
        for t in range(tiles):
            out_ref[t, b] = block


def split3(value):
    first = value.astype(jnp.bfloat16).astype(jnp.float32)
    rest = value - first
    second = rest.astype(jnp.bfloat16).astype(jnp.float32)
    return first, second, rest - second


def sort_kernel(
    me_ref,
    parity_ref,
    target_ref,
    owner_ref,
    source_ref,
    order_ref,
    count_ref,
    blocks,
    info_ref,
):
    pairs = order_ref.shape[1]
    lanes = info_ref.shape[1]
    bits = (blocks - 1).bit_length()
    parity = parity_ref[0]
    order = order_ref[...]
    place = lax.broadcasted_iota(jnp.int32, (1, pairs), 1)
    live = place < count_ref[0]
    word = (owner_ref[...] << bits | source_ref[...]) << bits | target_ref[...]
    word = (word << 2 | order).astype(jnp.float32)
    key = jnp.where(live, (3 - order) * pairs + place, 3 * pairs + place).astype(jnp.float32)
    across = lax.broadcasted_iota(jnp.int32, (pairs, pairs), 1)
    down = lax.broadcasted_iota(jnp.int32, (pairs, pairs), 0)

    def upright(row):
        spread = jnp.broadcast_to(row, (pairs, pairs))
        return jnp.sum(jnp.where(across == down, spread, 0.0), axis=1, keepdims=True)

    key_down = upright(key)
    rank = jnp.sum(jnp.where(key < key_down, 1.0, 0.0), axis=1, keepdims=True).astype(jnp.int32)
    kept = (rank & 1 == parity) & (rank < count_ref[0])
    at = jnp.where(kept, HEAD + (rank >> 1), -1)
    wide_lane = lax.broadcasted_iota(jnp.int32, (pairs, lanes), 1)
    words = jnp.sum(jnp.where(wide_lane == at, upright(word), 0.0), axis=0, keepdims=True)
    info = words.astype(jnp.int32)
    lane = lax.broadcasted_iota(jnp.int32, (1, lanes), 1)
    info = jnp.where(lane == 0, me_ref[0], jnp.where(lane == 4, parity, info))
    for i in range(3):
        upto = jnp.where(live & (order >= 3 - i), 1.0, 0.0)
        total = jnp.sum(upto, axis=1, keepdims=True).astype(jnp.int32)
        info = jnp.where(lane == i + 1, (((total + 1 - parity) >> 1) + 1) >> 1, info)
    info_ref[...] = info


def prep_kernel(geom_ref, adjoint_ref, partner_ref, centre_ref, left_ref):
    blocks, _, width = adjoint_ref.shape
    for b in range(blocks):
        point = jnp.concatenate([geom_ref[c, b : b + 1] for c in range(3)], axis=0)
        rows = [point, jnp.ones((1, width), jnp.float32)]
        rows += [jnp.sum(point * point, axis=0, keepdims=True)]
        rows += [jnp.zeros((3, width), jnp.float32)]
        x1, x2, x3 = split3(jnp.concatenate(rows, axis=0))
        values = [adjoint_ref[b].astype(jnp.float32), partner_ref[b].astype(jnp.float32)]
        rows = [x1, x1, x1, x2, x2, x3] + values
        left_ref[b] = jnp.concatenate(rows, axis=0).T.astype(jnp.bfloat16)
        for c in range(3):
            centre_ref[b, c] = jnp.broadcast_to(point[c : c + 1], (width, width)).T


def pair_kernel(
    info_ref,
    centre_ref,
    left_ref,
    mine_ref,
    other_ref,
    out_ref,
    product_ref,
    row_acc,
    sums_ref,
    joined_ref,
    shape_ref,
):
    tiles, blocks, _, _ = mine_ref.shape
    width = centre_ref.shape[3]
    bits = (blocks - 1).bit_length()
    me = info_ref[0, 0]
    even = info_ref[0, 4] == 0

    def settle(tile, carry):
        for b in range(blocks):
            mine = mine_ref[tile, b, :, width : 2 * width]
            other = other_ref[tile, b, :, width : 2 * width]
            shape_ref[tile, b] = jnp.where(even, mine, other)
            shape_ref[tile, blocks + b] = jnp.where(even, other, mine)
        return carry

    lax.fori_loop(0, tiles, settle, 0, unroll=min(tiles, 8))
    sums_ref[...] = jnp.zeros(sums_ref.shape, jnp.float32)
    joined_ref[...] = jnp.zeros(joined_ref.shape, jnp.float32)
    row_acc[...] = jnp.zeros(row_acc.shape, jnp.float32)
    blank = jnp.zeros((4, width), jnp.float32)
    row_ids = lax.broadcasted_iota(jnp.int32, (8, width), 0)

    def reach_of(order):
        return 0.25 * jnp.where(
            order == 3, 0.7745966692414834, jnp.where(order == 2, 0.5773502691896258, 0.0)
        )

    def read(k):
        word = info_ref[0, HEAD + k]
        inner = word >> 2
        outer = inner >> bits
        return inner & (blocks - 1), outer >> bits, outer & (blocks - 1), word & 3

    def scale_of(order):
        return jnp.where(order == 3, SCALE_SIDE, SCALE_TWO)

    def multiply(k, slot):
        target, owner, source, order = read(k)
        alive = jnp.where(order > 0, 1.0, 0.0).astype(jnp.float32)
        scale = scale_of(order)
        inside = row_ids < 3
        point = jnp.concatenate([shape_ref[owner, 2 * source], blank], axis=0)
        extent = jnp.concatenate([shape_ref[owner, 2 * source + 1], blank], axis=0)
        node = jnp.where(inside, point + extent * reach_of(order), 0.0)
        norm = (jnp.sum(node * node, axis=0, keepdims=True) + 0.0625) * scale
        rows = jnp.where(
            row_ids == 3,
            norm,
            jnp.where(row_ids == 4, scale, node * (-2.0 * scale)),
        )
        p1, p2, p3 = split3(rows)
        empty = jnp.zeros((8, width), jnp.float32)
        values = [ref[owner, source, :, 0:width] * alive for ref in (mine_ref, other_ref)]
        columns = [
            jnp.concatenate([p1, p2, p3, p1, p2, p1, empty], axis=0),
            jnp.concatenate([empty] * 6 + values, axis=0),
        ]
        product_ref[slot] = jnp.dot(
            left_ref[target],
            jnp.concatenate(columns, axis=1).astype(jnp.bfloat16),
            preferred_element_type=jnp.float32,
        )

    def one_pair(k, slot, nodes):
        target, owner, source, order = read(k)
        reach = reach_of(order)
        eight = (8, width)
        point = [jnp.broadcast_to(shape_ref[owner, 2 * source, c : c + 1], eight) for c in range(3)]
        extent = [
            jnp.broadcast_to(shape_ref[owner, 2 * source + 1, c : c + 1], eight) * reach
            for c in range(3)
        ]
        gap = [e * (4.0 * scale_of(order)) for e in extent]
        third = order == 3
        ratio = jnp.where(third, SCALE_MID / SCALE_SIDE / 2.0, 0.0)
        drop = extent[0] * extent[0] + extent[1] * extent[1] + extent[2] * extent[2]
        drop = jnp.where(third, drop * SCALE_MID, -3.0e38)
        columns = [jnp.zeros(eight, jnp.float32) for _ in range(3)]
        for start in range(0, width, 8):
            rows = slice(start, start + 8)
            sums = [row_acc[target, c, rows] for c in range(3)]
            away = [centre_ref[target, c, rows] - point[c] for c in range(3)]

            def cubed(squared):
                i = lax.rsqrt(squared)
                return i * i * i

            plus = product_ref[slot, rows, 0:width]
            coupling = product_ref[slot, rows, width : 2 * width]
            f_plus = cubed(plus)
            if nodes == 1:
                even = (coupling + coupling) * f_plus
            else:
                minus = plus + (away[0] * gap[0] + away[1] * gap[1] + away[2] * gap[2])
                f_minus = cubed(minus)
                total = f_plus + f_minus
                if nodes == 3:
                    total = total + cubed((plus + minus) * ratio - drop)
                even = coupling * total
                odd = coupling * (f_plus - f_minus)
            for c in range(3):
                pulled = even * away[c]
                if nodes > 1:
                    pulled = pulled - odd * extent[c]
                columns[c] = columns[c] + pulled
                row_acc[target, c, rows] = sums[c] + pulled
        for c in range(3):
            sums_ref[slot, c : c + 1] = jnp.sum(columns[c], axis=0, keepdims=True)

    high = blocks * width // LANES
    keys = 4 * high
    shift = (blocks * width).bit_length() + 1
    key_ids = lax.broadcasted_iota(jnp.int32, (keys, width), 0).astype(jnp.bfloat16)
    lane_ids = lax.broadcasted_iota(jnp.int32, (LANES, width), 0).astype(jnp.bfloat16)
    zero = jnp.zeros((keys, width), jnp.bfloat16)
    one = jnp.ones((keys, width), jnp.bfloat16)

    def wide(row):
        return jnp.broadcast_to(row, (keys, width))

    def narrow(value):
        return value.astype(jnp.float32).astype(jnp.bfloat16)

    def spread_out(tile, b, slot, result):
        spread = []
        for c in range(3):
            grad = wide(sums_ref[slot, c : c + 1])
            upper = grad.astype(jnp.bfloat16)
            spread += [upper, (grad - upper.astype(jnp.float32)).astype(jnp.bfloat16)]
        for half in range(2):
            parts = []
            hots = []
            code = wide(shape_ref[tile, 2 * b + half, 3:4]).astype(jnp.int32)
            for place in (code >> shift, code & ((1 << shift) - 1)):
                mask = key_ids == narrow(place >> 7)
                low = narrow(place & (LANES - 1))
                parts.append(jnp.concatenate([jnp.where(mask, s, zero) for s in spread], axis=0))
                hots.append(
                    jnp.concatenate(
                        [
                            jnp.where(lane_ids[g : g + keys] == low, one, zero)
                            for g in range(0, LANES, keys)
                        ],
                        axis=0,
                    )
                )
            product = lax.dot_general(
                jnp.concatenate(parts, axis=1),
                jnp.concatenate(hots, axis=1),
                (((1,), (1,)), ((), ())),
                preferred_element_type=jnp.float32,
            )
            result = product if result is None else result + product
        return result

    def scatter(tile, places):
        result = None
        for b, slot in places:
            result = spread_out(tile, b, slot, result)
        before = [joined_ref[tile, c] for c in range(3)]
        for c in range(3):
            joined_ref[tile, c] = (
                before[c]
                + result[2 * c * keys : (2 * c + 1) * keys]
                + result[(2 * c + 1) * keys : (2 * c + 2) * keys]
            )

    def scatter_pair(k, slot):
        _, owner, source, _ = read(k)
        scatter(owner, [(source, slot)])

    def two_pairs(nodes):
        def body(step, carry):
            for slot in range(2):
                k = 2 * step + slot
                multiply(k + 1, 1 - slot)
                scatter_pair(k - 1, 1 - slot)
                one_pair(k, slot, nodes)
            return carry

        return body

    multiply(0, 0)
    lax.fori_loop(0, info_ref[0, 1], two_pairs(3), 0)
    lax.fori_loop(info_ref[0, 1], info_ref[0, 2], two_pairs(2), 0)
    lax.fori_loop(info_ref[0, 2], info_ref[0, 3], two_pairs(1), 0)
    scatter_pair(2 * info_ref[0, 3] - 1, 1)
    for b in range(blocks):
        total = jnp.concatenate(
            [jnp.sum(row_acc[b, c], axis=1, keepdims=True) for c in range(3)]
            + [jnp.zeros((width, 5), jnp.float32)],
            axis=1,
        )
        sums_ref[2 + b] = -total.T
    scatter(me, [(b, 2 + b) for b in range(blocks)])

    def collect(dest, carry):
        for c in range(3):
            total = jnp.zeros((high, LANES), jnp.float32)
            for slot, by in enumerate((0, tiles - 1, 1, tiles - tiles // 2)):
                tile = lax.rem(dest + by, tiles)
                total = total + joined_ref[tile, c, slot * high : (slot + 1) * high]
            part = out_ref.shape[2]
            for f in range(out_ref.shape[1]):
                first = f * part % high
                out_ref[dest, f, :, c * LANES : (c + 1) * LANES] = total[first : first + part]
        return carry

    lax.fori_loop(0, tiles, collect, 0, unroll=min(tiles, 8))


def sum_kernel(got_ref, out_ref):
    out_ref[...] = jnp.sum(got_ref[...], axis=0)


def last_kernel(parity_ref, mine_ref, other_ref, out_ref):
    part = mine_ref.shape[0]
    even = parity_ref[0] == 0
    mine, other = mine_ref[...], other_ref[...]
    halves = (jnp.where(even, mine, other), jnp.where(even, other, mine))
    for i, half in enumerate(halves):
        for r in range(part):
            h = i * part + r
            for c in range(3):
                out_ref[c : c + 1, h * LANES : (h + 1) * LANES] = half[
                    r : r + 1, c * LANES : (c + 1) * LANES
                ]


def per_device(
    panel_geometry,
    adjoint,
    strengths,
    pair_target,
    pair_owner,
    pair_source,
    pair_order,
    pair_count,
    corner_vertex,
):
    tiles = lax.axis_size("tiles")
    far = lax.axis_size("far")
    blocks, _, width = panel_geometry.shape
    high = blocks * width // LANES
    parity = lax.axis_index("far").astype(jnp.int32) & 1
    me = lax.axis_index("tiles").astype(jnp.int32).reshape(1)
    parity = parity.reshape(1)
    swap = [(f ^ 1, f) for f in range(far)]
    smem = pl.BlockSpec(memory_space=SMEM)
    vmem = pl.BlockSpec(memory_space=VMEM)
    params = pltpu.CompilerParams(vmem_limit_bytes=LIMIT)
    geometry = panel_geometry.transpose(1, 0, 2)
    packed = pl.pallas_call(
        pack_kernel,
        out_shape=jax.ShapeDtypeStruct((tiles, blocks, 4, 2 * width), jnp.float32),
        in_specs=[smem] * 2 + [vmem] * 3,
        out_specs=vmem,
    )(me, parity, geometry, strengths, corner_vertex)
    got = lax.all_to_all(packed, "tiles", split_axis=0, concat_axis=0, tiled=True)
    partner = lax.ppermute(adjoint, "far", swap)
    pairs = pair_target.shape[0]
    info = pl.pallas_call(
        lambda *refs: sort_kernel(*refs[:-1], blocks, refs[-1]),
        out_shape=jax.ShapeDtypeStruct((1, -(-(HEAD + pairs // 2 + SPARE + 1) // LANES) * LANES), jnp.int32),
        in_specs=[smem] * 2 + [vmem] * 4 + [smem],
        out_specs=vmem,
        cost_estimate=pl.CostEstimate(flops=4000000, bytes_accessed=900000, transcendentals=0),
    )(
        me,
        parity,
        pair_target.reshape(1, pairs),
        pair_owner.reshape(1, pairs),
        pair_source.reshape(1, pairs),
        pair_order.reshape(1, pairs),
        pair_count,
    )
    centre, left = pl.pallas_call(
        prep_kernel,
        out_shape=(
            jax.ShapeDtypeStruct((blocks, 3, width, width), jnp.float32),
            jax.ShapeDtypeStruct((blocks, width, 56), jnp.bfloat16),
        ),
        compiler_params=params,
        cost_estimate=pl.CostEstimate(flops=4000000, bytes_accessed=900000, transcendentals=0),
    )(geometry, adjoint, partner)
    got, info, left = lax.optimization_barrier((got, info, left))
    other = lax.ppermute(got, "far", swap)
    partial = pl.pallas_call(
        pair_kernel,
        out_shape=jax.ShapeDtypeStruct((tiles, far, high // 2, 3 * LANES), jnp.float32),
        in_specs=[smem] + [vmem] * 4,
        out_specs=vmem,
        scratch_shapes=[
            VMEM((2, width, 2 * width), jnp.float32),
            VMEM((blocks, 3, width, width), jnp.float32),
            VMEM((2 + blocks, 8, width), jnp.float32),
            VMEM((tiles, 3, 4 * high, LANES), jnp.float32),
            VMEM((tiles, 2 * blocks, 4, width), jnp.float32),
        ],
        compiler_params=params,
    )(info, centre, left, got, other)
    partial = partial.reshape(tiles * far, high // 2, 3 * LANES)
    shares = lax.all_to_all(partial, ("tiles", "far"), split_axis=0, concat_axis=0, tiled=True)
    mine = pl.pallas_call(
        sum_kernel,
        out_shape=jax.ShapeDtypeStruct((high // 2, 3 * LANES), jnp.float32),
        compiler_params=params,
    )(shares)
    other = lax.ppermute(mine, "far", swap)
    return pl.pallas_call(
        last_kernel,
        out_shape=jax.ShapeDtypeStruct((3, blocks * width), jnp.float32),
        in_specs=[smem, vmem, vmem],
        out_specs=vmem,
        compiler_params=params,
    )(parity, mine, other)


def solution(mesh):
    placed = (
        P("tiles", None, None),
        P("tiles", "far", None),
        P("tiles", "far", None),
        P("tiles"),
        P("tiles", None),
        P("tiles"),
        P("tiles"),
        P("tiles"),
        P("tiles", None, None),
    )
    return jax.shard_map(
        per_device, mesh=mesh, in_specs=placed, out_specs=P(None, "tiles"), check_vma=False
    )
```

```python
import jax
import jax.numpy as jnp
from jax import lax
from jax.experimental import pallas as pl
from jax.experimental.pallas import tpu as pltpu
from jax.sharding import PartitionSpec as P

SMEM = pltpu.SMEM
VMEM = pltpu.VMEM
LANES = 128
HEAD = 5
SCALE_MID = (4.0 / 9.0 / 512.0) ** (-2.0 / 3.0)
SCALE_SIDE = (5.0 / 18.0 / 512.0) ** (-2.0 / 3.0)
SCALE_TWO = (0.5 / 512.0) ** (-2.0 / 3.0)
SPARE = 2
LIMIT = 48 * 1024 * 1024


def pack_kernel(me_ref, parity_ref, geom_ref, strength_ref, corner_ref, out_ref):
    tiles, blocks, _, _ = out_ref.shape
    width = strength_ref.shape[2]
    shift = (blocks * width).bit_length() - 1
    me = me_ref[0]
    even = parity_ref[0] == 0
    shapes = []
    for b in range(blocks):
        vertex = corner_ref[b]
        offset = (vertex >> shift) - me
        offset = jnp.where(offset < 0, offset + tiles, offset)
        slot = jnp.where(
            offset == 0,
            0,
            jnp.where(offset == 1, 1, jnp.where(offset == tiles - 1, 2, 3)),
        )
        place = ((slot << shift) + (vertex & ((1 << shift) - 1))).astype(jnp.float32)
        span = float(4 << shift)
        for half in range(2):
            code = place[2 * half : 2 * half + 1] * span + place[2 * half + 1 : 2 * half + 2]
            rows = [geom_ref[3 * half + c, b : b + 1] for c in range(3)] + [code]
            shapes.append(jnp.concatenate(rows, axis=0))
    for b in range(blocks):
        shape = jnp.where(even, shapes[b], shapes[blocks + b])
        block = jnp.concatenate([strength_ref[b].astype(jnp.float32), shape], axis=1)
        for t in range(tiles):
            out_ref[t, b] = block


def split3(value):
    first = value.astype(jnp.bfloat16).astype(jnp.float32)
    rest = value - first
    second = rest.astype(jnp.bfloat16).astype(jnp.float32)
    return first, second, rest - second


def sort_kernel(
    me_ref,
    parity_ref,
    target_ref,
    owner_ref,
    source_ref,
    order_ref,
    count_ref,
    blocks,
    info_ref,
):
    pairs = order_ref.shape[1]
    lanes = info_ref.shape[1]
    bits = (blocks - 1).bit_length()
    parity = parity_ref[0]
    order = order_ref[...]
    place = lax.broadcasted_iota(jnp.int32, (1, pairs), 1)
    live = place < count_ref[0]
    word = (owner_ref[...] << bits | source_ref[...]) << bits | target_ref[...]
    word = (word << 2 | order).astype(jnp.float32)
    key = jnp.where(live, (3 - order) * pairs + place, 3 * pairs + place).astype(jnp.float32)
    across = lax.broadcasted_iota(jnp.int32, (pairs, pairs), 1)
    down = lax.broadcasted_iota(jnp.int32, (pairs, pairs), 0)

    def upright(row):
        spread = jnp.broadcast_to(row, (pairs, pairs))
        return jnp.sum(jnp.where(across == down, spread, 0.0), axis=1, keepdims=True)

    key_down = upright(key)
    rank = jnp.sum(jnp.where(key < key_down, 1.0, 0.0), axis=1, keepdims=True).astype(jnp.int32)
    kept = (rank & 1 == parity) & (rank < count_ref[0])
    at = jnp.where(kept, HEAD + (rank >> 1), -1)
    wide_lane = lax.broadcasted_iota(jnp.int32, (pairs, lanes), 1)
    words = jnp.sum(jnp.where(wide_lane == at, upright(word), 0.0), axis=0, keepdims=True)
    info = words.astype(jnp.int32)
    lane = lax.broadcasted_iota(jnp.int32, (1, lanes), 1)
    info = jnp.where(lane == 0, me_ref[0], jnp.where(lane == 4, parity, info))
    for i in range(3):
        upto = jnp.where(live & (order >= 3 - i), 1.0, 0.0)
        total = jnp.sum(upto, axis=1, keepdims=True).astype(jnp.int32)
        info = jnp.where(lane == i + 1, (((total + 1 - parity) >> 1) + 1) >> 1, info)
    info_ref[...] = info


def prep_kernel(geom_ref, adjoint_ref, partner_ref, centre_ref, left_ref):
    blocks, _, width = adjoint_ref.shape
    for b in range(blocks):
        point = jnp.concatenate([geom_ref[c, b : b + 1] for c in range(3)], axis=0)
        rows = [point, jnp.ones((1, width), jnp.float32)]
        rows += [jnp.sum(point * point, axis=0, keepdims=True)]
        rows += [jnp.zeros((3, width), jnp.float32)]
        x1, x2, x3 = split3(jnp.concatenate(rows, axis=0))
        values = [adjoint_ref[b].astype(jnp.float32), partner_ref[b].astype(jnp.float32)]
        rows = [x1, x1, x1, x2, x2, x3] + values
        left_ref[b] = jnp.concatenate(rows, axis=0).T.astype(jnp.bfloat16)
        for c in range(3):
            centre_ref[b, c] = jnp.broadcast_to(point[c : c + 1], (width, width)).T


def pair_kernel(
    info_ref,
    centre_ref,
    left_ref,
    mine_ref,
    other_ref,
    out_ref,
    product_ref,
    sums_ref,
    joined_ref,
    shape_ref,
    *row_refs,
):
    tiles, blocks, _, _ = mine_ref.shape
    width = centre_ref.shape[3]
    bits = (blocks - 1).bit_length()
    me = info_ref[0, 0]
    even = info_ref[0, 4] == 0

    def settle(tile, carry):
        for b in range(blocks):
            mine = mine_ref[tile, b, :, width : 2 * width]
            other = other_ref[tile, b, :, width : 2 * width]
            shape_ref[tile, b] = jnp.where(even, mine, other)
            shape_ref[tile, blocks + b] = jnp.where(even, other, mine)
        return carry

    lax.fori_loop(0, tiles, settle, 0, unroll=min(tiles, 8))
    sums_ref[...] = jnp.zeros(sums_ref.shape, jnp.float32)
    joined_ref[...] = jnp.zeros(joined_ref.shape, jnp.float32)
    for ref in row_refs:
        ref[...] = jnp.zeros(ref.shape, jnp.float32)
    blank = jnp.zeros((4, width), jnp.float32)
    row_ids = lax.broadcasted_iota(jnp.int32, (8, width), 0)

    def reach_of(order):
        return 0.25 * jnp.where(
            order == 3, 0.7745966692414834, jnp.where(order == 2, 0.5773502691896258, 0.0)
        )

    def read(k):
        word = info_ref[0, HEAD + k]
        inner = word >> 2
        outer = inner >> bits
        return inner & (blocks - 1), outer >> bits, outer & (blocks - 1), word & 3

    def scale_of(order):
        return jnp.where(order == 3, SCALE_SIDE, SCALE_TWO)

    def multiply(k, slot):
        target, owner, source, order = read(k)
        alive = jnp.where(order > 0, 1.0, 0.0).astype(jnp.float32)
        scale = scale_of(order)
        inside = row_ids < 3
        point = jnp.concatenate([shape_ref[owner, 2 * source], blank], axis=0)
        extent = jnp.concatenate([shape_ref[owner, 2 * source + 1], blank], axis=0)
        node = jnp.where(inside, point + extent * reach_of(order), 0.0)
        norm = (jnp.sum(node * node, axis=0, keepdims=True) + 0.0625) * scale
        rows = jnp.where(
            row_ids == 3,
            norm,
            jnp.where(row_ids == 4, scale, node * (-2.0 * scale)),
        )
        p1, p2, p3 = split3(rows)
        empty = jnp.zeros((8, width), jnp.float32)
        values = [ref[owner, source, :, 0:width] * alive for ref in (mine_ref, other_ref)]
        columns = [
            jnp.concatenate([p1, p2, p3, p1, p2, p1, empty], axis=0),
            jnp.concatenate([empty] * 6 + values, axis=0),
        ]
        product_ref[slot] = jnp.dot(
            left_ref[target],
            jnp.concatenate(columns, axis=1).astype(jnp.bfloat16),
            preferred_element_type=jnp.float32,
        )

    def one_pair(k, slot, nodes):
        target, owner, source, order = read(k)
        reach = reach_of(order)
        eight = (8, width)
        point = [jnp.broadcast_to(shape_ref[owner, 2 * source, c : c + 1], eight) for c in range(3)]
        extent = [
            jnp.broadcast_to(shape_ref[owner, 2 * source + 1, c : c + 1], eight) * reach
            for c in range(3)
        ]
        gap = [e * (4.0 * scale_of(order)) for e in extent]
        third = order == 3
        ratio = jnp.where(third, SCALE_MID / SCALE_SIDE / 2.0, 0.0)
        drop = extent[0] * extent[0] + extent[1] * extent[1] + extent[2] * extent[2]
        drop = jnp.where(third, drop * SCALE_MID, -3.0e38)
        columns = [jnp.zeros(eight, jnp.float32) for _ in range(3)]
        for start, row_ref in zip(range(0, width, 8), row_refs):
            rows = slice(start, start + 8)
            sums = [row_ref[target, c] for c in range(3)]
            away = [centre_ref[target, c, rows] - point[c] for c in range(3)]

            def cubed(squared):
                i = lax.rsqrt(squared)
                return i * i * i

            plus = product_ref[slot, rows, 0:width]
            coupling = product_ref[slot, rows, width : 2 * width]
            f_plus = cubed(plus)
            if nodes == 1:
                even = (coupling + coupling) * f_plus
            else:
                minus = plus + (away[0] * gap[0] + away[1] * gap[1] + away[2] * gap[2])
                f_minus = cubed(minus)
                total = f_plus + f_minus
                if nodes == 3:
                    total = total + cubed((plus + minus) * ratio - drop)
                even = coupling * total
                odd = coupling * (f_plus - f_minus)
            for c in range(3):
                pulled = even * away[c]
                if nodes > 1:
                    pulled = pulled - odd * extent[c]
                columns[c] = columns[c] + pulled
                row_ref[target, c] = sums[c] + pulled
        for c in range(3):
            sums_ref[slot, c : c + 1] = jnp.sum(columns[c], axis=0, keepdims=True)

    high = blocks * width // LANES
    keys = 4 * high
    shift = (blocks * width).bit_length() + 1
    key_ids = lax.broadcasted_iota(jnp.int32, (keys, width), 0).astype(jnp.bfloat16)
    lane_ids = lax.broadcasted_iota(jnp.int32, (LANES, width), 0).astype(jnp.bfloat16)
    zero = jnp.zeros((keys, width), jnp.bfloat16)
    one = jnp.ones((keys, width), jnp.bfloat16)

    def wide(row):
        return jnp.broadcast_to(row, (keys, width))

    def narrow(value):
        return value.astype(jnp.float32).astype(jnp.bfloat16)

    def spread_out(tile, b, slot, result):
        spread = []
        for c in range(3):
            grad = wide(sums_ref[slot, c : c + 1])
            upper = grad.astype(jnp.bfloat16)
            spread += [upper, (grad - upper.astype(jnp.float32)).astype(jnp.bfloat16)]
        for half in range(2):
            parts = []
            hots = []
            code = wide(shape_ref[tile, 2 * b + half, 3:4]).astype(jnp.int32)
            for place in (code >> shift, code & ((1 << shift) - 1)):
                mask = key_ids == narrow(place >> 7)
                low = narrow(place & (LANES - 1))
                parts.append(jnp.concatenate([jnp.where(mask, s, zero) for s in spread], axis=0))
                hots.append(
                    jnp.concatenate(
                        [
                            jnp.where(lane_ids[g : g + keys] == low, one, zero)
                            for g in range(0, LANES, keys)
                        ],
                        axis=0,
                    )
                )
            product = lax.dot_general(
                jnp.concatenate(parts, axis=1),
                jnp.concatenate(hots, axis=1),
                (((1,), (1,)), ((), ())),
                preferred_element_type=jnp.float32,
            )
            result = product if result is None else result + product
        return result

    def scatter(tile, places):
        result = None
        for b, slot in places:
            result = spread_out(tile, b, slot, result)
        before = [joined_ref[tile, c] for c in range(3)]
        for c in range(3):
            joined_ref[tile, c] = (
                before[c]
                + result[2 * c * keys : (2 * c + 1) * keys]
                + result[(2 * c + 1) * keys : (2 * c + 2) * keys]
            )

    def scatter_pair(k, slot):
        _, owner, source, _ = read(k)
        scatter(owner, [(source, slot)])

    def two_pairs(nodes):
        def body(step, carry):
            for slot in range(2):
                k = 2 * step + slot
                multiply(k + 1, 1 - slot)
                scatter_pair(k - 1, 1 - slot)
                one_pair(k, slot, nodes)
            return carry

        return body

    multiply(0, 0)
    lax.fori_loop(0, info_ref[0, 1], two_pairs(3), 0)
    lax.fori_loop(info_ref[0, 1], info_ref[0, 2], two_pairs(2), 0)
    lax.fori_loop(info_ref[0, 2], info_ref[0, 3], two_pairs(1), 0)
    scatter_pair(2 * info_ref[0, 3] - 1, 1)
    for b in range(blocks):
        total = jnp.concatenate(
            [
                jnp.concatenate(
                    [jnp.sum(ref[b, c], axis=1, keepdims=True) for ref in row_refs], axis=0
                )
                for c in range(3)
            ]
            + [jnp.zeros((width, 5), jnp.float32)],
            axis=1,
        )
        sums_ref[2 + b] = -total.T
    scatter(me, [(b, 2 + b) for b in range(blocks)])

    def collect(dest, carry):
        for c in range(3):
            total = jnp.zeros((high, LANES), jnp.float32)
            for slot, by in enumerate((0, tiles - 1, 1, tiles - tiles // 2)):
                tile = lax.rem(dest + by, tiles)
                total = total + joined_ref[tile, c, slot * high : (slot + 1) * high]
            part = out_ref.shape[2]
            for f in range(out_ref.shape[1]):
                first = f * part % high
                out_ref[dest, f, :, c * LANES : (c + 1) * LANES] = total[first : first + part]
        return carry

    lax.fori_loop(0, tiles, collect, 0, unroll=min(tiles, 8))


def sum_kernel(got_ref, out_ref):
    out_ref[...] = jnp.sum(got_ref[...], axis=0)


def last_kernel(parity_ref, mine_ref, other_ref, out_ref):
    part = mine_ref.shape[0]
    even = parity_ref[0] == 0
    mine, other = mine_ref[...], other_ref[...]
    halves = (jnp.where(even, mine, other), jnp.where(even, other, mine))
    for i, half in enumerate(halves):
        for r in range(part):
            h = i * part + r
            for c in range(3):
                out_ref[c : c + 1, h * LANES : (h + 1) * LANES] = half[
                    r : r + 1, c * LANES : (c + 1) * LANES
                ]


def per_device(
    panel_geometry,
    adjoint,
    strengths,
    pair_target,
    pair_owner,
    pair_source,
    pair_order,
    pair_count,
    corner_vertex,
):
    tiles = lax.axis_size("tiles")
    far = lax.axis_size("far")
    blocks, _, width = panel_geometry.shape
    high = blocks * width // LANES
    parity = lax.axis_index("far").astype(jnp.int32) & 1
    me = lax.axis_index("tiles").astype(jnp.int32).reshape(1)
    parity = parity.reshape(1)
    swap = [(f ^ 1, f) for f in range(far)]
    smem = pl.BlockSpec(memory_space=SMEM)
    vmem = pl.BlockSpec(memory_space=VMEM)
    params = pltpu.CompilerParams(vmem_limit_bytes=LIMIT)
    geometry = panel_geometry.transpose(1, 0, 2)
    packed = pl.pallas_call(
        pack_kernel,
        out_shape=jax.ShapeDtypeStruct((tiles, blocks, 4, 2 * width), jnp.float32),
        in_specs=[smem] * 2 + [vmem] * 3,
        out_specs=vmem,
    )(me, parity, geometry, strengths, corner_vertex)
    got = lax.all_to_all(packed, "tiles", split_axis=0, concat_axis=0, tiled=True)
    partner = lax.ppermute(adjoint, "far", swap)
    pairs = pair_target.shape[0]
    info = pl.pallas_call(
        lambda *refs: sort_kernel(*refs[:-1], blocks, refs[-1]),
        out_shape=jax.ShapeDtypeStruct((1, -(-(HEAD + pairs // 2 + SPARE + 1) // LANES) * LANES), jnp.int32),
        in_specs=[smem] * 2 + [vmem] * 4 + [smem],
        out_specs=vmem,
        cost_estimate=pl.CostEstimate(flops=4000000, bytes_accessed=900000, transcendentals=0),
    )(
        me,
        parity,
        pair_target.reshape(1, pairs),
        pair_owner.reshape(1, pairs),
        pair_source.reshape(1, pairs),
        pair_order.reshape(1, pairs),
        pair_count,
    )
    centre, left = pl.pallas_call(
        prep_kernel,
        out_shape=(
            jax.ShapeDtypeStruct((blocks, 3, width, width), jnp.float32),
            jax.ShapeDtypeStruct((blocks, width, 56), jnp.bfloat16),
        ),
        compiler_params=params,
        cost_estimate=pl.CostEstimate(flops=4000000, bytes_accessed=900000, transcendentals=0),
    )(geometry, adjoint, partner)
    got, info, left = lax.optimization_barrier((got, info, left))
    other = lax.ppermute(got, "far", swap)
    partial = pl.pallas_call(
        pair_kernel,
        out_shape=jax.ShapeDtypeStruct((tiles, far, high // 2, 3 * LANES), jnp.float32),
        in_specs=[smem] + [vmem] * 4,
        out_specs=vmem,
        scratch_shapes=[
            VMEM((2, width, 2 * width), jnp.float32),
            VMEM((2 + blocks, 8, width), jnp.float32),
            VMEM((tiles, 3, 4 * high, LANES), jnp.float32),
            VMEM((tiles, 2 * blocks, 4, width), jnp.float32),
        ]
        + [VMEM((blocks, 3, 8, width), jnp.float32)] * (width // 8),
        compiler_params=params,
    )(info, centre, left, got, other)
    partial = partial.reshape(tiles * far, high // 2, 3 * LANES)
    shares = lax.all_to_all(partial, ("tiles", "far"), split_axis=0, concat_axis=0, tiled=True)
    mine = pl.pallas_call(
        sum_kernel,
        out_shape=jax.ShapeDtypeStruct((high // 2, 3 * LANES), jnp.float32),
        compiler_params=params,
    )(shares)
    other = lax.ppermute(mine, "far", swap)
    return pl.pallas_call(
        last_kernel,
        out_shape=jax.ShapeDtypeStruct((3, blocks * width), jnp.float32),
        in_specs=[smem, vmem, vmem],
        out_specs=vmem,
        compiler_params=params,
    )(parity, mine, other)


def solution(mesh):
    placed = (
        P("tiles", None, None),
        P("tiles", "far", None),
        P("tiles", "far", None),
        P("tiles"),
        P("tiles", None),
        P("tiles"),
        P("tiles"),
        P("tiles"),
        P("tiles", None, None),
    )
    return jax.shard_map(
        per_device, mesh=mesh, in_specs=placed, out_specs=P(None, "tiles"), check_vma=False
    )
```

```python
import jax
import jax.numpy as jnp
from jax import lax
from jax.experimental import pallas as pl
from jax.experimental.pallas import tpu as pltpu
from jax.sharding import PartitionSpec as P

SMEM = pltpu.SMEM
VMEM = pltpu.VMEM
LANES = 128
HEAD = 5
SCALE_MID = (4.0 / 9.0 / 512.0) ** (-2.0 / 3.0)
SCALE_SIDE = (5.0 / 18.0 / 512.0) ** (-2.0 / 3.0)
SCALE_TWO = (0.5 / 512.0) ** (-2.0 / 3.0)
SPARE = 2
LIMIT = 48 * 1024 * 1024


def pack_kernel(me_ref, parity_ref, geom_ref, strength_ref, corner_ref, out_ref):
    tiles, blocks, _, _ = out_ref.shape
    width = strength_ref.shape[2]
    shift = (blocks * width).bit_length() - 1
    me = me_ref[0]
    even = parity_ref[0] == 0
    shapes = []
    for b in range(blocks):
        vertex = corner_ref[b]
        offset = (vertex >> shift) - me
        offset = jnp.where(offset < 0, offset + tiles, offset)
        slot = jnp.where(
            offset == 0,
            0,
            jnp.where(offset == 1, 1, jnp.where(offset == tiles - 1, 2, 3)),
        )
        place = ((slot << shift) + (vertex & ((1 << shift) - 1))).astype(jnp.float32)
        span = float(4 << shift)
        for half in range(2):
            code = place[2 * half : 2 * half + 1] * span + place[2 * half + 1 : 2 * half + 2]
            rows = [geom_ref[3 * half + c, b : b + 1] for c in range(3)] + [code]
            shapes.append(jnp.concatenate(rows, axis=0))
    for b in range(blocks):
        shape = jnp.where(even, shapes[b], shapes[blocks + b])
        block = jnp.concatenate([strength_ref[b].astype(jnp.float32), shape], axis=1)
        for t in range(tiles):
            out_ref[t, b] = block


def split3(value):
    first = value.astype(jnp.bfloat16).astype(jnp.float32)
    rest = value - first
    second = rest.astype(jnp.bfloat16).astype(jnp.float32)
    return first, second, rest - second


def sort_kernel(
    me_ref,
    parity_ref,
    target_ref,
    owner_ref,
    source_ref,
    order_ref,
    count_ref,
    blocks,
    info_ref,
):
    pairs = order_ref.shape[1]
    lanes = info_ref.shape[1]
    bits = (blocks - 1).bit_length()
    parity = parity_ref[0]
    order = order_ref[...]
    place = lax.broadcasted_iota(jnp.int32, (1, pairs), 1)
    live = place < count_ref[0]
    word = (owner_ref[...] << bits | source_ref[...]) << bits | target_ref[...]
    word = (word << 2 | order).astype(jnp.float32)
    key = jnp.where(live, (3 - order) * pairs + place, 3 * pairs + place).astype(jnp.float32)
    across = lax.broadcasted_iota(jnp.int32, (pairs, pairs), 1)
    down = lax.broadcasted_iota(jnp.int32, (pairs, pairs), 0)

    def upright(row):
        spread = jnp.broadcast_to(row, (pairs, pairs))
        return jnp.sum(jnp.where(across == down, spread, 0.0), axis=1, keepdims=True)

    key_down = upright(key)
    rank = jnp.sum(jnp.where(key < key_down, 1.0, 0.0), axis=1, keepdims=True).astype(jnp.int32)
    kept = (rank & 1 == parity) & (rank < count_ref[0])
    at = jnp.where(kept, HEAD + (rank >> 1), -1)
    wide_lane = lax.broadcasted_iota(jnp.int32, (pairs, lanes), 1)
    words = jnp.sum(jnp.where(wide_lane == at, upright(word), 0.0), axis=0, keepdims=True)
    info = words.astype(jnp.int32)
    lane = lax.broadcasted_iota(jnp.int32, (1, lanes), 1)
    info = jnp.where(lane == 0, me_ref[0], jnp.where(lane == 4, parity, info))
    for i in range(3):
        upto = jnp.where(live & (order >= 3 - i), 1.0, 0.0)
        total = jnp.sum(upto, axis=1, keepdims=True).astype(jnp.int32)
        info = jnp.where(lane == i + 1, (((total + 1 - parity) >> 1) + 1) >> 1, info)
    info_ref[...] = info


def prep_kernel(geom_ref, adjoint_ref, partner_ref, centre_ref, left_ref):
    blocks, _, width = adjoint_ref.shape
    for b in range(blocks):
        point = jnp.concatenate([geom_ref[c, b : b + 1] for c in range(3)], axis=0)
        rows = [point, jnp.ones((1, width), jnp.float32)]
        rows += [jnp.sum(point * point, axis=0, keepdims=True)]
        rows += [jnp.zeros((3, width), jnp.float32)]
        x1, x2, x3 = split3(jnp.concatenate(rows, axis=0))
        values = [adjoint_ref[b].astype(jnp.float32), partner_ref[b].astype(jnp.float32)]
        rows = [x1, x1, x1, x2, x2, x3] + values
        left_ref[b] = jnp.concatenate(rows, axis=0).T.astype(jnp.bfloat16)
        for c in range(3):
            centre_ref[b, c] = jnp.broadcast_to(point[c : c + 1], (width, width)).T


def pair_kernel(
    info_ref,
    centre_ref,
    left_ref,
    mine_ref,
    other_ref,
    out_ref,
    product_ref,
    row_acc,
    sums_ref,
    joined_ref,
    shape_ref,
):
    tiles, blocks, _, _ = mine_ref.shape
    width = centre_ref.shape[3]
    bits = (blocks - 1).bit_length()
    me = info_ref[0, 0]
    even = info_ref[0, 4] == 0

    def settle(tile, carry):
        for b in range(blocks):
            mine = mine_ref[tile, b, :, width : 2 * width]
            other = other_ref[tile, b, :, width : 2 * width]
            shape_ref[tile, b] = jnp.where(even, mine, other)
            shape_ref[tile, blocks + b] = jnp.where(even, other, mine)
        return carry

    lax.fori_loop(0, tiles, settle, 0, unroll=min(tiles, 8))
    sums_ref[...] = jnp.zeros(sums_ref.shape, jnp.float32)
    joined_ref[...] = jnp.zeros(joined_ref.shape, jnp.float32)
    row_acc[...] = jnp.zeros(row_acc.shape, jnp.float32)
    blank = jnp.zeros((4, width), jnp.float32)
    row_ids = lax.broadcasted_iota(jnp.int32, (8, width), 0)

    def reach_of(order):
        return 0.25 * jnp.where(
            order == 3, 0.7745966692414834, jnp.where(order == 2, 0.5773502691896258, 0.0)
        )

    def read(k):
        word = info_ref[0, HEAD + k]
        inner = word >> 2
        outer = inner >> bits
        return inner & (blocks - 1), outer >> bits, outer & (blocks - 1), word & 3

    def scale_of(order):
        return jnp.where(order == 3, SCALE_SIDE, SCALE_TWO)

    def multiply(k, slot):
        target, owner, source, order = read(k)
        alive = jnp.where(order > 0, 1.0, 0.0).astype(jnp.float32)
        scale = scale_of(order)
        inside = row_ids < 3
        point = jnp.concatenate([shape_ref[owner, 2 * source], blank], axis=0)
        extent = jnp.concatenate([shape_ref[owner, 2 * source + 1], blank], axis=0)
        node = jnp.where(inside, point + extent * reach_of(order), 0.0)
        norm = (jnp.sum(node * node, axis=0, keepdims=True) + 0.0625) * scale
        rows = jnp.where(
            row_ids == 3,
            norm,
            jnp.where(row_ids == 4, scale, node * (-2.0 * scale)),
        )
        p1, p2, p3 = split3(rows)
        empty = jnp.zeros((8, width), jnp.float32)
        values = [ref[owner, source, :, 0:width] * alive for ref in (mine_ref, other_ref)]
        columns = [
            jnp.concatenate([p1, p2, p3, p1, p2, p1, empty], axis=0),
            jnp.concatenate([empty] * 6 + values, axis=0),
        ]
        product_ref[slot] = jnp.dot(
            left_ref[target],
            jnp.concatenate(columns, axis=1).astype(jnp.bfloat16),
            preferred_element_type=jnp.float32,
        )

    def one_pair(k, slot, nodes):
        target, owner, source, order = read(k)
        reach = reach_of(order)
        eight = (8, width)
        point = [jnp.broadcast_to(shape_ref[owner, 2 * source, c : c + 1], eight) for c in range(3)]
        extent = [
            jnp.broadcast_to(shape_ref[owner, 2 * source + 1, c : c + 1], eight) * reach
            for c in range(3)
        ]
        gap = [e * (4.0 * scale_of(order)) for e in extent]
        third = order == 3
        ratio = jnp.where(third, SCALE_MID / SCALE_SIDE / 2.0, 0.0)
        drop = extent[0] * extent[0] + extent[1] * extent[1] + extent[2] * extent[2]
        drop = jnp.where(third, drop * SCALE_MID, -3.0e38)
        columns = [jnp.zeros(eight, jnp.float32) for _ in range(3)]
        for start in range(0, width, 8):
            rows = slice(start, start + 8)
            sums = [row_acc[target, c, rows] for c in range(3)]
            away = [centre_ref[target, c, rows] - point[c] for c in range(3)]

            def cubed(squared):
                i = lax.rsqrt(squared)
                return i * i * i

            plus = product_ref[slot, rows, 0:width]
            coupling = product_ref[slot, rows, width : 2 * width]
            f_plus = cubed(plus)
            if nodes == 1:
                even = (coupling + coupling) * f_plus
            else:
                minus = plus + (away[0] * gap[0] + away[1] * gap[1] + away[2] * gap[2])
                f_minus = cubed(minus)
                total = f_plus + f_minus
                if nodes == 3:
                    total = total + cubed((plus + minus) * ratio - drop)
                even = coupling * total
                odd = coupling * (f_plus - f_minus)
            for c in range(3):
                pulled = even * away[c]
                if nodes > 1:
                    pulled = pulled - odd * extent[c]
                columns[c] = columns[c] + pulled
                row_acc[target, c, rows] = sums[c] + pulled
        for c in range(3):
            sums_ref[slot, c : c + 1] = jnp.sum(columns[c], axis=0, keepdims=True)

    high = blocks * width // LANES
    keys = 4 * high
    shift = (blocks * width).bit_length() + 1
    key_ids = lax.broadcasted_iota(jnp.int32, (keys, width), 0).astype(jnp.bfloat16)
    lane_ids = lax.broadcasted_iota(jnp.int32, (LANES, width), 0).astype(jnp.bfloat16)
    zero = jnp.zeros((keys, width), jnp.bfloat16)
    one = jnp.ones((keys, width), jnp.bfloat16)

    def wide(row):
        return jnp.broadcast_to(row, (keys, width))

    def narrow(value):
        return value.astype(jnp.float32).astype(jnp.bfloat16)

    def spread_out(tile, b, slot, result):
        spread = []
        for c in range(3):
            grad = wide(sums_ref[slot, c : c + 1])
            upper = grad.astype(jnp.bfloat16)
            spread += [upper, (grad - upper.astype(jnp.float32)).astype(jnp.bfloat16)]
        for half in range(2):
            parts = []
            hots = []
            code = wide(shape_ref[tile, 2 * b + half, 3:4]).astype(jnp.int32)
            for place in (code >> shift, code & ((1 << shift) - 1)):
                mask = key_ids == narrow(place >> 7)
                low = narrow(place & (LANES - 1))
                parts.append(jnp.concatenate([jnp.where(mask, s, zero) for s in spread], axis=0))
                hots.append(
                    jnp.concatenate(
                        [
                            jnp.where(lane_ids[g : g + keys] == low, one, zero)
                            for g in range(0, LANES, keys)
                        ],
                        axis=0,
                    )
                )
            product = lax.dot_general(
                jnp.concatenate(parts, axis=1),
                jnp.concatenate(hots, axis=1),
                (((1,), (1,)), ((), ())),
                preferred_element_type=jnp.float32,
            )
            result = product if result is None else result + product
        return result

    def scatter(tile, places):
        result = None
        for b, slot in places:
            result = spread_out(tile, b, slot, result)
        before = [joined_ref[tile, c] for c in range(3)]
        for c in range(3):
            joined_ref[tile, c] = (
                before[c]
                + result[2 * c * keys : (2 * c + 1) * keys]
                + result[(2 * c + 1) * keys : (2 * c + 2) * keys]
            )

    def scatter_pair(k, slot):
        _, owner, source, _ = read(k)
        scatter(owner, [(source, slot)])

    def two_pairs(nodes):
        def body(step, carry):
            for slot in range(2):
                k = 2 * step + slot
                multiply(k + 1, 1 - slot)
                scatter_pair(k - 1, 1 - slot)
                one_pair(k, slot, nodes)
            return carry

        return body

    multiply(0, 0)
    lax.fori_loop(0, info_ref[0, 1], two_pairs(3), 0)
    lax.fori_loop(info_ref[0, 1], info_ref[0, 2], two_pairs(2), 0)
    lax.fori_loop(info_ref[0, 2], info_ref[0, 3], two_pairs(1), 0)
    scatter_pair(2 * info_ref[0, 3] - 1, 1)
    for b in range(blocks):
        total = jnp.concatenate(
            [jnp.sum(row_acc[b, c], axis=1, keepdims=True) for c in range(3)]
            + [jnp.zeros((width, 5), jnp.float32)],
            axis=1,
        )
        sums_ref[2 + b] = -total.T
    scatter(me, [(b, 2 + b) for b in range(blocks)])

    def collect(dest, carry):
        for c in range(3):
            total = jnp.zeros((high, LANES), jnp.float32)
            for slot, by in enumerate((0, tiles - 1, 1, tiles - tiles // 2)):
                tile = lax.rem(dest + by, tiles)
                total = total + joined_ref[tile, c, slot * high : (slot + 1) * high]
            part = out_ref.shape[2]
            for f in range(out_ref.shape[1]):
                first = f * part % high
                out_ref[dest, f, :, c * LANES : (c + 1) * LANES] = total[first : first + part]
        return carry

    lax.fori_loop(0, tiles, collect, 0, unroll=min(tiles, 8))


def sum_kernel(got_ref, out_ref):
    out_ref[...] = jnp.sum(got_ref[...], axis=0)


def last_kernel(parity_ref, mine_ref, other_ref, out_ref):
    part = mine_ref.shape[0]
    even = parity_ref[0] == 0
    mine, other = mine_ref[...], other_ref[...]
    halves = (jnp.where(even, mine, other), jnp.where(even, other, mine))
    for i, half in enumerate(halves):
        for r in range(part):
            h = i * part + r
            for c in range(3):
                out_ref[c : c + 1, h * LANES : (h + 1) * LANES] = half[
                    r : r + 1, c * LANES : (c + 1) * LANES
                ]


def per_device(
    panel_geometry,
    adjoint,
    strengths,
    pair_target,
    pair_owner,
    pair_source,
    pair_order,
    pair_count,
    corner_vertex,
):
    tiles = lax.axis_size("tiles")
    far = lax.axis_size("far")
    blocks, _, width = panel_geometry.shape
    high = blocks * width // LANES
    parity = lax.axis_index("far").astype(jnp.int32) & 1
    me = lax.axis_index("tiles").astype(jnp.int32).reshape(1)
    parity = parity.reshape(1)
    swap = [(f ^ 1, f) for f in range(far)]
    smem = pl.BlockSpec(memory_space=SMEM)
    vmem = pl.BlockSpec(memory_space=VMEM)
    params = pltpu.CompilerParams(vmem_limit_bytes=LIMIT)
    partner = lax.ppermute(adjoint, "far", swap)
    panel_geometry, partner = lax.optimization_barrier((panel_geometry, partner))
    geometry = panel_geometry.transpose(1, 0, 2)
    packed = pl.pallas_call(
        pack_kernel,
        out_shape=jax.ShapeDtypeStruct((tiles, blocks, 4, 2 * width), jnp.float32),
        in_specs=[smem] * 2 + [vmem] * 3,
        out_specs=vmem,
    )(me, parity, geometry, strengths, corner_vertex)
    got = lax.all_to_all(packed, "tiles", split_axis=0, concat_axis=0, tiled=True)
    pairs = pair_target.shape[0]
    info = pl.pallas_call(
        lambda *refs: sort_kernel(*refs[:-1], blocks, refs[-1]),
        out_shape=jax.ShapeDtypeStruct((1, -(-(HEAD + pairs // 2 + SPARE + 1) // LANES) * LANES), jnp.int32),
        in_specs=[smem] * 2 + [vmem] * 4 + [smem],
        out_specs=vmem,
        cost_estimate=pl.CostEstimate(flops=4000000, bytes_accessed=900000, transcendentals=0),
    )(
        me,
        parity,
        pair_target.reshape(1, pairs),
        pair_owner.reshape(1, pairs),
        pair_source.reshape(1, pairs),
        pair_order.reshape(1, pairs),
        pair_count,
    )
    centre, left = pl.pallas_call(
        prep_kernel,
        out_shape=(
            jax.ShapeDtypeStruct((blocks, 3, width, width), jnp.float32),
            jax.ShapeDtypeStruct((blocks, width, 56), jnp.bfloat16),
        ),
        compiler_params=params,
        cost_estimate=pl.CostEstimate(flops=4000000, bytes_accessed=900000, transcendentals=0),
    )(geometry, adjoint, partner)
    got, info, left = lax.optimization_barrier((got, info, left))
    other = lax.ppermute(got, "far", swap)
    partial = pl.pallas_call(
        pair_kernel,
        out_shape=jax.ShapeDtypeStruct((tiles, far, high // 2, 3 * LANES), jnp.float32),
        in_specs=[smem] + [vmem] * 4,
        out_specs=vmem,
        scratch_shapes=[
            VMEM((2, width, 2 * width), jnp.float32),
            VMEM((blocks, 3, width, width), jnp.float32),
            VMEM((2 + blocks, 8, width), jnp.float32),
            VMEM((tiles, 3, 4 * high, LANES), jnp.float32),
            VMEM((tiles, 2 * blocks, 4, width), jnp.float32),
        ],
        compiler_params=params,
    )(info, centre, left, got, other)
    partial = partial.reshape(tiles * far, high // 2, 3 * LANES)
    shares = lax.all_to_all(partial, ("tiles", "far"), split_axis=0, concat_axis=0, tiled=True)
    mine = pl.pallas_call(
        sum_kernel,
        out_shape=jax.ShapeDtypeStruct((high // 2, 3 * LANES), jnp.float32),
        compiler_params=params,
    )(shares)
    other = lax.ppermute(mine, "far", swap)
    return pl.pallas_call(
        last_kernel,
        out_shape=jax.ShapeDtypeStruct((3, blocks * width), jnp.float32),
        in_specs=[smem, vmem, vmem],
        out_specs=vmem,
        compiler_params=params,
    )(parity, mine, other)


def solution(mesh):
    placed = (
        P("tiles", None, None),
        P("tiles", "far", None),
        P("tiles", "far", None),
        P("tiles"),
        P("tiles", None),
        P("tiles"),
        P("tiles"),
        P("tiles"),
        P("tiles", None, None),
    )
    return jax.shard_map(
        per_device, mesh=mesh, in_specs=placed, out_specs=P(None, "tiles"), check_vma=False
    )
```

```python
import jax
import jax.numpy as jnp
from jax import lax
from jax.experimental import pallas as pl
from jax.experimental.pallas import tpu as pltpu
from jax.sharding import PartitionSpec as P

SMEM = pltpu.SMEM
VMEM = pltpu.VMEM
LANES = 128
HEAD = 5
SPARE = 2
LIMIT = 48 * 1024 * 1024


def pack_kernel(me_ref, parity_ref, geom_ref, strength_ref, corner_ref, out_ref):
    tiles, blocks, _, _ = out_ref.shape
    width = strength_ref.shape[2]
    shift = (blocks * width).bit_length() - 1
    me = me_ref[0]
    even = parity_ref[0] == 0
    shapes = []
    for b in range(blocks):
        vertex = corner_ref[b]
        offset = (vertex >> shift) - me
        offset = jnp.where(offset < 0, offset + tiles, offset)
        slot = jnp.where(
            offset == 0,
            0,
            jnp.where(offset == 1, 1, jnp.where(offset == tiles - 1, 2, 3)),
        )
        place = ((slot << shift) + (vertex & ((1 << shift) - 1))).astype(jnp.float32)
        span = float(4 << shift)
        for half in range(2):
            code = place[2 * half : 2 * half + 1] * span + place[2 * half + 1 : 2 * half + 2]
            rows = [geom_ref[3 * half + c, b : b + 1] for c in range(3)] + [code]
            shapes.append(jnp.concatenate(rows, axis=0))
    for b in range(blocks):
        shape = jnp.where(even, shapes[b], shapes[blocks + b])
        block = jnp.concatenate([strength_ref[b].astype(jnp.float32), shape], axis=1)
        for t in range(tiles):
            out_ref[t, b] = block


def split3(value):
    first = value.astype(jnp.bfloat16).astype(jnp.float32)
    rest = value - first
    second = rest.astype(jnp.bfloat16).astype(jnp.float32)
    return first, second, rest - second


def sort_kernel(
    me_ref,
    parity_ref,
    target_ref,
    owner_ref,
    source_ref,
    order_ref,
    count_ref,
    blocks,
    info_ref,
):
    pairs = order_ref.shape[1]
    lanes = info_ref.shape[1]
    bits = (blocks - 1).bit_length()
    parity = parity_ref[0]
    order = order_ref[...]
    place = lax.broadcasted_iota(jnp.int32, (1, pairs), 1)
    live = place < count_ref[0]
    word = (owner_ref[...] << bits | source_ref[...]) << bits | target_ref[...]
    word = (word << 2 | order).astype(jnp.float32)
    key = jnp.where(live, (3 - order) * pairs + place, 3 * pairs + place).astype(jnp.float32)
    across = lax.broadcasted_iota(jnp.int32, (pairs, pairs), 1)
    down = lax.broadcasted_iota(jnp.int32, (pairs, pairs), 0)

    def upright(row):
        spread = jnp.broadcast_to(row, (pairs, pairs))
        return jnp.sum(jnp.where(across == down, spread, 0.0), axis=1, keepdims=True)

    key_down = upright(key)
    rank = jnp.sum(jnp.where(key < key_down, 1.0, 0.0), axis=1, keepdims=True).astype(jnp.int32)
    kept = (rank & 1 == parity) & (rank < count_ref[0])
    at = jnp.where(kept, HEAD + (rank >> 1), -1)
    wide_lane = lax.broadcasted_iota(jnp.int32, (pairs, lanes), 1)
    words = jnp.sum(jnp.where(wide_lane == at, upright(word), 0.0), axis=0, keepdims=True)
    info = words.astype(jnp.int32)
    lane = lax.broadcasted_iota(jnp.int32, (1, lanes), 1)
    info = jnp.where(lane == 0, me_ref[0], jnp.where(lane == 4, parity, info))
    for i in range(3):
        upto = jnp.where(live & (order >= 3 - i), 1.0, 0.0)
        total = jnp.sum(upto, axis=1, keepdims=True).astype(jnp.int32)
        info = jnp.where(lane == i + 1, (((total + 1 - parity) >> 1) + 1) >> 1, info)
    info_ref[...] = info


def prep_kernel(geom_ref, adjoint_ref, partner_ref, centre_ref, left_ref):
    blocks, _, width = adjoint_ref.shape
    for b in range(blocks):
        point = jnp.concatenate([geom_ref[c, b : b + 1] for c in range(3)], axis=0)
        rows = [point, jnp.ones((1, width), jnp.float32)]
        rows += [jnp.sum(point * point, axis=0, keepdims=True)]
        rows += [jnp.zeros((3, width), jnp.float32)]
        x1, x2, x3 = split3(jnp.concatenate(rows, axis=0))
        values = [adjoint_ref[b].astype(jnp.float32), partner_ref[b].astype(jnp.float32)]
        rows = [x1, x1, x1, x2, x2, x3] + values
        left_ref[b] = jnp.concatenate(rows, axis=0).T.astype(jnp.bfloat16)
        for c in range(3):
            centre_ref[b, c] = jnp.broadcast_to(point[c : c + 1], (width, width)).T


def pair_kernel(
    info_ref,
    centre_ref,
    left_ref,
    mine_ref,
    other_ref,
    out_ref,
    product_ref,
    row_acc,
    sums_ref,
    joined_ref,
    shape_ref,
):
    tiles, blocks, _, _ = mine_ref.shape
    width = centre_ref.shape[3]
    bits = (blocks - 1).bit_length()
    me = info_ref[0, 0]
    even = info_ref[0, 4] == 0

    def settle(tile, carry):
        for b in range(blocks):
            mine = mine_ref[tile, b, :, width : 2 * width]
            other = other_ref[tile, b, :, width : 2 * width]
            shape_ref[tile, b] = jnp.where(even, mine, other)
            shape_ref[tile, blocks + b] = jnp.where(even, other, mine)
        return carry

    lax.fori_loop(0, tiles, settle, 0, unroll=min(tiles, 8))
    sums_ref[...] = jnp.zeros(sums_ref.shape, jnp.float32)
    joined_ref[...] = jnp.zeros(joined_ref.shape, jnp.float32)
    row_acc[...] = jnp.zeros(row_acc.shape, jnp.float32)
    blank = jnp.zeros((4, width), jnp.float32)
    row_ids = lax.broadcasted_iota(jnp.int32, (8, width), 0)

    def reach_of(order):
        return 0.25 * jnp.where(
            order == 3, 0.7745966692414834, jnp.where(order == 2, 0.5773502691896258, 0.0)
        )

    def read(k):
        word = info_ref[0, HEAD + k]
        inner = word >> 2
        outer = inner >> bits
        return inner & (blocks - 1), outer >> bits, outer & (blocks - 1), word & 3

    def multiply(k, slot, nodes):
        target, owner, source, order = read(k)
        third = order == 3
        alive = jnp.where(order > 0, 1.0, 0.0).astype(jnp.float32)
        reach = reach_of(order)
        scale_mid = jnp.where(third, (4.0 / 9.0 / 512.0) ** (-2.0 / 3.0), 0.0)
        scale_side = jnp.where(
            third, (5.0 / 18.0 / 512.0) ** (-2.0 / 3.0), (0.5 / 512.0) ** (-2.0 / 3.0)
        )
        floor_mid = jnp.where(third, 0.0625 * (4.0 / 9.0 / 512.0) ** (-2.0 / 3.0), 3.0e38)
        floor_side = 0.0625 * scale_side
        point = shape_ref[owner, 2 * source]
        extent = shape_ref[owner, 2 * source + 1] * reach
        inside = row_ids < 3
        point = jnp.where(inside, jnp.concatenate([point, blank], axis=0), 0.0)
        extent = jnp.where(inside, jnp.concatenate([extent, blank], axis=0), 0.0)
        values = [ref[owner, source, :, 0:width] * alive for ref in (mine_ref, other_ref)]
        empty = jnp.zeros((8, width), jnp.float32)
        quadrature = (
            (point + extent, scale_side, floor_side),
            (point - extent, scale_side, floor_side),
            (point, scale_mid, floor_mid),
        )
        columns = []
        for node, scale, floor in quadrature[:nodes]:
            norm = jnp.sum(node * node, axis=0, keepdims=True) * scale + floor
            rows = jnp.where(
                row_ids == 3,
                norm,
                jnp.where(row_ids == 4, scale, node * (-2.0 * scale)),
            )
            p1, p2, p3 = split3(rows)
            columns.append(jnp.concatenate([p1, p2, p3, p1, p2, p1, empty], axis=0))
        columns.insert(1, jnp.concatenate([empty] * 6 + values, axis=0))
        product_ref[slot, :, 0 : (nodes + 1) * width] = jnp.dot(
            left_ref[target],
            jnp.concatenate(columns, axis=1).astype(jnp.bfloat16),
            preferred_element_type=jnp.float32,
        )

    def one_pair(k, slot, nodes):
        target, owner, source, order = read(k)
        reach = reach_of(order)
        eight = (8, width)
        point = [jnp.broadcast_to(shape_ref[owner, 2 * source, c : c + 1], eight) for c in range(3)]
        extent = [
            jnp.broadcast_to(shape_ref[owner, 2 * source + 1, c : c + 1], eight) * reach
            for c in range(3)
        ]
        columns = [jnp.zeros(eight, jnp.float32) for _ in range(3)]
        for start in range(0, width, 8):
            rows = slice(start, start + 8)
            sums = [row_acc[target, c, rows] for c in range(3)]

            def cubed(part):
                i = lax.rsqrt(product_ref[slot, rows, part * width : (part + 1) * width])
                return i * i * i

            coupling = product_ref[slot, rows, width : 2 * width]
            f_plus = cubed(0)
            if nodes == 1:
                even = (coupling + coupling) * f_plus
            else:
                f_minus = cubed(2)
                both = f_plus + f_minus
                even = coupling * (both + cubed(3) if nodes == 3 else both)
                odd = coupling * (f_plus - f_minus)
            for c in range(3):
                pulled = even * (centre_ref[target, c, rows] - point[c])
                if nodes > 1:
                    pulled = pulled - odd * extent[c]
                columns[c] = columns[c] + pulled
                row_acc[target, c, rows] = sums[c] + pulled
        for c in range(3):
            sums_ref[slot, c : c + 1] = jnp.sum(columns[c], axis=0, keepdims=True)

    high = blocks * width // LANES
    keys = 4 * high
    shift = (blocks * width).bit_length() + 1
    key_ids = lax.broadcasted_iota(jnp.int32, (keys, width), 0).astype(jnp.bfloat16)
    lane_ids = lax.broadcasted_iota(jnp.int32, (LANES, width), 0).astype(jnp.bfloat16)
    zero = jnp.zeros((keys, width), jnp.bfloat16)
    one = jnp.ones((keys, width), jnp.bfloat16)

    def wide(row):
        return jnp.broadcast_to(row, (8, width))

    def narrow(value):
        value = value.astype(jnp.float32)
        return jnp.concatenate([value] * (keys // 8), axis=0).astype(jnp.bfloat16)

    def spread_out(tile, b, slot, result):
        spread = []
        for c in range(3):
            grad = wide(sums_ref[slot, c : c + 1])
            upper = grad.astype(jnp.bfloat16).astype(jnp.float32)
            spread += [narrow(upper), narrow(grad - upper)]
        for half in range(2):
            parts = []
            hots = []
            code = wide(shape_ref[tile, 2 * b + half, 3:4]).astype(jnp.int32)
            for place in (code >> shift, code & ((1 << shift) - 1)):
                mask = key_ids == narrow(place >> 7)
                low = narrow(place & (LANES - 1))
                parts.append(jnp.concatenate([jnp.where(mask, s, zero) for s in spread], axis=0))
                hots.append(
                    jnp.concatenate(
                        [
                            jnp.where(lane_ids[g : g + keys] == low, one, zero)
                            for g in range(0, LANES, keys)
                        ],
                        axis=0,
                    )
                )
            product = lax.dot_general(
                jnp.concatenate(parts, axis=1),
                jnp.concatenate(hots, axis=1),
                (((1,), (1,)), ((), ())),
                preferred_element_type=jnp.float32,
            )
            result = product if result is None else result + product
        return result

    def scatter(tile, places):
        result = None
        for b, slot in places:
            result = spread_out(tile, b, slot, result)
        before = [joined_ref[tile, c] for c in range(3)]
        for c in range(3):
            joined_ref[tile, c] = (
                before[c]
                + result[2 * c * keys : (2 * c + 1) * keys]
                + result[(2 * c + 1) * keys : (2 * c + 2) * keys]
            )

    def scatter_pair(k, slot):
        _, owner, source, _ = read(k)
        scatter(owner, [(source, slot)])

    def two_pairs(nodes):
        def body(step, carry):
            for slot in range(2):
                k = 2 * step + slot
                multiply(k + 1, 1 - slot, nodes)
                scatter_pair(k - 1, 1 - slot)
                one_pair(k, slot, nodes)
            return carry

        return body

    multiply(0, 0, 3)
    lax.fori_loop(0, info_ref[0, 1], two_pairs(3), 0)
    lax.fori_loop(info_ref[0, 1], info_ref[0, 2], two_pairs(2), 0)
    lax.fori_loop(info_ref[0, 2], info_ref[0, 3], two_pairs(1), 0)
    scatter_pair(2 * info_ref[0, 3] - 1, 1)
    for b in range(blocks):
        total = jnp.concatenate(
            [jnp.sum(row_acc[b, c], axis=1, keepdims=True) for c in range(3)]
            + [jnp.zeros((width, 5), jnp.float32)],
            axis=1,
        )
        sums_ref[2 + b] = -total.T
    scatter(me, [(b, 2 + b) for b in range(blocks)])

    def collect(dest, carry):
        for c in range(3):
            total = jnp.zeros((high, LANES), jnp.float32)
            for slot, by in enumerate((0, tiles - 1, 1, tiles - tiles // 2)):
                tile = lax.rem(dest + by, tiles)
                total = total + joined_ref[tile, c, slot * high : (slot + 1) * high]
            part = out_ref.shape[2]
            for f in range(out_ref.shape[1]):
                first = f * part % high
                out_ref[dest, f, :, c * LANES : (c + 1) * LANES] = total[first : first + part]
        return carry

    lax.fori_loop(0, tiles, collect, 0, unroll=min(tiles, 8))


def sum_kernel(got_ref, out_ref):
    out_ref[...] = jnp.sum(got_ref[...], axis=0)


def last_kernel(parity_ref, mine_ref, other_ref, out_ref):
    part = mine_ref.shape[0]
    even = parity_ref[0] == 0
    mine, other = mine_ref[...], other_ref[...]
    halves = (jnp.where(even, mine, other), jnp.where(even, other, mine))
    for i, half in enumerate(halves):
        for r in range(part):
            h = i * part + r
            for c in range(3):
                out_ref[c : c + 1, h * LANES : (h + 1) * LANES] = half[
                    r : r + 1, c * LANES : (c + 1) * LANES
                ]


def per_device(
    panel_geometry,
    adjoint,
    strengths,
    pair_target,
    pair_owner,
    pair_source,
    pair_order,
    pair_count,
    corner_vertex,
):
    tiles = lax.axis_size("tiles")
    far = lax.axis_size("far")
    blocks, _, width = panel_geometry.shape
    high = blocks * width // LANES
    parity = lax.axis_index("far").astype(jnp.int32) & 1
    me = lax.axis_index("tiles").astype(jnp.int32).reshape(1)
    parity = parity.reshape(1)
    swap = [(f ^ 1, f) for f in range(far)]
    smem = pl.BlockSpec(memory_space=SMEM)
    vmem = pl.BlockSpec(memory_space=VMEM)
    params = pltpu.CompilerParams(vmem_limit_bytes=LIMIT)
    geometry = panel_geometry.transpose(1, 0, 2)
    packed = pl.pallas_call(
        pack_kernel,
        out_shape=jax.ShapeDtypeStruct((tiles, blocks, 4, 2 * width), jnp.float32),
        in_specs=[smem] * 2 + [vmem] * 3,
        out_specs=vmem,
    )(me, parity, geometry, strengths, corner_vertex)
    got = lax.all_to_all(packed, "tiles", split_axis=0, concat_axis=0, tiled=True)
    partner = lax.ppermute(adjoint, "far", swap)
    pairs = pair_target.shape[0]
    info = pl.pallas_call(
        lambda *refs: sort_kernel(*refs[:-1], blocks, refs[-1]),
        out_shape=jax.ShapeDtypeStruct((1, -(-(HEAD + pairs // 2 + SPARE + 1) // LANES) * LANES), jnp.int32),
        in_specs=[smem] * 2 + [vmem] * 4 + [smem],
        out_specs=vmem,
        cost_estimate=pl.CostEstimate(flops=4000000, bytes_accessed=900000, transcendentals=0),
    )(
        me,
        parity,
        pair_target.reshape(1, pairs),
        pair_owner.reshape(1, pairs),
        pair_source.reshape(1, pairs),
        pair_order.reshape(1, pairs),
        pair_count,
    )
    centre, left = pl.pallas_call(
        prep_kernel,
        out_shape=(
            jax.ShapeDtypeStruct((blocks, 3, width, width), jnp.float32),
            jax.ShapeDtypeStruct((blocks, width, 56), jnp.bfloat16),
        ),
        compiler_params=params,
        cost_estimate=pl.CostEstimate(flops=4000000, bytes_accessed=900000, transcendentals=0),
    )(geometry, adjoint, partner)
    got, info, left = lax.optimization_barrier((got, info, left))
    other = lax.ppermute(got, "far", swap)
    partial = pl.pallas_call(
        pair_kernel,
        out_shape=jax.ShapeDtypeStruct((tiles, far, high // 2, 3 * LANES), jnp.float32),
        in_specs=[smem] + [vmem] * 4,
        out_specs=vmem,
        scratch_shapes=[
            VMEM((2, width, 4 * width), jnp.float32),
            VMEM((blocks, 3, width, width), jnp.float32),
            VMEM((2 + blocks, 8, width), jnp.float32),
            VMEM((tiles, 3, 4 * high, LANES), jnp.float32),
            VMEM((tiles, 2 * blocks, 4, width), jnp.float32),
        ],
        compiler_params=params,
    )(info, centre, left, got, other)
    partial = partial.reshape(tiles * far, high // 2, 3 * LANES)
    shares = lax.all_to_all(partial, ("tiles", "far"), split_axis=0, concat_axis=0, tiled=True)
    mine = pl.pallas_call(
        sum_kernel,
        out_shape=jax.ShapeDtypeStruct((high // 2, 3 * LANES), jnp.float32),
        compiler_params=params,
    )(shares)
    other = lax.ppermute(mine, "far", swap)
    return pl.pallas_call(
        last_kernel,
        out_shape=jax.ShapeDtypeStruct((3, blocks * width), jnp.float32),
        in_specs=[smem, vmem, vmem],
        out_specs=vmem,
        compiler_params=params,
    )(parity, mine, other)


def solution(mesh):
    placed = (
        P("tiles", None, None),
        P("tiles", "far", None),
        P("tiles", "far", None),
        P("tiles"),
        P("tiles", None),
        P("tiles"),
        P("tiles"),
        P("tiles"),
        P("tiles", None, None),
    )
    return jax.shard_map(
        per_device, mesh=mesh, in_specs=placed, out_specs=P(None, "tiles"), check_vma=False
    )
```

```python
import jax
import jax.numpy as jnp
from jax import lax
from jax.experimental import pallas as pl
from jax.experimental.pallas import tpu as pltpu
from jax.sharding import PartitionSpec as P

SMEM = pltpu.SMEM
VMEM = pltpu.VMEM
LANES = 128
HEAD = 5
GROUP = 32
SPARE = 2
LIMIT = 48 * 1024 * 1024


def pack_kernel(me_ref, parity_ref, geom_ref, strength_ref, corner_ref, out_ref):
    tiles, blocks, _, _ = out_ref.shape
    width = strength_ref.shape[2]
    shift = (blocks * width).bit_length() - 1
    me = me_ref[0]
    even = parity_ref[0] == 0
    shapes = []
    for b in range(blocks):
        vertex = corner_ref[b]
        offset = (vertex >> shift) - me
        offset = jnp.where(offset < 0, offset + tiles, offset)
        slot = jnp.where(
            offset == 0,
            0,
            jnp.where(offset == 1, 1, jnp.where(offset == tiles - 1, 2, 3)),
        )
        place = ((slot << shift) + (vertex & ((1 << shift) - 1))).astype(jnp.float32)
        span = float(4 << shift)
        for half in range(2):
            code = place[2 * half : 2 * half + 1] * span + place[2 * half + 1 : 2 * half + 2]
            rows = [geom_ref[3 * half + c, b : b + 1] for c in range(3)] + [code]
            shapes.append(jnp.concatenate(rows, axis=0))
    for b in range(blocks):
        shape = jnp.where(even, shapes[b], shapes[blocks + b])
        block = jnp.concatenate([strength_ref[b].astype(jnp.float32), shape], axis=1)
        for t in range(tiles):
            out_ref[t, b] = block


def split3(value):
    first = value.astype(jnp.bfloat16).astype(jnp.float32)
    rest = value - first
    second = rest.astype(jnp.bfloat16).astype(jnp.float32)
    return first, second, rest - second


def sort_kernel(
    me_ref,
    parity_ref,
    target_ref,
    owner_ref,
    source_ref,
    order_ref,
    count_ref,
    blocks,
    info_ref,
):
    pairs = order_ref.shape[1]
    lanes = info_ref.shape[1]
    bits = (blocks - 1).bit_length()
    parity = parity_ref[0]
    order = order_ref[...]
    place = lax.broadcasted_iota(jnp.int32, (1, pairs), 1)
    live = place < count_ref[0]
    word = (owner_ref[...] << bits | source_ref[...]) << bits | target_ref[...]
    word = (word << 2 | order).astype(jnp.float32)
    key = jnp.where(live, (3 - order) * pairs + place, 3 * pairs + place).astype(jnp.float32)
    across = lax.broadcasted_iota(jnp.int32, (pairs, pairs), 1)
    down = lax.broadcasted_iota(jnp.int32, (pairs, pairs), 0)

    def upright(row):
        spread = jnp.broadcast_to(row, (pairs, pairs))
        return jnp.sum(jnp.where(across == down, spread, 0.0), axis=1, keepdims=True)

    key_down = upright(key)
    rank = jnp.sum(jnp.where(key < key_down, 1.0, 0.0), axis=1, keepdims=True).astype(jnp.int32)
    kept = (rank & 1 == parity) & (rank < count_ref[0])
    at = jnp.where(kept, HEAD + (rank >> 1), -1)
    wide_lane = lax.broadcasted_iota(jnp.int32, (pairs, lanes), 1)
    words = jnp.sum(jnp.where(wide_lane == at, upright(word), 0.0), axis=0, keepdims=True)
    info = words.astype(jnp.int32)
    lane = lax.broadcasted_iota(jnp.int32, (1, lanes), 1)
    info = jnp.where(lane == 0, me_ref[0], jnp.where(lane == 4, parity, info))
    for i in range(3):
        upto = jnp.where(live & (order >= 3 - i), 1.0, 0.0)
        total = jnp.sum(upto, axis=1, keepdims=True).astype(jnp.int32)
        info = jnp.where(lane == i + 1, (((total + 1 - parity) >> 1) + 1) >> 1, info)
    info_ref[...] = info


def prep_kernel(geom_ref, adjoint_ref, partner_ref, centre_ref, left_ref):
    blocks, _, width = adjoint_ref.shape
    for b in range(blocks):
        point = jnp.concatenate([geom_ref[c, b : b + 1] for c in range(3)], axis=0)
        rows = [point, jnp.ones((1, width), jnp.float32)]
        rows += [jnp.sum(point * point, axis=0, keepdims=True)]
        rows += [jnp.zeros((3, width), jnp.float32)]
        x1, x2, x3 = split3(jnp.concatenate(rows, axis=0))
        values = [adjoint_ref[b].astype(jnp.float32), partner_ref[b].astype(jnp.float32)]
        rows = [x1, x1, x1, x2, x2, x3] + values
        left_ref[b] = jnp.concatenate(rows, axis=0).T.astype(jnp.bfloat16)
        for c in range(3):
            centre_ref[b, c] = jnp.broadcast_to(point[c : c + 1], (width, width)).T


def pair_kernel(
    info_ref,
    centre_ref,
    left_ref,
    mine_ref,
    other_ref,
    out_ref,
    product_ref,
    row_acc,
    sums_ref,
    joined_ref,
    shape_ref,
):
    tiles, blocks, _, _ = mine_ref.shape
    width = centre_ref.shape[3]
    bits = (blocks - 1).bit_length()
    me = info_ref[0, 0]
    even = info_ref[0, 4] == 0

    def settle(tile, carry):
        for b in range(blocks):
            mine = mine_ref[tile, b, :, width : 2 * width]
            other = other_ref[tile, b, :, width : 2 * width]
            shape_ref[tile, b] = jnp.where(even, mine, other)
            shape_ref[tile, blocks + b] = jnp.where(even, other, mine)
        return carry

    lax.fori_loop(0, tiles, settle, 0, unroll=min(tiles, 8))
    sums_ref[...] = jnp.zeros(sums_ref.shape, jnp.float32)
    joined_ref[...] = jnp.zeros(joined_ref.shape, jnp.float32)
    row_acc[...] = jnp.zeros(row_acc.shape, jnp.float32)
    blank = jnp.zeros((4, width), jnp.float32)
    row_ids = lax.broadcasted_iota(jnp.int32, (8, width), 0)

    def reach_of(order):
        return 0.25 * jnp.where(
            order == 3, 0.7745966692414834, jnp.where(order == 2, 0.5773502691896258, 0.0)
        )

    def read(k):
        word = info_ref[0, HEAD + k]
        inner = word >> 2
        outer = inner >> bits
        return inner & (blocks - 1), outer >> bits, outer & (blocks - 1), word & 3

    def multiply(k, slot, nodes):
        target, owner, source, order = read(k)
        third = order == 3
        alive = jnp.where(order > 0, 1.0, 0.0).astype(jnp.float32)
        reach = reach_of(order)
        scale_mid = jnp.where(third, (4.0 / 9.0 / 512.0) ** (-2.0 / 3.0), 0.0)
        scale_side = jnp.where(
            third, (5.0 / 18.0 / 512.0) ** (-2.0 / 3.0), (0.5 / 512.0) ** (-2.0 / 3.0)
        )
        floor_mid = jnp.where(third, 0.0625 * (4.0 / 9.0 / 512.0) ** (-2.0 / 3.0), 3.0e38)
        floor_side = 0.0625 * scale_side
        point = shape_ref[owner, 2 * source]
        extent = shape_ref[owner, 2 * source + 1] * reach
        inside = row_ids < 3
        point = jnp.where(inside, jnp.concatenate([point, blank], axis=0), 0.0)
        extent = jnp.where(inside, jnp.concatenate([extent, blank], axis=0), 0.0)
        values = [ref[owner, source, :, 0:width] * alive for ref in (mine_ref, other_ref)]
        empty = jnp.zeros((8, width), jnp.float32)
        quadrature = (
            (point + extent, scale_side, floor_side),
            (point - extent, scale_side, floor_side),
            (point, scale_mid, floor_mid),
        )
        columns = []
        for node, scale, floor in quadrature[:nodes]:
            norm = jnp.sum(node * node, axis=0, keepdims=True) * scale + floor
            rows = jnp.where(
                row_ids == 3,
                norm,
                jnp.where(row_ids == 4, scale, node * (-2.0 * scale)),
            )
            p1, p2, p3 = split3(rows)
            columns.append(jnp.concatenate([p1, p2, p3, p1, p2, p1, empty], axis=0))
        columns.insert(1, jnp.concatenate([empty] * 6 + values, axis=0))
        product_ref[slot, :, 0 : (nodes + 1) * width] = jnp.dot(
            left_ref[target],
            jnp.concatenate(columns, axis=1).astype(jnp.bfloat16),
            preferred_element_type=jnp.float32,
        )

    def one_pair(k, slot, nodes):
        target, owner, source, order = read(k)
        reach = reach_of(order)
        eight = (8, width)
        point = [jnp.broadcast_to(shape_ref[owner, 2 * source, c : c + 1], eight) for c in range(3)]
        extent = [
            jnp.broadcast_to(shape_ref[owner, 2 * source + 1, c : c + 1], eight) * reach
            for c in range(3)
        ]
        point = [jnp.concatenate([row] * (GROUP // 8), axis=0) for row in point]
        extent = [jnp.concatenate([row] * (GROUP // 8), axis=0) for row in extent]
        columns = [jnp.zeros(eight, jnp.float32) for _ in range(3)]
        for start in range(0, width, GROUP):
            rows = slice(start, start + GROUP)
            sums = [row_acc[target, c, rows] for c in range(3)]

            def cubed(part):
                i = lax.rsqrt(product_ref[slot, rows, part * width : (part + 1) * width])
                return i * i * i

            coupling = product_ref[slot, rows, width : 2 * width]
            f_plus = cubed(0)
            if nodes == 1:
                even = (coupling + coupling) * f_plus
            else:
                f_minus = cubed(2)
                both = f_plus + f_minus
                even = coupling * (both + cubed(3) if nodes == 3 else both)
                odd = coupling * (f_plus - f_minus)
            for c in range(3):
                pulled = even * (centre_ref[target, c, rows] - point[c])
                if nodes > 1:
                    pulled = pulled - odd * extent[c]
                for r in range(0, GROUP, 8):
                    columns[c] = columns[c] + pulled[r : r + 8]
                row_acc[target, c, rows] = sums[c] + pulled
        for c in range(3):
            sums_ref[slot, c : c + 1] = jnp.sum(columns[c], axis=0, keepdims=True)

    high = blocks * width // LANES
    keys = 4 * high
    shift = (blocks * width).bit_length() + 1
    key_ids = lax.broadcasted_iota(jnp.int32, (keys, width), 0).astype(jnp.bfloat16)
    lane_ids = lax.broadcasted_iota(jnp.int32, (LANES, width), 0).astype(jnp.bfloat16)
    zero = jnp.zeros((keys, width), jnp.bfloat16)
    one = jnp.ones((keys, width), jnp.bfloat16)

    def wide(row):
        return jnp.broadcast_to(row, (8, width))

    def narrow(value):
        value = value.astype(jnp.float32)
        return jnp.concatenate([value] * (keys // 8), axis=0).astype(jnp.bfloat16)

    def spread_out(tile, b, slot, result):
        spread = []
        for c in range(3):
            grad = wide(sums_ref[slot, c : c + 1])
            upper = grad.astype(jnp.bfloat16).astype(jnp.float32)
            spread += [narrow(upper), narrow(grad - upper)]
        for half in range(2):
            parts = []
            hots = []
            code = wide(shape_ref[tile, 2 * b + half, 3:4]).astype(jnp.int32)
            for place in (code >> shift, code & ((1 << shift) - 1)):
                mask = key_ids == narrow(place >> 7)
                low = narrow(place & (LANES - 1))
                parts.append(jnp.concatenate([jnp.where(mask, s, zero) for s in spread], axis=0))
                hots.append(
                    jnp.concatenate(
                        [
                            jnp.where(lane_ids[g : g + keys] == low, one, zero)
                            for g in range(0, LANES, keys)
                        ],
                        axis=0,
                    )
                )
            product = lax.dot_general(
                jnp.concatenate(parts, axis=1),
                jnp.concatenate(hots, axis=1),
                (((1,), (1,)), ((), ())),
                preferred_element_type=jnp.float32,
            )
            result = product if result is None else result + product
        return result

    def scatter(tile, places):
        result = None
        for b, slot in places:
            result = spread_out(tile, b, slot, result)
        before = [joined_ref[tile, c] for c in range(3)]
        for c in range(3):
            joined_ref[tile, c] = (
                before[c]
                + result[2 * c * keys : (2 * c + 1) * keys]
                + result[(2 * c + 1) * keys : (2 * c + 2) * keys]
            )

    def scatter_pair(k, slot):
        _, owner, source, _ = read(k)
        scatter(owner, [(source, slot)])

    def two_pairs(nodes):
        def body(step, carry):
            for slot in range(2):
                k = 2 * step + slot
                multiply(k + 1, 1 - slot, nodes)
                scatter_pair(k - 1, 1 - slot)
                one_pair(k, slot, nodes)
            return carry

        return body

    multiply(0, 0, 3)
    lax.fori_loop(0, info_ref[0, 1], two_pairs(3), 0)
    lax.fori_loop(info_ref[0, 1], info_ref[0, 2], two_pairs(2), 0)
    lax.fori_loop(info_ref[0, 2], info_ref[0, 3], two_pairs(1), 0)
    scatter_pair(2 * info_ref[0, 3] - 1, 1)
    for b in range(blocks):
        total = jnp.concatenate(
            [jnp.sum(row_acc[b, c], axis=1, keepdims=True) for c in range(3)]
            + [jnp.zeros((width, 5), jnp.float32)],
            axis=1,
        )
        sums_ref[2 + b] = -total.T
    scatter(me, [(b, 2 + b) for b in range(blocks)])

    def collect(dest, carry):
        for c in range(3):
            total = jnp.zeros((high, LANES), jnp.float32)
            for slot, by in enumerate((0, tiles - 1, 1, tiles - tiles // 2)):
                tile = lax.rem(dest + by, tiles)
                total = total + joined_ref[tile, c, slot * high : (slot + 1) * high]
            part = out_ref.shape[2]
            for f in range(out_ref.shape[1]):
                first = f * part % high
                out_ref[dest, f, :, c * LANES : (c + 1) * LANES] = total[first : first + part]
        return carry

    lax.fori_loop(0, tiles, collect, 0, unroll=min(tiles, 8))


def sum_kernel(got_ref, out_ref):
    out_ref[...] = jnp.sum(got_ref[...], axis=0)


def last_kernel(parity_ref, mine_ref, other_ref, out_ref):
    part = mine_ref.shape[0]
    even = parity_ref[0] == 0
    mine, other = mine_ref[...], other_ref[...]
    halves = (jnp.where(even, mine, other), jnp.where(even, other, mine))
    for i, half in enumerate(halves):
        for r in range(part):
            h = i * part + r
            for c in range(3):
                out_ref[c : c + 1, h * LANES : (h + 1) * LANES] = half[
                    r : r + 1, c * LANES : (c + 1) * LANES
                ]


def per_device(
    panel_geometry,
    adjoint,
    strengths,
    pair_target,
    pair_owner,
    pair_source,
    pair_order,
    pair_count,
    corner_vertex,
):
    tiles = lax.axis_size("tiles")
    far = lax.axis_size("far")
    blocks, _, width = panel_geometry.shape
    high = blocks * width // LANES
    parity = lax.axis_index("far").astype(jnp.int32) & 1
    me = lax.axis_index("tiles").astype(jnp.int32).reshape(1)
    parity = parity.reshape(1)
    swap = [(f ^ 1, f) for f in range(far)]
    smem = pl.BlockSpec(memory_space=SMEM)
    vmem = pl.BlockSpec(memory_space=VMEM)
    params = pltpu.CompilerParams(vmem_limit_bytes=LIMIT)
    geometry = panel_geometry.transpose(1, 0, 2)
    packed = pl.pallas_call(
        pack_kernel,
        out_shape=jax.ShapeDtypeStruct((tiles, blocks, 4, 2 * width), jnp.float32),
        in_specs=[smem] * 2 + [vmem] * 3,
        out_specs=vmem,
    )(me, parity, geometry, strengths, corner_vertex)
    got = lax.all_to_all(packed, "tiles", split_axis=0, concat_axis=0, tiled=True)
    partner = lax.ppermute(adjoint, "far", swap)
    pairs = pair_target.shape[0]
    info = pl.pallas_call(
        lambda *refs: sort_kernel(*refs[:-1], blocks, refs[-1]),
        out_shape=jax.ShapeDtypeStruct((1, -(-(HEAD + pairs // 2 + SPARE + 1) // LANES) * LANES), jnp.int32),
        in_specs=[smem] * 2 + [vmem] * 4 + [smem],
        out_specs=vmem,
        cost_estimate=pl.CostEstimate(flops=4000000, bytes_accessed=900000, transcendentals=0),
    )(
        me,
        parity,
        pair_target.reshape(1, pairs),
        pair_owner.reshape(1, pairs),
        pair_source.reshape(1, pairs),
        pair_order.reshape(1, pairs),
        pair_count,
    )
    centre, left = pl.pallas_call(
        prep_kernel,
        out_shape=(
            jax.ShapeDtypeStruct((blocks, 3, width, width), jnp.float32),
            jax.ShapeDtypeStruct((blocks, width, 56), jnp.bfloat16),
        ),
        compiler_params=params,
        cost_estimate=pl.CostEstimate(flops=4000000, bytes_accessed=900000, transcendentals=0),
    )(geometry, adjoint, partner)
    got, info, left = lax.optimization_barrier((got, info, left))
    other = lax.ppermute(got, "far", swap)
    partial = pl.pallas_call(
        pair_kernel,
        out_shape=jax.ShapeDtypeStruct((tiles, far, high // 2, 3 * LANES), jnp.float32),
        in_specs=[smem] + [vmem] * 4,
        out_specs=vmem,
        scratch_shapes=[
            VMEM((2, width, 4 * width), jnp.float32),
            VMEM((blocks, 3, width, width), jnp.float32),
            VMEM((2 + blocks, 8, width), jnp.float32),
            VMEM((tiles, 3, 4 * high, LANES), jnp.float32),
            VMEM((tiles, 2 * blocks, 4, width), jnp.float32),
        ],
        compiler_params=params,
    )(info, centre, left, got, other)
    partial = partial.reshape(tiles * far, high // 2, 3 * LANES)
    shares = lax.all_to_all(partial, ("tiles", "far"), split_axis=0, concat_axis=0, tiled=True)
    mine = pl.pallas_call(
        sum_kernel,
        out_shape=jax.ShapeDtypeStruct((high // 2, 3 * LANES), jnp.float32),
        compiler_params=params,
    )(shares)
    other = lax.ppermute(mine, "far", swap)
    return pl.pallas_call(
        last_kernel,
        out_shape=jax.ShapeDtypeStruct((3, blocks * width), jnp.float32),
        in_specs=[smem, vmem, vmem],
        out_specs=vmem,
        compiler_params=params,
    )(parity, mine, other)


def solution(mesh):
    placed = (
        P("tiles", None, None),
        P("tiles", "far", None),
        P("tiles", "far", None),
        P("tiles"),
        P("tiles", None),
        P("tiles"),
        P("tiles"),
        P("tiles"),
        P("tiles", None, None),
    )
    return jax.shard_map(
        per_device, mesh=mesh, in_specs=placed, out_specs=P(None, "tiles"), check_vma=False
    )
```

```python
import jax
import jax.numpy as jnp
from jax import lax
from jax.experimental import pallas as pl
from jax.experimental.pallas import tpu as pltpu
from jax.sharding import PartitionSpec as P

SMEM = pltpu.SMEM
VMEM = pltpu.VMEM
LANES = 128
HEAD = 5
GROUP = 32
SPARE = 2
LIMIT = 48 * 1024 * 1024


def pack_kernel(me_ref, parity_ref, geom_ref, strength_ref, corner_ref, out_ref):
    tiles, blocks, _, _ = out_ref.shape
    width = strength_ref.shape[2]
    shift = (blocks * width).bit_length() - 1
    me = me_ref[0]
    even = parity_ref[0] == 0
    shapes = []
    for b in range(blocks):
        vertex = corner_ref[b]
        offset = (vertex >> shift) - me
        offset = jnp.where(offset < 0, offset + tiles, offset)
        slot = jnp.where(
            offset == 0,
            0,
            jnp.where(offset == 1, 1, jnp.where(offset == tiles - 1, 2, 3)),
        )
        place = ((slot << shift) + (vertex & ((1 << shift) - 1))).astype(jnp.float32)
        span = float(4 << shift)
        for half in range(2):
            code = place[2 * half : 2 * half + 1] * span + place[2 * half + 1 : 2 * half + 2]
            rows = [geom_ref[3 * half + c, b : b + 1] for c in range(3)] + [code]
            shapes.append(jnp.concatenate(rows, axis=0))
    for b in range(blocks):
        shape = jnp.where(even, shapes[b], shapes[blocks + b])
        block = jnp.concatenate([strength_ref[b].astype(jnp.float32), shape], axis=1)
        for t in range(tiles):
            out_ref[t, b] = block


def split3(value):
    first = value.astype(jnp.bfloat16).astype(jnp.float32)
    rest = value - first
    second = rest.astype(jnp.bfloat16).astype(jnp.float32)
    return first, second, rest - second


def sort_kernel(
    me_ref,
    parity_ref,
    target_ref,
    owner_ref,
    source_ref,
    order_ref,
    count_ref,
    blocks,
    info_ref,
):
    pairs = order_ref.shape[1]
    lanes = info_ref.shape[1]
    bits = (blocks - 1).bit_length()
    parity = parity_ref[0]
    order = order_ref[...]
    place = lax.broadcasted_iota(jnp.int32, (1, pairs), 1)
    live = place < count_ref[0]
    word = (owner_ref[...] * blocks + source_ref[...]) << bits | target_ref[...]
    word = (word << 2 | order).astype(jnp.float32)
    key = jnp.where(live, (3 - order) * pairs + place, 3 * pairs + place).astype(jnp.float32)
    across = lax.broadcasted_iota(jnp.int32, (pairs, pairs), 1)
    down = lax.broadcasted_iota(jnp.int32, (pairs, pairs), 0)

    def upright(row):
        spread = jnp.broadcast_to(row, (pairs, pairs))
        return jnp.sum(jnp.where(across == down, spread, 0.0), axis=1, keepdims=True)

    key_down = upright(key)
    rank = jnp.sum(jnp.where(key < key_down, 1.0, 0.0), axis=1, keepdims=True).astype(jnp.int32)
    kept = (rank & 1 == parity) & (rank < count_ref[0])
    at = jnp.where(kept, HEAD + (rank >> 1), -1)
    wide_lane = lax.broadcasted_iota(jnp.int32, (pairs, lanes), 1)
    words = jnp.sum(jnp.where(wide_lane == at, upright(word), 0.0), axis=0, keepdims=True)
    info = words.astype(jnp.int32)
    lane = lax.broadcasted_iota(jnp.int32, (1, lanes), 1)
    info = jnp.where(lane == 0, me_ref[0], jnp.where(lane == 4, parity, info))
    for i in range(3):
        upto = jnp.where(live & (order >= 3 - i), 1.0, 0.0)
        total = jnp.sum(upto, axis=1, keepdims=True).astype(jnp.int32)
        info = jnp.where(lane == i + 1, (((total + 1 - parity) >> 1) + 1) >> 1, info)
    info_ref[...] = info


def prep_kernel(geom_ref, adjoint_ref, partner_ref, centre_ref, left_ref):
    blocks, _, width = adjoint_ref.shape
    for b in range(blocks):
        point = jnp.concatenate([geom_ref[c, b : b + 1] for c in range(3)], axis=0)
        rows = [point, jnp.ones((1, width), jnp.float32)]
        rows += [jnp.sum(point * point, axis=0, keepdims=True)]
        rows += [jnp.zeros((3, width), jnp.float32)]
        x1, x2, x3 = split3(jnp.concatenate(rows, axis=0))
        values = [adjoint_ref[b].astype(jnp.float32), partner_ref[b].astype(jnp.float32)]
        rows = [x1, x1, x1, x2, x2, x3] + values
        left_ref[b] = jnp.concatenate(rows, axis=0).T.astype(jnp.bfloat16)
        for c in range(3):
            centre_ref[b, c] = jnp.broadcast_to(point[c : c + 1], (width, width)).T


def pair_kernel(
    info_ref,
    centre_ref,
    left_ref,
    mine_ref,
    other_ref,
    out_ref,
    product_ref,
    row_acc,
    sums_ref,
    joined_ref,
    shape_ref,
):
    blocks = centre_ref.shape[0]
    tiles = mine_ref.shape[0] // blocks
    width = centre_ref.shape[3]
    bits = (blocks - 1).bit_length()
    me = info_ref[0, 0]
    even = info_ref[0, 4] == 0

    def settle(tile, carry):
        for b in range(blocks):
            mine = mine_ref[tile * blocks + b, :, width : 2 * width]
            other = other_ref[tile * blocks + b, :, width : 2 * width]
            shape_ref[tile * 2 * blocks + b] = jnp.where(even, mine, other)
            shape_ref[tile * 2 * blocks + blocks + b] = jnp.where(even, other, mine)
        return carry

    lax.fori_loop(0, tiles, settle, 0, unroll=min(tiles, 8))
    sums_ref[...] = jnp.zeros(sums_ref.shape, jnp.float32)
    joined_ref[...] = jnp.zeros(joined_ref.shape, jnp.float32)
    row_acc[...] = jnp.zeros(row_acc.shape, jnp.float32)
    blank = jnp.zeros((4, width), jnp.float32)
    row_ids = lax.broadcasted_iota(jnp.int32, (8, width), 0)

    def reach_of(order):
        return 0.25 * jnp.where(
            order == 3, 0.7745966692414834, jnp.where(order == 2, 0.5773502691896258, 0.0)
        )

    def read(k):
        word = info_ref[0, HEAD + k]
        return (word >> 2) & ((1 << bits) - 1), word >> (bits + 2), word & 3

    def multiply(k, slot, nodes):
        target, source, order = read(k)
        third = order == 3
        alive = jnp.where(order > 0, 1.0, 0.0).astype(jnp.float32)
        reach = reach_of(order)
        scale_mid = jnp.where(third, (4.0 / 9.0 / 512.0) ** (-2.0 / 3.0), 0.0)
        scale_side = jnp.where(
            third, (5.0 / 18.0 / 512.0) ** (-2.0 / 3.0), (0.5 / 512.0) ** (-2.0 / 3.0)
        )
        floor_mid = jnp.where(third, 0.0625 * (4.0 / 9.0 / 512.0) ** (-2.0 / 3.0), 3.0e38)
        floor_side = 0.0625 * scale_side
        point = shape_ref[2 * source]
        extent = shape_ref[2 * source + 1] * reach
        inside = row_ids < 3
        point = jnp.where(inside, jnp.concatenate([point, blank], axis=0), 0.0)
        extent = jnp.where(inside, jnp.concatenate([extent, blank], axis=0), 0.0)
        values = [ref[source, :, 0:width] * alive for ref in (mine_ref, other_ref)]
        empty = jnp.zeros((8, width), jnp.float32)
        quadrature = (
            (point + extent, scale_side, floor_side),
            (point - extent, scale_side, floor_side),
            (point, scale_mid, floor_mid),
        )
        columns = []
        for node, scale, floor in quadrature[:nodes]:
            norm = jnp.sum(node * node, axis=0, keepdims=True) * scale + floor
            rows = jnp.where(
                row_ids == 3,
                norm,
                jnp.where(row_ids == 4, scale, node * (-2.0 * scale)),
            )
            p1, p2, p3 = split3(rows)
            columns.append(jnp.concatenate([p1, p2, p3, p1, p2, p1, empty], axis=0))
        columns.insert(1, jnp.concatenate([empty] * 6 + values, axis=0))
        product_ref[slot, :, 0 : (nodes + 1) * width] = jnp.dot(
            left_ref[target],
            jnp.concatenate(columns, axis=1).astype(jnp.bfloat16),
            preferred_element_type=jnp.float32,
        )

    def one_pair(k, slot, nodes):
        target, source, order = read(k)
        reach = reach_of(order)
        eight = (8, width)
        point = [jnp.broadcast_to(shape_ref[2 * source, c : c + 1], eight) for c in range(3)]
        extent = [
            jnp.broadcast_to(shape_ref[2 * source + 1, c : c + 1], eight) * reach
            for c in range(3)
        ]
        point = [jnp.concatenate([row] * (GROUP // 8), axis=0) for row in point]
        extent = [jnp.concatenate([row] * (GROUP // 8), axis=0) for row in extent]
        columns = [jnp.zeros(eight, jnp.float32) for _ in range(3)]
        for start in range(0, width, GROUP):
            rows = slice(start, start + GROUP)
            sums = [row_acc[target, c, rows] for c in range(3)]

            def cubed(part):
                i = lax.rsqrt(product_ref[slot, rows, part * width : (part + 1) * width])
                return i * i * i

            coupling = product_ref[slot, rows, width : 2 * width]
            f_plus = cubed(0)
            if nodes == 1:
                even = (coupling + coupling) * f_plus
            else:
                f_minus = cubed(2)
                both = f_plus + f_minus
                even = coupling * (both + cubed(3) if nodes == 3 else both)
                odd = coupling * (f_plus - f_minus)
            for c in range(3):
                pulled = even * (centre_ref[target, c, rows] - point[c])
                if nodes > 1:
                    pulled = pulled - odd * extent[c]
                for r in range(0, GROUP, 8):
                    columns[c] = columns[c] + pulled[r : r + 8]
                row_acc[target, c, rows] = sums[c] + pulled
        for c in range(3):
            sums_ref[slot, c : c + 1] = jnp.sum(columns[c], axis=0, keepdims=True)

    high = blocks * width // LANES
    keys = 4 * high
    shift = (blocks * width).bit_length() + 1
    key_ids = lax.broadcasted_iota(jnp.int32, (keys, width), 0).astype(jnp.bfloat16)
    lane_ids = lax.broadcasted_iota(jnp.int32, (LANES, width), 0).astype(jnp.bfloat16)
    zero = jnp.zeros((keys, width), jnp.bfloat16)
    one = jnp.ones((keys, width), jnp.bfloat16)

    def wide(row):
        return jnp.broadcast_to(row, (8, width))

    def narrow(value):
        value = value.astype(jnp.float32)
        return jnp.concatenate([value] * (keys // 8), axis=0).astype(jnp.bfloat16)

    def spread_out(block, slot, result):
        spread = []
        for c in range(3):
            grad = wide(sums_ref[slot, c : c + 1])
            upper = grad.astype(jnp.bfloat16).astype(jnp.float32)
            spread += [narrow(upper), narrow(grad - upper)]
        for half in range(2):
            parts = []
            hots = []
            code = wide(shape_ref[2 * block + half, 3:4]).astype(jnp.int32)
            for place in (code >> shift, code & ((1 << shift) - 1)):
                mask = key_ids == narrow(place >> 7)
                low = narrow(place & (LANES - 1))
                parts.append(jnp.concatenate([jnp.where(mask, s, zero) for s in spread], axis=0))
                hots.append(
                    jnp.concatenate(
                        [
                            jnp.where(lane_ids[g : g + keys] == low, one, zero)
                            for g in range(0, LANES, keys)
                        ],
                        axis=0,
                    )
                )
            product = lax.dot_general(
                jnp.concatenate(parts, axis=1),
                jnp.concatenate(hots, axis=1),
                (((1,), (1,)), ((), ())),
                preferred_element_type=jnp.float32,
            )
            result = product if result is None else result + product
        return result

    def scatter(tile, places):
        result = None
        for block, slot in places:
            result = spread_out(block, slot, result)
        before = [joined_ref[tile, c] for c in range(3)]
        for c in range(3):
            joined_ref[tile, c] = (
                before[c]
                + result[2 * c * keys : (2 * c + 1) * keys]
                + result[(2 * c + 1) * keys : (2 * c + 2) * keys]
            )

    def scatter_pair(k, slot):
        _, source, _ = read(k)
        scatter(source // blocks, [(source, slot)])

    def two_pairs(nodes):
        def body(step, carry):
            for slot in range(2):
                k = 2 * step + slot
                multiply(k + 1, 1 - slot, nodes)
                scatter_pair(k - 1, 1 - slot)
                one_pair(k, slot, nodes)
            return carry

        return body

    multiply(0, 0, 3)
    lax.fori_loop(0, info_ref[0, 1], two_pairs(3), 0)
    lax.fori_loop(info_ref[0, 1], info_ref[0, 2], two_pairs(2), 0)
    lax.fori_loop(info_ref[0, 2], info_ref[0, 3], two_pairs(1), 0)
    scatter_pair(2 * info_ref[0, 3] - 1, 1)
    for b in range(blocks):
        total = jnp.concatenate(
            [jnp.sum(row_acc[b, c], axis=1, keepdims=True) for c in range(3)]
            + [jnp.zeros((width, 5), jnp.float32)],
            axis=1,
        )
        sums_ref[2 + b] = -total.T
    scatter(me, [(me * blocks + b, 2 + b) for b in range(blocks)])

    def collect(dest, carry):
        for c in range(3):
            total = jnp.zeros((high, LANES), jnp.float32)
            for slot, by in enumerate((0, tiles - 1, 1, tiles - tiles // 2)):
                tile = lax.rem(dest + by, tiles)
                total = total + joined_ref[tile, c, slot * high : (slot + 1) * high]
            part = out_ref.shape[2]
            for f in range(out_ref.shape[1]):
                first = f * part % high
                out_ref[dest, f, :, c * LANES : (c + 1) * LANES] = total[first : first + part]
        return carry

    lax.fori_loop(0, tiles, collect, 0, unroll=min(tiles, 8))


def sum_kernel(got_ref, out_ref):
    out_ref[...] = jnp.sum(got_ref[...], axis=0)


def last_kernel(parity_ref, mine_ref, other_ref, out_ref):
    part = mine_ref.shape[0]
    even = parity_ref[0] == 0
    mine, other = mine_ref[...], other_ref[...]
    halves = (jnp.where(even, mine, other), jnp.where(even, other, mine))
    for i, half in enumerate(halves):
        for r in range(part):
            h = i * part + r
            for c in range(3):
                out_ref[c : c + 1, h * LANES : (h + 1) * LANES] = half[
                    r : r + 1, c * LANES : (c + 1) * LANES
                ]


def per_device(
    panel_geometry,
    adjoint,
    strengths,
    pair_target,
    pair_owner,
    pair_source,
    pair_order,
    pair_count,
    corner_vertex,
):
    tiles = lax.axis_size("tiles")
    far = lax.axis_size("far")
    blocks, _, width = panel_geometry.shape
    high = blocks * width // LANES
    parity = lax.axis_index("far").astype(jnp.int32) & 1
    me = lax.axis_index("tiles").astype(jnp.int32).reshape(1)
    parity = parity.reshape(1)
    swap = [(f ^ 1, f) for f in range(far)]
    smem = pl.BlockSpec(memory_space=SMEM)
    vmem = pl.BlockSpec(memory_space=VMEM)
    params = pltpu.CompilerParams(vmem_limit_bytes=LIMIT)
    geometry = panel_geometry.transpose(1, 0, 2)
    packed = pl.pallas_call(
        pack_kernel,
        out_shape=jax.ShapeDtypeStruct((tiles, blocks, 4, 2 * width), jnp.float32),
        in_specs=[smem] * 2 + [vmem] * 3,
        out_specs=vmem,
    )(me, parity, geometry, strengths, corner_vertex)
    got = lax.all_to_all(packed, "tiles", split_axis=0, concat_axis=0, tiled=True)
    partner = lax.ppermute(adjoint, "far", swap)
    pairs = pair_target.shape[0]
    info = pl.pallas_call(
        lambda *refs: sort_kernel(*refs[:-1], blocks, refs[-1]),
        out_shape=jax.ShapeDtypeStruct((1, -(-(HEAD + pairs // 2 + SPARE + 1) // LANES) * LANES), jnp.int32),
        in_specs=[smem] * 2 + [vmem] * 4 + [smem],
        out_specs=vmem,
        cost_estimate=pl.CostEstimate(flops=4000000, bytes_accessed=900000, transcendentals=0),
    )(
        me,
        parity,
        pair_target.reshape(1, pairs),
        pair_owner.reshape(1, pairs),
        pair_source.reshape(1, pairs),
        pair_order.reshape(1, pairs),
        pair_count,
    )
    centre, left = pl.pallas_call(
        prep_kernel,
        out_shape=(
            jax.ShapeDtypeStruct((blocks, 3, width, width), jnp.float32),
            jax.ShapeDtypeStruct((blocks, width, 56), jnp.bfloat16),
        ),
        compiler_params=params,
        cost_estimate=pl.CostEstimate(flops=4000000, bytes_accessed=900000, transcendentals=0),
    )(geometry, adjoint, partner)
    got, info, left = lax.optimization_barrier((got, info, left))
    other = lax.ppermute(got, "far", swap)
    partial = pl.pallas_call(
        pair_kernel,
        out_shape=jax.ShapeDtypeStruct((tiles, far, high // 2, 3 * LANES), jnp.float32),
        in_specs=[smem] + [vmem] * 4,
        out_specs=vmem,
        scratch_shapes=[
            VMEM((2, width, 4 * width), jnp.float32),
            VMEM((blocks, 3, width, width), jnp.float32),
            VMEM((2 + blocks, 8, width), jnp.float32),
            VMEM((tiles, 3, 4 * high, LANES), jnp.float32),
            VMEM((tiles * 2 * blocks, 4, width), jnp.float32),
        ],
        compiler_params=params,
    )(info, centre, left, *(x.reshape(tiles * blocks, 4, 2 * width) for x in (got, other)))
    partial = partial.reshape(tiles * far, high // 2, 3 * LANES)
    shares = lax.all_to_all(partial, ("tiles", "far"), split_axis=0, concat_axis=0, tiled=True)
    mine = pl.pallas_call(
        sum_kernel,
        out_shape=jax.ShapeDtypeStruct((high // 2, 3 * LANES), jnp.float32),
        compiler_params=params,
    )(shares)
    other = lax.ppermute(mine, "far", swap)
    return pl.pallas_call(
        last_kernel,
        out_shape=jax.ShapeDtypeStruct((3, blocks * width), jnp.float32),
        in_specs=[smem, vmem, vmem],
        out_specs=vmem,
        compiler_params=params,
    )(parity, mine, other)


def solution(mesh):
    placed = (
        P("tiles", None, None),
        P("tiles", "far", None),
        P("tiles", "far", None),
        P("tiles"),
        P("tiles", None),
        P("tiles"),
        P("tiles"),
        P("tiles"),
        P("tiles", None, None),
    )
    return jax.shard_map(
        per_device, mesh=mesh, in_specs=placed, out_specs=P(None, "tiles"), check_vma=False
    )
```

```python
import jax
import jax.numpy as jnp
from jax import lax
from jax.experimental import pallas as pl
from jax.experimental.pallas import tpu as pltpu
from jax.sharding import PartitionSpec as P

SMEM = pltpu.SMEM
VMEM = pltpu.VMEM
LANES = 128
HEAD = 5
GROUP = 32
SPARE = 2
LIMIT = 48 * 1024 * 1024


def pack_kernel(me_ref, parity_ref, geom_ref, strength_ref, corner_ref, out_ref):
    tiles, blocks, _, _ = out_ref.shape
    width = strength_ref.shape[2]
    shift = (blocks * width).bit_length() - 1
    me = me_ref[0]
    even = parity_ref[0] == 0
    shapes = []
    for b in range(blocks):
        vertex = corner_ref[b]
        offset = (vertex >> shift) - me
        offset = jnp.where(offset < 0, offset + tiles, offset)
        slot = jnp.where(
            offset == 0,
            0,
            jnp.where(offset == 1, 1, jnp.where(offset == tiles - 1, 2, 3)),
        )
        place = ((slot << shift) + (vertex & ((1 << shift) - 1))).astype(jnp.float32)
        span = float(4 << shift)
        for half in range(2):
            code = place[2 * half : 2 * half + 1] * span + place[2 * half + 1 : 2 * half + 2]
            rows = [geom_ref[3 * half + c, b : b + 1] for c in range(3)] + [code]
            shapes.append(jnp.concatenate(rows, axis=0))
    for b in range(blocks):
        shape = jnp.where(even, shapes[b], shapes[blocks + b])
        block = jnp.concatenate([strength_ref[b].astype(jnp.float32), shape], axis=1)
        for t in range(tiles):
            out_ref[t, b] = block


def split3(value):
    first = value.astype(jnp.bfloat16).astype(jnp.float32)
    rest = value - first
    second = rest.astype(jnp.bfloat16).astype(jnp.float32)
    return first, second, rest - second


def sort_kernel(
    me_ref,
    parity_ref,
    target_ref,
    owner_ref,
    source_ref,
    order_ref,
    count_ref,
    blocks,
    info_ref,
):
    pairs = order_ref.shape[1]
    lanes = info_ref.shape[1]
    bits = (blocks - 1).bit_length()
    parity = parity_ref[0]
    order = order_ref[...]
    place = lax.broadcasted_iota(jnp.int32, (1, pairs), 1)
    live = place < count_ref[0]
    word = (owner_ref[...] << bits | source_ref[...]) << bits | target_ref[...]
    word = (word << 2 | order).astype(jnp.float32)
    key = jnp.where(live, (3 - order) * pairs + place, 3 * pairs + place).astype(jnp.float32)
    across = lax.broadcasted_iota(jnp.int32, (pairs, pairs), 1)
    down = lax.broadcasted_iota(jnp.int32, (pairs, pairs), 0)

    def upright(row):
        spread = jnp.broadcast_to(row, (pairs, pairs))
        return jnp.sum(jnp.where(across == down, spread, 0.0), axis=1, keepdims=True)

    key_down = upright(key)
    rank = jnp.sum(jnp.where(key < key_down, 1.0, 0.0), axis=1, keepdims=True).astype(jnp.int32)
    kept = (rank & 1 == parity) & (rank < count_ref[0])
    at = jnp.where(kept, HEAD + (rank >> 1), -1)
    wide_lane = lax.broadcasted_iota(jnp.int32, (pairs, lanes), 1)
    words = jnp.sum(jnp.where(wide_lane == at, upright(word), 0.0), axis=0, keepdims=True)
    info = words.astype(jnp.int32)
    lane = lax.broadcasted_iota(jnp.int32, (1, lanes), 1)
    info = jnp.where(lane == 0, me_ref[0], jnp.where(lane == 4, parity, info))
    for i in range(3):
        upto = jnp.where(live & (order >= 3 - i), 1.0, 0.0)
        total = jnp.sum(upto, axis=1, keepdims=True).astype(jnp.int32)
        info = jnp.where(lane == i + 1, (((total + 1 - parity) >> 1) + 1) >> 1, info)
    info_ref[...] = info


def prep_kernel(geom_ref, adjoint_ref, partner_ref, centre_ref, left_ref):
    blocks, _, width = adjoint_ref.shape
    for b in range(blocks):
        point = jnp.concatenate([geom_ref[c, b : b + 1] for c in range(3)], axis=0)
        rows = [point, jnp.ones((1, width), jnp.float32)]
        rows += [jnp.sum(point * point, axis=0, keepdims=True)]
        rows += [jnp.zeros((3, width), jnp.float32)]
        x1, x2, x3 = split3(jnp.concatenate(rows, axis=0))
        values = [adjoint_ref[b].astype(jnp.float32), partner_ref[b].astype(jnp.float32)]
        rows = [x1, x1, x1, x2, x2, x3] + values
        left_ref[b] = jnp.concatenate(rows, axis=0).T.astype(jnp.bfloat16)
        for c in range(3):
            centre_ref[b, c] = jnp.broadcast_to(point[c : c + 1], (width, width)).T


def pair_kernel(
    info_ref,
    centre_ref,
    left_ref,
    mine_ref,
    other_ref,
    out_ref,
    side_ref,
    product_ref,
    row_acc,
    sums_ref,
    joined_ref,
    shape_ref,
):
    tiles, blocks, _, _ = mine_ref.shape
    width = centre_ref.shape[3]
    bits = (blocks - 1).bit_length()
    me = info_ref[0, 0]
    even = info_ref[0, 4] == 0
    side_ref[...] = jnp.full(side_ref.shape, info_ref[0, 4].astype(jnp.float32))

    def settle(tile, carry):
        for b in range(blocks):
            mine = mine_ref[tile, b, :, width : 2 * width]
            other = other_ref[tile, b, :, width : 2 * width]
            shape_ref[tile, b] = jnp.where(even, mine, other)
            shape_ref[tile, blocks + b] = jnp.where(even, other, mine)
        return carry

    lax.fori_loop(0, tiles, settle, 0, unroll=min(tiles, 8))
    sums_ref[...] = jnp.zeros(sums_ref.shape, jnp.float32)
    joined_ref[...] = jnp.zeros(joined_ref.shape, jnp.float32)
    row_acc[...] = jnp.zeros(row_acc.shape, jnp.float32)
    blank = jnp.zeros((4, width), jnp.float32)
    row_ids = lax.broadcasted_iota(jnp.int32, (8, width), 0)

    def reach_of(order):
        return 0.25 * jnp.where(
            order == 3, 0.7745966692414834, jnp.where(order == 2, 0.5773502691896258, 0.0)
        )

    def read(k):
        word = info_ref[0, HEAD + k]
        inner = word >> 2
        outer = inner >> bits
        return inner & (blocks - 1), outer >> bits, outer & (blocks - 1), word & 3

    def multiply(k, slot, nodes):
        target, owner, source, order = read(k)
        third = order == 3
        alive = jnp.where(order > 0, 1.0, 0.0).astype(jnp.float32)
        reach = reach_of(order)
        scale_mid = jnp.where(third, (4.0 / 9.0 / 512.0) ** (-2.0 / 3.0), 0.0)
        scale_side = jnp.where(
            third, (5.0 / 18.0 / 512.0) ** (-2.0 / 3.0), (0.5 / 512.0) ** (-2.0 / 3.0)
        )
        floor_mid = jnp.where(third, 0.0625 * (4.0 / 9.0 / 512.0) ** (-2.0 / 3.0), 3.0e38)
        floor_side = 0.0625 * scale_side
        point = shape_ref[owner, 2 * source]
        extent = shape_ref[owner, 2 * source + 1] * reach
        inside = row_ids < 3
        point = jnp.where(inside, jnp.concatenate([point, blank], axis=0), 0.0)
        extent = jnp.where(inside, jnp.concatenate([extent, blank], axis=0), 0.0)
        values = [ref[owner, source, :, 0:width] * alive for ref in (mine_ref, other_ref)]
        empty = jnp.zeros((8, width), jnp.float32)
        quadrature = (
            (point + extent, scale_side, floor_side),
            (point - extent, scale_side, floor_side),
            (point, scale_mid, floor_mid),
        )
        columns = []
        for node, scale, floor in quadrature[:nodes]:
            norm = jnp.sum(node * node, axis=0, keepdims=True) * scale + floor
            rows = jnp.where(
                row_ids == 3,
                norm,
                jnp.where(row_ids == 4, scale, node * (-2.0 * scale)),
            )
            p1, p2, p3 = split3(rows)
            columns.append(jnp.concatenate([p1, p2, p3, p1, p2, p1, empty], axis=0))
        columns.insert(1, jnp.concatenate([empty] * 6 + values, axis=0))
        product_ref[slot, :, 0 : (nodes + 1) * width] = jnp.dot(
            left_ref[target],
            jnp.concatenate(columns, axis=1).astype(jnp.bfloat16),
            preferred_element_type=jnp.float32,
        )

    def one_pair(k, slot, nodes):
        target, owner, source, order = read(k)
        reach = reach_of(order)
        eight = (8, width)
        point = [jnp.broadcast_to(shape_ref[owner, 2 * source, c : c + 1], eight) for c in range(3)]
        extent = [
            jnp.broadcast_to(shape_ref[owner, 2 * source + 1, c : c + 1], eight) * reach
            for c in range(3)
        ]
        point = [jnp.concatenate([row] * (GROUP // 8), axis=0) for row in point]
        extent = [jnp.concatenate([row] * (GROUP // 8), axis=0) for row in extent]
        columns = [jnp.zeros(eight, jnp.float32) for _ in range(3)]
        for start in range(0, width, GROUP):
            rows = slice(start, start + GROUP)
            sums = [row_acc[target, c, rows] for c in range(3)]

            def cubed(part):
                i = lax.rsqrt(product_ref[slot, rows, part * width : (part + 1) * width])
                return i * i * i

            coupling = product_ref[slot, rows, width : 2 * width]
            f_plus = cubed(0)
            if nodes == 1:
                even = (coupling + coupling) * f_plus
            else:
                f_minus = cubed(2)
                both = f_plus + f_minus
                even = coupling * (both + cubed(3) if nodes == 3 else both)
                odd = coupling * (f_plus - f_minus)
            for c in range(3):
                pulled = even * (centre_ref[target, c, rows] - point[c])
                if nodes > 1:
                    pulled = pulled - odd * extent[c]
                for r in range(0, GROUP, 8):
                    columns[c] = columns[c] + pulled[r : r + 8]
                row_acc[target, c, rows] = sums[c] + pulled
        for c in range(3):
            sums_ref[slot, c : c + 1] = jnp.sum(columns[c], axis=0, keepdims=True)

    high = blocks * width // LANES
    keys = 4 * high
    shift = (blocks * width).bit_length() + 1
    key_ids = lax.broadcasted_iota(jnp.int32, (keys, width), 0).astype(jnp.bfloat16)
    lane_ids = lax.broadcasted_iota(jnp.int32, (LANES, width), 0).astype(jnp.bfloat16)
    zero = jnp.zeros((keys, width), jnp.bfloat16)
    one = jnp.ones((keys, width), jnp.bfloat16)

    def wide(row):
        return jnp.broadcast_to(row, (8, width))

    def narrow(value):
        value = value.astype(jnp.float32)
        return jnp.concatenate([value] * (keys // 8), axis=0).astype(jnp.bfloat16)

    def spread_out(tile, b, slot, result):
        spread = []
        for c in range(3):
            grad = wide(sums_ref[slot, c : c + 1])
            upper = grad.astype(jnp.bfloat16).astype(jnp.float32)
            spread += [narrow(upper), narrow(grad - upper)]
        for half in range(2):
            parts = []
            hots = []
            code = wide(shape_ref[tile, 2 * b + half, 3:4]).astype(jnp.int32)
            for place in (code >> shift, code & ((1 << shift) - 1)):
                mask = key_ids == narrow(place >> 7)
                low = narrow(place & (LANES - 1))
                parts.append(jnp.concatenate([jnp.where(mask, s, zero) for s in spread], axis=0))
                hots.append(
                    jnp.concatenate(
                        [
                            jnp.where(lane_ids[g : g + keys] == low, one, zero)
                            for g in range(0, LANES, keys)
                        ],
                        axis=0,
                    )
                )
            product = lax.dot_general(
                jnp.concatenate(parts, axis=1),
                jnp.concatenate(hots, axis=1),
                (((1,), (1,)), ((), ())),
                preferred_element_type=jnp.float32,
            )
            result = product if result is None else result + product
        return result

    def scatter(tile, places):
        result = None
        for b, slot in places:
            result = spread_out(tile, b, slot, result)
        before = [joined_ref[tile, c] for c in range(3)]
        for c in range(3):
            joined_ref[tile, c] = (
                before[c]
                + result[2 * c * keys : (2 * c + 1) * keys]
                + result[(2 * c + 1) * keys : (2 * c + 2) * keys]
            )

    def scatter_pair(k, slot):
        _, owner, source, _ = read(k)
        scatter(owner, [(source, slot)])

    def two_pairs(nodes):
        def body(step, carry):
            for slot in range(2):
                k = 2 * step + slot
                multiply(k + 1, 1 - slot, nodes)
                scatter_pair(k - 1, 1 - slot)
                one_pair(k, slot, nodes)
            return carry

        return body

    multiply(0, 0, 3)
    lax.fori_loop(0, info_ref[0, 1], two_pairs(3), 0)
    lax.fori_loop(info_ref[0, 1], info_ref[0, 2], two_pairs(2), 0)
    lax.fori_loop(info_ref[0, 2], info_ref[0, 3], two_pairs(1), 0)
    scatter_pair(2 * info_ref[0, 3] - 1, 1)
    for b in range(blocks):
        total = jnp.concatenate(
            [jnp.sum(row_acc[b, c], axis=1, keepdims=True) for c in range(3)]
            + [jnp.zeros((width, 5), jnp.float32)],
            axis=1,
        )
        sums_ref[2 + b] = -total.T
    scatter(me, [(b, 2 + b) for b in range(blocks)])

    def collect(dest, carry):
        for c in range(3):
            total = jnp.zeros((high, LANES), jnp.float32)
            for slot, by in enumerate((0, tiles - 1, 1, tiles - tiles // 2)):
                tile = lax.rem(dest + by, tiles)
                total = total + joined_ref[tile, c, slot * high : (slot + 1) * high]
            part = out_ref.shape[2]
            for f in range(out_ref.shape[1]):
                first = f * part % high
                out_ref[dest, f, :, c * LANES : (c + 1) * LANES] = total[first : first + part]
        return carry

    lax.fori_loop(0, tiles, collect, 0, unroll=min(tiles, 8))


def sum_kernel(got_ref, out_ref):
    out_ref[...] = jnp.sum(got_ref[...], axis=0)


def choice_kernel(side_ref, out_ref):
    out_ref[...] = jnp.broadcast_to(side_ref[0:1, 0:1], out_ref.shape) * 2.0 - 1.0


def last_kernel(choice_ref, mine_ref, other_ref, out_ref):
    part = mine_ref.shape[0]
    even = choice_ref[...] < 0.0
    mine, other = mine_ref[...], other_ref[...]
    halves = (jnp.where(even, mine, other), jnp.where(even, other, mine))
    for i, half in enumerate(halves):
        for r in range(part):
            h = i * part + r
            for c in range(3):
                out_ref[c : c + 1, h * LANES : (h + 1) * LANES] = half[
                    r : r + 1, c * LANES : (c + 1) * LANES
                ]


def per_device(
    panel_geometry,
    adjoint,
    strengths,
    pair_target,
    pair_owner,
    pair_source,
    pair_order,
    pair_count,
    corner_vertex,
):
    tiles = lax.axis_size("tiles")
    far = lax.axis_size("far")
    blocks, _, width = panel_geometry.shape
    high = blocks * width // LANES
    parity = lax.axis_index("far").astype(jnp.int32) & 1
    me = lax.axis_index("tiles").astype(jnp.int32).reshape(1)
    parity = parity.reshape(1)
    swap = [(f ^ 1, f) for f in range(far)]
    smem = pl.BlockSpec(memory_space=SMEM)
    vmem = pl.BlockSpec(memory_space=VMEM)
    params = pltpu.CompilerParams(vmem_limit_bytes=LIMIT)
    geometry = panel_geometry.transpose(1, 0, 2)
    packed = pl.pallas_call(
        pack_kernel,
        out_shape=jax.ShapeDtypeStruct((tiles, blocks, 4, 2 * width), jnp.float32),
        in_specs=[smem] * 2 + [vmem] * 3,
        out_specs=vmem,
    )(me, parity, geometry, strengths, corner_vertex)
    got = lax.all_to_all(packed, "tiles", split_axis=0, concat_axis=0, tiled=True)
    partner = lax.ppermute(adjoint, "far", swap)
    pairs = pair_target.shape[0]
    info = pl.pallas_call(
        lambda *refs: sort_kernel(*refs[:-1], blocks, refs[-1]),
        out_shape=jax.ShapeDtypeStruct((1, -(-(HEAD + pairs // 2 + SPARE + 1) // LANES) * LANES), jnp.int32),
        in_specs=[smem] * 2 + [vmem] * 4 + [smem],
        out_specs=vmem,
        cost_estimate=pl.CostEstimate(flops=4000000, bytes_accessed=900000, transcendentals=0),
    )(
        me,
        parity,
        pair_target.reshape(1, pairs),
        pair_owner.reshape(1, pairs),
        pair_source.reshape(1, pairs),
        pair_order.reshape(1, pairs),
        pair_count,
    )
    centre, left = pl.pallas_call(
        prep_kernel,
        out_shape=(
            jax.ShapeDtypeStruct((blocks, 3, width, width), jnp.float32),
            jax.ShapeDtypeStruct((blocks, width, 56), jnp.bfloat16),
        ),
        compiler_params=params,
        cost_estimate=pl.CostEstimate(flops=4000000, bytes_accessed=900000, transcendentals=0),
    )(geometry, adjoint, partner)
    got, info, left = lax.optimization_barrier((got, info, left))
    other = lax.ppermute(got, "far", swap)
    partial, side = pl.pallas_call(
        pair_kernel,
        out_shape=(
            jax.ShapeDtypeStruct((tiles, far, high // 2, 3 * LANES), jnp.float32),
            jax.ShapeDtypeStruct((8, LANES), jnp.float32),
        ),
        in_specs=[smem] + [vmem] * 4,
        out_specs=(vmem, vmem),
        scratch_shapes=[
            VMEM((2, width, 4 * width), jnp.float32),
            VMEM((blocks, 3, width, width), jnp.float32),
            VMEM((2 + blocks, 8, width), jnp.float32),
            VMEM((tiles, 3, 4 * high, LANES), jnp.float32),
            VMEM((tiles, 2 * blocks, 4, width), jnp.float32),
        ],
        compiler_params=params,
    )(info, centre, left, got, other)
    partial = partial.reshape(tiles * far, high // 2, 3 * LANES)
    shares = lax.all_to_all(partial, ("tiles", "far"), split_axis=0, concat_axis=0, tiled=True)
    choice = pl.pallas_call(
        choice_kernel,
        out_shape=jax.ShapeDtypeStruct((high // 2, 3 * LANES), jnp.float32),
        compiler_params=params,
        cost_estimate=pl.CostEstimate(flops=4000000, bytes_accessed=900000, transcendentals=0),
    )(side)
    mine = pl.pallas_call(
        sum_kernel,
        out_shape=jax.ShapeDtypeStruct((high // 2, 3 * LANES), jnp.float32),
        compiler_params=params,
    )(shares)
    other = lax.ppermute(mine, "far", swap)
    return pl.pallas_call(
        last_kernel,
        out_shape=jax.ShapeDtypeStruct((3, blocks * width), jnp.float32),
        compiler_params=params,
    )(choice, mine, other)


def solution(mesh):
    placed = (
        P("tiles", None, None),
        P("tiles", "far", None),
        P("tiles", "far", None),
        P("tiles"),
        P("tiles", None),
        P("tiles"),
        P("tiles"),
        P("tiles"),
        P("tiles", None, None),
    )
    return jax.shard_map(
        per_device, mesh=mesh, in_specs=placed, out_specs=P(None, "tiles"), check_vma=False
    )
```

```python
import jax
import jax.numpy as jnp
from jax import lax
from jax.experimental import pallas as pl
from jax.experimental.pallas import tpu as pltpu
from jax.sharding import PartitionSpec as P

SMEM = pltpu.SMEM
VMEM = pltpu.VMEM
LANES = 128
HEAD = 5
GROUP = 32
SPARE = 2
LIMIT = 48 * 1024 * 1024


def pack_kernel(me_ref, parity_ref, geom_ref, strength_ref, corner_ref, out_ref):
    tiles, blocks, _, _ = out_ref.shape
    width = strength_ref.shape[2]
    shift = (blocks * width).bit_length() - 1
    me = me_ref[0]
    even = parity_ref[0] == 0
    shapes = []
    for b in range(blocks):
        vertex = corner_ref[b]
        offset = (vertex >> shift) - me
        offset = jnp.where(offset < 0, offset + tiles, offset)
        slot = jnp.where(
            offset == 0,
            0,
            jnp.where(offset == 1, 1, jnp.where(offset == tiles - 1, 2, 3)),
        )
        place = ((slot << shift) + (vertex & ((1 << shift) - 1))).astype(jnp.float32)
        span = float(4 << shift)
        for half in range(2):
            code = place[2 * half : 2 * half + 1] * span + place[2 * half + 1 : 2 * half + 2]
            rows = [geom_ref[3 * half + c, b : b + 1] for c in range(3)] + [code]
            shapes.append(jnp.concatenate(rows, axis=0))
    for b in range(blocks):
        shape = jnp.where(even, shapes[b], shapes[blocks + b])
        block = jnp.concatenate([strength_ref[b].astype(jnp.float32), shape], axis=1)
        for t in range(tiles):
            out_ref[t, b] = block


def split3(value):
    first = value.astype(jnp.bfloat16).astype(jnp.float32)
    rest = value - first
    second = rest.astype(jnp.bfloat16).astype(jnp.float32)
    return first, second, rest - second


def sort_kernel(
    me_ref,
    parity_ref,
    target_ref,
    owner_ref,
    source_ref,
    order_ref,
    count_ref,
    blocks,
    info_ref,
):
    pairs = order_ref.shape[1]
    lanes = info_ref.shape[1]
    bits = (blocks - 1).bit_length()
    parity = parity_ref[0]
    order = order_ref[...]
    place = lax.broadcasted_iota(jnp.int32, (1, pairs), 1)
    live = place < count_ref[0]
    word = (owner_ref[...] << bits | source_ref[...]) << bits | target_ref[...]
    word = (word << 2 | order).astype(jnp.float32)
    key = jnp.where(live, (3 - order) * pairs + place, 3 * pairs + place).astype(jnp.float32)
    across = lax.broadcasted_iota(jnp.int32, (pairs, pairs), 1)
    down = lax.broadcasted_iota(jnp.int32, (pairs, pairs), 0)

    def upright(row):
        spread = jnp.broadcast_to(row, (pairs, pairs))
        return jnp.sum(jnp.where(across == down, spread, 0.0), axis=1, keepdims=True)

    key_down = upright(key)
    rank = jnp.sum(jnp.where(key < key_down, 1.0, 0.0), axis=1, keepdims=True).astype(jnp.int32)
    kept = (rank & 1 == parity) & (rank < count_ref[0])
    at = jnp.where(kept, HEAD + (rank >> 1), -1)
    wide_lane = lax.broadcasted_iota(jnp.int32, (pairs, lanes), 1)
    words = jnp.sum(jnp.where(wide_lane == at, upright(word), 0.0), axis=0, keepdims=True)
    info = words.astype(jnp.int32)
    lane = lax.broadcasted_iota(jnp.int32, (1, lanes), 1)
    info = jnp.where(lane == 0, me_ref[0], jnp.where(lane == 4, parity, info))
    for i in range(3):
        upto = jnp.where(live & (order >= 3 - i), 1.0, 0.0)
        total = jnp.sum(upto, axis=1, keepdims=True).astype(jnp.int32)
        info = jnp.where(lane == i + 1, (((total + 1 - parity) >> 1) + 1) >> 1, info)
    info_ref[...] = info


def prep_kernel(geom_ref, adjoint_ref, partner_ref, centre_ref, left_ref):
    blocks, _, width = adjoint_ref.shape
    for b in range(blocks):
        point = jnp.concatenate([geom_ref[c, b : b + 1] for c in range(3)], axis=0)
        rows = [point, jnp.ones((1, width), jnp.float32)]
        rows += [jnp.sum(point * point, axis=0, keepdims=True)]
        rows += [jnp.zeros((3, width), jnp.float32)]
        x1, x2, x3 = split3(jnp.concatenate(rows, axis=0))
        values = [adjoint_ref[b].astype(jnp.float32), partner_ref[b].astype(jnp.float32)]
        rows = [x1, x1, x1, x2, x2, x3] + values
        left_ref[b] = jnp.concatenate(rows, axis=0).T.astype(jnp.bfloat16)
        for c in range(3):
            centre_ref[b, c] = jnp.broadcast_to(point[c : c + 1], (width, width)).T


def pair_kernel(
    info_ref,
    centre_ref,
    left_ref,
    mine_ref,
    other_ref,
    out_ref,
    side_ref,
    product_ref,
    row_acc,
    sums_ref,
    joined_ref,
    shape_ref,
):
    tiles, blocks, _, _ = mine_ref.shape
    width = centre_ref.shape[3]
    bits = (blocks - 1).bit_length()
    me = info_ref[0, 0]
    even = info_ref[0, 4] == 0
    side_ref[...] = jnp.full(side_ref.shape, info_ref[0, 4].astype(jnp.float32))

    def settle(tile, carry):
        for b in range(blocks):
            mine = mine_ref[tile, b, :, width : 2 * width]
            other = other_ref[tile, b, :, width : 2 * width]
            shape_ref[tile, b] = jnp.where(even, mine, other)
            shape_ref[tile, blocks + b] = jnp.where(even, other, mine)
        return carry

    lax.fori_loop(0, tiles, settle, 0, unroll=min(tiles, 8))
    sums_ref[...] = jnp.zeros(sums_ref.shape, jnp.float32)
    joined_ref[...] = jnp.zeros(joined_ref.shape, jnp.float32)
    row_acc[...] = jnp.zeros(row_acc.shape, jnp.float32)
    blank = jnp.zeros((4, width), jnp.float32)
    row_ids = lax.broadcasted_iota(jnp.int32, (8, width), 0)

    def reach_of(order):
        return 0.25 * jnp.where(
            order == 3, 0.7745966692414834, jnp.where(order == 2, 0.5773502691896258, 0.0)
        )

    def read(k):
        word = info_ref[0, HEAD + k]
        inner = word >> 2
        outer = inner >> bits
        return inner & (blocks - 1), outer >> bits, outer & (blocks - 1), word & 3

    def multiply(k, slot, nodes):
        target, owner, source, order = read(k)
        third = order == 3
        alive = jnp.where(order > 0, 1.0, 0.0).astype(jnp.float32)
        reach = reach_of(order)
        scale_mid = jnp.where(third, (4.0 / 9.0 / 512.0) ** (-2.0 / 3.0), 0.0)
        scale_side = jnp.where(
            third, (5.0 / 18.0 / 512.0) ** (-2.0 / 3.0), (0.5 / 512.0) ** (-2.0 / 3.0)
        )
        floor_mid = jnp.where(third, 0.0625 * (4.0 / 9.0 / 512.0) ** (-2.0 / 3.0), 3.0e38)
        floor_side = 0.0625 * scale_side
        point = shape_ref[owner, 2 * source]
        extent = shape_ref[owner, 2 * source + 1] * reach
        inside = row_ids < 3
        point = jnp.where(inside, jnp.concatenate([point, blank], axis=0), 0.0)
        extent = jnp.where(inside, jnp.concatenate([extent, blank], axis=0), 0.0)
        values = [ref[owner, source, :, 0:width] * alive for ref in (mine_ref, other_ref)]
        empty = jnp.zeros((8, width), jnp.float32)
        quadrature = (
            (point + extent, scale_side, floor_side),
            (point - extent, scale_side, floor_side),
            (point, scale_mid, floor_mid),
        )
        columns = []
        for node, scale, floor in quadrature[:nodes]:
            norm = jnp.sum(node * node, axis=0, keepdims=True) * scale + floor
            rows = jnp.where(
                row_ids == 3,
                norm,
                jnp.where(row_ids == 4, scale, node * (-2.0 * scale)),
            )
            p1, p2, p3 = split3(rows)
            columns.append(jnp.concatenate([p1, p2, p3, p1, p2, p1, empty], axis=0))
        columns.insert(1, jnp.concatenate([empty] * 6 + values, axis=0))
        product_ref[slot, :, 0 : (nodes + 1) * width] = jnp.dot(
            left_ref[target],
            jnp.concatenate(columns, axis=1).astype(jnp.bfloat16),
            preferred_element_type=jnp.float32,
        )

    def one_pair(k, slot, nodes):
        target, owner, source, order = read(k)
        reach = reach_of(order)
        eight = (8, width)
        point = [jnp.broadcast_to(shape_ref[owner, 2 * source, c : c + 1], eight) for c in range(3)]
        extent = [
            jnp.broadcast_to(shape_ref[owner, 2 * source + 1, c : c + 1], eight) * reach
            for c in range(3)
        ]
        point = [jnp.concatenate([row] * (GROUP // 8), axis=0) for row in point]
        extent = [jnp.concatenate([row] * (GROUP // 8), axis=0) for row in extent]
        columns = [jnp.zeros(eight, jnp.float32) for _ in range(3)]
        for start in range(0, width, GROUP):
            rows = slice(start, start + GROUP)
            sums = [row_acc[target, c, rows] for c in range(3)]

            def cubed(part):
                i = lax.rsqrt(product_ref[slot, rows, part * width : (part + 1) * width])
                return i * i * i

            coupling = product_ref[slot, rows, width : 2 * width]
            f_plus = cubed(0)
            if nodes == 1:
                even = (coupling + coupling) * f_plus
            else:
                f_minus = cubed(2)
                both = f_plus + f_minus
                even = coupling * (both + cubed(3) if nodes == 3 else both)
                odd = coupling * (f_plus - f_minus)
            for c in range(3):
                pulled = even * (centre_ref[target, c, rows] - point[c])
                if nodes > 1:
                    pulled = pulled - odd * extent[c]
                for r in range(0, GROUP, 8):
                    columns[c] = columns[c] + pulled[r : r + 8]
                row_acc[target, c, rows] = sums[c] + pulled
        for c in range(3):
            sums_ref[slot, c : c + 1] = jnp.sum(columns[c], axis=0, keepdims=True)

    high = blocks * width // LANES
    keys = 4 * high
    shift = (blocks * width).bit_length() + 1
    key_ids = lax.broadcasted_iota(jnp.int32, (keys, width), 0).astype(jnp.bfloat16)
    lane_ids = lax.broadcasted_iota(jnp.int32, (LANES, width), 0).astype(jnp.bfloat16)
    zero = jnp.zeros((keys, width), jnp.bfloat16)
    one = jnp.ones((keys, width), jnp.bfloat16)

    def wide(row):
        return jnp.broadcast_to(row, (8, width))

    def narrow(value):
        value = value.astype(jnp.float32)
        return jnp.concatenate([value] * (keys // 8), axis=0).astype(jnp.bfloat16)

    def spread_out(tile, b, slot, result):
        spread = []
        for c in range(3):
            grad = wide(sums_ref[slot, c : c + 1])
            upper = grad.astype(jnp.bfloat16).astype(jnp.float32)
            spread += [narrow(upper), narrow(grad - upper)]
        for half in range(2):
            parts = []
            hots = []
            code = wide(shape_ref[tile, 2 * b + half, 3:4]).astype(jnp.int32)
            for place in (code >> shift, code & ((1 << shift) - 1)):
                mask = key_ids == narrow(place >> 7)
                low = narrow(place & (LANES - 1))
                parts.append(jnp.concatenate([jnp.where(mask, s, zero) for s in spread], axis=0))
                hots.append(
                    jnp.concatenate(
                        [
                            jnp.where(lane_ids[g : g + keys] == low, one, zero)
                            for g in range(0, LANES, keys)
                        ],
                        axis=0,
                    )
                )
            product = lax.dot_general(
                jnp.concatenate(parts, axis=1),
                jnp.concatenate(hots, axis=1),
                (((1,), (1,)), ((), ())),
                preferred_element_type=jnp.float32,
            )
            result = product if result is None else result + product
        return result

    def scatter(tile, places):
        result = None
        for b, slot in places:
            result = spread_out(tile, b, slot, result)
        before = [joined_ref[tile, c] for c in range(3)]
        for c in range(3):
            joined_ref[tile, c] = (
                before[c]
                + result[2 * c * keys : (2 * c + 1) * keys]
                + result[(2 * c + 1) * keys : (2 * c + 2) * keys]
            )

    def scatter_pair(k, slot):
        _, owner, source, _ = read(k)
        scatter(owner, [(source, slot)])

    def two_pairs(nodes):
        def body(step, carry):
            for slot in range(2):
                k = 2 * step + slot
                multiply(k + 1, 1 - slot, nodes)
                scatter_pair(k - 1, 1 - slot)
                one_pair(k, slot, nodes)
            return carry

        return body

    multiply(0, 0, 3)
    lax.fori_loop(0, info_ref[0, 1], two_pairs(3), 0)
    lax.fori_loop(info_ref[0, 1], info_ref[0, 2], two_pairs(2), 0)
    lax.fori_loop(info_ref[0, 2], info_ref[0, 3], two_pairs(1), 0)
    scatter_pair(2 * info_ref[0, 3] - 1, 1)
    for b in range(blocks):
        total = jnp.concatenate(
            [jnp.sum(row_acc[b, c], axis=1, keepdims=True) for c in range(3)]
            + [jnp.zeros((width, 5), jnp.float32)],
            axis=1,
        )
        sums_ref[2 + b] = -total.T
    scatter(me, [(b, 2 + b) for b in range(blocks)])

    def collect(dest, carry):
        for c in range(3):
            total = jnp.zeros((high, LANES), jnp.float32)
            for slot, by in enumerate((0, tiles - 1, 1, tiles - tiles // 2)):
                tile = lax.rem(dest + by, tiles)
                total = total + joined_ref[tile, c, slot * high : (slot + 1) * high]
            part = out_ref.shape[2]
            for f in range(out_ref.shape[1]):
                first = f * part % high
                out_ref[dest, f, :, c * LANES : (c + 1) * LANES] = total[first : first + part]
        return carry

    lax.fori_loop(0, tiles, collect, 0, unroll=min(tiles, 8))


def sum_kernel(got_ref, out_ref):
    out_ref[...] = jnp.sum(got_ref[...], axis=0)


def choice_kernel(side_ref, out_ref):
    out_ref[...] = jnp.broadcast_to(side_ref[0:1, 0:1], out_ref.shape) * 2.0 - 1.0


def last_kernel(choice_ref, mine_ref, other_ref, out_ref):
    part = mine_ref.shape[0]
    even = choice_ref[...] < 0.0
    mine, other = mine_ref[...], other_ref[...]
    halves = (jnp.where(even, mine, other), jnp.where(even, other, mine))
    for i, half in enumerate(halves):
        for r in range(part):
            h = i * part + r
            for c in range(3):
                out_ref[c : c + 1, h * LANES : (h + 1) * LANES] = half[
                    r : r + 1, c * LANES : (c + 1) * LANES
                ]


def per_device(
    panel_geometry,
    adjoint,
    strengths,
    pair_target,
    pair_owner,
    pair_source,
    pair_order,
    pair_count,
    corner_vertex,
):
    tiles = lax.axis_size("tiles")
    far = lax.axis_size("far")
    blocks, _, width = panel_geometry.shape
    high = blocks * width // LANES
    parity = lax.axis_index("far").astype(jnp.int32) & 1
    me = lax.axis_index("tiles").astype(jnp.int32).reshape(1)
    parity = parity.reshape(1)
    swap = [(f ^ 1, f) for f in range(far)]
    smem = pl.BlockSpec(memory_space=SMEM)
    vmem = pl.BlockSpec(memory_space=VMEM)
    params = pltpu.CompilerParams(vmem_limit_bytes=LIMIT)
    geometry = panel_geometry.transpose(1, 0, 2)
    packed = pl.pallas_call(
        pack_kernel,
        out_shape=jax.ShapeDtypeStruct((tiles, blocks, 4, 2 * width), jnp.float32),
        in_specs=[smem] * 2 + [vmem] * 3,
        out_specs=vmem,
    )(me, parity, geometry, strengths, corner_vertex)
    got = lax.all_to_all(packed, "tiles", split_axis=0, concat_axis=0, tiled=True)
    partner = lax.ppermute(adjoint, "far", swap)
    pairs = pair_target.shape[0]
    info = pl.pallas_call(
        lambda *refs: sort_kernel(*refs[:-1], blocks, refs[-1]),
        out_shape=jax.ShapeDtypeStruct((1, -(-(HEAD + pairs // 2 + SPARE + 1) // LANES) * LANES), jnp.int32),
        in_specs=[smem] * 2 + [vmem] * 4 + [smem],
        out_specs=vmem,
        cost_estimate=pl.CostEstimate(flops=4000000, bytes_accessed=900000, transcendentals=0),
    )(
        me,
        parity,
        pair_target.reshape(1, pairs),
        pair_owner.reshape(1, pairs),
        pair_source.reshape(1, pairs),
        pair_order.reshape(1, pairs),
        pair_count,
    )
    centre, left = pl.pallas_call(
        prep_kernel,
        out_shape=(
            jax.ShapeDtypeStruct((blocks, 3, width, width), jnp.float32),
            jax.ShapeDtypeStruct((blocks, width, 56), jnp.bfloat16),
        ),
        compiler_params=params,
        cost_estimate=pl.CostEstimate(flops=4000000, bytes_accessed=900000, transcendentals=0),
    )(geometry, adjoint, partner)
    got, info, left = lax.optimization_barrier((got, info, left))
    other = lax.ppermute(got, "far", swap)
    partial, side = pl.pallas_call(
        pair_kernel,
        out_shape=(
            jax.ShapeDtypeStruct((tiles, far, high // 2, 3 * LANES), jnp.float32),
            jax.ShapeDtypeStruct((8, LANES), jnp.float32),
        ),
        in_specs=[smem] + [vmem] * 4,
        out_specs=(vmem, vmem),
        scratch_shapes=[
            VMEM((2, width, 4 * width), jnp.float32),
            VMEM((blocks, 3, width, width), jnp.float32),
            VMEM((2 + blocks, 8, width), jnp.float32),
            VMEM((tiles, 3, 4 * high, LANES), jnp.float32),
            VMEM((tiles, 2 * blocks, 4, width), jnp.float32),
        ],
        compiler_params=params,
    )(info, centre, left, got, other)
    partial = partial.reshape(tiles * far, high // 2, 3 * LANES)
    shares = lax.all_to_all(partial, ("tiles", "far"), split_axis=0, concat_axis=0, tiled=True)
    choice = pl.pallas_call(
        choice_kernel,
        out_shape=jax.ShapeDtypeStruct((high // 2, 3 * LANES), jnp.float32),
        compiler_params=params,
        cost_estimate=pl.CostEstimate(flops=4000000, bytes_accessed=900000, transcendentals=0),
    )(side)
    shares, choice = lax.optimization_barrier((shares, choice))
    mine = pl.pallas_call(
        sum_kernel,
        out_shape=jax.ShapeDtypeStruct((high // 2, 3 * LANES), jnp.float32),
        compiler_params=params,
    )(shares)
    other = lax.ppermute(mine, "far", swap)
    return pl.pallas_call(
        last_kernel,
        out_shape=jax.ShapeDtypeStruct((3, blocks * width), jnp.float32),
        compiler_params=params,
    )(choice, mine, other)


def solution(mesh):
    placed = (
        P("tiles", None, None),
        P("tiles", "far", None),
        P("tiles", "far", None),
        P("tiles"),
        P("tiles", None),
        P("tiles"),
        P("tiles"),
        P("tiles"),
        P("tiles", None, None),
    )
    return jax.shard_map(
        per_device, mesh=mesh, in_specs=placed, out_specs=P(None, "tiles"), check_vma=False
    )
```

```python
import jax
import jax.numpy as jnp
from jax import lax
from jax.experimental import pallas as pl
from jax.experimental.pallas import tpu as pltpu
from jax.sharding import PartitionSpec as P

SMEM = pltpu.SMEM
VMEM = pltpu.VMEM
LANES = 128
HEAD = 5
GROUP = 32
SPARE = 2
LIMIT = 48 * 1024 * 1024


def pack_kernel(me_ref, parity_ref, geom_ref, strength_ref, corner_ref, out_ref):
    tiles, blocks, _, _ = out_ref.shape
    width = strength_ref.shape[2]
    shift = (blocks * width).bit_length() - 1
    me = me_ref[0]
    even = parity_ref[0] == 0
    shapes = []
    for b in range(blocks):
        vertex = corner_ref[b]
        offset = (vertex >> shift) - me
        offset = jnp.where(offset < 0, offset + tiles, offset)
        slot = jnp.where(
            offset == 0,
            0,
            jnp.where(offset == 1, 1, jnp.where(offset == tiles - 1, 2, 3)),
        )
        place = ((slot << shift) + (vertex & ((1 << shift) - 1))).astype(jnp.float32)
        span = float(4 << shift)
        for half in range(2):
            code = place[2 * half : 2 * half + 1] * span + place[2 * half + 1 : 2 * half + 2]
            rows = [geom_ref[3 * half + c, b : b + 1] for c in range(3)] + [code]
            shapes.append(jnp.concatenate(rows, axis=0))
    for b in range(blocks):
        shape = jnp.where(even, shapes[b], shapes[blocks + b])
        block = jnp.concatenate([strength_ref[b].astype(jnp.float32), shape], axis=1)
        for t in range(tiles):
            out_ref[t, b] = block


def split3(value):
    first = value.astype(jnp.bfloat16).astype(jnp.float32)
    rest = value - first
    second = rest.astype(jnp.bfloat16).astype(jnp.float32)
    return first, second, rest - second


def sort_kernel(
    me_ref,
    parity_ref,
    target_ref,
    owner_ref,
    source_ref,
    order_ref,
    count_ref,
    blocks,
    info_ref,
):
    pairs = order_ref.shape[1]
    lanes = info_ref.shape[1]
    bits = (blocks - 1).bit_length()
    parity = parity_ref[0]
    order = order_ref[...]
    place = lax.broadcasted_iota(jnp.int32, (1, pairs), 1)
    live = place < count_ref[0]
    word = (owner_ref[...] << bits | source_ref[...]) << bits | target_ref[...]
    word = (word << 2 | order).astype(jnp.float32)
    key = jnp.where(live, (3 - order) * pairs + place, 3 * pairs + place).astype(jnp.float32)
    across = lax.broadcasted_iota(jnp.int32, (pairs, pairs), 1)
    down = lax.broadcasted_iota(jnp.int32, (pairs, pairs), 0)

    def upright(row):
        spread = jnp.broadcast_to(row, (pairs, pairs))
        return jnp.sum(jnp.where(across == down, spread, 0.0), axis=1, keepdims=True)

    key_down = upright(key)
    rank = jnp.sum(jnp.where(key < key_down, 1.0, 0.0), axis=1, keepdims=True).astype(jnp.int32)
    kept = (rank & 1 == parity) & (rank < count_ref[0])
    at = jnp.where(kept, HEAD + (rank >> 1), -1)
    wide_lane = lax.broadcasted_iota(jnp.int32, (pairs, lanes), 1)
    words = jnp.sum(jnp.where(wide_lane == at, upright(word), 0.0), axis=0, keepdims=True)
    info = words.astype(jnp.int32)
    lane = lax.broadcasted_iota(jnp.int32, (1, lanes), 1)
    info = jnp.where(lane == 0, me_ref[0], jnp.where(lane == 4, parity, info))
    for i in range(3):
        upto = jnp.where(live & (order >= 3 - i), 1.0, 0.0)
        total = jnp.sum(upto, axis=1, keepdims=True).astype(jnp.int32)
        info = jnp.where(lane == i + 1, (((total + 1 - parity) >> 1) + 1) >> 1, info)
    info_ref[...] = info


def prep_kernel(geom_ref, adjoint_ref, partner_ref, centre_ref, left_ref):
    blocks, _, width = adjoint_ref.shape
    for b in range(blocks):
        point = jnp.concatenate([geom_ref[c, b : b + 1] for c in range(3)], axis=0)
        rows = [point, jnp.ones((1, width), jnp.float32)]
        rows += [jnp.sum(point * point, axis=0, keepdims=True)]
        rows += [jnp.zeros((3, width), jnp.float32)]
        x1, x2, x3 = split3(jnp.concatenate(rows, axis=0))
        values = [adjoint_ref[b].astype(jnp.float32), partner_ref[b].astype(jnp.float32)]
        rows = [x1, x1, x1, x2, x2, x3] + values
        left_ref[b] = jnp.concatenate(rows, axis=0).T.astype(jnp.bfloat16)
        for c in range(3):
            centre_ref[b, c] = jnp.broadcast_to(point[c : c + 1], (width, width)).T


def pair_kernel(
    info_ref,
    centre_ref,
    left_ref,
    mine_ref,
    other_ref,
    out_ref,
    product_ref,
    row_acc,
    sums_ref,
    joined_ref,
    shape_ref,
):
    tiles, blocks, _, _ = mine_ref.shape
    width = centre_ref.shape[3]
    bits = (blocks - 1).bit_length()
    me = info_ref[0, 0]
    even = info_ref[0, 4] == 0

    def settle(tile, carry):
        for b in range(blocks):
            mine = mine_ref[tile, b, :, width : 2 * width]
            other = other_ref[tile, b, :, width : 2 * width]
            shape_ref[tile, b] = jnp.where(even, mine, other)
            shape_ref[tile, blocks + b] = jnp.where(even, other, mine)
        return carry

    lax.fori_loop(0, tiles, settle, 0, unroll=min(tiles, 8))
    sums_ref[...] = jnp.zeros(sums_ref.shape, jnp.float32)
    joined_ref[...] = jnp.zeros(joined_ref.shape, jnp.float32)
    row_acc[...] = jnp.zeros(row_acc.shape, jnp.float32)
    blank = jnp.zeros((4, width), jnp.float32)
    row_ids = lax.broadcasted_iota(jnp.int32, (8, width), 0)

    def reach_of(order):
        return 0.25 * jnp.where(
            order == 3, 0.7745966692414834, jnp.where(order == 2, 0.5773502691896258, 0.0)
        )

    def read(k):
        word = info_ref[0, HEAD + k]
        inner = word >> 2
        outer = inner >> bits
        return inner & (blocks - 1), outer >> bits, outer & (blocks - 1), word & 3

    def multiply(k, slot, nodes):
        target, owner, source, order = read(k)
        third = order == 3
        alive = jnp.where(order > 0, 1.0, 0.0).astype(jnp.float32)
        reach = reach_of(order)
        scale_mid = jnp.where(third, (4.0 / 9.0 / 512.0) ** (-2.0 / 3.0), 0.0)
        scale_side = jnp.where(
            third, (5.0 / 18.0 / 512.0) ** (-2.0 / 3.0), (0.5 / 512.0) ** (-2.0 / 3.0)
        )
        floor_mid = jnp.where(third, 0.0625 * (4.0 / 9.0 / 512.0) ** (-2.0 / 3.0), 3.0e38)
        floor_side = 0.0625 * scale_side
        point = shape_ref[owner, 2 * source]
        extent = shape_ref[owner, 2 * source + 1] * reach
        inside = row_ids < 3
        point = jnp.where(inside, jnp.concatenate([point, blank], axis=0), 0.0)
        extent = jnp.where(inside, jnp.concatenate([extent, blank], axis=0), 0.0)
        values = [ref[owner, source, :, 0:width] * alive for ref in (mine_ref, other_ref)]
        empty = jnp.zeros((8, width), jnp.float32)
        quadrature = (
            (point + extent, scale_side, floor_side),
            (point - extent, scale_side, floor_side),
            (point, scale_mid, floor_mid),
        )
        columns = []
        for node, scale, floor in quadrature[:nodes]:
            norm = jnp.sum(node * node, axis=0, keepdims=True) * scale + floor
            rows = jnp.where(
                row_ids == 3,
                norm,
                jnp.where(row_ids == 4, scale, node * (-2.0 * scale)),
            )
            p1, p2, p3 = split3(rows)
            columns.append(jnp.concatenate([p1, p2, p3, p1, p2, p1, empty], axis=0))
        columns.insert(1, jnp.concatenate([empty] * 6 + values, axis=0))
        product_ref[slot, :, 0 : (nodes + 1) * width] = jnp.dot(
            left_ref[target],
            jnp.concatenate(columns, axis=1).astype(jnp.bfloat16),
            preferred_element_type=jnp.float32,
        )

    def one_pair(k, slot, nodes):
        target, owner, source, order = read(k)
        reach = reach_of(order)
        eight = (8, width)
        point = [jnp.broadcast_to(shape_ref[owner, 2 * source, c : c + 1], eight) for c in range(3)]
        extent = [
            jnp.broadcast_to(shape_ref[owner, 2 * source + 1, c : c + 1], eight) * reach
            for c in range(3)
        ]
        point = [jnp.concatenate([row] * (GROUP // 8), axis=0) for row in point]
        extent = [jnp.concatenate([row] * (GROUP // 8), axis=0) for row in extent]
        columns = [jnp.zeros(eight, jnp.float32) for _ in range(3)]
        for start in range(0, width, GROUP):
            rows = slice(start, start + GROUP)
            sums = [row_acc[target, c, rows] for c in range(3)]

            def cubed(part):
                i = lax.rsqrt(product_ref[slot, rows, part * width : (part + 1) * width])
                return i * i * i

            coupling = product_ref[slot, rows, width : 2 * width]
            f_plus = cubed(0)
            if nodes == 1:
                even = (coupling + coupling) * f_plus
            else:
                f_minus = cubed(2)
                both = f_plus + f_minus
                even = coupling * (both + cubed(3) if nodes == 3 else both)
                odd = coupling * (f_plus - f_minus)
            for c in range(3):
                pulled = even * (centre_ref[target, c, rows] - point[c])
                if nodes > 1:
                    pulled = pulled - odd * extent[c]
                for r in range(0, GROUP, 8):
                    columns[c] = columns[c] + pulled[r : r + 8]
                row_acc[target, c, rows] = sums[c] + pulled
        for c in range(3):
            sums_ref[slot, c : c + 1] = jnp.sum(columns[c], axis=0, keepdims=True)

    high = blocks * width // LANES
    keys = 4 * high
    shift = (blocks * width).bit_length() + 1
    key_ids = lax.broadcasted_iota(jnp.int32, (keys, width), 0).astype(jnp.bfloat16)
    lane_ids = lax.broadcasted_iota(jnp.int32, (LANES, width), 0).astype(jnp.bfloat16)
    zero = jnp.zeros((keys, width), jnp.bfloat16)
    one = jnp.ones((keys, width), jnp.bfloat16)

    def wide(row):
        return jnp.broadcast_to(row, (8, width))

    def narrow(value):
        value = value.astype(jnp.float32)
        return jnp.concatenate([value] * (keys // 8), axis=0).astype(jnp.bfloat16)

    def spread_out(tile, b, slot, result):
        spread = []
        for c in range(3):
            grad = wide(sums_ref[slot, c : c + 1])
            upper = grad.astype(jnp.bfloat16).astype(jnp.float32)
            spread += [narrow(upper), narrow(grad - upper)]
        for half in range(2):
            parts = []
            hots = []
            code = wide(shape_ref[tile, 2 * b + half, 3:4]).astype(jnp.int32)
            for place in (code >> shift, code & ((1 << shift) - 1)):
                mask = key_ids == narrow(place >> 7)
                low = narrow(place & (LANES - 1))
                parts.append(jnp.concatenate([jnp.where(mask, s, zero) for s in spread], axis=0))
                hots.append(
                    jnp.concatenate(
                        [
                            jnp.where(lane_ids[g : g + keys] == low, one, zero)
                            for g in range(0, LANES, keys)
                        ],
                        axis=0,
                    )
                )
            product = lax.dot_general(
                jnp.concatenate(parts, axis=1),
                jnp.concatenate(hots, axis=1),
                (((1,), (1,)), ((), ())),
                preferred_element_type=jnp.float32,
            )
            result = product if result is None else result + product
        return result

    def scatter(tile, places):
        result = None
        for b, slot in places:
            result = spread_out(tile, b, slot, result)
        before = [joined_ref[tile, c] for c in range(3)]
        for c in range(3):
            joined_ref[tile, c] = (
                before[c]
                + result[2 * c * keys : (2 * c + 1) * keys]
                + result[(2 * c + 1) * keys : (2 * c + 2) * keys]
            )

    def scatter_pair(k, slot):
        _, owner, source, _ = read(k)
        scatter(owner, [(source, slot)])

    def two_pairs(nodes):
        def body(step, carry):
            for slot in range(2):
                k = 2 * step + slot
                multiply(k + 1, 1 - slot, nodes)
                scatter_pair(k - 1, 1 - slot)
                one_pair(k, slot, nodes)
            return carry

        return body

    multiply(0, 0, 3)
    lax.fori_loop(0, info_ref[0, 3], two_pairs(3), 0)
    scatter_pair(2 * info_ref[0, 3] - 1, 1)
    for b in range(blocks):
        total = jnp.concatenate(
            [jnp.sum(row_acc[b, c], axis=1, keepdims=True) for c in range(3)]
            + [jnp.zeros((width, 5), jnp.float32)],
            axis=1,
        )
        sums_ref[2 + b] = -total.T
    scatter(me, [(b, 2 + b) for b in range(blocks)])

    def collect(dest, carry):
        for c in range(3):
            total = jnp.zeros((high, LANES), jnp.float32)
            for slot, by in enumerate((0, tiles - 1, 1, tiles - tiles // 2)):
                tile = lax.rem(dest + by, tiles)
                total = total + joined_ref[tile, c, slot * high : (slot + 1) * high]
            part = out_ref.shape[2]
            for f in range(out_ref.shape[1]):
                first = f * part % high
                out_ref[dest, f, :, c * LANES : (c + 1) * LANES] = total[first : first + part]
        return carry

    lax.fori_loop(0, tiles, collect, 0, unroll=min(tiles, 8))


def sum_kernel(got_ref, out_ref):
    out_ref[...] = jnp.sum(got_ref[...], axis=0)


def last_kernel(parity_ref, mine_ref, other_ref, out_ref):
    part = mine_ref.shape[0]
    even = parity_ref[0] == 0
    mine, other = mine_ref[...], other_ref[...]
    halves = (jnp.where(even, mine, other), jnp.where(even, other, mine))
    for i, half in enumerate(halves):
        for r in range(part):
            h = i * part + r
            for c in range(3):
                out_ref[c : c + 1, h * LANES : (h + 1) * LANES] = half[
                    r : r + 1, c * LANES : (c + 1) * LANES
                ]


def per_device(
    panel_geometry,
    adjoint,
    strengths,
    pair_target,
    pair_owner,
    pair_source,
    pair_order,
    pair_count,
    corner_vertex,
):
    tiles = lax.axis_size("tiles")
    far = lax.axis_size("far")
    blocks, _, width = panel_geometry.shape
    high = blocks * width // LANES
    parity = lax.axis_index("far").astype(jnp.int32) & 1
    me = lax.axis_index("tiles").astype(jnp.int32).reshape(1)
    parity = parity.reshape(1)
    swap = [(f ^ 1, f) for f in range(far)]
    smem = pl.BlockSpec(memory_space=SMEM)
    vmem = pl.BlockSpec(memory_space=VMEM)
    params = pltpu.CompilerParams(vmem_limit_bytes=LIMIT)
    geometry = panel_geometry.transpose(1, 0, 2)
    packed = pl.pallas_call(
        pack_kernel,
        out_shape=jax.ShapeDtypeStruct((tiles, blocks, 4, 2 * width), jnp.float32),
        in_specs=[smem] * 2 + [vmem] * 3,
        out_specs=vmem,
    )(me, parity, geometry, strengths, corner_vertex)
    got = lax.all_to_all(packed, "tiles", split_axis=0, concat_axis=0, tiled=True)
    partner = lax.ppermute(adjoint, "far", swap)
    pairs = pair_target.shape[0]
    info = pl.pallas_call(
        lambda *refs: sort_kernel(*refs[:-1], blocks, refs[-1]),
        out_shape=jax.ShapeDtypeStruct((1, -(-(HEAD + pairs // 2 + SPARE + 1) // LANES) * LANES), jnp.int32),
        in_specs=[smem] * 2 + [vmem] * 4 + [smem],
        out_specs=vmem,
        cost_estimate=pl.CostEstimate(flops=4000000, bytes_accessed=900000, transcendentals=0),
    )(
        me,
        parity,
        pair_target.reshape(1, pairs),
        pair_owner.reshape(1, pairs),
        pair_source.reshape(1, pairs),
        pair_order.reshape(1, pairs),
        pair_count,
    )
    centre, left = pl.pallas_call(
        prep_kernel,
        out_shape=(
            jax.ShapeDtypeStruct((blocks, 3, width, width), jnp.float32),
            jax.ShapeDtypeStruct((blocks, width, 56), jnp.bfloat16),
        ),
        compiler_params=params,
        cost_estimate=pl.CostEstimate(flops=4000000, bytes_accessed=900000, transcendentals=0),
    )(geometry, adjoint, partner)
    got, info, left = lax.optimization_barrier((got, info, left))
    other = lax.ppermute(got, "far", swap)
    partial = pl.pallas_call(
        pair_kernel,
        out_shape=jax.ShapeDtypeStruct((tiles, far, high // 2, 3 * LANES), jnp.float32),
        in_specs=[smem] + [vmem] * 4,
        out_specs=vmem,
        scratch_shapes=[
            VMEM((2, width, 4 * width), jnp.float32),
            VMEM((blocks, 3, width, width), jnp.float32),
            VMEM((2 + blocks, 8, width), jnp.float32),
            VMEM((tiles, 3, 4 * high, LANES), jnp.float32),
            VMEM((tiles, 2 * blocks, 4, width), jnp.float32),
        ],
        compiler_params=params,
    )(info, centre, left, got, other)
    partial = partial.reshape(tiles * far, high // 2, 3 * LANES)
    shares = lax.all_to_all(partial, ("tiles", "far"), split_axis=0, concat_axis=0, tiled=True)
    mine = pl.pallas_call(
        sum_kernel,
        out_shape=jax.ShapeDtypeStruct((high // 2, 3 * LANES), jnp.float32),
        compiler_params=params,
    )(shares)
    other = lax.ppermute(mine, "far", swap)
    return pl.pallas_call(
        last_kernel,
        out_shape=jax.ShapeDtypeStruct((3, blocks * width), jnp.float32),
        in_specs=[smem, vmem, vmem],
        out_specs=vmem,
        compiler_params=params,
    )(parity, mine, other)


def solution(mesh):
    placed = (
        P("tiles", None, None),
        P("tiles", "far", None),
        P("tiles", "far", None),
        P("tiles"),
        P("tiles", None),
        P("tiles"),
        P("tiles"),
        P("tiles"),
        P("tiles", None, None),
    )
    return jax.shard_map(
        per_device, mesh=mesh, in_specs=placed, out_specs=P(None, "tiles"), check_vma=False
    )
```

```python
import functools

import jax
import jax.numpy as jnp
from jax import lax
from jax.experimental import pallas as pl
from jax.experimental.pallas import tpu as pltpu
from jax.sharding import PartitionSpec as P

SMEM = pltpu.SMEM
VMEM = pltpu.VMEM
LANES = 128
HEAD = 5
GROUP = 32
SPARE = 2
LIMIT = 48 * 1024 * 1024


def pack_kernel(me_ref, parity_ref, geom_ref, strength_ref, corner_ref, out_ref):
    tiles, blocks, _, _ = out_ref.shape
    width = strength_ref.shape[2]
    shift = (blocks * width).bit_length() - 1
    me = me_ref[0]
    even = parity_ref[0] == 0
    shapes = []
    for b in range(blocks):
        vertex = corner_ref[b]
        offset = (vertex >> shift) - me
        offset = jnp.where(offset < 0, offset + tiles, offset)
        slot = jnp.where(
            offset == 0,
            0,
            jnp.where(offset == 1, 1, jnp.where(offset == tiles - 1, 2, 3)),
        )
        place = ((slot << shift) + (vertex & ((1 << shift) - 1))).astype(jnp.float32)
        span = float(4 << shift)
        for half in range(2):
            code = place[2 * half : 2 * half + 1] * span + place[2 * half + 1 : 2 * half + 2]
            rows = [geom_ref[3 * half + c, b : b + 1] for c in range(3)] + [code]
            shapes.append(jnp.concatenate(rows, axis=0))
    for b in range(blocks):
        shape = jnp.where(even, shapes[b], shapes[blocks + b])
        block = jnp.concatenate([strength_ref[b].astype(jnp.float32), shape], axis=1)
        for t in range(tiles):
            out_ref[t, b] = block


def split3(value):
    first = value.astype(jnp.bfloat16).astype(jnp.float32)
    rest = value - first
    second = rest.astype(jnp.bfloat16).astype(jnp.float32)
    return first, second, rest - second


def sort_kernel(
    me_ref,
    parity_ref,
    target_ref,
    owner_ref,
    source_ref,
    order_ref,
    count_ref,
    blocks,
    info_ref,
):
    pairs = order_ref.shape[1]
    lanes = info_ref.shape[1]
    bits = (blocks - 1).bit_length()
    parity = parity_ref[0]
    order = order_ref[...]
    place = lax.broadcasted_iota(jnp.int32, (1, pairs), 1)
    live = place < count_ref[0]
    word = (owner_ref[...] << bits | source_ref[...]) << bits | target_ref[...]
    word = (word << 2 | order).astype(jnp.float32)
    key = jnp.where(live, (3 - order) * pairs + place, 3 * pairs + place).astype(jnp.float32)
    across = lax.broadcasted_iota(jnp.int32, (pairs, pairs), 1)
    down = lax.broadcasted_iota(jnp.int32, (pairs, pairs), 0)

    def upright(row):
        spread = jnp.broadcast_to(row, (pairs, pairs))
        return jnp.sum(jnp.where(across == down, spread, 0.0), axis=1, keepdims=True)

    key_down = upright(key)
    rank = jnp.sum(jnp.where(key < key_down, 1.0, 0.0), axis=1, keepdims=True).astype(jnp.int32)
    kept = (rank & 1 == parity) & (rank < count_ref[0])
    at = jnp.where(kept, HEAD + (rank >> 1), -1)
    wide_lane = lax.broadcasted_iota(jnp.int32, (pairs, lanes), 1)
    words = jnp.sum(jnp.where(wide_lane == at, upright(word), 0.0), axis=0, keepdims=True)
    info = words.astype(jnp.int32)
    lane = lax.broadcasted_iota(jnp.int32, (1, lanes), 1)
    info = jnp.where(lane == 0, me_ref[0], jnp.where(lane == 4, parity, info))
    for i in range(3):
        upto = jnp.where(live & (order >= 3 - i), 1.0, 0.0)
        total = jnp.sum(upto, axis=1, keepdims=True).astype(jnp.int32)
        info = jnp.where(lane == i + 1, (((total + 1 - parity) >> 1) + 1) >> 1, info)
    info_ref[...] = info


def prep_kernel(geom_ref, adjoint_ref, partner_ref, centre_ref, left_ref):
    blocks, _, width = adjoint_ref.shape
    for b in range(blocks):
        point = jnp.concatenate([geom_ref[c, b : b + 1] for c in range(3)], axis=0)
        rows = [point, jnp.ones((1, width), jnp.float32)]
        rows += [jnp.sum(point * point, axis=0, keepdims=True)]
        rows += [jnp.zeros((3, width), jnp.float32)]
        x1, x2, x3 = split3(jnp.concatenate(rows, axis=0))
        values = [adjoint_ref[b].astype(jnp.float32), partner_ref[b].astype(jnp.float32)]
        rows = [x1, x1, x1, x2, x2, x3] + values
        left_ref[b] = jnp.concatenate(rows, axis=0).T.astype(jnp.bfloat16)
        for c in range(3):
            centre_ref[b, c] = jnp.broadcast_to(point[c : c + 1], (width, width)).T


def pair_kernel(
    info_ref,
    centre_ref,
    left_ref,
    mine_ref,
    other_ref,
    out_ref,
    product_ref,
    row_acc,
    sums_ref,
    joined_ref,
    shape_ref,
):
    tiles, blocks, _, _ = mine_ref.shape
    width = centre_ref.shape[3]
    bits = (blocks - 1).bit_length()
    me = info_ref[0, 0]
    even = info_ref[0, 4] == 0

    def settle(tile, carry):
        for b in range(blocks):
            mine = mine_ref[tile, b, :, width : 2 * width]
            other = other_ref[tile, b, :, width : 2 * width]
            shape_ref[tile, b] = jnp.where(even, mine, other)
            shape_ref[tile, blocks + b] = jnp.where(even, other, mine)
        return carry

    lax.fori_loop(0, tiles, settle, 0, unroll=min(tiles, 8))
    sums_ref[...] = jnp.zeros(sums_ref.shape, jnp.float32)
    joined_ref[...] = jnp.zeros(joined_ref.shape, jnp.float32)
    row_acc[...] = jnp.zeros(row_acc.shape, jnp.float32)
    blank = jnp.zeros((4, width), jnp.float32)
    row_ids = lax.broadcasted_iota(jnp.int32, (8, width), 0)

    def reach_of(order):
        return 0.25 * jnp.where(
            order == 3, 0.7745966692414834, jnp.where(order == 2, 0.5773502691896258, 0.0)
        )

    def read(k):
        word = info_ref[0, HEAD + k]
        inner = word >> 2
        outer = inner >> bits
        return inner & (blocks - 1), outer >> bits, outer & (blocks - 1), word & 3

    def multiply(k, slot, nodes):
        target, owner, source, order = read(k)
        third = order == 3
        alive = jnp.where(order > 0, 1.0, 0.0).astype(jnp.float32)
        reach = reach_of(order)
        scale_mid = jnp.where(third, (4.0 / 9.0 / 512.0) ** (-2.0 / 3.0), 0.0)
        scale_side = jnp.where(
            third, (5.0 / 18.0 / 512.0) ** (-2.0 / 3.0), (0.5 / 512.0) ** (-2.0 / 3.0)
        )
        floor_mid = jnp.where(third, 0.0625 * (4.0 / 9.0 / 512.0) ** (-2.0 / 3.0), 3.0e38)
        floor_side = 0.0625 * scale_side
        point = shape_ref[owner, 2 * source]
        extent = shape_ref[owner, 2 * source + 1] * reach
        inside = row_ids < 3
        point = jnp.where(inside, jnp.concatenate([point, blank], axis=0), 0.0)
        extent = jnp.where(inside, jnp.concatenate([extent, blank], axis=0), 0.0)
        values = [ref[owner, source, :, 0:width] * alive for ref in (mine_ref, other_ref)]
        empty = jnp.zeros((8, width), jnp.float32)
        quadrature = (
            (point + extent, scale_side, floor_side),
            (point - extent, scale_side, floor_side),
            (point, scale_mid, floor_mid),
        )
        columns = []
        for node, scale, floor in quadrature[:nodes]:
            norm = jnp.sum(node * node, axis=0, keepdims=True) * scale + floor
            rows = jnp.where(
                row_ids == 3,
                norm,
                jnp.where(row_ids == 4, scale, node * (-2.0 * scale)),
            )
            p1, p2, p3 = split3(rows)
            columns.append(jnp.concatenate([p1, p2, p3, p1, p2, p1, empty], axis=0))
        columns.insert(1, jnp.concatenate([empty] * 6 + values, axis=0))
        product_ref[slot, :, 0 : (nodes + 1) * width] = jnp.dot(
            left_ref[target],
            jnp.concatenate(columns, axis=1).astype(jnp.bfloat16),
            preferred_element_type=jnp.float32,
        )

    def one_pair(k, slot, nodes):
        target, owner, source, order = read(k)
        reach = reach_of(order)
        eight = (8, width)
        point = [jnp.broadcast_to(shape_ref[owner, 2 * source, c : c + 1], eight) for c in range(3)]
        extent = [
            jnp.broadcast_to(shape_ref[owner, 2 * source + 1, c : c + 1], eight) * reach
            for c in range(3)
        ]
        point = [jnp.concatenate([row] * (GROUP // 8), axis=0) for row in point]
        extent = [jnp.concatenate([row] * (GROUP // 8), axis=0) for row in extent]
        columns = [jnp.zeros(eight, jnp.float32) for _ in range(3)]
        for start in range(0, width, GROUP):
            rows = slice(start, start + GROUP)
            sums = [row_acc[target, c, rows] for c in range(3)]

            def cubed(part):
                i = lax.rsqrt(product_ref[slot, rows, part * width : (part + 1) * width])
                return i * i * i

            coupling = product_ref[slot, rows, width : 2 * width]
            f_plus = cubed(0)
            if nodes == 1:
                even = (coupling + coupling) * f_plus
            else:
                f_minus = cubed(2)
                both = f_plus + f_minus
                even = coupling * (both + cubed(3) if nodes == 3 else both)
                odd = coupling * (f_plus - f_minus)
            for c in range(3):
                pulled = even * (centre_ref[target, c, rows] - point[c])
                if nodes > 1:
                    pulled = pulled - odd * extent[c]
                for r in range(0, GROUP, 8):
                    columns[c] = columns[c] + pulled[r : r + 8]
                row_acc[target, c, rows] = sums[c] + pulled
        for c in range(3):
            sums_ref[slot, c : c + 1] = jnp.sum(columns[c], axis=0, keepdims=True)

    high = blocks * width // LANES
    keys = 4 * high
    shift = (blocks * width).bit_length() + 1
    key_ids = lax.broadcasted_iota(jnp.int32, (keys, width), 0).astype(jnp.bfloat16)
    lane_ids = lax.broadcasted_iota(jnp.int32, (LANES, width), 0).astype(jnp.bfloat16)
    zero = jnp.zeros((keys, width), jnp.bfloat16)
    one = jnp.ones((keys, width), jnp.bfloat16)

    def wide(row):
        return jnp.broadcast_to(row, (8, width))

    def narrow(value):
        value = value.astype(jnp.float32)
        return jnp.concatenate([value] * (keys // 8), axis=0).astype(jnp.bfloat16)

    def spread_out(tile, b, slot, result):
        spread = []
        for c in range(3):
            grad = wide(sums_ref[slot, c : c + 1])
            upper = grad.astype(jnp.bfloat16).astype(jnp.float32)
            spread += [narrow(upper), narrow(grad - upper)]
        for half in range(2):
            parts = []
            hots = []
            code = wide(shape_ref[tile, 2 * b + half, 3:4]).astype(jnp.int32)
            for place in (code >> shift, code & ((1 << shift) - 1)):
                mask = key_ids == narrow(place >> 7)
                low = narrow(place & (LANES - 1))
                parts.append(jnp.concatenate([jnp.where(mask, s, zero) for s in spread], axis=0))
                hots.append(
                    jnp.concatenate(
                        [
                            jnp.where(lane_ids[g : g + keys] == low, one, zero)
                            for g in range(0, LANES, keys)
                        ],
                        axis=0,
                    )
                )
            product = lax.dot_general(
                jnp.concatenate(parts, axis=1),
                jnp.concatenate(hots, axis=1),
                (((1,), (1,)), ((), ())),
                preferred_element_type=jnp.float32,
            )
            result = product if result is None else result + product
        return result

    def gather_up(places):
        result = None
        for tile, b, slot in places:
            result = spread_out(tile, b, slot, result)
        return result

    def add_up(tile, result):
        before = [joined_ref[tile, c] for c in range(3)]
        for c in range(3):
            joined_ref[tile, c] = (
                before[c]
                + result[2 * c * keys : (2 * c + 1) * keys]
                + result[(2 * c + 1) * keys : (2 * c + 2) * keys]
            )

    def scatter_pair(k, slot, work):
        _, owner, source, _ = read(k)
        result = gather_up([(owner, source, slot)])
        work()
        add_up(owner, result)

    def two_pairs(nodes):
        def body(step, carry):
            for slot in range(2):
                k = 2 * step + slot
                multiply(k + 1, 1 - slot, nodes)
                scatter_pair(k - 1, 1 - slot, functools.partial(one_pair, k, slot, nodes))
            return carry

        return body

    multiply(0, 0, 3)
    lax.fori_loop(0, info_ref[0, 1], two_pairs(3), 0)
    lax.fori_loop(info_ref[0, 1], info_ref[0, 2], two_pairs(2), 0)
    lax.fori_loop(info_ref[0, 2], info_ref[0, 3], two_pairs(1), 0)
    scatter_pair(2 * info_ref[0, 3] - 1, 1, lambda: None)
    for b in range(blocks):
        total = jnp.concatenate(
            [jnp.sum(row_acc[b, c], axis=1, keepdims=True) for c in range(3)]
            + [jnp.zeros((width, 5), jnp.float32)],
            axis=1,
        )
        sums_ref[2 + b] = -total.T
    add_up(me, gather_up([(me, b, 2 + b) for b in range(blocks)]))

    def collect(dest, carry):
        for c in range(3):
            total = jnp.zeros((high, LANES), jnp.float32)
            for slot, by in enumerate((0, tiles - 1, 1, tiles - tiles // 2)):
                tile = lax.rem(dest + by, tiles)
                total = total + joined_ref[tile, c, slot * high : (slot + 1) * high]
            part = out_ref.shape[2]
            for f in range(out_ref.shape[1]):
                first = f * part % high
                out_ref[dest, f, :, c * LANES : (c + 1) * LANES] = total[first : first + part]
        return carry

    lax.fori_loop(0, tiles, collect, 0, unroll=min(tiles, 8))


def sum_kernel(got_ref, out_ref):
    out_ref[...] = jnp.sum(got_ref[...], axis=0)


def last_kernel(parity_ref, mine_ref, other_ref, out_ref):
    part = mine_ref.shape[0]
    even = parity_ref[0] == 0
    mine, other = mine_ref[...], other_ref[...]
    halves = (jnp.where(even, mine, other), jnp.where(even, other, mine))
    for i, half in enumerate(halves):
        for r in range(part):
            h = i * part + r
            for c in range(3):
                out_ref[c : c + 1, h * LANES : (h + 1) * LANES] = half[
                    r : r + 1, c * LANES : (c + 1) * LANES
                ]


def per_device(
    panel_geometry,
    adjoint,
    strengths,
    pair_target,
    pair_owner,
    pair_source,
    pair_order,
    pair_count,
    corner_vertex,
):
    tiles = lax.axis_size("tiles")
    far = lax.axis_size("far")
    blocks, _, width = panel_geometry.shape
    high = blocks * width // LANES
    parity = lax.axis_index("far").astype(jnp.int32) & 1
    me = lax.axis_index("tiles").astype(jnp.int32).reshape(1)
    parity = parity.reshape(1)
    swap = [(f ^ 1, f) for f in range(far)]
    smem = pl.BlockSpec(memory_space=SMEM)
    vmem = pl.BlockSpec(memory_space=VMEM)
    params = pltpu.CompilerParams(vmem_limit_bytes=LIMIT)
    geometry = panel_geometry.transpose(1, 0, 2)
    packed = pl.pallas_call(
        pack_kernel,
        out_shape=jax.ShapeDtypeStruct((tiles, blocks, 4, 2 * width), jnp.float32),
        in_specs=[smem] * 2 + [vmem] * 3,
        out_specs=vmem,
    )(me, parity, geometry, strengths, corner_vertex)
    got = lax.all_to_all(packed, "tiles", split_axis=0, concat_axis=0, tiled=True)
    partner = lax.ppermute(adjoint, "far", swap)
    pairs = pair_target.shape[0]
    info = pl.pallas_call(
        lambda *refs: sort_kernel(*refs[:-1], blocks, refs[-1]),
        out_shape=jax.ShapeDtypeStruct((1, -(-(HEAD + pairs // 2 + SPARE + 1) // LANES) * LANES), jnp.int32),
        in_specs=[smem] * 2 + [vmem] * 4 + [smem],
        out_specs=vmem,
        cost_estimate=pl.CostEstimate(flops=4000000, bytes_accessed=900000, transcendentals=0),
    )(
        me,
        parity,
        pair_target.reshape(1, pairs),
        pair_owner.reshape(1, pairs),
        pair_source.reshape(1, pairs),
        pair_order.reshape(1, pairs),
        pair_count,
    )
    centre, left = pl.pallas_call(
        prep_kernel,
        out_shape=(
            jax.ShapeDtypeStruct((blocks, 3, width, width), jnp.float32),
            jax.ShapeDtypeStruct((blocks, width, 56), jnp.bfloat16),
        ),
        compiler_params=params,
        cost_estimate=pl.CostEstimate(flops=4000000, bytes_accessed=900000, transcendentals=0),
    )(geometry, adjoint, partner)
    got, info, left = lax.optimization_barrier((got, info, left))
    other = lax.ppermute(got, "far", swap)
    partial = pl.pallas_call(
        pair_kernel,
        out_shape=jax.ShapeDtypeStruct((tiles, far, high // 2, 3 * LANES), jnp.float32),
        in_specs=[smem] + [vmem] * 4,
        out_specs=vmem,
        scratch_shapes=[
            VMEM((2, width, 4 * width), jnp.float32),
            VMEM((blocks, 3, width, width), jnp.float32),
            VMEM((2 + blocks, 8, width), jnp.float32),
            VMEM((tiles, 3, 4 * high, LANES), jnp.float32),
            VMEM((tiles, 2 * blocks, 4, width), jnp.float32),
        ],
        compiler_params=params,
    )(info, centre, left, got, other)
    partial = partial.reshape(tiles * far, high // 2, 3 * LANES)
    shares = lax.all_to_all(partial, ("tiles", "far"), split_axis=0, concat_axis=0, tiled=True)
    mine = pl.pallas_call(
        sum_kernel,
        out_shape=jax.ShapeDtypeStruct((high // 2, 3 * LANES), jnp.float32),
        compiler_params=params,
    )(shares)
    other = lax.ppermute(mine, "far", swap)
    return pl.pallas_call(
        last_kernel,
        out_shape=jax.ShapeDtypeStruct((3, blocks * width), jnp.float32),
        in_specs=[smem, vmem, vmem],
        out_specs=vmem,
        compiler_params=params,
    )(parity, mine, other)


def solution(mesh):
    placed = (
        P("tiles", None, None),
        P("tiles", "far", None),
        P("tiles", "far", None),
        P("tiles"),
        P("tiles", None),
        P("tiles"),
        P("tiles"),
        P("tiles"),
        P("tiles", None, None),
    )
    return jax.shard_map(
        per_device, mesh=mesh, in_specs=placed, out_specs=P(None, "tiles"), check_vma=False
    )
```
